32 devices in a mesh: head: 2 (over y), blk: 16 (over z, x, core).
Axes of the slice: x: 2, y: 2, z: 4, core: 2. Of those that a mesh axis runs over, the one named last changes fastest.
Arguments:
- hidden_in: float32 [128, 1024], P('blk'), may hold values from -41 to 41
- attention_gain: float32 [1024], replicated, may hold values from 0.1 to 1.9
- mlp_gain: float32 [1024], replicated, may hold values from 0.1 to 1.9
- qkv_weight: bfloat16 [3, 1024, 1024], P(None, None, 'head'), may hold values from -1 to 1
- out_weight: bfloat16 [1024, 1024], P('head'), may hold values from -0.1875 to 0.1875
- up_weight: bfloat16 [1024, 4096], P(None, 'head'), may hold values from -0.1875 to 0.1875
- down_weight: bfloat16 [4096, 1024], P('head'), may hold values from -0.09375 to 0.09375
- position_bias: float32 [32, 16], P(None, 'head'), may hold values from -6 to 303
- bucket_edges: int32 [31], replicated, may hold values from 1 to 1035, as said below
- cache_keys: bfloat16 [384, 128, 1024], P('blk', None, 'head'), may hold values from -2 to 2
- cache_values: bfloat16 [384, 128, 1024], P('blk', None, 'head'), may hold values from -6 to 6
- lengths: int32 [128], replicated, may hold values from 1 to 16384, as said below
- page_request: int32 [384], P('blk'), may hold values from -1 to 127, as said below
- page_index: int32 [384], P('blk'), may hold values from 0 to 127, as said below
Outputs:
- new_hidden: float32 [128, 1024], P('blk', 'head')
The draws below stay inside these ranges and needn't reach their ends.
Inputs may be any that keep to these rules, and one draw needn't show every extreme that they name: Request r holds lengths[r] cached tokens; for each k below ceil(lengths[r] / 128) exactly one slot s has page_request[s] = r and page_index[s] = k, and no other slot names r. Every request has at least one page; some request has 16384 tokens. `page_request`: -1 marks a free slot. A free slot has page_index 0. `bucket_edges`: strictly rising; its first 15 entries are 1, 2, 3 and so on.
All inputs are finite; a program needn't handle non-finite values.
Results may differ from the reference program's by a relative error of at most 0.009.
Values may be sent and summed in bfloat16 or wider, within the bound.
No kernel may reach another device: no remote copies, remote signals or barrier semaphores. Data moves between devices by JAX's collectives and lax.ppermute only.
A program may use at most 64 MiB of HBM per device.

```python
import jax
import jax.numpy as jnp
from jax import lax

D = 1024
HEADS = 16
HEAD_DIM = 64
FF = 4096
BUCKETS = 32
PAGE = 128
REQUESTS = 128
TOTAL_PAGES = 384
MAX_PAGES = 128
N_BLK = 16


def layout(key):
    key_expo = jax.random.fold_in(key, 101)
    key_count = jax.random.fold_in(key, 102)
    key_long = jax.random.fold_in(key, 103)
    key_tail = jax.random.fold_in(key, 104)
    key_perm = jax.random.fold_in(key, 105)
    request_ids = jnp.arange(REQUESTS, dtype=jnp.int32)
    expo = jax.random.randint(key_expo, (REQUESTS,), 0, 4)
    limit = jnp.left_shift(jnp.ones((REQUESTS,), jnp.int32), expo) + 1
    wanted = jax.random.randint(key_count, (REQUESTS,), 1, limit).astype(jnp.int32)
    longest = jax.random.randint(key_long, (), 0, REQUESTS).astype(jnp.int32)
    is_long = request_ids == longest
    extra = jnp.where(is_long, 0, wanted - 1).astype(jnp.int32)
    spare = TOTAL_PAGES - MAX_PAGES - (REQUESTS - 1)
    extra_start = (jnp.cumsum(extra) - extra).astype(jnp.int32)
    granted = jnp.clip(spare - extra_start, 0, extra).astype(jnp.int32)
    counts = jnp.where(is_long, MAX_PAGES, 1 + granted).astype(jnp.int32)
    others = jnp.where(is_long, 0, counts).astype(jnp.int32)
    start = (jnp.cumsum(others) - others + MAX_PAGES).astype(jnp.int32)
    start = jnp.where(is_long, 0, start).astype(jnp.int32)
    tail = jax.random.randint(key_tail, (REQUESTS,), 1, PAGE + 1).astype(jnp.int32)
    tail = jnp.where(is_long, PAGE, tail)
    lengths = ((counts - 1) * PAGE + tail).astype(jnp.int32)
    slot_ids = jnp.arange(TOTAL_PAGES, dtype=jnp.int32)
    inside = (slot_ids[:, None] >= start[None, :]) & (slot_ids[:, None] < (start + counts)[None, :])
    used = jnp.any(inside, axis=1)
    owner = jnp.sum(jnp.where(inside, request_ids[None, :], 0), axis=1).astype(jnp.int32)
    first_slot = jnp.sum(jnp.where(inside, start[None, :], 0), axis=1).astype(jnp.int32)
    owner = jnp.where(used, owner, -1).astype(jnp.int32)
    number = jnp.where(used, slot_ids - first_slot, 0).astype(jnp.int32)
    placing = jax.random.permutation(key_perm, TOTAL_PAGES)
    page_request = jnp.zeros((TOTAL_PAGES,), jnp.int32).at[placing].set(owner)
    page_index = jnp.zeros((TOTAL_PAGES,), jnp.int32).at[placing].set(number)
    return (lengths, page_request, page_index)


def draw_lengths(key, part):
    return layout(key)[0]


def draw_page_request(key, part):
    return layout(key)[1]


def draw_page_index(key, part):
    return layout(key)[2]


def draw_bucket_edges(key, part):
    half_count = BUCKETS // 2
    lower = jnp.arange(1, half_count, dtype=jnp.int32)
    steps_ids = jnp.arange(half_count, dtype=jnp.int32)
    limit = 2 * jnp.left_shift(jnp.ones((half_count,), jnp.int32), steps_ids // 2) + 1
    gaps = jax.random.randint(jax.random.fold_in(key, 201), (half_count,), 1, limit).astype(jnp.int32)
    upper = (half_count - 1 + jnp.cumsum(gaps)).astype(jnp.int32)
    top_edge = half_count - 1 + 4 * (2 ** (BUCKETS // 4) - 1)
    upper = jnp.where(steps_ids == half_count - 1, top_edge, upper).astype(jnp.int32)
    return jnp.concatenate([lower, upper]).astype(jnp.int32)


def draw_position_bias(key, part):
    base_key = jax.random.fold_in(key, 301)
    return jnp.clip(jax.random.normal(base_key, (BUCKETS, HEADS), jnp.float32) * 1.5, -6.0, 6.0)


def draw_hidden_in(key, part):
    column = jnp.exp(jax.random.uniform(jax.random.fold_in(key, 401), (D,), jnp.float32, -1.15, 1.15))
    row_scale = jnp.exp(jax.random.uniform(jax.random.fold_in(key, 402), (REQUESTS, 1), jnp.float32, -1.15, 1.15))
    base = jnp.clip(jax.random.normal(jax.random.fold_in(key, 403), (REQUESTS, D), jnp.float32), -4.0, 4.0)
    return base * column[None, :] * row_scale


def draw_qkv_weight(key, part):
    shape = (3, D, HEADS * HEAD_DIM)
    scale = 1.0 / D ** 0.5
    return (jnp.clip(jax.random.normal(jax.random.fold_in(key, 501), shape, jnp.float32), -6.0, 6.0) * scale).astype(jnp.bfloat16)


def draw_cache_keys(key, part):
    shape = (TOTAL_PAGES, PAGE, HEADS * HEAD_DIM)
    return jnp.clip(0.35 * jax.random.normal(jax.random.fold_in(key, 601), shape, jnp.float32), -2.0, 2.0).astype(jnp.bfloat16)


def steps_of(rng, dims, shards, low, top_value):
    def one(axis_at, parts):
        heights = jax.random.uniform(jax.random.fold_in(jax.random.fold_in(rng, 6), axis_at), (parts,), jnp.float32, low / len(shards), top_value / len(shards))
        return jnp.repeat(jnp.exp(heights), dims[axis_at] // parts).reshape((-1,) + (1,) * (len(dims) - axis_at - 1))

    level = one(*shards[0])
    for cut in shards[1:]:
        level = level * one(*cut)
    return level


def scatter_about(key, shape, width, reach, pieces=(), held_as=jnp.bfloat16):
    result = width * jax.random.normal(key, shape, jnp.float32)
    if pieces:
        result = result * steps_of(key, shape, pieces, -0.22, 0.18)
    return jnp.clip(result, -reach, reach).astype(held_as)


def setup_inputs(seed: int = 0) -> dict:
    key_list = jax.random.split(jax.random.key(seed), 15)
    return {
        "hidden_in": draw_hidden_in(jax.random.fold_in(key_list[14], 71), 0),
        "attention_gain": jnp.clip(1.0 + 0.18 * jax.random.normal(key_list[1], (D,), jnp.float32), 0.1, 1.9),
        "mlp_gain": jnp.clip(1.0 + 0.18 * jax.random.normal(key_list[2], (D,), jnp.float32), 0.1, 1.9),
        "qkv_weight": draw_qkv_weight(jax.random.fold_in(key_list[14], 71), 0),
        "out_weight": scatter_about(key_list[4], (HEADS * HEAD_DIM, D), (HEADS * HEAD_DIM) ** -0.5, 0.1875, ((0, 2),)),
        "up_weight": scatter_about(key_list[5], (D, FF), D ** -0.5, 0.1875, ((1, 2),)),
        "down_weight": scatter_about(key_list[6], (FF, D), FF ** -0.5, 0.09375, ((0, 2),)),
        "position_bias": draw_position_bias(jax.random.fold_in(key_list[14], 71), 0),
        "bucket_edges": draw_bucket_edges(jax.random.fold_in(key_list[14], 71), 0),
        "cache_keys": draw_cache_keys(jax.random.fold_in(key_list[14], 71), 0),
        "cache_values": scatter_about(key_list[10], (TOTAL_PAGES, PAGE, HEADS * HEAD_DIM), 1.0, 6.0, ((0, 16), (2, 2))),
        "lengths": draw_lengths(jax.random.fold_in(key_list[14], 71), 0),
        "page_request": draw_page_request(jax.random.fold_in(key_list[14], 71), 0),
        "page_index": draw_page_index(jax.random.fold_in(key_list[14], 71), 0),
    }


far_below = -1e+30
epsilon = 1e-06

def rms_scale(values):
    return lax.rsqrt(lax.optimization_barrier(jnp.mean(values * values, axis=1, keepdims=True)) + epsilon)

def reference(hidden_in, attention_gain, mlp_gain, qkv_weight, out_weight, up_weight, down_weight, position_bias, bucket_edges, cache_keys, cache_values, lengths, page_request, page_index):
    requests = hidden_in.shape[0]
    normed = (hidden_in * rms_scale(hidden_in) * attention_gain).astype(jnp.bfloat16)
    query = jnp.dot(normed, qkv_weight[0], preferred_element_type=jnp.float32).astype(jnp.bfloat16)
    key_new = jnp.dot(normed, qkv_weight[1], preferred_element_type=jnp.float32).astype(jnp.bfloat16)
    value_new = jnp.dot(normed, qkv_weight[2], preferred_element_type=jnp.float32).astype(jnp.bfloat16)
    slot_count = page_request.shape[0]
    occupied = page_request >= 0
    page_owner = jnp.maximum(page_request, 0).astype(jnp.int32)
    page_query = query[page_owner].reshape(slot_count, HEADS, HEAD_DIM)
    position = page_index[:, None] * PAGE + jnp.arange(PAGE, dtype=jnp.int32)[None, :]
    length_of = lengths[page_owner]
    usable = occupied[:, None] & (position < length_of[:, None])
    distance = length_of[:, None] - position
    bucket = lax.optimization_barrier(jnp.sum((bucket_edges[None, None, :] <= distance[:, :, None]).astype(jnp.int32), axis=-1))
    page_bias = position_bias[bucket]

    def grouped(array):
        return array.reshape((N_BLK, slot_count // N_BLK) + array.shape[1:])

    def scores_of(block):
        block_query, block_keys, block_bias, block_usable = block
        keys_f = block_keys.astype(jnp.float32).reshape(block_keys.shape[0], PAGE, HEADS, HEAD_DIM)
        scores = jnp.einsum('phd,pthd->pht', block_query.astype(jnp.float32), keys_f)
        scores = scores + jnp.transpose(block_bias, (0, 2, 1))
        return jnp.where(block_usable[:, None, :], scores, far_below)
    page_peak = lax.map(lambda block: lax.optimization_barrier(jnp.max(scores_of(block), axis=2)), (grouped(page_query), grouped(cache_keys), grouped(page_bias), grouped(usable)))
    page_peak = page_peak.reshape(slot_count, HEADS)
    own_score = lax.optimization_barrier(jnp.sum(query.reshape(requests, HEADS, HEAD_DIM).astype(jnp.float32) * key_new.reshape(requests, HEADS, HEAD_DIM).astype(jnp.float32), axis=2))
    own_score = own_score + position_bias[0][None, :]
    peak = jnp.full((requests, HEADS), far_below, jnp.float32)
    peak = peak.at[page_owner].max(jnp.where(occupied[:, None], page_peak, far_below))
    peak = jnp.maximum(peak, own_score)

    def weights_of(block):
        block_query, block_keys, block_values, block_bias, block_usable, block_peak = block
        scores = scores_of((block_query, block_keys, block_bias, block_usable))
        weights = jnp.where(block_usable[:, None, :], jnp.exp(scores - block_peak[:, :, None]), 0.0)
        rounded = lax.optimization_barrier(weights.astype(jnp.bfloat16)).astype(jnp.float32)
        values_f = block_values.astype(jnp.float32).reshape(block_values.shape[0], PAGE, HEADS, HEAD_DIM)
        page_mix = jnp.einsum('pht,pthd->phd', rounded, values_f)
        return (lax.optimization_barrier(jnp.sum(weights, axis=2)), page_mix.reshape(block_values.shape[0], HEADS * HEAD_DIM))
    page_total, page_mix = lax.map(weights_of, (grouped(page_query), grouped(cache_keys), grouped(cache_values), grouped(page_bias), grouped(usable), grouped(peak[page_owner])))
    page_total = page_total.reshape(slot_count, HEADS)
    page_mix = page_mix.reshape(slot_count, HEADS * HEAD_DIM)
    weight_sum = jax.ops.segment_sum(jnp.where(occupied[:, None], page_total, 0.0), page_owner, num_segments=requests)
    value_sum = jax.ops.segment_sum(jnp.where(occupied[:, None], page_mix, 0.0), page_owner, num_segments=requests)
    own_weight = jnp.exp(own_score - peak)
    own_rounded = lax.optimization_barrier(own_weight.astype(jnp.bfloat16)).astype(jnp.float32)
    weight_sum = weight_sum + own_weight
    value_sum = value_sum + jnp.repeat(own_rounded, HEAD_DIM, axis=1) * value_new.astype(jnp.float32)
    attention = (value_sum / jnp.repeat(weight_sum, HEAD_DIM, axis=1)).astype(jnp.bfloat16)
    middle = hidden_in + jnp.dot(attention, out_weight, preferred_element_type=jnp.float32)
    normed_mid = (middle * rms_scale(middle) * mlp_gain).astype(jnp.bfloat16)
    activated = jnp.maximum(jnp.dot(normed_mid, up_weight, preferred_element_type=jnp.float32), 0.0).astype(jnp.bfloat16)
    return middle + jnp.dot(activated, down_weight, preferred_element_type=jnp.float32)
```

```python
import functools

import jax
import jax.numpy as jnp
from jax import lax
from jax.experimental import pallas as pl
from jax.experimental.pallas import tpu as pltpu
from jax.sharding import PartitionSpec as P

HEAD_DIM = 64
PAGE = 128
LANES = 128

far_below = -1e30
epsilon = 1e-06

VMEM_SPEC = pl.BlockSpec(memory_space=pltpu.VMEM)
SMEM_SPEC = pl.BlockSpec(memory_space=pltpu.SMEM)
ANY_SPEC = pl.BlockSpec(memory_space=pl.ANY)
PARAMS = pltpu.CompilerParams(vmem_limit_bytes=40 * 1024 * 1024)

PIECE = 8
SUM_LANE = 3 * PIECE


def iota(shape, axis):
    return lax.broadcasted_iota(jnp.int32, shape, axis)


def pieces(x, count):
    parts = []
    for _ in range(count):
        part = x.astype(jnp.bfloat16)
        parts.append(part)
        x = x - part.astype(jnp.float32)
    return parts


def rms_normed(x, gain):
    scale = lax.rsqrt(jnp.mean(x * x, axis=1, keepdims=True) + epsilon)
    return (x * scale * gain).astype(jnp.bfloat16)


def dot(a, b, dims=((1,), (0,)), precision=None):
    return lax.dot_general(
        a, b, (dims, ((), ())), preferred_element_type=jnp.float32, precision=precision
    )


def query_kernel(hidden_ref, gain_ref, weight_ref, query_ref):
    normed = rms_normed(hidden_ref[...], gain_ref[...])
    query_ref[...] = dot(normed, weight_ref[0]).astype(jnp.bfloat16)


def side_kernel(
    hidden_ref, gain_ref, query_ref, table_ref, edges_ref, lengths_ref, request_ref, index_ref,
    weight_hbm,
    score_ref, value_ref, bias_ref,
    weight_vmem, sems,
):
    copies = [
        pltpu.make_async_copy(weight_hbm.at[1 + i], weight_vmem.at[i], sems.at[i]) for i in range(2)
    ]
    for copy in copies:
        copy.start()
    table = table_ref[...]
    buckets, heads = table.shape
    highest = lax.Precision.HIGHEST
    eye = (iota((PIECE, heads), 0) == iota((PIECE, heads), 1)).astype(jnp.float32)
    by_head = dot(eye, table, ((1,), (1,)), highest)
    spread = (iota((heads, LANES), 0) == iota((heads, LANES), 1)).astype(jnp.float32)
    nearest = dot(table[0:8], spread, precision=highest)[0:1]
    columns = [jnp.broadcast_to(by_head[:, k : k + 1], (PIECE, PAGE)) for k in range(buckets)]
    token = iota((PIECE, PAGE), 1)
    for p in range(request_ref.shape[0]):
        owner = request_ref[p]
        left = lengths_ref[jnp.maximum(owner, 0)] - index_ref[p] * PAGE
        distance = jnp.where(owner >= 0, left, 0) - token
        bias = columns[0]
        for k in range(buckets - 1):
            bias = jnp.where(distance >= edges_ref[k], columns[k + 1], bias)
        bias_ref[p] = jnp.where(distance > 0, bias, far_below)
    normed = rms_normed(hidden_ref[...], gain_ref[...])
    copies[0].wait()
    key = dot(normed, weight_vmem[0]).astype(jnp.bfloat16)
    product = query_ref[...].astype(jnp.float32) * key.astype(jnp.float32)
    width = product.shape[1]
    gather = (iota((width, LANES), 0) // HEAD_DIM == iota((width, LANES), 1)).astype(jnp.bfloat16)
    score = nearest
    for part in pieces(product, 3):
        score = score + dot(part, gather)
    score_ref[...] = score
    copies[1].wait()
    value_ref[...] = dot(normed, weight_vmem[1]).astype(jnp.bfloat16)


def attend_kernel(
    own_rows, groups, *refs,
):
    query_refs = refs[:groups]
    request_ref, bias_ref, keys_hbm, values_hbm, sums_ref, keys, values, sems = refs[groups:]
    page_count = request_ref.shape[0]
    width = keys.shape[2]
    chunk = 2
    chunks = page_count // chunk
    copies = []
    for kind, (source, target) in enumerate(((keys_hbm, keys), (values_hbm, values))):
        for c in range(chunks):
            pages = pl.ds(c * chunk, chunk)
            copy = pltpu.make_async_copy(source.at[pages], target.at[pages], sems.at[kind, c])
            copy.start()
            copies.append(copy)
    me = lax.axis_index("blk")
    requests = [request_ref[p] for p in range(page_count)]
    all_rows = sum(ref.shape[0] for ref in query_refs)
    column = iota((PIECE, all_rows), 1)
    picks = []
    for r in requests:
        slot = ((jnp.maximum(r, 0) // own_rows) ^ me) * own_rows + jnp.maximum(r, 0) % own_rows
        picks.append((column == jnp.where(r >= 0, slot, -1)).astype(jnp.float32))
    picks = jnp.concatenate(picks, axis=0).astype(jnp.bfloat16)
    queries = jnp.concatenate([ref[...] for ref in query_refs], axis=0)
    own_head = (iota((PIECE, width), 1) // HEAD_DIM == iota((PIECE, width), 0)).astype(jnp.float32)
    pair_heads = jnp.concatenate([own_head] * chunk, axis=0)
    chosen = dot(picks, queries)
    scores = []
    for c in range(chunks):
        rows = chosen[c * chunk * PIECE : (c + 1) * chunk * PIECE]
        split = (rows * pair_heads).astype(jnp.bfloat16)
        copies[c].wait()
        block = keys[c * chunk : (c + 1) * chunk].reshape(chunk * PAGE, width)
        raw = dot(split, block, ((1,), (1,)))
        for i in range(chunk):
            p = c * chunk + i
            part = raw[i * PIECE : (i + 1) * PIECE, i * PAGE : (i + 1) * PAGE]
            scores.append(part + bias_ref[p])
    tops = [jnp.max(s, axis=1, keepdims=True) for s in scores]
    peaks = list(tops)
    firsts = []
    for p in range(page_count):
        first = jnp.float32(1.0)
        for q in range(page_count):
            if q == p:
                continue
            same = requests[p] == requests[q]
            peaks[p] = jnp.maximum(peaks[p], tops[q] + jnp.where(same, 0.0, 2 * far_below))
            if q < p:
                first = jnp.where(same, 0.0, first)
        firsts.append(first)
    lane = iota((PIECE, LANES), 1)
    row = iota((PIECE, LANES), 0)
    mixes, stats = [], []
    nothing = jnp.zeros((PIECE, PAGE), jnp.float32)
    for c in range(chunks):
        blocks = []
        for i in range(chunk):
            p = c * chunk + i
            weight = jnp.exp(scores[p] - peaks[p])
            total = jnp.sum(weight, axis=1, keepdims=True)
            stats.append(
                jnp.where(
                    lane == row,
                    peaks[p] * firsts[p],
                    jnp.where(lane == row + SUM_LANE, total, 0.0),
                )
            )
            blocks.append(
                jnp.concatenate([weight if k == i else nothing for k in range(chunk)], axis=1)
            )
        weights = jnp.concatenate(blocks, axis=0).astype(jnp.bfloat16)
        copies[chunks + c].wait()
        block = values[c * chunk : (c + 1) * chunk].reshape(chunk * PAGE, width)
        mixes.append(dot(weights, block) * pair_heads)
    mix = jnp.concatenate(mixes, axis=0)
    stats = jnp.concatenate(stats, axis=0)
    place = column
    natural = []
    for r in requests:
        natural.append((place == r).astype(jnp.float32))
    natural = jnp.concatenate(natural, axis=0).astype(jnp.bfloat16)
    over_rows = ((0,), (0,))
    high, low = pieces(mix, 2)
    sums = dot(natural, high, over_rows) + dot(natural, low, over_rows)
    sums_ref[:, :width] = sums.astype(jnp.bfloat16)
    collected = sum(dot(natural, part, over_rows) for part in pieces(stats, 3))
    one, two, three = (part.astype(jnp.float32) for part in pieces(collected, 3))
    sums_ref[:, width:] = (
        one + pltpu.roll(two, PIECE, 1) + pltpu.roll(three, 2 * PIECE, 1)
    ).astype(jnp.bfloat16)


def merge_kernel(parts_ref, score_ref, value_ref, weight_ref, own_ref, send_ref):
    own_rows, width = value_ref.shape
    sources = parts_ref.shape[0] // own_rows
    stats = parts_ref[:, width:].astype(jnp.float32)
    stats = stats + pltpu.roll(stats, LANES - PIECE, 1) + pltpu.roll(stats, LANES - 2 * PIECE, 1)
    sums = pltpu.roll(stats, LANES - SUM_LANE, 1)
    heads = width // HEAD_DIM
    used = iota(stats.shape, 1) < heads
    peaks = jnp.where(used & (sums > 0.0), stats, far_below)
    sums = jnp.where(used, sums, 0.0)
    own_score = jnp.where(iota(score_ref.shape, 1) < heads, score_ref[...], 0.0)
    peak = own_score
    for s in range(sources):
        peak = jnp.maximum(peak, peaks[s * own_rows : (s + 1) * own_rows])
    own_weight = jnp.exp(own_score - peak)
    total = own_weight
    factors = []
    for s in range(sources):
        rows = slice(s * own_rows, (s + 1) * own_rows)
        factor = jnp.exp(peaks[rows] - peak)
        total = total + factor * sums[rows]
        factors.append(factor)
    factors.append(own_weight.astype(jnp.bfloat16).astype(jnp.float32))
    shares = jnp.concatenate([factor / total for factor in factors], axis=0)
    spread = (iota((LANES, width), 0) == iota((LANES, width), 1) // HEAD_DIM).astype(jnp.bfloat16)
    shares = sum(dot(part, spread) for part in pieces(shares, 3))
    mixed = value_ref[...].astype(jnp.float32) * shares[sources * own_rows :]
    for s in range(sources):
        rows = slice(s * own_rows, (s + 1) * own_rows)
        mixed = mixed + parts_ref[rows, :width].astype(jnp.float32) * shares[rows]
    projected = dot(mixed.astype(jnp.bfloat16), weight_ref[...])
    own_ref[...] = projected
    send_ref[...] = projected.astype(jnp.bfloat16)


def mlp_kernel(
    hidden_ref, own_ref, other_ref, gain_ref, up_hbm, down_hbm,
    middle_ref, down_ref,
    up, down, sems,
):
    units = up.shape[1]
    chunk = 256
    chunks = units // chunk
    ups, downs = [], []
    for c in range(chunks):
        span = pl.ds(c * chunk, chunk)
        ups.append(pltpu.make_async_copy(up_hbm.at[:, span], up.at[:, span], sems.at[0, c]))
        downs.append(pltpu.make_async_copy(down_hbm.at[span], down.at[span], sems.at[1, c]))
        ups[c].start()
        downs[c].start()
    middle = hidden_ref[...] + (own_ref[...] + other_ref[...].astype(jnp.float32))
    middle_ref[...] = middle
    normed = rms_normed(middle, gain_ref[...])
    total = None
    for c in range(chunks):
        span = slice(c * chunk, (c + 1) * chunk)
        ups[c].wait()
        active = jnp.maximum(dot(normed, up[:, span]), 0.0).astype(jnp.bfloat16)
        downs[c].wait()
        part = dot(active, down[span])
        total = part if total is None else total + part
    down_ref[...] = total


def xor_pairs(size, step):
    return [(i, i ^ step) for i in range(size)]


def per_device(
    hidden_in, attention_gain, mlp_gain, qkv_weight, out_weight, up_weight, down_weight,
    position_bias, bucket_edges, cache_keys, cache_values, lengths, page_request, page_index,
):
    f32, bf16 = jnp.float32, jnp.bfloat16
    own_rows, model = hidden_in.shape
    width = qkv_weight.shape[2]
    page_count = page_request.shape[0]
    blocks = lax.axis_size("blk")
    all_rows = own_rows * blocks
    gain = attention_gain.reshape(1, model)
    query = pl.pallas_call(
        query_kernel,
        out_shape=jax.ShapeDtypeStruct((own_rows, width), bf16),
        grid=(1,),
        in_specs=[
            pl.BlockSpec((own_rows, model), lambda i: (0, 0)),
            pl.BlockSpec((1, model), lambda i: (0, 0)),
            pl.BlockSpec((1, model, width), lambda i: (0, 0, 0)),
        ],
        out_specs=pl.BlockSpec((own_rows, width), lambda i: (0, 0)),
        compiler_params=PARAMS,
        name="query",
    )(hidden_in, gain, qkv_weight)

    inner = 1
    while inner * inner < blocks:
        inner *= 2
    near = [query] + [
        lax.ppermute(query, "blk", xor_pairs(blocks, step)) for step in range(1, inner)
    ]
    near = jnp.concatenate(near, axis=0)
    gathered = [near] + [
        lax.ppermute(near, "blk", xor_pairs(blocks, step * inner))
        for step in range(1, blocks // inner)
    ]

    own_score, value_new, bias = pl.pallas_call(
        side_kernel,
        out_shape=(
            jax.ShapeDtypeStruct((own_rows, LANES), f32),
            jax.ShapeDtypeStruct((own_rows, width), bf16),
            jax.ShapeDtypeStruct((page_count, PIECE, PAGE), f32),
        ),
        in_specs=[VMEM_SPEC] * 4 + [SMEM_SPEC] * 4 + [ANY_SPEC],
        out_specs=(VMEM_SPEC,) * 3,
        scratch_shapes=[
            pltpu.VMEM((2, model, width), bf16),
            pltpu.SemaphoreType.DMA((2,)),
        ],
        compiler_params=PARAMS,
        cost_estimate=pl.CostEstimate(
            flops=4 * own_rows * model * width,
            bytes_accessed=4 * model * width,
            transcendentals=0,
        ),
        name="side",
    )(
        hidden_in, gain, query, position_bias, bucket_edges, lengths, page_request, page_index,
        qkv_weight,
    )

    sums = pl.pallas_call(
        functools.partial(attend_kernel, own_rows, len(gathered)),
        out_shape=jax.ShapeDtypeStruct((all_rows, width + LANES), bf16),
        in_specs=[VMEM_SPEC] * len(gathered) + [SMEM_SPEC, VMEM_SPEC, ANY_SPEC, ANY_SPEC],
        out_specs=VMEM_SPEC,
        scratch_shapes=[
            pltpu.VMEM(cache_keys.shape, bf16),
            pltpu.VMEM(cache_values.shape, bf16),
            pltpu.SemaphoreType.DMA((2, page_count // 2)),
        ],
        compiler_params=PARAMS,
        name="attend",
    )(*gathered, page_request, bias, cache_keys, cache_values)

    parts = lax.all_to_all(sums, "blk", 0, 0, tiled=True)

    own_part, sent_part = pl.pallas_call(
        merge_kernel,
        out_shape=(
            jax.ShapeDtypeStruct((own_rows, model), f32),
            jax.ShapeDtypeStruct((own_rows, model), bf16),
        ),
        in_specs=[VMEM_SPEC] * 4,
        out_specs=(VMEM_SPEC,) * 2,
        compiler_params=PARAMS,
        name="merge",
    )(parts, own_score, value_new, out_weight)

    halves = lax.axis_size("head")
    if halves == 2:
        other_part = lax.ppermute(sent_part, "head", xor_pairs(2, 1))
    else:
        own_part = jnp.zeros_like(own_part)
        other_part = lax.psum(sent_part, "head")

    units = up_weight.shape[1]
    middle, down_part = pl.pallas_call(
        mlp_kernel,
        out_shape=(jax.ShapeDtypeStruct((own_rows, model), f32),) * 2,
        in_specs=[VMEM_SPEC] * 4 + [ANY_SPEC] * 2,
        out_specs=(VMEM_SPEC,) * 2,
        scratch_shapes=[
            pltpu.VMEM(up_weight.shape, bf16),
            pltpu.VMEM(down_weight.shape, bf16),
            pltpu.SemaphoreType.DMA((2, units // 256)),
        ],
        compiler_params=PARAMS,
        name="mlp",
    )(hidden_in, own_part, other_part, mlp_gain.reshape(1, model), up_weight, down_weight)

    columns = model // halves
    place = lax.axis_index("head")
    kept = lax.dynamic_slice_in_dim(middle, place * columns, columns, 1)
    if halves == 2:
        kept = kept + lax.dynamic_slice_in_dim(down_part, place * columns, columns, 1)
        leaving = lax.dynamic_slice_in_dim(down_part, (1 - place) * columns, columns, 1)
        arrived = lax.ppermute(leaving.astype(bf16), "head", xor_pairs(2, 1))
    else:
        arrived = lax.psum_scatter(
            down_part.astype(bf16), "head", scatter_dimension=1, tiled=True
        )
    return kept + arrived.astype(f32)


def solution(mesh):
    in_specs = (
        P("blk", None),
        P(),
        P(),
        P(None, None, "head"),
        P("head", None),
        P(None, "head"),
        P("head", None),
        P(None, "head"),
        P(),
        P("blk", None, "head"),
        P("blk", None, "head"),
        P(),
        P("blk"),
        P("blk"),
    )
    out_specs = P("blk", "head")
    return jax.shard_map(
        per_device, mesh=mesh, in_specs=in_specs, out_specs=out_specs, check_vma=False
    )
```

```python
import functools

import jax
import jax.numpy as jnp
from jax import lax
from jax.experimental import pallas as pl
from jax.experimental.pallas import tpu as pltpu
from jax.sharding import PartitionSpec as P

HEAD_DIM = 64
PAGE = 128
LANES = 128

far_below = -1e30
epsilon = 1e-06

VMEM_SPEC = pl.BlockSpec(memory_space=pltpu.VMEM)
SMEM_SPEC = pl.BlockSpec(memory_space=pltpu.SMEM)
ANY_SPEC = pl.BlockSpec(memory_space=pl.ANY)
HBM_SPEC = pl.BlockSpec(memory_space=pltpu.HBM)
PARAMS = pltpu.CompilerParams(vmem_limit_bytes=16 * 1024 * 1024)

PIECE = 8
SUM_LANE = 3 * PIECE


def iota(shape, axis):
    return lax.broadcasted_iota(jnp.int32, shape, axis)


def pieces(x, count):
    parts = []
    for _ in range(count):
        part = x.astype(jnp.bfloat16)
        parts.append(part)
        x = x - part.astype(jnp.float32)
    return parts


def rms_normed(x, gain):
    scale = lax.rsqrt(jnp.mean(x * x, axis=1, keepdims=True) + epsilon)
    return (x * scale * gain).astype(jnp.bfloat16)


def dot(a, b, dims=((1,), (0,)), precision=None):
    return lax.dot_general(
        a, b, (dims, ((), ())), preferred_element_type=jnp.float32, precision=precision
    )


def query_kernel(hidden_hbm, gain_hbm, weight_hbm, query_ref, hidden, gain, weight, sems):
    model = hidden.shape[1]
    small = [
        pltpu.make_async_copy(hidden_hbm, hidden, sems.at[0]),
        pltpu.make_async_copy(gain_hbm, gain, sems.at[1]),
    ]
    half = model // 2
    large = [
        pltpu.make_async_copy(
            weight_hbm.at[0, pl.ds(i * half, half)], weight.at[pl.ds(i * half, half)], sems.at[2 + i]
        )
        for i in range(2)
    ]
    for copy in small + large:
        copy.start()
    for copy in small:
        copy.wait()
    normed = rms_normed(hidden[...], gain[...])
    query = None
    for i, copy in enumerate(large):
        copy.wait()
        span = slice(i * half, (i + 1) * half)
        part = dot(normed[:, span], weight[span])
        query = part if query is None else query + part
    query_ref[...] = query.astype(jnp.bfloat16)


def page_kernel(
    own_rows, inner, outer, query_ref, table_ref, edges_ref, lengths_ref, request_ref, index_ref,
    keys_hbm, values_hbm,
    keys_ref, values_ref, bias_ref, pick_ref, place_ref, first_ref, apart_ref,
    sems,
):
    copies = [
        pltpu.make_async_copy(keys_hbm, keys_ref, sems.at[0]),
        pltpu.make_async_copy(values_hbm, values_ref, sems.at[1]),
    ]
    for copy in copies:
        copy.start()
    me = lax.axis_index("blk")
    table = table_ref[...]
    buckets, heads = table.shape
    page_count = request_ref.shape[0]
    all_rows, depth = place_ref.shape
    eye = (iota((PIECE, heads), 0) == iota((PIECE, heads), 1)).astype(jnp.float32)
    by_head = dot(eye, table, ((1,), (1,)), lax.Precision.HIGHEST)
    columns = [jnp.broadcast_to(by_head[:, k : k + 1], (PIECE, PAGE)) for k in range(buckets)]
    token = iota((PIECE, PAGE), 1)
    row_of = iota((PIECE, all_rows), 1)
    page_of = iota((1, depth), 1) // PIECE
    lane = iota((1, LANES), 1)
    requests = [request_ref[p] for p in range(page_count)]
    owners = jnp.full((1, depth), -1, jnp.int32)
    by_lane = jnp.full((1, LANES), -2, jnp.int32)
    for p in range(page_count):
        owners = jnp.where(page_of == p, requests[p], owners)
        by_lane = jnp.where(lane == p, requests[p], by_lane)
    leads = jnp.full((1, depth), -1, jnp.int32)
    for p in range(page_count):
        owner = requests[p]
        left = lengths_ref[jnp.maximum(owner, 0)] - index_ref[p] * PAGE
        distance = jnp.where(owner >= 0, left, 0) - token
        bias = columns[0]
        for k in range(buckets - 1):
            bias = jnp.where(distance >= edges_ref[k], columns[k + 1], bias)
        bias_ref[p] = jnp.where(distance > 0, bias, far_below)
        known = jnp.maximum(owner, 0)
        apart_by = (known // own_rows) ^ me
        slot = (apart_by % inner) * outer + apart_by // inner
        slot = slot * own_rows + known % own_rows
        slot = jnp.where(owner >= 0, slot, -1)
        pick_ref[p] = (row_of == slot).astype(jnp.float32)
        same = by_lane == owner
        apart_ref[p : p + 1] = jnp.where(same, 0.0, 2 * far_below)
        earlier = jnp.max(jnp.where(same & (lane < p), 1, 0), axis=1, keepdims=True)
        leads = jnp.where((page_of == p) & (earlier == 0), owner, leads)
    row = iota((all_rows, depth), 0)
    place_ref[...] = (row == owners).astype(jnp.bfloat16)
    first_ref[...] = (row == leads).astype(jnp.bfloat16)
    for copy in copies:
        copy.wait()


def side_kernel(
    hidden_ref, gain_ref, query_ref, table_ref, weight_hbm, out_hbm, up_hbm, down_hbm, after_ref,
    score_ref, value_ref, out_ref, up_ref, down_ref,
    weight, sems,
):
    copies = [
        pltpu.make_async_copy(weight_hbm.at[1 + i], weight.at[i], sems.at[i]) for i in range(2)
    ]
    later = [
        pltpu.make_async_copy(out_hbm, out_ref, sems.at[2]),
        pltpu.make_async_copy(up_hbm, up_ref, sems.at[3]),
        pltpu.make_async_copy(down_hbm, down_ref, sems.at[4]),
    ]
    for copy in copies + later:
        copy.start()
    normed = rms_normed(hidden_ref[...], gain_ref[...])
    heads = table_ref.shape[1]
    spread = (iota((heads, LANES), 0) == iota((heads, LANES), 1)).astype(jnp.float32)
    score = dot(table_ref[0:8], spread, precision=lax.Precision.HIGHEST)[0:1]
    copies[0].wait()
    key = dot(normed, weight[0]).astype(jnp.bfloat16)
    product = query_ref[...].astype(jnp.float32) * key.astype(jnp.float32)
    width = product.shape[1]
    gather = (iota((width, LANES), 0) // HEAD_DIM == iota((width, LANES), 1)).astype(jnp.bfloat16)
    for part in pieces(product, 3):
        score = score + dot(part, gather)
    score_ref[...] = score
    copies[1].wait()
    value_ref[...] = dot(normed, weight[1]).astype(jnp.bfloat16)
    for copy in later:
        copy.wait()


def attend_kernel(groups, *refs):
    query_refs = refs[:groups]
    (bias_ref, pick_ref, place_ref, first_ref, apart_ref, keys_ref, values_ref, sums_ref) = refs[
        groups:
    ]
    page_count, _, all_rows = pick_ref.shape
    width = keys_ref.shape[2]
    chunk = 2
    chunks = page_count // chunk
    picks = pick_ref[...].reshape(page_count * PIECE, all_rows).astype(jnp.bfloat16)
    queries = jnp.concatenate([ref[...] for ref in query_refs], axis=0)
    own_head = (iota((PIECE, width), 1) // HEAD_DIM == iota((PIECE, width), 0)).astype(jnp.float32)
    pair_heads = jnp.concatenate([own_head] * chunk, axis=0)
    chosen = dot(picks, queries)
    lane = iota((PIECE, LANES), 1)
    row = iota((PIECE, LANES), 0)
    scores = []
    tops = jnp.zeros((PIECE, LANES), jnp.float32)
    for c in range(chunks):
        rows = chosen[c * chunk * PIECE : (c + 1) * chunk * PIECE]
        split = (rows * pair_heads).astype(jnp.bfloat16)
        block = keys_ref[c * chunk : (c + 1) * chunk].reshape(chunk * PAGE, width)
        raw = dot(split, block, ((1,), (1,)))
        for i in range(chunk):
            p = c * chunk + i
            part = raw[i * PIECE : (i + 1) * PIECE, i * PAGE : (i + 1) * PAGE]
            score = part + bias_ref[p]
            scores.append(score)
            tops = jnp.where(lane == p, jnp.max(score, axis=1, keepdims=True), tops)
    mixes, peaks, totals = [], [], []
    nothing = jnp.zeros((PIECE, PAGE), jnp.float32)
    for c in range(chunks):
        blocks = []
        for i in range(chunk):
            p = c * chunk + i
            peak = jnp.max(tops + apart_ref[p : p + 1], axis=1, keepdims=True)
            weight = jnp.exp(scores[p] - peak)
            total = jnp.sum(weight, axis=1, keepdims=True)
            peaks.append(jnp.where(lane == row, peak, 0.0))
            totals.append(jnp.where(lane == row + SUM_LANE, total, 0.0))
            blocks.append(
                jnp.concatenate([weight if k == i else nothing for k in range(chunk)], axis=1)
            )
        weights = jnp.concatenate(blocks, axis=0).astype(jnp.bfloat16)
        block = values_ref[c * chunk : (c + 1) * chunk].reshape(chunk * PAGE, width)
        mixes.append(dot(weights, block) * pair_heads)
    mix = jnp.concatenate(mixes, axis=0)
    place, first = place_ref[...], first_ref[...]
    high, low = pieces(mix, 2)
    sums = dot(place, high) + dot(place, low)
    sums_ref[:, :width] = sums.astype(jnp.bfloat16)
    collected = sum(dot(first, part) for part in pieces(jnp.concatenate(peaks, axis=0), 3))
    collected += sum(dot(place, part) for part in pieces(jnp.concatenate(totals, axis=0), 3))
    one, two, three = (part.astype(jnp.float32) for part in pieces(collected, 3))
    sums_ref[:, width:] = (
        one + pltpu.roll(two, PIECE, 1) + pltpu.roll(three, 2 * PIECE, 1)
    ).astype(jnp.bfloat16)


def merge_kernel(parts_ref, score_ref, value_ref, weight_ref, own_ref, send_ref):
    own_rows, width = value_ref.shape
    sources = parts_ref.shape[0] // own_rows
    stats = parts_ref[:, width:].astype(jnp.float32)
    stats = stats + pltpu.roll(stats, LANES - PIECE, 1) + pltpu.roll(stats, LANES - 2 * PIECE, 1)
    sums = pltpu.roll(stats, LANES - SUM_LANE, 1)
    heads = width // HEAD_DIM
    used = iota(stats.shape, 1) < heads
    peaks = jnp.where(used & (sums > 0.0), stats, far_below)
    sums = jnp.where(used, sums, 0.0)
    own_score = jnp.where(iota(score_ref.shape, 1) < heads, score_ref[...], 0.0)
    peak = own_score
    for s in range(sources):
        peak = jnp.maximum(peak, peaks[s * own_rows : (s + 1) * own_rows])
    own_weight = jnp.exp(own_score - peak)
    total = own_weight
    factors = []
    for s in range(sources):
        rows = slice(s * own_rows, (s + 1) * own_rows)
        factor = jnp.exp(peaks[rows] - peak)
        total = total + factor * sums[rows]
        factors.append(factor)
    factors.append(own_weight.astype(jnp.bfloat16).astype(jnp.float32))
    shares = jnp.concatenate([factor / total for factor in factors], axis=0)
    spread = (iota((LANES, width), 0) == iota((LANES, width), 1) // HEAD_DIM).astype(jnp.bfloat16)
    shares = sum(dot(part, spread) for part in pieces(shares, 3))
    mixed = value_ref[...].astype(jnp.float32) * shares[sources * own_rows :]
    for s in range(sources):
        rows = slice(s * own_rows, (s + 1) * own_rows)
        mixed = mixed + parts_ref[rows, :width].astype(jnp.float32) * shares[rows]
    projected = dot(mixed.astype(jnp.bfloat16), weight_ref[...])
    own_ref[...] = projected
    send_ref[...] = projected.astype(jnp.bfloat16)


def mlp_kernel(exchanged, hidden_ref, own_ref, other_ref, gain_ref, up_ref, down_ref, *outs):
    middle = hidden_ref[...] + (own_ref[...] + other_ref[...].astype(jnp.float32))
    normed = rms_normed(middle, gain_ref[...])
    active = jnp.maximum(dot(normed, up_ref[...]), 0.0).astype(jnp.bfloat16)
    down = dot(active, down_ref[...])
    if exchanged:
        kept_ref, sent_ref = outs
        columns = kept_ref.shape[1]
        low = lax.axis_index("head") == 0
        left, right = slice(0, columns), slice(columns, 2 * columns)
        kept = middle + down

        @pl.when(low)
        def _():
            kept_ref[...] = kept[:, left]
            sent_ref[...] = down[:, right].astype(jnp.bfloat16)

        @pl.when(jnp.logical_not(low))
        def _():
            kept_ref[...] = kept[:, right]
            sent_ref[...] = down[:, left].astype(jnp.bfloat16)

    else:
        middle_ref, down_out_ref = outs
        middle_ref[...] = middle
        down_out_ref[...] = down.astype(jnp.bfloat16)


def in_hbm(*arrays):
    return [pltpu.with_memory_space_constraint(array, pltpu.HBM) for array in arrays]


def xor_pairs(size, step):
    return [(i, i ^ step) for i in range(size)]


def per_device(
    hidden_in, attention_gain, mlp_gain, qkv_weight, out_weight, up_weight, down_weight,
    position_bias, bucket_edges, cache_keys, cache_values, lengths, page_request, page_index,
):
    f32, bf16 = jnp.float32, jnp.bfloat16
    shape = jax.ShapeDtypeStruct
    own_rows, model = hidden_in.shape
    width = qkv_weight.shape[2]
    page_count = page_request.shape[0]
    blocks = lax.axis_size("blk")
    all_rows = own_rows * blocks
    gain = attention_gain.reshape(1, model)
    query = pl.pallas_call(
        query_kernel,
        out_shape=shape((own_rows, width), bf16),
        in_specs=[HBM_SPEC] * 3,
        out_specs=VMEM_SPEC,
        scratch_shapes=[
            pltpu.VMEM((own_rows, model), f32),
            pltpu.VMEM((1, model), f32),
            pltpu.VMEM((model, width), bf16),
            pltpu.SemaphoreType.DMA((4,)),
        ],
        compiler_params=PARAMS,
        name="query",
    )(*in_hbm(hidden_in, gain, qkv_weight))

    inner = 1
    while inner * inner < blocks:
        inner *= 2
    far = [query] + [
        lax.ppermute(query, "blk", xor_pairs(blocks, step * inner))
        for step in range(1, blocks // inner)
    ]
    depth = page_count * PIECE
    keys, values, bias, picks, place, first, apart = pl.pallas_call(
        functools.partial(page_kernel, own_rows, inner, blocks // inner),
        out_shape=(
            pltpu.VMEM(cache_keys.shape, bf16),
            pltpu.VMEM(cache_values.shape, bf16),
            shape((page_count, PIECE, PAGE), f32),
            shape((page_count, PIECE, all_rows), f32),
            shape((all_rows, depth), bf16),
            shape((all_rows, depth), bf16),
            shape((page_count, LANES), f32),
        ),
        in_specs=[VMEM_SPEC] * 2 + [SMEM_SPEC] * 4 + [HBM_SPEC] * 2,
        out_specs=(VMEM_SPEC,) * 7,
        scratch_shapes=[pltpu.SemaphoreType.DMA((2,))],
        compiler_params=PARAMS,
        cost_estimate=pl.CostEstimate(
            flops=0, bytes_accessed=4 * cache_keys.size, transcendentals=0
        ),
        name="pages",
    )(
        query, position_bias, bucket_edges, lengths, page_request, page_index,
        *in_hbm(cache_keys, cache_values),
    )
    near, bias = lax.optimization_barrier((jnp.concatenate(far, axis=0), bias))
    gathered = [near] + [
        lax.ppermute(near, "blk", xor_pairs(blocks, step)) for step in range(1, inner)
    ]
    own_score, value_new, out_near, up_near, down_near = pl.pallas_call(
        side_kernel,
        out_shape=(
            shape((own_rows, LANES), f32),
            shape((own_rows, width), bf16),
            pltpu.VMEM(out_weight.shape, bf16),
            pltpu.VMEM(up_weight.shape, bf16),
            pltpu.VMEM(down_weight.shape, bf16),
        ),
        in_specs=[VMEM_SPEC] * 4 + [HBM_SPEC] * 4 + [ANY_SPEC],
        out_specs=(VMEM_SPEC,) * 5,
        scratch_shapes=[
            pltpu.VMEM((2, model, width), bf16),
            pltpu.SemaphoreType.DMA((5,)),
        ],
        compiler_params=PARAMS,
        cost_estimate=pl.CostEstimate(
            flops=0, bytes_accessed=4 * (up_weight.size + model * width), transcendentals=0
        ),
        name="side",
    )(
        hidden_in, gain, query, position_bias,
        *in_hbm(qkv_weight, out_weight, up_weight, down_weight), near,
    )

    sums = pl.pallas_call(
        functools.partial(attend_kernel, len(gathered)),
        out_shape=shape((all_rows, width + LANES), bf16),
        in_specs=[VMEM_SPEC] * (len(gathered) + 7),
        out_specs=VMEM_SPEC,
        compiler_params=PARAMS,
        name="attend",
    )(*gathered, bias, picks, place, first, apart, keys, values)

    parts = lax.all_to_all(sums, "blk", 0, 0, tiled=True)

    own_part, sent_part = pl.pallas_call(
        merge_kernel,
        out_shape=(shape((own_rows, model), f32), shape((own_rows, model), bf16)),
        in_specs=[VMEM_SPEC] * 4,
        out_specs=(VMEM_SPEC,) * 2,
        compiler_params=PARAMS,
        name="merge",
    )(parts, own_score, value_new, out_near)

    halves = lax.axis_size("head")
    columns = model // halves
    exchanged = halves == 2
    if exchanged:
        other_part = lax.ppermute(sent_part, "head", xor_pairs(2, 1))
        mlp_out = (shape((own_rows, columns), f32), shape((own_rows, columns), bf16))
    else:
        own_part = jnp.zeros_like(own_part)
        other_part = lax.psum(sent_part, "head")
        mlp_out = (shape((own_rows, model), f32), shape((own_rows, model), bf16))

    kept, leaving = pl.pallas_call(
        functools.partial(mlp_kernel, exchanged),
        out_shape=mlp_out,
        in_specs=[VMEM_SPEC] * 6,
        out_specs=(VMEM_SPEC,) * 2,
        compiler_params=PARAMS,
        name="mlp",
    )(hidden_in, own_part, other_part, mlp_gain.reshape(1, model), up_near, down_near)

    if exchanged:
        arrived = lax.ppermute(leaving, "head", xor_pairs(2, 1))
    else:
        kept = lax.dynamic_slice_in_dim(kept, lax.axis_index("head") * columns, columns, 1)
        arrived = lax.psum_scatter(leaving, "head", scatter_dimension=1, tiled=True)
    return kept + arrived.astype(f32)


def solution(mesh):
    in_specs = (
        P("blk", None),
        P(),
        P(),
        P(None, None, "head"),
        P("head", None),
        P(None, "head"),
        P("head", None),
        P(None, "head"),
        P(),
        P("blk", None, "head"),
        P("blk", None, "head"),
        P(),
        P("blk"),
        P("blk"),
    )
    out_specs = P("blk", "head")
    return jax.shard_map(
        per_device, mesh=mesh, in_specs=in_specs, out_specs=out_specs, check_vma=False
    )
```

```python
import functools

import jax
import jax.numpy as jnp
from jax import lax
from jax.experimental import pallas as pl
from jax.experimental.pallas import tpu as pltpu
from jax.sharding import PartitionSpec as P

HEAD_DIM = 64
PAGE = 128
LANES = 128

far_below = -1e30
epsilon = 1e-06

VMEM_SPEC = pl.BlockSpec(memory_space=pltpu.VMEM)
SMEM_SPEC = pl.BlockSpec(memory_space=pltpu.SMEM)
ANY_SPEC = pl.BlockSpec(memory_space=pl.ANY)
HBM_SPEC = pl.BlockSpec(memory_space=pltpu.HBM)
PARAMS = pltpu.CompilerParams(vmem_limit_bytes=16 * 1024 * 1024)

PIECE = 8
SUM_LANE = 3 * PIECE


def iota(shape, axis):
    return lax.broadcasted_iota(jnp.int32, shape, axis)


def pieces(x, count):
    parts = []
    for _ in range(count):
        part = x.astype(jnp.bfloat16)
        parts.append(part)
        x = x - part.astype(jnp.float32)
    return parts


def rms_normed(x, gain):
    scale = lax.rsqrt(jnp.mean(x * x, axis=1, keepdims=True) + epsilon)
    return (x * scale * gain).astype(jnp.bfloat16)


def dot(a, b, dims=((1,), (0,)), precision=None):
    return lax.dot_general(
        a, b, (dims, ((), ())), preferred_element_type=jnp.float32, precision=precision
    )


def split_copies(source, target, sems, count):
    size = source.shape[0] // count
    return [
        pltpu.make_async_copy(
            source.at[pl.ds(i * size, size)], target.at[pl.ds(i * size, size)], sems.at[i]
        )
        for i in range(count)
    ]


def query_kernel(hidden_hbm, gain_hbm, weight_hbm, query_ref, hidden, gain, weight, sems):
    model = hidden.shape[1]
    small = [
        pltpu.make_async_copy(hidden_hbm, hidden, sems.at[0]),
        pltpu.make_async_copy(gain_hbm, gain, sems.at[1]),
    ]
    half = model // 2
    large = [
        pltpu.make_async_copy(
            weight_hbm.at[0, pl.ds(i * half, half)], weight.at[pl.ds(i * half, half)], sems.at[2 + i]
        )
        for i in range(2)
    ]
    for copy in small + large:
        copy.start()
    for copy in small:
        copy.wait()
    normed = rms_normed(hidden[...], gain[...])
    query = None
    for i, copy in enumerate(large):
        copy.wait()
        span = slice(i * half, (i + 1) * half)
        part = dot(normed[:, span], weight[span])
        query = part if query is None else query + part
    query_ref[...] = query.astype(jnp.bfloat16)


def page_kernel(
    own_rows, inner, outer, query_ref, table_ref, edges_ref, lengths_ref, request_ref, index_ref,
    keys_hbm,
    keys_ref, bias_ref, pick_ref, place_ref, first_ref, apart_ref,
    sems,
):
    copies = split_copies(keys_hbm, keys_ref, sems, sems.shape[0])
    for copy in copies:
        copy.start()
    me = lax.axis_index("blk")
    table = table_ref[...]
    buckets, heads = table.shape
    page_count = request_ref.shape[0]
    all_rows, depth = place_ref.shape
    eye = (iota((PIECE, heads), 0) == iota((PIECE, heads), 1)).astype(jnp.float32)
    by_head = dot(eye, table, ((1,), (1,)), lax.Precision.HIGHEST)
    columns = [jnp.broadcast_to(by_head[:, k : k + 1], (PIECE, PAGE)) for k in range(buckets)]
    token = iota((PIECE, PAGE), 1)
    row_of = iota((PIECE, all_rows), 1)
    page_of = iota((1, depth), 1) // PIECE
    lane = iota((1, LANES), 1)
    requests = [request_ref[p] for p in range(page_count)]
    owners = jnp.full((1, depth), -1, jnp.int32)
    by_lane = jnp.full((1, LANES), -2, jnp.int32)
    for p in range(page_count):
        owners = jnp.where(page_of == p, requests[p], owners)
        by_lane = jnp.where(lane == p, requests[p], by_lane)
    leads = jnp.full((1, depth), -1, jnp.int32)
    for p in range(page_count):
        owner = requests[p]
        left = lengths_ref[jnp.maximum(owner, 0)] - index_ref[p] * PAGE
        distance = jnp.where(owner >= 0, left, 0) - token
        bias = columns[0]
        for k in range(buckets - 1):
            bias = jnp.where(distance >= edges_ref[k], columns[k + 1], bias)
        bias_ref[p] = jnp.where(distance > 0, bias, far_below)
        known = jnp.maximum(owner, 0)
        apart_by = (known // own_rows) ^ me
        slot = (apart_by % inner) * outer + apart_by // inner
        slot = slot * own_rows + known % own_rows
        slot = jnp.where(owner >= 0, slot, -1)
        pick_ref[p] = (row_of == slot).astype(jnp.float32)
        same = by_lane == owner
        apart_ref[p : p + 1] = jnp.where(same, 0.0, 2 * far_below)
        earlier = jnp.max(jnp.where(same & (lane < p), 1, 0), axis=1, keepdims=True)
        leads = jnp.where((page_of == p) & (earlier == 0), owner, leads)
    row = iota((all_rows, depth), 0)
    place_ref[...] = (row == owners).astype(jnp.bfloat16)
    first_ref[...] = (row == leads).astype(jnp.bfloat16)
    for copy in copies:
        copy.wait()


def side_kernel(
    hidden_ref, gain_ref, query_ref, table_ref, weight_hbm, values_hbm, after_ref,
    score_ref, value_ref, values_ref,
    weight, weight_sems, sems,
):
    copies = [
        pltpu.make_async_copy(weight_hbm.at[1 + i], weight.at[i], weight_sems.at[i])
        for i in range(2)
    ]
    later = split_copies(values_hbm, values_ref, sems, sems.shape[0])
    for copy in copies + later:
        copy.start()
    normed = rms_normed(hidden_ref[...], gain_ref[...])
    heads = table_ref.shape[1]
    spread = (iota((heads, LANES), 0) == iota((heads, LANES), 1)).astype(jnp.float32)
    score = dot(table_ref[0:8], spread, precision=lax.Precision.HIGHEST)[0:1]
    copies[0].wait()
    key = dot(normed, weight[0]).astype(jnp.bfloat16)
    product = query_ref[...].astype(jnp.float32) * key.astype(jnp.float32)
    width = product.shape[1]
    gather = (iota((width, LANES), 0) // HEAD_DIM == iota((width, LANES), 1)).astype(jnp.bfloat16)
    for part in pieces(product, 3):
        score = score + dot(part, gather)
    score_ref[...] = score
    copies[1].wait()
    value_ref[...] = dot(normed, weight[1]).astype(jnp.bfloat16)
    for copy in later:
        copy.wait()


def load_kernel(*refs):
    count = (len(refs) - 2) // 2
    sources, targets, sems = refs[:count], refs[count + 1 : -1], refs[-1]
    copies = []
    for i, (source, target) in enumerate(zip(sources, targets)):
        copies += split_copies(source, target, sems.at[i], sems.shape[1])
    for copy in copies:
        copy.start()
    for copy in copies:
        copy.wait()


def attend_kernel(groups, *refs):
    query_refs = refs[:groups]
    (bias_ref, pick_ref, place_ref, first_ref, apart_ref, keys_ref, values_ref, sums_ref) = refs[
        groups:
    ]
    page_count, _, all_rows = pick_ref.shape
    width = keys_ref.shape[2]
    chunk = 2
    chunks = page_count // chunk
    picks = pick_ref[...].reshape(page_count * PIECE, all_rows).astype(jnp.bfloat16)
    queries = jnp.concatenate([ref[...] for ref in query_refs], axis=0)
    own_head = (iota((PIECE, width), 1) // HEAD_DIM == iota((PIECE, width), 0)).astype(jnp.float32)
    pair_heads = jnp.concatenate([own_head] * chunk, axis=0)
    chosen = dot(picks, queries)
    lane = iota((PIECE, LANES), 1)
    row = iota((PIECE, LANES), 0)
    scores = []
    tops = jnp.zeros((PIECE, LANES), jnp.float32)
    for c in range(chunks):
        rows = chosen[c * chunk * PIECE : (c + 1) * chunk * PIECE]
        split = (rows * pair_heads).astype(jnp.bfloat16)
        block = keys_ref[c * chunk : (c + 1) * chunk].reshape(chunk * PAGE, width)
        raw = dot(split, block, ((1,), (1,)))
        for i in range(chunk):
            p = c * chunk + i
            part = raw[i * PIECE : (i + 1) * PIECE, i * PAGE : (i + 1) * PAGE]
            score = part + bias_ref[p]
            scores.append(score)
            tops = jnp.where(lane == p, jnp.max(score, axis=1, keepdims=True), tops)
    mixes, peaks, totals = [], [], []
    nothing = jnp.zeros((PIECE, PAGE), jnp.float32)
    for c in range(chunks):
        blocks = []
        for i in range(chunk):
            p = c * chunk + i
            peak = jnp.max(tops + apart_ref[p : p + 1], axis=1, keepdims=True)
            weight = jnp.exp(scores[p] - peak)
            total = jnp.sum(weight, axis=1, keepdims=True)
            peaks.append(jnp.where(lane == row, peak, 0.0))
            totals.append(jnp.where(lane == row + SUM_LANE, total, 0.0))
            blocks.append(
                jnp.concatenate([weight if k == i else nothing for k in range(chunk)], axis=1)
            )
        weights = jnp.concatenate(blocks, axis=0).astype(jnp.bfloat16)
        block = values_ref[c * chunk : (c + 1) * chunk].reshape(chunk * PAGE, width)
        mixes.append(dot(weights, block) * pair_heads)
    mix = jnp.concatenate(mixes, axis=0)
    place, first = place_ref[...], first_ref[...]
    high, low = pieces(mix, 2)
    sums = dot(place, high) + dot(place, low)
    sums_ref[:, :width] = sums.astype(jnp.bfloat16)
    collected = sum(dot(first, part) for part in pieces(jnp.concatenate(peaks, axis=0), 3))
    collected += sum(dot(place, part) for part in pieces(jnp.concatenate(totals, axis=0), 3))
    one, two, three = (part.astype(jnp.float32) for part in pieces(collected, 3))
    sums_ref[:, width:] = (
        one + pltpu.roll(two, PIECE, 1) + pltpu.roll(three, 2 * PIECE, 1)
    ).astype(jnp.bfloat16)


def merge_kernel(parts_ref, score_ref, value_ref, weight_ref, own_ref, send_ref):
    own_rows, width = value_ref.shape
    sources = parts_ref.shape[0] // own_rows
    stats = parts_ref[:, width:].astype(jnp.float32)
    stats = stats + pltpu.roll(stats, LANES - PIECE, 1) + pltpu.roll(stats, LANES - 2 * PIECE, 1)
    sums = pltpu.roll(stats, LANES - SUM_LANE, 1)
    heads = width // HEAD_DIM
    used = iota(stats.shape, 1) < heads
    peaks = jnp.where(used & (sums > 0.0), stats, far_below)
    sums = jnp.where(used, sums, 0.0)
    own_score = jnp.where(iota(score_ref.shape, 1) < heads, score_ref[...], 0.0)
    peak = own_score
    for s in range(sources):
        peak = jnp.maximum(peak, peaks[s * own_rows : (s + 1) * own_rows])
    own_weight = jnp.exp(own_score - peak)
    total = own_weight
    factors = []
    for s in range(sources):
        rows = slice(s * own_rows, (s + 1) * own_rows)
        factor = jnp.exp(peaks[rows] - peak)
        total = total + factor * sums[rows]
        factors.append(factor)
    factors.append(own_weight.astype(jnp.bfloat16).astype(jnp.float32))
    shares = jnp.concatenate([factor / total for factor in factors], axis=0)
    spread = (iota((LANES, width), 0) == iota((LANES, width), 1) // HEAD_DIM).astype(jnp.bfloat16)
    shares = sum(dot(part, spread) for part in pieces(shares, 3))
    mixed = value_ref[...].astype(jnp.float32) * shares[sources * own_rows :]
    for s in range(sources):
        rows = slice(s * own_rows, (s + 1) * own_rows)
        mixed = mixed + parts_ref[rows, :width].astype(jnp.float32) * shares[rows]
    projected = dot(mixed.astype(jnp.bfloat16), weight_ref[...])
    own_ref[...] = projected
    send_ref[...] = projected.astype(jnp.bfloat16)


def mlp_kernel(exchanged, hidden_ref, own_ref, other_ref, gain_ref, up_ref, down_ref, *outs):
    middle = hidden_ref[...] + (own_ref[...] + other_ref[...].astype(jnp.float32))
    normed = rms_normed(middle, gain_ref[...])
    active = jnp.maximum(dot(normed, up_ref[...]), 0.0).astype(jnp.bfloat16)
    down = dot(active, down_ref[...])
    if exchanged:
        kept_ref, sent_ref = outs
        columns = kept_ref.shape[1]
        low = lax.axis_index("head") == 0
        left, right = slice(0, columns), slice(columns, 2 * columns)
        kept = middle + down

        @pl.when(low)
        def _():
            kept_ref[...] = kept[:, left]
            sent_ref[...] = down[:, right].astype(jnp.bfloat16)

        @pl.when(jnp.logical_not(low))
        def _():
            kept_ref[...] = kept[:, right]
            sent_ref[...] = down[:, left].astype(jnp.bfloat16)

    else:
        middle_ref, down_out_ref = outs
        middle_ref[...] = middle
        down_out_ref[...] = down.astype(jnp.bfloat16)


def in_hbm(*arrays):
    return [pltpu.with_memory_space_constraint(array, pltpu.HBM) for array in arrays]


def xor_pairs(size, step):
    return [(i, i ^ step) for i in range(size)]


def per_device(
    hidden_in, attention_gain, mlp_gain, qkv_weight, out_weight, up_weight, down_weight,
    position_bias, bucket_edges, cache_keys, cache_values, lengths, page_request, page_index,
):
    f32, bf16 = jnp.float32, jnp.bfloat16
    shape = jax.ShapeDtypeStruct
    own_rows, model = hidden_in.shape
    width = qkv_weight.shape[2]
    page_count = page_request.shape[0]
    blocks = lax.axis_size("blk")
    all_rows = own_rows * blocks
    gain = attention_gain.reshape(1, model)
    query = pl.pallas_call(
        query_kernel,
        out_shape=shape((own_rows, width), bf16),
        in_specs=[HBM_SPEC] * 3,
        out_specs=VMEM_SPEC,
        scratch_shapes=[
            pltpu.VMEM((own_rows, model), f32),
            pltpu.VMEM((1, model), f32),
            pltpu.VMEM((model, width), bf16),
            pltpu.SemaphoreType.DMA((4,)),
        ],
        compiler_params=PARAMS,
        name="query",
    )(*in_hbm(hidden_in, gain, qkv_weight))

    inner = 1
    while inner * inner < blocks:
        inner *= 2
    far = [query] + [
        lax.ppermute(query, "blk", xor_pairs(blocks, step * inner))
        for step in range(1, blocks // inner)
    ]
    depth = page_count * PIECE
    keys, bias, picks, place, first, apart = pl.pallas_call(
        functools.partial(page_kernel, own_rows, inner, blocks // inner),
        out_shape=(
            pltpu.VMEM(cache_keys.shape, bf16),
            shape((page_count, PIECE, PAGE), f32),
            shape((page_count, PIECE, all_rows), f32),
            shape((all_rows, depth), bf16),
            shape((all_rows, depth), bf16),
            shape((page_count, LANES), f32),
        ),
        in_specs=[VMEM_SPEC] * 2 + [SMEM_SPEC] * 4 + [HBM_SPEC],
        out_specs=(VMEM_SPEC,) * 6,
        scratch_shapes=[pltpu.SemaphoreType.DMA((6,))],
        compiler_params=PARAMS,
        cost_estimate=pl.CostEstimate(
            flops=0, bytes_accessed=2 * cache_keys.size, transcendentals=0
        ),
        name="pages",
    )(
        query, position_bias, bucket_edges, lengths, page_request, page_index,
        *in_hbm(cache_keys),
    )
    near, bias = lax.optimization_barrier((jnp.concatenate(far, axis=0), bias))
    gathered = [near] + [
        lax.ppermute(near, "blk", xor_pairs(blocks, step)) for step in range(1, inner)
    ]
    own_score, value_new, values = pl.pallas_call(
        side_kernel,
        out_shape=(
            shape((own_rows, LANES), f32),
            shape((own_rows, width), bf16),
            pltpu.VMEM(cache_values.shape, bf16),
        ),
        in_specs=[VMEM_SPEC] * 4 + [HBM_SPEC] * 2 + [ANY_SPEC],
        out_specs=(VMEM_SPEC,) * 3,
        scratch_shapes=[
            pltpu.VMEM((2, model, width), bf16),
            pltpu.SemaphoreType.DMA((2,)),
            pltpu.SemaphoreType.DMA((6,)),
        ],
        compiler_params=PARAMS,
        cost_estimate=pl.CostEstimate(
            flops=0, bytes_accessed=2 * cache_values.size + 4 * model * width, transcendentals=0
        ),
        name="side",
    )(hidden_in, gain, query, position_bias, *in_hbm(qkv_weight, cache_values), near)

    sums = pl.pallas_call(
        functools.partial(attend_kernel, len(gathered)),
        out_shape=shape((all_rows, width + LANES), bf16),
        in_specs=[VMEM_SPEC] * (len(gathered) + 7),
        out_specs=VMEM_SPEC,
        compiler_params=PARAMS,
        name="attend",
    )(*gathered, bias, picks, place, first, apart, keys, values)

    loaded = (out_weight, up_weight, down_weight)
    out_near, up_near, down_near = (
        pltpu.with_memory_space_constraint(array, pltpu.VMEM)
        for array in pl.pallas_call(
            load_kernel,
            out_shape=tuple(pltpu.VMEM(array.shape, bf16) for array in loaded),
            in_specs=[HBM_SPEC] * 3 + [ANY_SPEC],
            out_specs=(VMEM_SPEC,) * 3,
            scratch_shapes=[pltpu.SemaphoreType.DMA((3, 8))],
            compiler_params=PARAMS,
            cost_estimate=pl.CostEstimate(
                flops=0, bytes_accessed=2 * sum(a.size for a in loaded), transcendentals=0
            ),
            name="load",
        )(*in_hbm(*loaded), sums)
    )

    parts = lax.all_to_all(sums, "blk", 0, 0, tiled=True)

    own_part, sent_part = pl.pallas_call(
        merge_kernel,
        out_shape=(shape((own_rows, model), f32), shape((own_rows, model), bf16)),
        in_specs=[VMEM_SPEC] * 4,
        out_specs=(VMEM_SPEC,) * 2,
        compiler_params=PARAMS,
        name="merge",
    )(parts, own_score, value_new, out_near)

    halves = lax.axis_size("head")
    columns = model // halves
    exchanged = halves == 2
    if exchanged:
        other_part = lax.ppermute(sent_part, "head", xor_pairs(2, 1))
        mlp_out = (shape((own_rows, columns), f32), shape((own_rows, columns), bf16))
    else:
        own_part = jnp.zeros_like(own_part)
        other_part = lax.psum(sent_part, "head")
        mlp_out = (shape((own_rows, model), f32), shape((own_rows, model), bf16))

    kept, leaving = pl.pallas_call(
        functools.partial(mlp_kernel, exchanged),
        out_shape=mlp_out,
        in_specs=[VMEM_SPEC] * 6,
        out_specs=(VMEM_SPEC,) * 2,
        compiler_params=PARAMS,
        name="mlp",
    )(hidden_in, own_part, other_part, mlp_gain.reshape(1, model), up_near, down_near)

    if exchanged:
        arrived = lax.ppermute(leaving, "head", xor_pairs(2, 1))
    else:
        kept = lax.dynamic_slice_in_dim(kept, lax.axis_index("head") * columns, columns, 1)
        arrived = lax.psum_scatter(leaving, "head", scatter_dimension=1, tiled=True)
    return kept + arrived.astype(f32)


def solution(mesh):
    in_specs = (
        P("blk", None),
        P(),
        P(),
        P(None, None, "head"),
        P("head", None),
        P(None, "head"),
        P("head", None),
        P(None, "head"),
        P(),
        P("blk", None, "head"),
        P("blk", None, "head"),
        P(),
        P("blk"),
        P("blk"),
    )
    out_specs = P("blk", "head")
    return jax.shard_map(
        per_device, mesh=mesh, in_specs=in_specs, out_specs=out_specs, check_vma=False
    )
```

```python
import functools

import jax
import jax.numpy as jnp
from jax import lax
from jax.experimental import pallas as pl
from jax.experimental.pallas import tpu as pltpu
from jax.sharding import PartitionSpec as P

HEAD_DIM = 64
PAGE = 128
LANES = 128

far_below = -1e30
epsilon = 1e-06

VMEM_SPEC = pl.BlockSpec(memory_space=pltpu.VMEM)
SMEM_SPEC = pl.BlockSpec(memory_space=pltpu.SMEM)
ANY_SPEC = pl.BlockSpec(memory_space=pl.ANY)
HBM_SPEC = pl.BlockSpec(memory_space=pltpu.HBM)
PARAMS = pltpu.CompilerParams(vmem_limit_bytes=16 * 1024 * 1024)

PIECE = 8
SUM_LANE = 3 * PIECE


def iota(shape, axis):
    return lax.broadcasted_iota(jnp.int32, shape, axis)


def pieces(x, count):
    parts = []
    for _ in range(count):
        part = x.astype(jnp.bfloat16)
        parts.append(part)
        x = x - part.astype(jnp.float32)
    return parts


def rms_normed(x, gain):
    scale = lax.rsqrt(jnp.mean(x * x, axis=1, keepdims=True) + epsilon)
    return (x * scale * gain).astype(jnp.bfloat16)


def dot(a, b, dims=((1,), (0,)), precision=None):
    return lax.dot_general(
        a, b, (dims, ((), ())), preferred_element_type=jnp.float32, precision=precision
    )


def split_copies(source, target, sems, count):
    size = source.shape[0] // count
    return [
        pltpu.make_async_copy(
            source.at[pl.ds(i * size, size)], target.at[pl.ds(i * size, size)], sems.at[i]
        )
        for i in range(count)
    ]


def query_kernel(hidden_hbm, gain_hbm, weight_hbm, query_ref, hidden, gain, weight, sems):
    model = hidden.shape[1]
    small = [
        pltpu.make_async_copy(hidden_hbm, hidden, sems.at[0]),
        pltpu.make_async_copy(gain_hbm, gain, sems.at[1]),
    ]
    half = model // 2
    large = [
        pltpu.make_async_copy(
            weight_hbm.at[0, pl.ds(i * half, half)], weight.at[pl.ds(i * half, half)], sems.at[2 + i]
        )
        for i in range(2)
    ]
    for copy in small + large:
        copy.start()
    for copy in small:
        copy.wait()
    normed = rms_normed(hidden[...], gain[...])
    query = None
    for i, copy in enumerate(large):
        copy.wait()
        span = slice(i * half, (i + 1) * half)
        part = dot(normed[:, span], weight[span])
        query = part if query is None else query + part
    query_ref[...] = query.astype(jnp.bfloat16)


def page_kernel(
    own_rows, inner, outer, query_ref, request_ref, keys_hbm,
    keys_ref, pick_ref, place_ref, first_ref, apart_ref,
    sems,
):
    copies = split_copies(keys_hbm, keys_ref, sems, sems.shape[0])
    for copy in copies:
        copy.start()
    me = lax.axis_index("blk")
    page_count = request_ref.shape[0]
    all_rows, depth = place_ref.shape
    row_of = iota((PIECE, all_rows), 1)
    page_of = iota((1, depth), 1) // PIECE
    lane = iota((1, LANES), 1)
    requests = [request_ref[p] for p in range(page_count)]
    owners = jnp.full((1, depth), -1, jnp.int32)
    by_lane = jnp.full((1, LANES), -2, jnp.int32)
    for p in range(page_count):
        owners = jnp.where(page_of == p, requests[p], owners)
        by_lane = jnp.where(lane == p, requests[p], by_lane)
    leads = jnp.full((1, depth), -1, jnp.int32)
    for p in range(page_count):
        owner = requests[p]
        known = jnp.maximum(owner, 0)
        apart_by = (known // own_rows) ^ me
        slot = (apart_by % inner) * outer + apart_by // inner
        slot = slot * own_rows + known % own_rows
        slot = jnp.where(owner >= 0, slot, -1)
        pick_ref[p] = (row_of == slot).astype(jnp.float32)
        same = by_lane == owner
        apart_ref[p : p + 1] = jnp.where(same, 0.0, 2 * far_below)
        earlier = jnp.max(jnp.where(same & (lane < p), 1, 0), axis=1, keepdims=True)
        leads = jnp.where((page_of == p) & (earlier == 0), owner, leads)
    row = iota((all_rows, depth), 0)
    place_ref[...] = (row == owners).astype(jnp.bfloat16)
    first_ref[...] = (row == leads).astype(jnp.bfloat16)
    for copy in copies:
        copy.wait()


def bias_kernel(
    table_ref, edges_ref, lengths_ref, request_ref, index_ref, values_hbm, after_ref,
    values_ref, bias_ref,
    sems,
):
    copies = split_copies(values_hbm, values_ref, sems, sems.shape[0])
    for copy in copies:
        copy.start()
    table = table_ref[...]
    buckets, heads = table.shape
    eye = (iota((PIECE, heads), 0) == iota((PIECE, heads), 1)).astype(jnp.float32)
    by_head = dot(eye, table, ((1,), (1,)), lax.Precision.HIGHEST)
    columns = [jnp.broadcast_to(by_head[:, k : k + 1], (PIECE, PAGE)) for k in range(buckets)]
    token = iota((PIECE, PAGE), 1)
    for p in range(request_ref.shape[0]):
        owner = request_ref[p]
        left = lengths_ref[jnp.maximum(owner, 0)] - index_ref[p] * PAGE
        distance = jnp.where(owner >= 0, left, 0) - token
        bias = columns[0]
        for k in range(buckets - 1):
            bias = jnp.where(distance >= edges_ref[k], columns[k + 1], bias)
        bias_ref[p] = jnp.where(distance > 0, bias, far_below)
    for copy in copies:
        copy.wait()


def side_kernel(
    hidden_ref, gain_ref, query_ref, table_ref, weight_hbm, out_hbm, up_hbm, after_ref,
    score_ref, value_ref, out_ref, up_ref,
    weight, weight_sems, sems,
):
    copies = [
        pltpu.make_async_copy(weight_hbm.at[1 + i], weight.at[i], weight_sems.at[i])
        for i in range(2)
    ]
    later = split_copies(out_hbm, out_ref, sems.at[0], 2)
    later += split_copies(up_hbm, up_ref, sems.at[1], sems.shape[1])
    for copy in copies + later:
        copy.start()
    normed = rms_normed(hidden_ref[...], gain_ref[...])
    heads = table_ref.shape[1]
    spread = (iota((heads, LANES), 0) == iota((heads, LANES), 1)).astype(jnp.float32)
    score = dot(table_ref[0:8], spread, precision=lax.Precision.HIGHEST)[0:1]
    copies[0].wait()
    key = dot(normed, weight[0]).astype(jnp.bfloat16)
    product = query_ref[...].astype(jnp.float32) * key.astype(jnp.float32)
    width = product.shape[1]
    gather = (iota((width, LANES), 0) // HEAD_DIM == iota((width, LANES), 1)).astype(jnp.bfloat16)
    for part in pieces(product, 3):
        score = score + dot(part, gather)
    score_ref[...] = score
    copies[1].wait()
    value_ref[...] = dot(normed, weight[1]).astype(jnp.bfloat16)
    for copy in later:
        copy.wait()


def load_kernel(source, after_ref, target, sems):
    copies = split_copies(source, target, sems, sems.shape[0])
    for copy in copies:
        copy.start()
    for copy in copies:
        copy.wait()


def attend_kernel(groups, *refs):
    query_refs = refs[:groups]
    (bias_ref, pick_ref, place_ref, first_ref, apart_ref, keys_ref, values_ref, sums_ref) = refs[
        groups:
    ]
    page_count, _, all_rows = pick_ref.shape
    width = keys_ref.shape[2]
    chunk = 2
    chunks = page_count // chunk
    picks = pick_ref[...].reshape(page_count * PIECE, all_rows).astype(jnp.bfloat16)
    queries = jnp.concatenate([ref[...] for ref in query_refs], axis=0)
    own_head = (iota((PIECE, width), 1) // HEAD_DIM == iota((PIECE, width), 0)).astype(jnp.float32)
    pair_heads = jnp.concatenate([own_head] * chunk, axis=0)
    chosen = dot(picks, queries)
    lane = iota((PIECE, LANES), 1)
    row = iota((PIECE, LANES), 0)
    scores = []
    tops = jnp.zeros((PIECE, LANES), jnp.float32)
    for c in range(chunks):
        rows = chosen[c * chunk * PIECE : (c + 1) * chunk * PIECE]
        split = (rows * pair_heads).astype(jnp.bfloat16)
        block = keys_ref[c * chunk : (c + 1) * chunk].reshape(chunk * PAGE, width)
        raw = dot(split, block, ((1,), (1,)))
        for i in range(chunk):
            p = c * chunk + i
            part = raw[i * PIECE : (i + 1) * PIECE, i * PAGE : (i + 1) * PAGE]
            score = part + bias_ref[p]
            scores.append(score)
            tops = jnp.where(lane == p, jnp.max(score, axis=1, keepdims=True), tops)
    mixes, peaks, totals = [], [], []
    nothing = jnp.zeros((PIECE, PAGE), jnp.float32)
    for c in range(chunks):
        blocks = []
        for i in range(chunk):
            p = c * chunk + i
            peak = jnp.max(tops + apart_ref[p : p + 1], axis=1, keepdims=True)
            weight = jnp.exp(scores[p] - peak)
            total = jnp.sum(weight, axis=1, keepdims=True)
            peaks.append(jnp.where(lane == row, peak, 0.0))
            totals.append(jnp.where(lane == row + SUM_LANE, total, 0.0))
            blocks.append(
                jnp.concatenate([weight if k == i else nothing for k in range(chunk)], axis=1)
            )
        weights = jnp.concatenate(blocks, axis=0).astype(jnp.bfloat16)
        block = values_ref[c * chunk : (c + 1) * chunk].reshape(chunk * PAGE, width)
        mixes.append(dot(weights, block) * pair_heads)
    mix = jnp.concatenate(mixes, axis=0)
    place, first = place_ref[...], first_ref[...]
    high, low = pieces(mix, 2)
    sums = dot(place, high) + dot(place, low)
    sums_ref[:, :width] = sums.astype(jnp.bfloat16)
    collected = sum(dot(first, part) for part in pieces(jnp.concatenate(peaks, axis=0), 3))
    collected += sum(dot(place, part) for part in pieces(jnp.concatenate(totals, axis=0), 3))
    one, two, three = (part.astype(jnp.float32) for part in pieces(collected, 3))
    sums_ref[:, width:] = (
        one + pltpu.roll(two, PIECE, 1) + pltpu.roll(three, 2 * PIECE, 1)
    ).astype(jnp.bfloat16)


def merge_kernel(parts_ref, score_ref, value_ref, weight_ref, own_ref, send_ref):
    own_rows, width = value_ref.shape
    sources = parts_ref.shape[0] // own_rows
    stats = parts_ref[:, width:].astype(jnp.float32)
    stats = stats + pltpu.roll(stats, LANES - PIECE, 1) + pltpu.roll(stats, LANES - 2 * PIECE, 1)
    sums = pltpu.roll(stats, LANES - SUM_LANE, 1)
    heads = width // HEAD_DIM
    used = iota(stats.shape, 1) < heads
    peaks = jnp.where(used & (sums > 0.0), stats, far_below)
    sums = jnp.where(used, sums, 0.0)
    own_score = jnp.where(iota(score_ref.shape, 1) < heads, score_ref[...], 0.0)
    peak = own_score
    for s in range(sources):
        peak = jnp.maximum(peak, peaks[s * own_rows : (s + 1) * own_rows])
    own_weight = jnp.exp(own_score - peak)
    total = own_weight
    factors = []
    for s in range(sources):
        rows = slice(s * own_rows, (s + 1) * own_rows)
        factor = jnp.exp(peaks[rows] - peak)
        total = total + factor * sums[rows]
        factors.append(factor)
    factors.append(own_weight.astype(jnp.bfloat16).astype(jnp.float32))
    shares = jnp.concatenate([factor / total for factor in factors], axis=0)
    spread = (iota((LANES, width), 0) == iota((LANES, width), 1) // HEAD_DIM).astype(jnp.bfloat16)
    shares = sum(dot(part, spread) for part in pieces(shares, 3))
    mixed = value_ref[...].astype(jnp.float32) * shares[sources * own_rows :]
    for s in range(sources):
        rows = slice(s * own_rows, (s + 1) * own_rows)
        mixed = mixed + parts_ref[rows, :width].astype(jnp.float32) * shares[rows]
    projected = dot(mixed.astype(jnp.bfloat16), weight_ref[...])
    own_ref[...] = projected
    send_ref[...] = projected.astype(jnp.bfloat16)


def mlp_kernel(exchanged, hidden_ref, own_ref, other_ref, gain_ref, up_ref, down_ref, *outs):
    middle = hidden_ref[...] + (own_ref[...] + other_ref[...].astype(jnp.float32))
    normed = rms_normed(middle, gain_ref[...])
    active = jnp.maximum(dot(normed, up_ref[...]), 0.0).astype(jnp.bfloat16)
    down = dot(active, down_ref[...])
    if exchanged:
        kept_ref, sent_ref = outs
        columns = kept_ref.shape[1]
        low = lax.axis_index("head") == 0
        left, right = slice(0, columns), slice(columns, 2 * columns)
        kept = middle + down

        @pl.when(low)
        def _():
            kept_ref[...] = kept[:, left]
            sent_ref[...] = down[:, right].astype(jnp.bfloat16)

        @pl.when(jnp.logical_not(low))
        def _():
            kept_ref[...] = kept[:, right]
            sent_ref[...] = down[:, left].astype(jnp.bfloat16)

    else:
        middle_ref, down_out_ref = outs
        middle_ref[...] = middle
        down_out_ref[...] = down.astype(jnp.bfloat16)


def loading(*arrays):
    return pl.CostEstimate(
        flops=0, bytes_accessed=sum(2 * array.size for array in arrays), transcendentals=0
    )


def in_hbm(*arrays):
    return [pltpu.with_memory_space_constraint(array, pltpu.HBM) for array in arrays]


def xor_pairs(size, step):
    return [(i, i ^ step) for i in range(size)]


def per_device(
    hidden_in, attention_gain, mlp_gain, qkv_weight, out_weight, up_weight, down_weight,
    position_bias, bucket_edges, cache_keys, cache_values, lengths, page_request, page_index,
):
    f32, bf16 = jnp.float32, jnp.bfloat16
    shape = jax.ShapeDtypeStruct
    own_rows, model = hidden_in.shape
    width = qkv_weight.shape[2]
    page_count = page_request.shape[0]
    blocks = lax.axis_size("blk")
    all_rows = own_rows * blocks
    gain = attention_gain.reshape(1, model)
    query = pl.pallas_call(
        query_kernel,
        out_shape=shape((own_rows, width), bf16),
        in_specs=[HBM_SPEC] * 3,
        out_specs=VMEM_SPEC,
        scratch_shapes=[
            pltpu.VMEM((own_rows, model), f32),
            pltpu.VMEM((1, model), f32),
            pltpu.VMEM((model, width), bf16),
            pltpu.SemaphoreType.DMA((4,)),
        ],
        compiler_params=PARAMS,
        name="query",
    )(*in_hbm(hidden_in, gain, qkv_weight))

    inner = 1
    while inner * inner < blocks:
        inner *= 2
    far = [query] + [
        lax.ppermute(query, "blk", xor_pairs(blocks, step * inner))
        for step in range(1, blocks // inner)
    ]
    depth = page_count * PIECE
    keys, picks, place, first, apart = pl.pallas_call(
        functools.partial(page_kernel, own_rows, inner, blocks // inner),
        out_shape=(
            pltpu.VMEM(cache_keys.shape, bf16),
            shape((page_count, PIECE, all_rows), f32),
            shape((all_rows, depth), bf16),
            shape((all_rows, depth), bf16),
            shape((page_count, LANES), f32),
        ),
        in_specs=[ANY_SPEC, SMEM_SPEC, HBM_SPEC],
        out_specs=(VMEM_SPEC,) * 5,
        scratch_shapes=[pltpu.SemaphoreType.DMA((6,))],
        compiler_params=PARAMS,
        cost_estimate=loading(cache_keys),
        name="pages",
    )(query, page_request, *in_hbm(cache_keys))
    near, apart = lax.optimization_barrier((jnp.concatenate(far, axis=0), apart))
    gathered = [near] + [
        lax.ppermute(near, "blk", xor_pairs(blocks, step)) for step in range(1, inner)
    ]
    values, bias = pl.pallas_call(
        bias_kernel,
        out_shape=(
            pltpu.VMEM(cache_values.shape, bf16),
            shape((page_count, PIECE, PAGE), f32),
        ),
        in_specs=[VMEM_SPEC] + [SMEM_SPEC] * 4 + [HBM_SPEC, ANY_SPEC],
        out_specs=(VMEM_SPEC,) * 2,
        scratch_shapes=[pltpu.SemaphoreType.DMA((6,))],
        compiler_params=PARAMS,
        cost_estimate=loading(cache_values),
        name="bias",
    )(
        position_bias, bucket_edges, lengths, page_request, page_index,
        *in_hbm(cache_values), near,
    )

    sums = pl.pallas_call(
        functools.partial(attend_kernel, len(gathered)),
        out_shape=shape((all_rows, width + LANES), bf16),
        in_specs=[VMEM_SPEC] * (len(gathered) + 7),
        out_specs=VMEM_SPEC,
        compiler_params=PARAMS,
        name="attend",
    )(*gathered, bias, picks, place, first, apart, keys, values)

    own_score, value_new, out_near, up_near = pl.pallas_call(
        side_kernel,
        out_shape=(
            shape((own_rows, LANES), f32),
            shape((own_rows, width), bf16),
            pltpu.VMEM(out_weight.shape, bf16),
            pltpu.VMEM(up_weight.shape, bf16),
        ),
        in_specs=[VMEM_SPEC] * 4 + [HBM_SPEC] * 3 + [ANY_SPEC],
        out_specs=(VMEM_SPEC,) * 4,
        scratch_shapes=[
            pltpu.VMEM((2, model, width), bf16),
            pltpu.SemaphoreType.DMA((2,)),
            pltpu.SemaphoreType.DMA((2, 8)),
        ],
        compiler_params=PARAMS,
        cost_estimate=loading(up_weight, out_weight, out_weight, out_weight),
        name="side",
    )(
        hidden_in, gain, query, position_bias,
        *in_hbm(qkv_weight, out_weight, up_weight), sums,
    )

    parts = lax.all_to_all(sums, "blk", 0, 0, tiled=True)

    own_part, sent_part = pl.pallas_call(
        merge_kernel,
        out_shape=(shape((own_rows, model), f32), shape((own_rows, model), bf16)),
        in_specs=[VMEM_SPEC] * 4,
        out_specs=(VMEM_SPEC,) * 2,
        compiler_params=PARAMS,
        name="merge",
    )(parts, own_score, value_new, out_near)

    halves = lax.axis_size("head")
    columns = model // halves
    exchanged = halves == 2
    down_near = pl.pallas_call(
        load_kernel,
        out_shape=pltpu.VMEM(down_weight.shape, bf16),
        in_specs=[HBM_SPEC, ANY_SPEC],
        out_specs=VMEM_SPEC,
        scratch_shapes=[pltpu.SemaphoreType.DMA((8,))],
        compiler_params=PARAMS,
        cost_estimate=loading(down_weight),
        name="load",
    )(*in_hbm(down_weight), sent_part)
    if exchanged:
        other_part = lax.ppermute(sent_part, "head", xor_pairs(2, 1))
        mlp_out = (shape((own_rows, columns), f32), shape((own_rows, columns), bf16))
    else:
        own_part = jnp.zeros_like(own_part)
        other_part = lax.psum(sent_part, "head")
        mlp_out = (shape((own_rows, model), f32), shape((own_rows, model), bf16))

    kept, leaving = pl.pallas_call(
        functools.partial(mlp_kernel, exchanged),
        out_shape=mlp_out,
        in_specs=[VMEM_SPEC] * 6,
        out_specs=(VMEM_SPEC,) * 2,
        compiler_params=PARAMS,
        name="mlp",
    )(hidden_in, own_part, other_part, mlp_gain.reshape(1, model), up_near, down_near)

    if exchanged:
        arrived = lax.ppermute(leaving, "head", xor_pairs(2, 1))
    else:
        kept = lax.dynamic_slice_in_dim(kept, lax.axis_index("head") * columns, columns, 1)
        arrived = lax.psum_scatter(leaving, "head", scatter_dimension=1, tiled=True)
    return kept + arrived.astype(f32)


def solution(mesh):
    in_specs = (
        P("blk", None),
        P(),
        P(),
        P(None, None, "head"),
        P("head", None),
        P(None, "head"),
        P("head", None),
        P(None, "head"),
        P(),
        P("blk", None, "head"),
        P("blk", None, "head"),
        P(),
        P("blk"),
        P("blk"),
    )
    out_specs = P("blk", "head")
    return jax.shard_map(
        per_device, mesh=mesh, in_specs=in_specs, out_specs=out_specs, check_vma=False
    )
```

```python
import functools

import jax
import jax.numpy as jnp
from jax import lax
from jax.experimental import pallas as pl
from jax.experimental.pallas import tpu as pltpu
from jax.sharding import PartitionSpec as P

HEAD_DIM = 64
PAGE = 128
LANES = 128

far_below = -1e30
epsilon = 1e-06

VMEM_SPEC = pl.BlockSpec(memory_space=pltpu.VMEM)
SMEM_SPEC = pl.BlockSpec(memory_space=pltpu.SMEM)
ANY_SPEC = pl.BlockSpec(memory_space=pl.ANY)
HBM_SPEC = pl.BlockSpec(memory_space=pltpu.HBM)
PARAMS = pltpu.CompilerParams(vmem_limit_bytes=16 * 1024 * 1024)

PIECE = 8
SUM_LANE = 3 * PIECE


def iota(shape, axis):
    return lax.broadcasted_iota(jnp.int32, shape, axis)


def split_index(x, size):
    if size & (size - 1):
        return lax.div(x, size), lax.rem(x, size)
    return x >> (size.bit_length() - 1), x & (size - 1)


def head_of(shape, axis):
    return split_index(iota(shape, axis), HEAD_DIM)[0]


def pieces(x, count):
    parts = []
    for _ in range(count):
        part = x.astype(jnp.bfloat16)
        parts.append(part)
        x = x - part.astype(jnp.float32)
    return parts


def rms_normed(x, gain):
    scale = lax.rsqrt(jnp.mean(x * x, axis=1, keepdims=True) + epsilon)
    return (x * scale * gain).astype(jnp.bfloat16)


def dot(a, b, dims=((1,), (0,)), precision=None):
    return lax.dot_general(
        a, b, (dims, ((), ())), preferred_element_type=jnp.float32, precision=precision
    )


def split_copies(source, target, sems, count):
    size = source.shape[0] // count
    return [
        pltpu.make_async_copy(
            source.at[pl.ds(i * size, size)], target.at[pl.ds(i * size, size)], sems.at[i]
        )
        for i in range(count)
    ]


def query_kernel(hidden_hbm, gain_hbm, weight_hbm, query_ref, hidden, gain, weight, sems):
    model = hidden.shape[1]
    small = [
        pltpu.make_async_copy(hidden_hbm, hidden, sems.at[0]),
        pltpu.make_async_copy(gain_hbm, gain, sems.at[1]),
    ]
    half = model // 2
    large = [
        pltpu.make_async_copy(
            weight_hbm.at[0, pl.ds(i * half, half)], weight.at[pl.ds(i * half, half)], sems.at[2 + i]
        )
        for i in range(2)
    ]
    for copy in small + large:
        copy.start()
    for copy in small:
        copy.wait()
    normed = rms_normed(hidden[...], gain[...])
    query = None
    for i, copy in enumerate(large):
        copy.wait()
        span = slice(i * half, (i + 1) * half)
        part = dot(normed[:, span], weight[span])
        query = part if query is None else query + part
    query_ref[...] = query.astype(jnp.bfloat16)


def page_kernel(
    own_rows, inner, outer, query_ref, request_ref, keys_hbm,
    keys_ref, pick_ref, place_ref, first_ref, apart_ref,
    sems,
):
    copies = split_copies(keys_hbm, keys_ref, sems, sems.shape[0])
    for copy in copies:
        copy.start()
    me = lax.axis_index("blk")
    page_count = request_ref.shape[0]
    all_rows, depth = place_ref.shape
    row_of = iota((PIECE, all_rows), 1)
    page_of = split_index(iota((1, depth), 1), PIECE)[0]
    lane = iota((1, LANES), 1)
    requests = [request_ref[p] for p in range(page_count)]
    owners = jnp.full((1, depth), -1, jnp.int32)
    by_lane = jnp.full((1, LANES), -2, jnp.int32)
    for p in range(page_count):
        owners = jnp.where(page_of == p, requests[p], owners)
        by_lane = jnp.where(lane == p, requests[p], by_lane)
    leads = jnp.full((1, depth), -1, jnp.int32)
    for p in range(page_count):
        owner = requests[p]
        device, own_row = split_index(jnp.maximum(owner, 0), own_rows)
        high, low = split_index(device ^ me, inner)
        slot = (low * outer + high) * own_rows + own_row
        slot = jnp.where(owner >= 0, slot, -1)
        pick_ref[p] = (row_of == slot).astype(jnp.float32)
        same = by_lane == owner
        apart_ref[p : p + 1] = jnp.where(same, 0.0, 2 * far_below)
        earlier = jnp.max(jnp.where(same & (lane < p), 1, 0), axis=1, keepdims=True)
        leads = jnp.where((page_of == p) & (earlier == 0), owner, leads)
    row = iota((all_rows, depth), 0)
    place_ref[...] = (row == owners).astype(jnp.bfloat16)
    first_ref[...] = (row == leads).astype(jnp.bfloat16)
    for copy in copies:
        copy.wait()


def bias_kernel(
    table_hbm, edges_hbm, lengths_hbm, index_hbm, request_ref, values_hbm, after_ref,
    values_ref, bias_ref,
    table, edges_ref, lengths_ref, index_ref, small_sems, sems,
):
    sources = (table_hbm, edges_hbm, lengths_hbm, index_hbm)
    targets = (table, edges_ref, lengths_ref, index_ref)
    small = [
        pltpu.make_async_copy(source, target, small_sems.at[i])
        for i, (source, target) in enumerate(zip(sources, targets))
    ]
    first_pages = values_hbm.at[pl.ds(0, values_ref.shape[0])]
    copies = split_copies(first_pages, values_ref, sems, sems.shape[0])
    for copy in small + copies:
        copy.start()
    for copy in small:
        copy.wait()
    heads, buckets = table.shape
    by_head = table[...]
    if heads < PIECE:
        by_head = jnp.concatenate([by_head[min(h, heads - 1)][None] for h in range(PIECE)], axis=0)
    columns = [jnp.broadcast_to(by_head[:, k : k + 1], (PIECE, PAGE)) for k in range(buckets)]
    token = iota((PIECE, PAGE), 1)
    for p in range(request_ref.shape[0]):
        owner = request_ref[p]
        left = lengths_ref[jnp.maximum(owner, 0)] - index_ref[p] * PAGE
        distance = jnp.where(owner >= 0, left, 0) - token
        bias = columns[0]
        for k in range(buckets - 1):
            bias = jnp.where(distance >= edges_ref[k], columns[k + 1], bias)
        bias_ref[p] = jnp.where(distance > 0, bias, far_below)
    for copy in copies:
        copy.wait()


def side_kernel(
    hidden_ref, gain_ref, query_ref, table_ref, weight_hbm, out_hbm, after_ref,
    score_ref, value_ref, out_ref,
    weight, weight_sems, sems,
):
    copies = [
        pltpu.make_async_copy(weight_hbm.at[1 + i], weight.at[i], weight_sems.at[i])
        for i in range(2)
    ]
    later = split_copies(out_hbm, out_ref, sems, sems.shape[0])
    for copy in copies + later:
        copy.start()
    normed = rms_normed(hidden_ref[...], gain_ref[...])
    heads = table_ref.shape[0]
    spread = iota((heads, LANES), 0) == iota((heads, LANES), 1)
    score = jnp.sum(jnp.where(spread, table_ref[:, 0:1], 0.0), axis=0, keepdims=True)
    copies[0].wait()
    key = dot(normed, weight[0]).astype(jnp.bfloat16)
    product = query_ref[...].astype(jnp.float32) * key.astype(jnp.float32)
    width = product.shape[1]
    gather = (head_of((width, LANES), 0) == iota((width, LANES), 1)).astype(jnp.bfloat16)
    for part in pieces(product, 3):
        score = score + dot(part, gather)
    score_ref[...] = score
    copies[1].wait()
    value_ref[...] = dot(normed, weight[1]).astype(jnp.bfloat16)
    for copy in later:
        copy.wait()


def load_kernel(source, after_ref, target, sems):
    copies = split_copies(source, target, sems, sems.shape[0])
    for copy in copies:
        copy.start()
    for copy in copies:
        copy.wait()


def attend_kernel(groups, *refs):
    query_refs = refs[:groups]
    bias_ref, pick_ref, place_ref, first_ref, apart_ref, keys_ref, values_ref = refs[groups:-4]
    values_hbm, sums_ref, late, sems = refs[-4:]
    early = values_ref.shape[0]
    copies = split_copies(values_hbm.at[pl.ds(early, late.shape[0])], late, sems, sems.shape[0])
    for copy in copies:
        copy.start()
    page_count, _, all_rows = pick_ref.shape
    width = keys_ref.shape[2]
    chunk = 2
    chunks = page_count // chunk
    picks = pick_ref[...].reshape(page_count * PIECE, all_rows).astype(jnp.bfloat16)
    queries = jnp.concatenate([ref[...] for ref in query_refs], axis=0)
    own_head = (head_of((PIECE, width), 1) == iota((PIECE, width), 0)).astype(jnp.float32)
    pair_heads = jnp.concatenate([own_head] * chunk, axis=0)
    chosen = dot(picks, queries)
    lane = iota((PIECE, LANES), 1)
    row = iota((PIECE, LANES), 0)
    scores = []
    tops = jnp.zeros((PIECE, LANES), jnp.float32)
    for c in range(chunks):
        rows = chosen[c * chunk * PIECE : (c + 1) * chunk * PIECE]
        split = (rows * pair_heads).astype(jnp.bfloat16)
        block = keys_ref[c * chunk : (c + 1) * chunk].reshape(chunk * PAGE, width)
        raw = dot(split, block, ((1,), (1,)))
        for i in range(chunk):
            p = c * chunk + i
            part = raw[i * PIECE : (i + 1) * PIECE, i * PAGE : (i + 1) * PAGE]
            score = part + bias_ref[p]
            scores.append(score)
            tops = jnp.where(lane == p, jnp.max(score, axis=1, keepdims=True), tops)
    mixes, peaks, totals = [], [], []
    nothing = jnp.zeros((PIECE, PAGE), jnp.float32)
    for c in range(chunks):
        blocks = []
        for i in range(chunk):
            p = c * chunk + i
            peak = jnp.max(tops + apart_ref[p : p + 1], axis=1, keepdims=True)
            weight = jnp.exp(scores[p] - peak)
            total = jnp.sum(weight, axis=1, keepdims=True)
            peaks.append(jnp.where(lane == row, peak, 0.0))
            totals.append(jnp.where(lane == row + SUM_LANE, total, 0.0))
            blocks.append(
                jnp.concatenate([weight if k == i else nothing for k in range(chunk)], axis=1)
            )
        weights = jnp.concatenate(blocks, axis=0).astype(jnp.bfloat16)
        at = c * chunk
        if at == early:
            for copy in copies:
                copy.wait()
        block = values_ref[at : at + chunk] if at < early else late[at - early : at - early + chunk]
        block = block.reshape(chunk * PAGE, width)
        mixes.append(dot(weights, block) * pair_heads)
    mix = jnp.concatenate(mixes, axis=0)
    place, first = place_ref[...], first_ref[...]
    high, low = pieces(mix, 2)
    sums = dot(place, high) + dot(place, low)
    sums_ref[:, :width] = sums.astype(jnp.bfloat16)
    collected = sum(dot(first, part) for part in pieces(jnp.concatenate(peaks, axis=0), 3))
    collected += sum(dot(place, part) for part in pieces(jnp.concatenate(totals, axis=0), 3))
    one, two, three = (part.astype(jnp.float32) for part in pieces(collected, 3))
    sums_ref[:, width:] = (
        one + pltpu.roll(two, PIECE, 1) + pltpu.roll(three, 2 * PIECE, 1)
    ).astype(jnp.bfloat16)


def merge_kernel(parts_ref, score_ref, value_ref, weight_ref, own_ref, send_ref):
    own_rows, width = value_ref.shape
    sources = parts_ref.shape[0] // own_rows
    stats = parts_ref[:, width:].astype(jnp.float32)
    stats = stats + pltpu.roll(stats, LANES - PIECE, 1) + pltpu.roll(stats, LANES - 2 * PIECE, 1)
    sums = pltpu.roll(stats, LANES - SUM_LANE, 1)
    heads = width // HEAD_DIM
    used = iota(stats.shape, 1) < heads
    peaks = jnp.where(used & (sums > 0.0), stats, far_below)
    sums = jnp.where(used, sums, 0.0)
    own_score = jnp.where(iota(score_ref.shape, 1) < heads, score_ref[...], 0.0)
    peak = own_score
    for s in range(sources):
        peak = jnp.maximum(peak, peaks[s * own_rows : (s + 1) * own_rows])
    own_weight = jnp.exp(own_score - peak)
    total = own_weight
    factors = []
    for s in range(sources):
        rows = slice(s * own_rows, (s + 1) * own_rows)
        factor = jnp.exp(peaks[rows] - peak)
        total = total + factor * sums[rows]
        factors.append(factor)
    factors.append(own_weight.astype(jnp.bfloat16).astype(jnp.float32))
    shares = jnp.concatenate([factor / total for factor in factors], axis=0)
    spread = (iota((LANES, width), 0) == head_of((LANES, width), 1)).astype(jnp.bfloat16)
    shares = sum(dot(part, spread) for part in pieces(shares, 3))
    mixed = value_ref[...].astype(jnp.float32) * shares[sources * own_rows :]
    for s in range(sources):
        rows = slice(s * own_rows, (s + 1) * own_rows)
        mixed = mixed + parts_ref[rows, :width].astype(jnp.float32) * shares[rows]
    projected = dot(mixed.astype(jnp.bfloat16), weight_ref[...])
    own_ref[...] = projected
    send_ref[...] = projected.astype(jnp.bfloat16)


def mlp_kernel(exchanged, hidden_ref, own_ref, other_ref, gain_ref, up_ref, down_ref, *outs):
    middle = hidden_ref[...] + (own_ref[...] + other_ref[...].astype(jnp.float32))
    normed = rms_normed(middle, gain_ref[...])
    active = jnp.maximum(dot(normed, up_ref[...]), 0.0).astype(jnp.bfloat16)
    down = dot(active, down_ref[...])
    if exchanged:
        kept_ref, sent_ref = outs
        columns = kept_ref.shape[1]
        low = lax.axis_index("head") == 0
        left, right = slice(0, columns), slice(columns, 2 * columns)
        kept = middle + down

        @pl.when(low)
        def _():
            kept_ref[...] = kept[:, left]
            sent_ref[...] = down[:, right].astype(jnp.bfloat16)

        @pl.when(jnp.logical_not(low))
        def _():
            kept_ref[...] = kept[:, right]
            sent_ref[...] = down[:, left].astype(jnp.bfloat16)

    else:
        middle_ref, down_out_ref = outs
        middle_ref[...] = middle
        down_out_ref[...] = down.astype(jnp.bfloat16)


def loading(*arrays):
    return pl.CostEstimate(
        flops=0, bytes_accessed=sum(2 * array.size for array in arrays), transcendentals=0
    )


def in_hbm(*arrays):
    return [pltpu.with_memory_space_constraint(array, pltpu.HBM) for array in arrays]


def xor_pairs(size, step):
    return [(i, i ^ step) for i in range(size)]


def per_device(
    hidden_in, attention_gain, mlp_gain, qkv_weight, out_weight, up_weight, down_weight,
    position_bias, bucket_edges, cache_keys, cache_values, lengths, page_request, page_index,
):
    f32, bf16 = jnp.float32, jnp.bfloat16
    shape = jax.ShapeDtypeStruct
    own_rows, model = hidden_in.shape
    width = qkv_weight.shape[2]
    page_count = page_request.shape[0]
    blocks = lax.axis_size("blk")
    all_rows = own_rows * blocks
    gain = attention_gain.reshape(1, model)
    query = pl.pallas_call(
        query_kernel,
        out_shape=shape((own_rows, width), bf16),
        in_specs=[HBM_SPEC] * 3,
        out_specs=VMEM_SPEC,
        scratch_shapes=[
            pltpu.VMEM((own_rows, model), f32),
            pltpu.VMEM((1, model), f32),
            pltpu.VMEM((model, width), bf16),
            pltpu.SemaphoreType.DMA((4,)),
        ],
        compiler_params=PARAMS,
        name="query",
    )(*in_hbm(hidden_in, gain, qkv_weight))

    inner = 1
    while inner * inner < blocks:
        inner *= 2
    far = [query] + [
        lax.ppermute(query, "blk", xor_pairs(blocks, step * inner))
        for step in range(1, blocks // inner)
    ]
    depth = page_count * PIECE
    keys, picks, place, first, apart = pl.pallas_call(
        functools.partial(page_kernel, own_rows, inner, blocks // inner),
        out_shape=(
            pltpu.VMEM(cache_keys.shape, bf16),
            shape((page_count, PIECE, all_rows), f32),
            shape((all_rows, depth), bf16),
            shape((all_rows, depth), bf16),
            shape((page_count, LANES), f32),
        ),
        in_specs=[ANY_SPEC, SMEM_SPEC, HBM_SPEC],
        out_specs=(VMEM_SPEC,) * 5,
        scratch_shapes=[pltpu.SemaphoreType.DMA((6,))],
        compiler_params=PARAMS,
        cost_estimate=loading(cache_keys),
        name="pages",
    )(query, page_request, *in_hbm(cache_keys))
    near, apart = lax.optimization_barrier((jnp.concatenate(far, axis=0), apart))
    gathered = [near] + [
        lax.ppermute(near, "blk", xor_pairs(blocks, step)) for step in range(1, inner)
    ]
    early = page_count // 2
    table = position_bias.T
    values, bias = pl.pallas_call(
        bias_kernel,
        out_shape=(
            pltpu.VMEM((early,) + cache_values.shape[1:], bf16),
            shape((page_count, PIECE, PAGE), f32),
        ),
        in_specs=[HBM_SPEC] * 4 + [SMEM_SPEC, HBM_SPEC, ANY_SPEC],
        out_specs=(VMEM_SPEC,) * 2,
        scratch_shapes=[
            pltpu.VMEM(table.shape, f32),
            pltpu.SMEM(bucket_edges.shape, jnp.int32),
            pltpu.SMEM(lengths.shape, jnp.int32),
            pltpu.SMEM(page_index.shape, jnp.int32),
            pltpu.SemaphoreType.DMA((4,)),
            pltpu.SemaphoreType.DMA((4,)),
        ],
        compiler_params=PARAMS,
        cost_estimate=loading(cache_values),
        name="bias",
    )(
        *in_hbm(table, bucket_edges, lengths, page_index), page_request,
        *in_hbm(cache_values), near,
    )

    sums = pl.pallas_call(
        functools.partial(attend_kernel, len(gathered)),
        out_shape=shape((all_rows, width + LANES), bf16),
        in_specs=[VMEM_SPEC] * (len(gathered) + 7) + [HBM_SPEC],
        out_specs=VMEM_SPEC,
        scratch_shapes=[
            pltpu.VMEM((page_count - early,) + cache_values.shape[1:], bf16),
            pltpu.SemaphoreType.DMA((4,)),
        ],
        compiler_params=PARAMS,
        name="attend",
    )(*gathered, bias, picks, place, first, apart, keys, values, *in_hbm(cache_values))

    own_score, value_new, out_near = pl.pallas_call(
        side_kernel,
        out_shape=(
            shape((own_rows, LANES), f32),
            shape((own_rows, width), bf16),
            pltpu.VMEM(out_weight.shape, bf16),
        ),
        in_specs=[VMEM_SPEC] * 4 + [HBM_SPEC] * 2 + [ANY_SPEC],
        out_specs=(VMEM_SPEC,) * 3,
        scratch_shapes=[
            pltpu.VMEM((2, model, width), bf16),
            pltpu.SemaphoreType.DMA((2,)),
            pltpu.SemaphoreType.DMA((4,)),
        ],
        compiler_params=PARAMS,
        cost_estimate=loading(out_weight, out_weight, out_weight),
        name="side",
    )(
        hidden_in, gain, query, table,
        *in_hbm(qkv_weight, out_weight), sums,
    )

    parts = lax.all_to_all(sums, "blk", 0, 0, tiled=True)

    own_part, sent_part = pl.pallas_call(
        merge_kernel,
        out_shape=(shape((own_rows, model), f32), shape((own_rows, model), bf16)),
        in_specs=[VMEM_SPEC] * 4,
        out_specs=(VMEM_SPEC,) * 2,
        compiler_params=PARAMS,
        name="merge",
    )(parts, own_score, value_new, out_near)

    halves = lax.axis_size("head")
    columns = model // halves
    exchanged = halves == 2
    down_near = pl.pallas_call(
        load_kernel,
        out_shape=pltpu.VMEM(down_weight.shape, bf16),
        in_specs=[HBM_SPEC, ANY_SPEC],
        out_specs=VMEM_SPEC,
        scratch_shapes=[pltpu.SemaphoreType.DMA((8,))],
        compiler_params=PARAMS,
        cost_estimate=loading(down_weight),
        name="load",
    )(*in_hbm(down_weight), sent_part)
    if exchanged:
        other_part = lax.ppermute(sent_part, "head", xor_pairs(2, 1))
        mlp_out = (shape((own_rows, columns), f32), shape((own_rows, columns), bf16))
    else:
        own_part = jnp.zeros_like(own_part)
        other_part = lax.psum(sent_part, "head")
        mlp_out = (shape((own_rows, model), f32), shape((own_rows, model), bf16))

    kept, leaving = pl.pallas_call(
        functools.partial(mlp_kernel, exchanged),
        out_shape=mlp_out,
        in_specs=[VMEM_SPEC] * 6,
        out_specs=(VMEM_SPEC,) * 2,
        compiler_params=PARAMS,
        name="mlp",
    )(hidden_in, own_part, other_part, mlp_gain.reshape(1, model), up_weight, down_near)

    if exchanged:
        arrived = lax.ppermute(leaving, "head", xor_pairs(2, 1))
    else:
        kept = lax.dynamic_slice_in_dim(kept, lax.axis_index("head") * columns, columns, 1)
        arrived = lax.psum_scatter(leaving, "head", scatter_dimension=1, tiled=True)
    return kept + arrived.astype(f32)


def solution(mesh):
    in_specs = (
        P("blk", None),
        P(),
        P(),
        P(None, None, "head"),
        P("head", None),
        P(None, "head"),
        P("head", None),
        P(None, "head"),
        P(),
        P("blk", None, "head"),
        P("blk", None, "head"),
        P(),
        P("blk"),
        P("blk"),
    )
    out_specs = P("blk", "head")
    return jax.shard_map(
        per_device, mesh=mesh, in_specs=in_specs, out_specs=out_specs, check_vma=False
    )
```

```python
import functools

import jax
import jax.numpy as jnp
from jax import lax
from jax.experimental import pallas as pl
from jax.experimental.pallas import tpu as pltpu
from jax.sharding import PartitionSpec as P

HEAD_DIM = 64
PAGE = 128
LANES = 128

far_below = -1e30
epsilon = 1e-06

VMEM_SPEC = pl.BlockSpec(memory_space=pltpu.VMEM)
SMEM_SPEC = pl.BlockSpec(memory_space=pltpu.SMEM)
ANY_SPEC = pl.BlockSpec(memory_space=pl.ANY)
HBM_SPEC = pl.BlockSpec(memory_space=pltpu.HBM)
PARAMS = pltpu.CompilerParams(vmem_limit_bytes=16 * 1024 * 1024)

PIECE = 8
SUM_LANE = 3 * PIECE


def iota(shape, axis):
    return lax.broadcasted_iota(jnp.int32, shape, axis)


def split_index(x, size):
    if size & (size - 1):
        return lax.div(x, size), lax.rem(x, size)
    return x >> (size.bit_length() - 1), x & (size - 1)


def head_of(shape, axis):
    return split_index(iota(shape, axis), HEAD_DIM)[0]


def pieces(x, count):
    parts = []
    for _ in range(count):
        part = x.astype(jnp.bfloat16)
        parts.append(part)
        x = x - part.astype(jnp.float32)
    return parts


def rms_normed(x, gain):
    scale = lax.rsqrt(jnp.mean(x * x, axis=1, keepdims=True) + epsilon)
    return (x * scale * gain).astype(jnp.bfloat16)


def dot(a, b, dims=((1,), (0,)), precision=None):
    return lax.dot_general(
        a, b, (dims, ((), ())), preferred_element_type=jnp.float32, precision=precision
    )


def split_copies(source, target, sems, count):
    size = source.shape[0] // count
    return [
        pltpu.make_async_copy(
            source.at[pl.ds(i * size, size)], target.at[pl.ds(i * size, size)], sems.at[i]
        )
        for i in range(count)
    ]


def query_kernel(hidden_hbm, gain_hbm, weight_hbm, query_ref, hidden, gain, weight, sems):
    model = hidden.shape[1]
    small = [
        pltpu.make_async_copy(hidden_hbm, hidden, sems.at[0]),
        pltpu.make_async_copy(gain_hbm, gain, sems.at[1]),
    ]
    half = model // 2
    large = [
        pltpu.make_async_copy(
            weight_hbm.at[0, pl.ds(i * half, half)], weight.at[pl.ds(i * half, half)], sems.at[2 + i]
        )
        for i in range(2)
    ]
    for copy in small + large:
        copy.start()
    for copy in small:
        copy.wait()
    normed = rms_normed(hidden[...], gain[...])
    query = None
    for i, copy in enumerate(large):
        copy.wait()
        span = slice(i * half, (i + 1) * half)
        part = dot(normed[:, span], weight[span])
        query = part if query is None else query + part
    query_ref[...] = query.astype(jnp.bfloat16)


def page_kernel(
    own_rows, inner, outer, query_ref, request_ref, keys_hbm,
    keys_ref, pick_ref, place_ref, first_ref, apart_ref,
    sems,
):
    copies = split_copies(keys_hbm, keys_ref, sems, sems.shape[0])
    for copy in copies:
        copy.start()
    me = lax.axis_index("blk")
    page_count = request_ref.shape[0]
    all_rows, depth = place_ref.shape
    row_of = iota((PIECE, all_rows), 1)
    page_of = split_index(iota((1, depth), 1), PIECE)[0]
    lane = iota((1, LANES), 1)
    requests = [request_ref[p] for p in range(page_count)]
    owners = jnp.full((1, depth), -1, jnp.int32)
    by_lane = jnp.full((1, LANES), -2, jnp.int32)
    for p in range(page_count):
        owners = jnp.where(page_of == p, requests[p], owners)
        by_lane = jnp.where(lane == p, requests[p], by_lane)
    leads = jnp.full((1, depth), -1, jnp.int32)
    picks = []
    for p in range(page_count):
        owner = requests[p]
        device, own_row = split_index(jnp.maximum(owner, 0), own_rows)
        high, low = split_index(device ^ me, inner)
        slot = (low * outer + high) * own_rows + own_row
        slot = jnp.where(owner >= 0, slot, -1)
        picks.append((row_of == slot).astype(jnp.float32))
        same = by_lane == owner
        apart_ref[p : p + 1] = jnp.where(same, 0.0, 2 * far_below)
        earlier = jnp.max(jnp.where(same & (lane < p), 1, 0), axis=1, keepdims=True)
        leads = jnp.where((page_of == p) & (earlier == 0), owner, leads)
    pick_ref[...] = jnp.concatenate(picks, axis=0).astype(jnp.bfloat16)
    row = iota((all_rows, depth), 0)
    place_ref[...] = (row == owners).astype(jnp.bfloat16)
    first_ref[...] = (row == leads).astype(jnp.bfloat16)
    for copy in copies:
        copy.wait()


def bias_kernel(
    table_hbm, edges_hbm, lengths_hbm, index_hbm, request_ref, after_ref,
    bias_ref,
    table, edges_ref, lengths_ref, index_ref, small_sems,
):
    sources = (table_hbm, edges_hbm, lengths_hbm, index_hbm)
    targets = (table, edges_ref, lengths_ref, index_ref)
    small = [
        pltpu.make_async_copy(source, target, small_sems.at[i])
        for i, (source, target) in enumerate(zip(sources, targets))
    ]
    for copy in small:
        copy.start()
    for copy in small:
        copy.wait()
    heads, buckets = table.shape
    by_head = table[...]
    if heads < PIECE:
        by_head = jnp.concatenate([by_head[min(h, heads - 1)][None] for h in range(PIECE)], axis=0)
    columns = [jnp.broadcast_to(by_head[:, k : k + 1], (PIECE, PAGE)) for k in range(buckets)]
    token = iota((PIECE, PAGE), 1)
    for p in range(request_ref.shape[0]):
        owner = request_ref[p]
        left = lengths_ref[jnp.maximum(owner, 0)] - index_ref[p] * PAGE
        distance = jnp.where(owner >= 0, left, 0) - token
        bias = columns[0]
        for k in range(buckets - 1):
            bias = jnp.where(distance >= edges_ref[k], columns[k + 1], bias)
        bias_ref[p] = jnp.where(distance > 0, bias, far_below)


def side_kernel(
    hidden_ref, gain_ref, query_ref, table_ref, weight_hbm, out_hbm, after_ref,
    score_ref, value_ref, out_ref,
    weight, weight_sems, sems,
):
    copies = [
        pltpu.make_async_copy(weight_hbm.at[1 + i], weight.at[i], weight_sems.at[i])
        for i in range(2)
    ]
    later = split_copies(out_hbm, out_ref, sems, sems.shape[0])
    for copy in copies + later:
        copy.start()
    normed = rms_normed(hidden_ref[...], gain_ref[...])
    heads = table_ref.shape[0]
    spread = iota((heads, LANES), 0) == iota((heads, LANES), 1)
    score = jnp.sum(jnp.where(spread, table_ref[:, 0:1], 0.0), axis=0, keepdims=True)
    copies[0].wait()
    key = dot(normed, weight[0]).astype(jnp.bfloat16)
    product = query_ref[...].astype(jnp.float32) * key.astype(jnp.float32)
    width = product.shape[1]
    gather = (head_of((width, LANES), 0) == iota((width, LANES), 1)).astype(jnp.bfloat16)
    for part in pieces(product, 3):
        score = score + dot(part, gather)
    score_ref[...] = score
    copies[1].wait()
    value_ref[...] = dot(normed, weight[1]).astype(jnp.bfloat16)
    for copy in later:
        copy.wait()


def load_kernel(source, after_ref, target, sems):
    copies = split_copies(source, target, sems, sems.shape[0])
    for copy in copies:
        copy.start()
    for copy in copies:
        copy.wait()


def attend_kernel(groups, *refs):
    query_refs = refs[:groups]
    (bias_ref, pick_ref, place_ref, first_ref, apart_ref, keys_ref, values_ref, sums_ref) = refs[
        groups:
    ]
    page_count = apart_ref.shape[0]
    width = keys_ref.shape[2]
    chunk = 2
    chunks = page_count // chunk
    queries = jnp.concatenate([ref[...] for ref in query_refs], axis=0)
    own_head = (head_of((PIECE, width), 1) == iota((PIECE, width), 0)).astype(jnp.float32)
    pair_heads = jnp.concatenate([own_head] * chunk, axis=0)
    chosen = dot(pick_ref[...], queries)
    lane = iota((PIECE, LANES), 1)
    row = iota((PIECE, LANES), 0)
    scores = []
    tops = jnp.zeros((PIECE, LANES), jnp.float32)
    for c in range(chunks):
        rows = chosen[c * chunk * PIECE : (c + 1) * chunk * PIECE]
        split = (rows * pair_heads).astype(jnp.bfloat16)
        block = keys_ref[c * chunk : (c + 1) * chunk].reshape(chunk * PAGE, width)
        raw = dot(split, block, ((1,), (1,)))
        for i in range(chunk):
            p = c * chunk + i
            part = raw[i * PIECE : (i + 1) * PIECE, i * PAGE : (i + 1) * PAGE]
            score = part + bias_ref[p]
            scores.append(score)
            tops = jnp.where(lane == p, jnp.max(score, axis=1, keepdims=True), tops)
    mixes, peaks, totals = [], [], []
    nothing = jnp.zeros((PIECE, PAGE), jnp.float32)
    for c in range(chunks):
        blocks = []
        for i in range(chunk):
            p = c * chunk + i
            peak = jnp.max(tops + apart_ref[p : p + 1], axis=1, keepdims=True)
            weight = jnp.exp(scores[p] - peak)
            total = jnp.sum(weight, axis=1, keepdims=True)
            peaks.append(jnp.where(lane == row, peak, 0.0))
            totals.append(jnp.where(lane == row + SUM_LANE, total, 0.0))
            blocks.append(
                jnp.concatenate([weight if k == i else nothing for k in range(chunk)], axis=1)
            )
        weights = jnp.concatenate(blocks, axis=0).astype(jnp.bfloat16)
        block = values_ref[c * chunk : (c + 1) * chunk].reshape(chunk * PAGE, width)
        mixes.append(dot(weights, block) * pair_heads)
    mix = jnp.concatenate(mixes, axis=0)
    place, first = place_ref[...], first_ref[...]
    high, low = pieces(mix, 2)
    sums = dot(place, high) + dot(place, low)
    sums_ref[:, :width] = sums.astype(jnp.bfloat16)
    collected = sum(dot(first, part) for part in pieces(jnp.concatenate(peaks, axis=0), 3))
    collected += sum(dot(place, part) for part in pieces(jnp.concatenate(totals, axis=0), 3))
    one, two, three = (part.astype(jnp.float32) for part in pieces(collected, 3))
    sums_ref[:, width:] = (
        one + pltpu.roll(two, PIECE, 1) + pltpu.roll(three, 2 * PIECE, 1)
    ).astype(jnp.bfloat16)


def merge_kernel(parts_ref, score_ref, value_ref, weight_ref, own_ref, send_ref):
    own_rows, width = value_ref.shape
    sources = parts_ref.shape[0] // own_rows
    stats = parts_ref[:, width:].astype(jnp.float32)
    stats = stats + pltpu.roll(stats, LANES - PIECE, 1) + pltpu.roll(stats, LANES - 2 * PIECE, 1)
    sums = pltpu.roll(stats, LANES - SUM_LANE, 1)
    heads = width // HEAD_DIM
    used = iota(stats.shape, 1) < heads
    peaks = jnp.where(used & (sums > 0.0), stats, far_below)
    sums = jnp.where(used, sums, 0.0)
    own_score = jnp.where(iota(score_ref.shape, 1) < heads, score_ref[...], 0.0)
    peak = own_score
    for s in range(sources):
        peak = jnp.maximum(peak, peaks[s * own_rows : (s + 1) * own_rows])
    own_weight = jnp.exp(own_score - peak)
    total = own_weight
    factors = []
    for s in range(sources):
        rows = slice(s * own_rows, (s + 1) * own_rows)
        factor = jnp.exp(peaks[rows] - peak)
        total = total + factor * sums[rows]
        factors.append(factor)
    factors.append(own_weight.astype(jnp.bfloat16).astype(jnp.float32))
    shares = jnp.concatenate([factor / total for factor in factors], axis=0)
    spread = (iota((LANES, width), 0) == head_of((LANES, width), 1)).astype(jnp.bfloat16)
    shares = sum(dot(part, spread) for part in pieces(shares, 3))
    mixed = value_ref[...].astype(jnp.float32) * shares[sources * own_rows :]
    for s in range(sources):
        rows = slice(s * own_rows, (s + 1) * own_rows)
        mixed = mixed + parts_ref[rows, :width].astype(jnp.float32) * shares[rows]
    projected = dot(mixed.astype(jnp.bfloat16), weight_ref[...])
    own_ref[...] = projected
    send_ref[...] = projected.astype(jnp.bfloat16)


def mlp_kernel(exchanged, hidden_ref, own_ref, other_ref, gain_ref, up_ref, down_ref, *outs):
    middle = hidden_ref[...] + (own_ref[...] + other_ref[...].astype(jnp.float32))
    normed = rms_normed(middle, gain_ref[...])
    active = jnp.maximum(dot(normed, up_ref[...]), 0.0).astype(jnp.bfloat16)
    down = dot(active, down_ref[...])
    if exchanged:
        kept_ref, sent_ref = outs
        columns = kept_ref.shape[1]
        low = lax.axis_index("head") == 0
        left, right = slice(0, columns), slice(columns, 2 * columns)
        kept = middle + down

        @pl.when(low)
        def _():
            kept_ref[...] = kept[:, left]
            sent_ref[...] = down[:, right].astype(jnp.bfloat16)

        @pl.when(jnp.logical_not(low))
        def _():
            kept_ref[...] = kept[:, right]
            sent_ref[...] = down[:, left].astype(jnp.bfloat16)

    else:
        middle_ref, down_out_ref = outs
        middle_ref[...] = middle
        down_out_ref[...] = down.astype(jnp.bfloat16)


def loading(*arrays):
    return pl.CostEstimate(
        flops=0, bytes_accessed=sum(2 * array.size for array in arrays), transcendentals=0
    )


def in_hbm(*arrays):
    return [pltpu.with_memory_space_constraint(array, pltpu.HBM) for array in arrays]


def xor_pairs(size, step):
    return [(i, i ^ step) for i in range(size)]


def per_device(
    hidden_in, attention_gain, mlp_gain, qkv_weight, out_weight, up_weight, down_weight,
    position_bias, bucket_edges, cache_keys, cache_values, lengths, page_request, page_index,
):
    f32, bf16 = jnp.float32, jnp.bfloat16
    shape = jax.ShapeDtypeStruct
    own_rows, model = hidden_in.shape
    width = qkv_weight.shape[2]
    page_count = page_request.shape[0]
    blocks = lax.axis_size("blk")
    all_rows = own_rows * blocks
    gain = attention_gain.reshape(1, model)
    query = pl.pallas_call(
        query_kernel,
        out_shape=shape((own_rows, width), bf16),
        in_specs=[HBM_SPEC] * 3,
        out_specs=VMEM_SPEC,
        scratch_shapes=[
            pltpu.VMEM((own_rows, model), f32),
            pltpu.VMEM((1, model), f32),
            pltpu.VMEM((model, width), bf16),
            pltpu.SemaphoreType.DMA((4,)),
        ],
        compiler_params=PARAMS,
        name="query",
    )(*in_hbm(hidden_in, gain, qkv_weight))

    inner = 1
    while inner * inner < blocks:
        inner *= 2
    far = [query] + [
        lax.ppermute(query, "blk", xor_pairs(blocks, step * inner))
        for step in range(1, blocks // inner)
    ]
    depth = page_count * PIECE
    keys, picks, place, first, apart = pl.pallas_call(
        functools.partial(page_kernel, own_rows, inner, blocks // inner),
        out_shape=(
            pltpu.VMEM(cache_keys.shape, bf16),
            shape((depth, all_rows), bf16),
            shape((all_rows, depth), bf16),
            shape((all_rows, depth), bf16),
            shape((page_count, LANES), f32),
        ),
        in_specs=[ANY_SPEC, SMEM_SPEC, HBM_SPEC],
        out_specs=(VMEM_SPEC,) * 5,
        scratch_shapes=[pltpu.SemaphoreType.DMA((6,))],
        compiler_params=PARAMS,
        cost_estimate=loading(cache_keys),
        name="pages",
    )(query, page_request, *in_hbm(cache_keys))
    near, apart = lax.optimization_barrier((jnp.concatenate(far, axis=0), apart))
    gathered = [near] + [
        lax.ppermute(near, "blk", xor_pairs(blocks, step)) for step in range(1, inner)
    ]
    table = position_bias.T
    bias = pl.pallas_call(
        bias_kernel,
        out_shape=shape((page_count, PIECE, PAGE), f32),
        in_specs=[HBM_SPEC] * 4 + [SMEM_SPEC, ANY_SPEC],
        out_specs=VMEM_SPEC,
        scratch_shapes=[
            pltpu.VMEM(table.shape, f32),
            pltpu.SMEM(bucket_edges.shape, jnp.int32),
            pltpu.SMEM(lengths.shape, jnp.int32),
            pltpu.SMEM(page_index.shape, jnp.int32),
            pltpu.SemaphoreType.DMA((4,)),
        ],
        compiler_params=PARAMS,
        cost_estimate=loading(cache_values),
        name="bias",
    )(*in_hbm(table, bucket_edges, lengths, page_index), page_request, near)

    sums = pl.pallas_call(
        functools.partial(attend_kernel, len(gathered)),
        out_shape=shape((all_rows, width + LANES), bf16),
        in_specs=[VMEM_SPEC] * (len(gathered) + 7),
        out_specs=VMEM_SPEC,
        compiler_params=PARAMS,
        name="attend",
    )(*gathered, bias, picks, place, first, apart, keys, cache_values)

    own_score, value_new, out_near = pl.pallas_call(
        side_kernel,
        out_shape=(
            shape((own_rows, LANES), f32),
            shape((own_rows, width), bf16),
            pltpu.VMEM(out_weight.shape, bf16),
        ),
        in_specs=[VMEM_SPEC] * 4 + [HBM_SPEC] * 2 + [ANY_SPEC],
        out_specs=(VMEM_SPEC,) * 3,
        scratch_shapes=[
            pltpu.VMEM((2, model, width), bf16),
            pltpu.SemaphoreType.DMA((2,)),
            pltpu.SemaphoreType.DMA((4,)),
        ],
        compiler_params=PARAMS,
        cost_estimate=loading(out_weight, out_weight, out_weight),
        name="side",
    )(
        hidden_in, gain, query, table,
        *in_hbm(qkv_weight, out_weight), sums,
    )

    parts = lax.all_to_all(sums, "blk", 0, 0, tiled=True)

    own_part, sent_part = pl.pallas_call(
        merge_kernel,
        out_shape=(shape((own_rows, model), f32), shape((own_rows, model), bf16)),
        in_specs=[VMEM_SPEC] * 4,
        out_specs=(VMEM_SPEC,) * 2,
        compiler_params=PARAMS,
        name="merge",
    )(parts, own_score, value_new, out_near)

    halves = lax.axis_size("head")
    columns = model // halves
    exchanged = halves == 2
    down_near = pl.pallas_call(
        load_kernel,
        out_shape=pltpu.VMEM(down_weight.shape, bf16),
        in_specs=[HBM_SPEC, ANY_SPEC],
        out_specs=VMEM_SPEC,
        scratch_shapes=[pltpu.SemaphoreType.DMA((8,))],
        compiler_params=PARAMS,
        cost_estimate=loading(down_weight),
        name="load",
    )(*in_hbm(down_weight), sent_part)
    if exchanged:
        other_part = lax.ppermute(sent_part, "head", xor_pairs(2, 1))
        mlp_out = (shape((own_rows, columns), f32), shape((own_rows, columns), bf16))
    else:
        own_part = jnp.zeros_like(own_part)
        other_part = lax.psum(sent_part, "head")
        mlp_out = (shape((own_rows, model), f32), shape((own_rows, model), bf16))

    kept, leaving = pl.pallas_call(
        functools.partial(mlp_kernel, exchanged),
        out_shape=mlp_out,
        in_specs=[VMEM_SPEC] * 6,
        out_specs=(VMEM_SPEC,) * 2,
        compiler_params=PARAMS,
        name="mlp",
    )(hidden_in, own_part, other_part, mlp_gain.reshape(1, model), up_weight, down_near)

    if exchanged:
        arrived = lax.ppermute(leaving, "head", xor_pairs(2, 1))
    else:
        kept = lax.dynamic_slice_in_dim(kept, lax.axis_index("head") * columns, columns, 1)
        arrived = lax.psum_scatter(leaving, "head", scatter_dimension=1, tiled=True)
    return kept + arrived.astype(f32)


def solution(mesh):
    in_specs = (
        P("blk", None),
        P(),
        P(),
        P(None, None, "head"),
        P("head", None),
        P(None, "head"),
        P("head", None),
        P(None, "head"),
        P(),
        P("blk", None, "head"),
        P("blk", None, "head"),
        P(),
        P("blk"),
        P("blk"),
    )
    out_specs = P("blk", "head")
    return jax.shard_map(
        per_device, mesh=mesh, in_specs=in_specs, out_specs=out_specs, check_vma=False
    )
```

```python
import functools

import jax
import jax.numpy as jnp
from jax import lax
from jax.experimental import pallas as pl
from jax.experimental.pallas import tpu as pltpu
from jax.sharding import PartitionSpec as P

HEAD_DIM = 64
PAGE = 128
LANES = 128

far_below = -1e30
epsilon = 1e-06

VMEM_SPEC = pl.BlockSpec(memory_space=pltpu.VMEM)
SMEM_SPEC = pl.BlockSpec(memory_space=pltpu.SMEM)
ANY_SPEC = pl.BlockSpec(memory_space=pl.ANY)
HBM_SPEC = pl.BlockSpec(memory_space=pltpu.HBM)
PARAMS = pltpu.CompilerParams(vmem_limit_bytes=16 * 1024 * 1024)

PIECE = 8
SUM_LANE = 3 * PIECE


def iota(shape, axis):
    return lax.broadcasted_iota(jnp.int32, shape, axis)


def split_index(x, size):
    if size & (size - 1):
        return lax.div(x, size), lax.rem(x, size)
    return x >> (size.bit_length() - 1), x & (size - 1)


def head_of(shape, axis):
    return split_index(iota(shape, axis), HEAD_DIM)[0]


def pieces(x, count):
    parts = []
    for _ in range(count):
        part = x.astype(jnp.bfloat16)
        parts.append(part)
        x = x - part.astype(jnp.float32)
    return parts


def rms_normed(x, gain):
    scale = lax.rsqrt(jnp.mean(x * x, axis=1, keepdims=True) + epsilon)
    return (x * scale * gain).astype(jnp.bfloat16)


def dot(a, b, dims=((1,), (0,)), precision=None):
    return lax.dot_general(
        a, b, (dims, ((), ())), preferred_element_type=jnp.float32, precision=precision
    )


def split_copies(source, target, sems, count):
    size = source.shape[0] // count
    return [
        pltpu.make_async_copy(
            source.at[pl.ds(i * size, size)], target.at[pl.ds(i * size, size)], sems.at[i]
        )
        for i in range(count)
    ]


def query_kernel(hidden_hbm, gain_hbm, weight_hbm, query_ref, hidden, gain, weight, sems):
    model = hidden.shape[1]
    small = [
        pltpu.make_async_copy(hidden_hbm, hidden, sems.at[0]),
        pltpu.make_async_copy(gain_hbm, gain, sems.at[1]),
    ]
    half = model // 2
    large = [
        pltpu.make_async_copy(
            weight_hbm.at[0, pl.ds(i * half, half)], weight.at[pl.ds(i * half, half)], sems.at[2 + i]
        )
        for i in range(2)
    ]
    for copy in small + large:
        copy.start()
    for copy in small:
        copy.wait()
    normed = rms_normed(hidden[...], gain[...])
    query = None
    for i, copy in enumerate(large):
        copy.wait()
        span = slice(i * half, (i + 1) * half)
        part = dot(normed[:, span], weight[span])
        query = part if query is None else query + part
    query_ref[...] = query.astype(jnp.bfloat16)


def page_kernel(
    own_rows, inner, outer, query_ref, request_ref, keys_hbm,
    keys_ref, pick_ref, place_ref, first_ref, apart_ref,
    sems,
):
    copies = split_copies(
        keys_hbm.at[pl.ds(0, keys_ref.shape[0])], keys_ref, sems, sems.shape[0]
    )
    for copy in copies:
        copy.start()
    me = lax.axis_index("blk")
    page_count = request_ref.shape[0]
    all_rows, depth = place_ref.shape
    row_of = iota((PIECE, all_rows), 1)
    page_of = split_index(iota((1, depth), 1), PIECE)[0]
    lane = iota((1, LANES), 1)
    requests = [request_ref[p] for p in range(page_count)]
    by_lane = jnp.full((1, LANES), -2, jnp.int32)
    for p in range(page_count):
        by_lane = jnp.where(lane == p, requests[p], by_lane)
    slots = jnp.full((1, depth), -1, jnp.int32)
    leads = jnp.full((1, depth), -1, jnp.int32)
    picks = []
    for p in range(page_count):
        owner = requests[p]
        device, own_row = split_index(jnp.maximum(owner, 0), own_rows)
        high, low = split_index(device ^ me, inner)
        slot = (low * outer + high) * own_rows + own_row
        slot = jnp.where(owner >= 0, slot, -1)
        picks.append((row_of == slot).astype(jnp.float32))
        slots = jnp.where(page_of == p, slot, slots)
        same = by_lane == owner
        apart_ref[p : p + 1] = jnp.where(same, 0.0, 2 * far_below)
        earlier = jnp.max(jnp.where(same & (lane < p), 1, 0), axis=1, keepdims=True)
        leads = jnp.where((page_of == p) & (earlier == 0), slot, leads)
    pick_ref[...] = jnp.concatenate(picks, axis=0).astype(jnp.bfloat16)
    row = iota((all_rows, depth), 0)
    place_ref[...] = (row == slots).astype(jnp.bfloat16)
    first_ref[...] = (row == leads).astype(jnp.bfloat16)
    for copy in copies:
        copy.wait()


def bias_kernel(
    table_hbm, edges_hbm, lengths_hbm, index_hbm, request_ref, keys_hbm, after_ref,
    keys_ref, bias_ref,
    table, edges_ref, lengths_ref, index_ref, small_sems, sems,
):
    sources = (table_hbm, edges_hbm, lengths_hbm, index_hbm)
    targets = (table, edges_ref, lengths_ref, index_ref)
    small = [
        pltpu.make_async_copy(source, target, small_sems.at[i])
        for i, (source, target) in enumerate(zip(sources, targets))
    ]
    late = keys_ref.shape[0]
    copies = split_copies(
        keys_hbm.at[pl.ds(keys_hbm.shape[0] - late, late)], keys_ref, sems, sems.shape[0]
    )
    for copy in small + copies:
        copy.start()
    for copy in small:
        copy.wait()
    heads, buckets = table.shape
    by_head = table[...]
    if heads < PIECE:
        by_head = jnp.concatenate([by_head[min(h, heads - 1)][None] for h in range(PIECE)], axis=0)
    columns = [jnp.broadcast_to(by_head[:, k : k + 1], (PIECE, PAGE)) for k in range(buckets)]
    token = iota((PIECE, PAGE), 1)
    for p in range(request_ref.shape[0]):
        owner = request_ref[p]
        left = lengths_ref[jnp.maximum(owner, 0)] - index_ref[p] * PAGE
        distance = jnp.where(owner >= 0, left, 0) - token
        bias = columns[0]
        for k in range(buckets - 1):
            bias = jnp.where(distance >= edges_ref[k], columns[k + 1], bias)
        bias_ref[p] = jnp.where(distance > 0, bias, far_below)
    for copy in copies:
        copy.wait()


def side_kernel(
    hidden_ref, gain_ref, query_ref, table_ref, weight_hbm, out_hbm, after_ref,
    score_ref, value_ref, out_ref,
    weight, weight_sems, sems,
):
    copies = [
        pltpu.make_async_copy(weight_hbm.at[1 + i], weight.at[i], weight_sems.at[i])
        for i in range(2)
    ]
    later = split_copies(out_hbm, out_ref, sems, sems.shape[0])
    for copy in copies + later:
        copy.start()
    normed = rms_normed(hidden_ref[...], gain_ref[...])
    heads = table_ref.shape[0]
    spread = iota((heads, LANES), 0) == iota((heads, LANES), 1)
    score = jnp.sum(jnp.where(spread, table_ref[:, 0:1], 0.0), axis=0, keepdims=True)
    copies[0].wait()
    key = dot(normed, weight[0]).astype(jnp.bfloat16)
    product = query_ref[...].astype(jnp.float32) * key.astype(jnp.float32)
    width = product.shape[1]
    gather = (head_of((width, LANES), 0) == iota((width, LANES), 1)).astype(jnp.bfloat16)
    for part in pieces(product, 3):
        score = score + dot(part, gather)
    score_ref[...] = score
    copies[1].wait()
    value_ref[...] = dot(normed, weight[1]).astype(jnp.bfloat16)
    for copy in later:
        copy.wait()


def load_kernel(source, after_ref, target, sems):
    copies = split_copies(source, target, sems, sems.shape[0])
    for copy in copies:
        copy.start()
    for copy in copies:
        copy.wait()


def packed_stats(peaks, sums):
    one, two, three = (part.astype(jnp.float32) for part in pieces(peaks + sums, 3))
    packed = one + pltpu.roll(two, PIECE, 1) + pltpu.roll(three, 2 * PIECE, 1)
    return packed.astype(jnp.bfloat16)


def unpacked_stats(packed, heads):
    stats = packed.astype(jnp.float32)
    stats = stats + pltpu.roll(stats, LANES - PIECE, 1) + pltpu.roll(stats, LANES - 2 * PIECE, 1)
    sums = pltpu.roll(stats, LANES - SUM_LANE, 1)
    used = iota(stats.shape, 1) < heads
    return jnp.where(used & (sums > 0.0), stats, far_below), jnp.where(used, sums, 0.0)


def over_columns(values, width):
    spread = (iota((LANES, width), 0) == head_of((LANES, width), 1)).astype(jnp.bfloat16)
    return sum(dot(part, spread) for part in pieces(values, 3))


def attend_kernel(groups, *refs):
    query_refs, refs, sums_refs = refs[:groups], refs[groups:-groups], refs[-groups:]
    bias_ref, pick_ref, place_ref, first_ref, apart_ref, keys_ref, late_ref, values_ref = refs
    page_count = apart_ref.shape[0]
    width = keys_ref.shape[2]
    early = keys_ref.shape[0]
    chunk = 2
    chunks = page_count // chunk
    queries = jnp.concatenate([ref[...] for ref in query_refs], axis=0)
    own_head = (head_of((PIECE, width), 1) == iota((PIECE, width), 0)).astype(jnp.float32)
    pair_heads = jnp.concatenate([own_head] * chunk, axis=0)
    chosen = dot(pick_ref[...], queries)
    lane = iota((PIECE, LANES), 1)
    row = iota((PIECE, LANES), 0)
    scores = []
    tops = jnp.zeros((PIECE, LANES), jnp.float32)
    for c in range(chunks):
        rows = chosen[c * chunk * PIECE : (c + 1) * chunk * PIECE]
        split = (rows * pair_heads).astype(jnp.bfloat16)
        at = c * chunk
        block = keys_ref[at : at + chunk] if at < early else late_ref[at - early : at - early + chunk]
        block = block.reshape(chunk * PAGE, width)
        raw = dot(split, block, ((1,), (1,)))
        for i in range(chunk):
            p = c * chunk + i
            part = raw[i * PIECE : (i + 1) * PIECE, i * PAGE : (i + 1) * PAGE]
            score = part + bias_ref[p]
            scores.append(score)
            tops = jnp.where(lane == p, jnp.max(score, axis=1, keepdims=True), tops)
    mixes, peaks, totals = [], [], []
    nothing = jnp.zeros((PIECE, PAGE), jnp.float32)
    for c in range(chunks):
        blocks = []
        for i in range(chunk):
            p = c * chunk + i
            peak = jnp.max(tops + apart_ref[p : p + 1], axis=1, keepdims=True)
            weight = jnp.exp(scores[p] - peak)
            total = jnp.sum(weight, axis=1, keepdims=True)
            peaks.append(jnp.where(lane == row, peak, 0.0))
            totals.append(jnp.where(lane == row + SUM_LANE, total, 0.0))
            blocks.append(
                jnp.concatenate([weight if k == i else nothing for k in range(chunk)], axis=1)
            )
        weights = jnp.concatenate(blocks, axis=0).astype(jnp.bfloat16)
        block = values_ref[c * chunk : (c + 1) * chunk].reshape(chunk * PAGE, width)
        mixes.append(dot(weights, block) * pair_heads)
    mix = jnp.concatenate(mixes, axis=0)
    place, first = place_ref[...], first_ref[...]
    high, low = pieces(mix, 2)
    sums = dot(place, high) + dot(place, low)
    collected = sum(dot(first, part) for part in pieces(jnp.concatenate(peaks, axis=0), 3))
    collected += sum(dot(place, part) for part in pieces(jnp.concatenate(totals, axis=0), 3))
    stats = packed_stats(collected, 0.0)
    size = sums_refs[0].shape[0]
    for i, sums_ref in enumerate(sums_refs):
        span = slice(i * size, (i + 1) * size)
        sums_ref[:, :width] = sums[span].astype(jnp.bfloat16)
        sums_ref[:, width:] = stats[span]


def combine_kernel(sources, *refs):
    part_refs, sums_refs = refs[:sources], refs[sources:]
    rows, columns = part_refs[0].shape
    width = columns - LANES
    stats = [unpacked_stats(ref[:, width:], width // HEAD_DIM) for ref in part_refs]
    peak = stats[0][0]
    for peaks, _ in stats[1:]:
        peak = jnp.maximum(peak, peaks)
    factors = [jnp.exp(peaks - peak) for peaks, _ in stats]
    total = sum(factor * sums for factor, (_, sums) in zip(factors, stats))
    shares = over_columns(jnp.concatenate(factors, axis=0), width)
    mixed = sum(
        ref[:, :width].astype(jnp.float32) * shares[i * rows : (i + 1) * rows]
        for i, ref in enumerate(part_refs)
    )
    packed = packed_stats(
        jnp.where(total > 0.0, peak, 0.0), pltpu.roll(total, SUM_LANE, 1)
    ).astype(jnp.float32)
    size = sums_refs[0].shape[0]
    for i, sums_ref in enumerate(sums_refs):
        span = slice(i * size, (i + 1) * size)
        sums_ref[:, :width] = mixed[span].astype(jnp.bfloat16)
        sums_ref[:, width:] = packed[span].astype(jnp.bfloat16)


def merge_kernel(sources, *refs):
    part_refs, (score_ref, value_ref, weight_ref, own_ref, send_ref) = refs[:sources], refs[sources:]
    own_rows, width = value_ref.shape
    heads = width // HEAD_DIM
    stats = [unpacked_stats(ref[:, width:], heads) for ref in part_refs]
    own_score = jnp.where(iota(score_ref.shape, 1) < heads, score_ref[...], 0.0)
    peak = own_score
    for peaks, _ in stats:
        peak = jnp.maximum(peak, peaks)
    own_weight = jnp.exp(own_score - peak)
    total = own_weight
    factors = []
    for peaks, sums in stats:
        factor = jnp.exp(peaks - peak)
        total = total + factor * sums
        factors.append(factor)
    factors.append(own_weight.astype(jnp.bfloat16).astype(jnp.float32))
    shares = jnp.concatenate([factor / total for factor in factors], axis=0)
    shares = over_columns(shares, width)
    mixed = value_ref[...].astype(jnp.float32) * shares[sources * own_rows :]
    for i, ref in enumerate(part_refs):
        rows = slice(i * own_rows, (i + 1) * own_rows)
        mixed = mixed + ref[:, :width].astype(jnp.float32) * shares[rows]
    projected = dot(mixed.astype(jnp.bfloat16), weight_ref[...])
    own_ref[...] = projected
    send_ref[...] = projected.astype(jnp.bfloat16)


def mlp_kernel(exchanged, hidden_ref, own_ref, other_ref, gain_ref, up_ref, down_ref, *outs):
    middle = hidden_ref[...] + (own_ref[...] + other_ref[...].astype(jnp.float32))
    normed = rms_normed(middle, gain_ref[...])
    active = jnp.maximum(dot(normed, up_ref[...]), 0.0).astype(jnp.bfloat16)
    down = dot(active, down_ref[...])
    if exchanged:
        kept_ref, sent_ref = outs
        columns = kept_ref.shape[1]
        low = lax.axis_index("head") == 0
        left, right = slice(0, columns), slice(columns, 2 * columns)
        kept = middle + down

        @pl.when(low)
        def _():
            kept_ref[...] = kept[:, left]
            sent_ref[...] = down[:, right].astype(jnp.bfloat16)

        @pl.when(jnp.logical_not(low))
        def _():
            kept_ref[...] = kept[:, right]
            sent_ref[...] = down[:, left].astype(jnp.bfloat16)

    else:
        middle_ref, down_out_ref = outs
        middle_ref[...] = middle
        down_out_ref[...] = down.astype(jnp.bfloat16)


def loading(*arrays):
    return pl.CostEstimate(
        flops=0, bytes_accessed=sum(2 * array.size for array in arrays), transcendentals=0
    )


def in_hbm(*arrays):
    return [pltpu.with_memory_space_constraint(array, pltpu.HBM) for array in arrays]


def xor_pairs(size, step):
    return [(i, i ^ step) for i in range(size)]


def per_device(
    hidden_in, attention_gain, mlp_gain, qkv_weight, out_weight, up_weight, down_weight,
    position_bias, bucket_edges, cache_keys, cache_values, lengths, page_request, page_index,
):
    f32, bf16 = jnp.float32, jnp.bfloat16
    shape = jax.ShapeDtypeStruct
    own_rows, model = hidden_in.shape
    width = qkv_weight.shape[2]
    page_count = page_request.shape[0]
    blocks = lax.axis_size("blk")
    all_rows = own_rows * blocks
    gain = attention_gain.reshape(1, model)
    query = pl.pallas_call(
        query_kernel,
        out_shape=shape((own_rows, width), bf16),
        in_specs=[HBM_SPEC] * 3,
        out_specs=VMEM_SPEC,
        scratch_shapes=[
            pltpu.VMEM((own_rows, model), f32),
            pltpu.VMEM((1, model), f32),
            pltpu.VMEM((model, width), bf16),
            pltpu.SemaphoreType.DMA((4,)),
        ],
        compiler_params=PARAMS,
        name="query",
    )(*in_hbm(hidden_in, gain, qkv_weight))

    inner = 1
    while inner * inner < blocks:
        inner *= 2
    far = [query] + [
        lax.ppermute(query, "blk", xor_pairs(blocks, step * inner))
        for step in range(1, blocks // inner)
    ]
    depth = page_count * PIECE
    early = page_count // 2
    keys, picks, place, first, apart = pl.pallas_call(
        functools.partial(page_kernel, own_rows, inner, blocks // inner),
        out_shape=(
            pltpu.VMEM((early,) + cache_keys.shape[1:], bf16),
            shape((depth, all_rows), bf16),
            shape((all_rows, depth), bf16),
            shape((all_rows, depth), bf16),
            shape((page_count, LANES), f32),
        ),
        in_specs=[ANY_SPEC, SMEM_SPEC, HBM_SPEC],
        out_specs=(VMEM_SPEC,) * 5,
        scratch_shapes=[pltpu.SemaphoreType.DMA((4,))],
        compiler_params=PARAMS,
        cost_estimate=loading(cache_keys),
        name="pages",
    )(query, page_request, *in_hbm(cache_keys))
    near, apart = lax.optimization_barrier((jnp.concatenate(far, axis=0), apart))
    gathered = [near] + [
        lax.ppermute(near, "blk", xor_pairs(blocks, step)) for step in range(1, inner)
    ]
    table = position_bias.T
    late_keys, bias = pl.pallas_call(
        bias_kernel,
        out_shape=(
            pltpu.VMEM((page_count - early,) + cache_keys.shape[1:], bf16),
            shape((page_count, PIECE, PAGE), f32),
        ),
        in_specs=[HBM_SPEC] * 4 + [SMEM_SPEC, HBM_SPEC, ANY_SPEC],
        out_specs=(VMEM_SPEC,) * 2,
        scratch_shapes=[
            pltpu.VMEM(table.shape, f32),
            pltpu.SMEM(bucket_edges.shape, jnp.int32),
            pltpu.SMEM(lengths.shape, jnp.int32),
            pltpu.SMEM(page_index.shape, jnp.int32),
            pltpu.SemaphoreType.DMA((4,)),
            pltpu.SemaphoreType.DMA((4,)),
        ],
        compiler_params=PARAMS,
        cost_estimate=loading(cache_values),
        name="bias",
    )(
        *in_hbm(table, bucket_edges, lengths, page_index), page_request,
        *in_hbm(cache_keys), near,
    )

    groups = len(gathered)
    sums = pl.pallas_call(
        functools.partial(attend_kernel, groups),
        out_shape=(shape((all_rows // groups, width + LANES), bf16),) * groups,
        in_specs=[VMEM_SPEC] * (groups + 8),
        out_specs=(VMEM_SPEC,) * groups,
        compiler_params=PARAMS,
        name="attend",
    )(*gathered, bias, picks, place, first, apart, keys, late_keys, cache_values)
    near_sums = [sums[0]] + [
        lax.ppermute(sums[step], "blk", xor_pairs(blocks, step)) for step in range(1, inner)
    ]

    own_score, value_new, out_near = pl.pallas_call(
        side_kernel,
        out_shape=(
            shape((own_rows, LANES), f32),
            shape((own_rows, width), bf16),
            pltpu.VMEM(out_weight.shape, bf16),
        ),
        in_specs=[VMEM_SPEC] * 4 + [HBM_SPEC] * 2 + [ANY_SPEC],
        out_specs=(VMEM_SPEC,) * 3,
        scratch_shapes=[
            pltpu.VMEM((2, model, width), bf16),
            pltpu.SemaphoreType.DMA((2,)),
            pltpu.SemaphoreType.DMA((4,)),
        ],
        compiler_params=PARAMS,
        cost_estimate=loading(out_weight, out_weight, out_weight),
        name="side",
    )(
        hidden_in, gain, query, table,
        *in_hbm(qkv_weight, out_weight), sums[0],
    )

    outer = blocks // inner
    sums = pl.pallas_call(
        functools.partial(combine_kernel, inner),
        out_shape=(shape((own_rows, width + LANES), bf16),) * outer,
        in_specs=[VMEM_SPEC] * inner,
        out_specs=(VMEM_SPEC,) * outer,
        compiler_params=PARAMS,
        name="combine",
    )(*near_sums)
    parts = [sums[0]] + [
        lax.ppermute(sums[step], "blk", xor_pairs(blocks, step * inner)) for step in range(1, outer)
    ]

    own_part, sent_part = pl.pallas_call(
        functools.partial(merge_kernel, outer),
        out_shape=(shape((own_rows, model), f32), shape((own_rows, model), bf16)),
        in_specs=[VMEM_SPEC] * (outer + 3),
        out_specs=(VMEM_SPEC,) * 2,
        compiler_params=PARAMS,
        name="merge",
    )(*parts, own_score, value_new, out_near)

    halves = lax.axis_size("head")
    columns = model // halves
    exchanged = halves == 2
    down_near = pl.pallas_call(
        load_kernel,
        out_shape=pltpu.VMEM(down_weight.shape, bf16),
        in_specs=[HBM_SPEC, ANY_SPEC],
        out_specs=VMEM_SPEC,
        scratch_shapes=[pltpu.SemaphoreType.DMA((8,))],
        compiler_params=PARAMS,
        cost_estimate=loading(down_weight),
        name="load",
    )(*in_hbm(down_weight), sent_part)
    if exchanged:
        other_part = lax.ppermute(sent_part, "head", xor_pairs(2, 1))
        mlp_out = (shape((own_rows, columns), f32), shape((own_rows, columns), bf16))
    else:
        own_part = jnp.zeros_like(own_part)
        other_part = lax.psum(sent_part, "head")
        mlp_out = (shape((own_rows, model), f32), shape((own_rows, model), bf16))

    kept, leaving = pl.pallas_call(
        functools.partial(mlp_kernel, exchanged),
        out_shape=mlp_out,
        in_specs=[VMEM_SPEC] * 6,
        out_specs=(VMEM_SPEC,) * 2,
        compiler_params=PARAMS,
        name="mlp",
    )(hidden_in, own_part, other_part, mlp_gain.reshape(1, model), up_weight, down_near)

    if exchanged:
        arrived = lax.ppermute(leaving, "head", xor_pairs(2, 1))
    else:
        kept = lax.dynamic_slice_in_dim(kept, lax.axis_index("head") * columns, columns, 1)
        arrived = lax.psum_scatter(leaving, "head", scatter_dimension=1, tiled=True)
    return kept + arrived.astype(f32)


def solution(mesh):
    in_specs = (
        P("blk", None),
        P(),
        P(),
        P(None, None, "head"),
        P("head", None),
        P(None, "head"),
        P("head", None),
        P(None, "head"),
        P(),
        P("blk", None, "head"),
        P("blk", None, "head"),
        P(),
        P("blk"),
        P("blk"),
    )
    out_specs = P("blk", "head")
    return jax.shard_map(
        per_device, mesh=mesh, in_specs=in_specs, out_specs=out_specs, check_vma=False
    )
```

```python
import functools

import jax
import jax.numpy as jnp
from jax import lax
from jax.experimental import pallas as pl
from jax.experimental.pallas import tpu as pltpu
from jax.sharding import PartitionSpec as P

HEAD_DIM = 64
PAGE = 128
LANES = 128

far_below = -1e30
epsilon = 1e-06

VMEM_SPEC = pl.BlockSpec(memory_space=pltpu.VMEM)
SMEM_SPEC = pl.BlockSpec(memory_space=pltpu.SMEM)
ANY_SPEC = pl.BlockSpec(memory_space=pl.ANY)
HBM_SPEC = pl.BlockSpec(memory_space=pltpu.HBM)
PARAMS = pltpu.CompilerParams(vmem_limit_bytes=16 * 1024 * 1024)

PIECE = 8
SUM_LANE = 3 * PIECE


def iota(shape, axis):
    return lax.broadcasted_iota(jnp.int32, shape, axis)


def split_index(x, size):
    if size & (size - 1):
        return lax.div(x, size), lax.rem(x, size)
    return x >> (size.bit_length() - 1), x & (size - 1)


def head_of(shape, axis):
    return split_index(iota(shape, axis), HEAD_DIM)[0]


def pieces(x, count):
    parts = []
    for _ in range(count):
        part = x.astype(jnp.bfloat16)
        parts.append(part)
        x = x - part.astype(jnp.float32)
    return parts


def rms_normed(x, gain):
    scale = lax.rsqrt(jnp.mean(x * x, axis=1, keepdims=True) + epsilon)
    return (x * scale * gain).astype(jnp.bfloat16)


def dot(a, b, dims=((1,), (0,)), precision=None):
    return lax.dot_general(
        a, b, (dims, ((), ())), preferred_element_type=jnp.float32, precision=precision
    )


def split_copies(source, target, sems, count):
    size = source.shape[0] // count
    return [
        pltpu.make_async_copy(
            source.at[pl.ds(i * size, size)], target.at[pl.ds(i * size, size)], sems.at[i]
        )
        for i in range(count)
    ]


def query_kernel(hidden_hbm, gain_hbm, weight_hbm, query_ref, hidden, gain, weight, sems):
    model = hidden.shape[1]
    small = [
        pltpu.make_async_copy(hidden_hbm, hidden, sems.at[0]),
        pltpu.make_async_copy(gain_hbm, gain, sems.at[1]),
    ]
    half = model // 2
    large = [
        pltpu.make_async_copy(
            weight_hbm.at[0, pl.ds(i * half, half)], weight.at[pl.ds(i * half, half)], sems.at[2 + i]
        )
        for i in range(2)
    ]
    for copy in small + large:
        copy.start()
    for copy in small:
        copy.wait()
    normed = rms_normed(hidden[...], gain[...])
    query = None
    for i, copy in enumerate(large):
        copy.wait()
        span = slice(i * half, (i + 1) * half)
        part = dot(normed[:, span], weight[span])
        query = part if query is None else query + part
    query_ref[...] = query.astype(jnp.bfloat16)


def page_kernel(
    own_rows, inner, outer, query_ref, request_ref, keys_hbm,
    keys_ref, pick_ref, place_ref, first_ref, apart_ref,
    sems,
):
    copies = split_copies(
        keys_hbm.at[pl.ds(0, keys_ref.shape[0])], keys_ref, sems, sems.shape[0]
    )
    for copy in copies:
        copy.start()
    me = lax.axis_index("blk")
    page_count = request_ref.shape[0]
    all_rows, depth = place_ref.shape
    row_of = iota((PIECE, all_rows), 1)
    page_of = split_index(iota((1, depth), 1), PIECE)[0]
    lane = iota((1, LANES), 1)
    requests = [request_ref[p] for p in range(page_count)]
    by_lane = jnp.full((1, LANES), -2, jnp.int32)
    for p in range(page_count):
        by_lane = jnp.where(lane == p, requests[p], by_lane)
    slots = jnp.full((1, depth), -1, jnp.int32)
    leads = jnp.full((1, depth), -1, jnp.int32)
    picks = []
    for p in range(page_count):
        owner = requests[p]
        device, own_row = split_index(jnp.maximum(owner, 0), own_rows)
        high, low = split_index(device ^ me, inner)
        slot = (low * outer + high) * own_rows + own_row
        slot = jnp.where(owner >= 0, slot, -1)
        out_slot = (low * outer + split_index(device, inner)[0]) * own_rows + own_row
        out_slot = jnp.where(owner >= 0, out_slot, -1)
        picks.append((row_of == slot).astype(jnp.float32))
        slots = jnp.where(page_of == p, out_slot, slots)
        same = by_lane == owner
        apart_ref[p : p + 1] = jnp.where(same, 0.0, 2 * far_below)
        earlier = jnp.max(jnp.where(same & (lane < p), 1, 0), axis=1, keepdims=True)
        leads = jnp.where((page_of == p) & (earlier == 0), out_slot, leads)
    pick_ref[...] = jnp.concatenate(picks, axis=0).astype(jnp.bfloat16)
    row = iota((all_rows, depth), 0)
    place_ref[...] = (row == slots).astype(jnp.bfloat16)
    first_ref[...] = (row == leads).astype(jnp.bfloat16)
    for copy in copies:
        copy.wait()


def bias_kernel(
    table_hbm, edges_hbm, lengths_hbm, index_hbm, request_ref, keys_hbm, after_ref,
    keys_ref, bias_ref,
    table, edges_ref, lengths_ref, index_ref, small_sems, sems,
):
    sources = (table_hbm, edges_hbm, lengths_hbm, index_hbm)
    targets = (table, edges_ref, lengths_ref, index_ref)
    small = [
        pltpu.make_async_copy(source, target, small_sems.at[i])
        for i, (source, target) in enumerate(zip(sources, targets))
    ]
    late = keys_ref.shape[0]
    copies = split_copies(
        keys_hbm.at[pl.ds(keys_hbm.shape[0] - late, late)], keys_ref, sems, sems.shape[0]
    )
    for copy in small + copies:
        copy.start()
    for copy in small:
        copy.wait()
    heads, buckets = table.shape
    by_head = table[...]
    if heads < PIECE:
        by_head = jnp.concatenate([by_head[min(h, heads - 1)][None] for h in range(PIECE)], axis=0)
    columns = [jnp.broadcast_to(by_head[:, k : k + 1], (PIECE, PAGE)) for k in range(buckets)]
    token = iota((PIECE, PAGE), 1)
    for p in range(request_ref.shape[0]):
        owner = request_ref[p]
        left = lengths_ref[jnp.maximum(owner, 0)] - index_ref[p] * PAGE
        distance = jnp.where(owner >= 0, left, 0) - token
        bias = columns[0]
        for k in range(buckets - 1):
            bias = jnp.where(distance >= edges_ref[k], columns[k + 1], bias)
        bias_ref[p] = jnp.where(distance > 0, bias, far_below)
    for copy in copies:
        copy.wait()


def side_kernel(
    hidden_ref, gain_ref, query_ref, table_ref, weight_hbm, out_hbm, after_ref,
    score_ref, value_ref, out_ref,
    weight, weight_sems, sems,
):
    copies = [
        pltpu.make_async_copy(weight_hbm.at[1 + i], weight.at[i], weight_sems.at[i])
        for i in range(2)
    ]
    later = split_copies(out_hbm, out_ref, sems, sems.shape[0])
    for copy in copies + later:
        copy.start()
    normed = rms_normed(hidden_ref[...], gain_ref[...])
    heads = table_ref.shape[0]
    spread = iota((heads, LANES), 0) == iota((heads, LANES), 1)
    score = jnp.sum(jnp.where(spread, table_ref[:, 0:1], 0.0), axis=0, keepdims=True)
    copies[0].wait()
    key = dot(normed, weight[0]).astype(jnp.bfloat16)
    product = query_ref[...].astype(jnp.float32) * key.astype(jnp.float32)
    width = product.shape[1]
    gather = (head_of((width, LANES), 0) == iota((width, LANES), 1)).astype(jnp.bfloat16)
    for part in pieces(product, 3):
        score = score + dot(part, gather)
    score_ref[...] = score
    copies[1].wait()
    value_ref[...] = dot(normed, weight[1]).astype(jnp.bfloat16)
    for copy in later:
        copy.wait()


def load_kernel(source, after_ref, target, sems):
    copies = split_copies(source, target, sems, sems.shape[0])
    for copy in copies:
        copy.start()
    for copy in copies:
        copy.wait()


def packed_stats(peaks, sums):
    one, two, three = (part.astype(jnp.float32) for part in pieces(peaks + sums, 3))
    packed = one + pltpu.roll(two, PIECE, 1) + pltpu.roll(three, 2 * PIECE, 1)
    return packed.astype(jnp.bfloat16)


def unpacked_stats(packed, heads):
    stats = packed.astype(jnp.float32)
    stats = stats + pltpu.roll(stats, LANES - PIECE, 1) + pltpu.roll(stats, LANES - 2 * PIECE, 1)
    sums = pltpu.roll(stats, LANES - SUM_LANE, 1)
    used = iota(stats.shape, 1) < heads
    return jnp.where(used & (sums > 0.0), stats, far_below), jnp.where(used, sums, 0.0)


def over_columns(values, width):
    spread = (iota((LANES, width), 0) == head_of((LANES, width), 1)).astype(jnp.bfloat16)
    return sum(dot(part, spread) for part in pieces(values, 3))


def attend_kernel(groups, *refs):
    query_refs, refs, sums_refs = refs[:groups], refs[groups:-groups], refs[-groups:]
    bias_ref, pick_ref, place_ref, first_ref, apart_ref, keys_ref, late_ref, values_ref = refs
    page_count = apart_ref.shape[0]
    width = keys_ref.shape[2]
    early = keys_ref.shape[0]
    chunk = 2
    chunks = page_count // chunk
    queries = jnp.concatenate([ref[...] for ref in query_refs], axis=0)
    own_head = (head_of((PIECE, width), 1) == iota((PIECE, width), 0)).astype(jnp.float32)
    pair_heads = jnp.concatenate([own_head] * chunk, axis=0)
    chosen = dot(pick_ref[...], queries)
    lane = iota((PIECE, LANES), 1)
    row = iota((PIECE, LANES), 0)
    scores = []
    tops = jnp.zeros((PIECE, LANES), jnp.float32)
    for c in range(chunks):
        rows = chosen[c * chunk * PIECE : (c + 1) * chunk * PIECE]
        split = (rows * pair_heads).astype(jnp.bfloat16)
        at = c * chunk
        block = keys_ref[at : at + chunk] if at < early else late_ref[at - early : at - early + chunk]
        block = block.reshape(chunk * PAGE, width)
        raw = dot(split, block, ((1,), (1,)))
        for i in range(chunk):
            p = c * chunk + i
            part = raw[i * PIECE : (i + 1) * PIECE, i * PAGE : (i + 1) * PAGE]
            score = part + bias_ref[p]
            scores.append(score)
            tops = jnp.where(lane == p, jnp.max(score, axis=1, keepdims=True), tops)
    mixes, peaks, totals = [], [], []
    nothing = jnp.zeros((PIECE, PAGE), jnp.float32)
    for c in range(chunks):
        blocks = []
        for i in range(chunk):
            p = c * chunk + i
            peak = jnp.max(tops + apart_ref[p : p + 1], axis=1, keepdims=True)
            weight = jnp.exp(scores[p] - peak)
            total = jnp.sum(weight, axis=1, keepdims=True)
            peaks.append(jnp.where(lane == row, peak, 0.0))
            totals.append(jnp.where(lane == row + SUM_LANE, total, 0.0))
            blocks.append(
                jnp.concatenate([weight if k == i else nothing for k in range(chunk)], axis=1)
            )
        weights = jnp.concatenate(blocks, axis=0).astype(jnp.bfloat16)
        block = values_ref[c * chunk : (c + 1) * chunk].reshape(chunk * PAGE, width)
        mixes.append(dot(weights, block) * pair_heads)
    mix = jnp.concatenate(mixes, axis=0)
    place, first = place_ref[...], first_ref[...]
    high, low = pieces(mix, 2)
    sums = dot(place, high) + dot(place, low)
    collected = sum(dot(first, part) for part in pieces(jnp.concatenate(peaks, axis=0), 3))
    collected += sum(dot(place, part) for part in pieces(jnp.concatenate(totals, axis=0), 3))
    stats = packed_stats(collected, 0.0)
    size = sums_refs[0].shape[0]
    for i, sums_ref in enumerate(sums_refs):
        span = slice(i * size, (i + 1) * size)
        sums_ref[:, :width] = sums[span].astype(jnp.bfloat16)
        sums_ref[:, width:] = stats[span]


def combine_kernel(sources, *refs):
    part_refs, sums_ref = refs[:sources], refs[sources]
    rows, columns = part_refs[0].shape
    width = columns - LANES
    stats = [unpacked_stats(ref[:, width:], width // HEAD_DIM) for ref in part_refs]
    peak = stats[0][0]
    for peaks, _ in stats[1:]:
        peak = jnp.maximum(peak, peaks)
    factors = [jnp.exp(peaks - peak) for peaks, _ in stats]
    total = sum(factor * sums for factor, (_, sums) in zip(factors, stats))
    shares = over_columns(jnp.concatenate(factors, axis=0), width)
    mixed = sum(
        ref[:, :width].astype(jnp.float32) * shares[i * rows : (i + 1) * rows]
        for i, ref in enumerate(part_refs)
    )
    sums_ref[:, :width] = mixed.astype(jnp.bfloat16)
    sums_ref[:, width:] = packed_stats(
        jnp.where(total > 0.0, peak, 0.0), pltpu.roll(total, SUM_LANE, 1)
    )


def merge_kernel(parts_ref, score_ref, value_ref, weight_ref, own_ref, send_ref):
    own_rows, width = value_ref.shape
    sources = parts_ref.shape[0] // own_rows
    heads = width // HEAD_DIM
    peaks, sums = unpacked_stats(parts_ref[:, width:], heads)
    mixes = parts_ref[:, :width].astype(jnp.float32)
    rows = [slice(i * own_rows, (i + 1) * own_rows) for i in range(sources)]
    stats = [(peaks[span], sums[span]) for span in rows]
    own_score = jnp.where(iota(score_ref.shape, 1) < heads, score_ref[...], 0.0)
    peak = own_score
    for peaks, _ in stats:
        peak = jnp.maximum(peak, peaks)
    own_weight = jnp.exp(own_score - peak)
    total = own_weight
    factors = []
    for peaks, sums in stats:
        factor = jnp.exp(peaks - peak)
        total = total + factor * sums
        factors.append(factor)
    factors.append(own_weight.astype(jnp.bfloat16).astype(jnp.float32))
    shares = jnp.concatenate([factor / total for factor in factors], axis=0)
    shares = over_columns(shares, width)
    mixed = value_ref[...].astype(jnp.float32) * shares[sources * own_rows :]
    for span in rows:
        mixed = mixed + mixes[span] * shares[span]
    projected = dot(mixed.astype(jnp.bfloat16), weight_ref[...])
    own_ref[...] = projected
    send_ref[...] = projected.astype(jnp.bfloat16)


def mlp_kernel(exchanged, hidden_ref, own_ref, other_ref, gain_ref, up_ref, down_ref, *outs):
    middle = hidden_ref[...] + (own_ref[...] + other_ref[...].astype(jnp.float32))
    normed = rms_normed(middle, gain_ref[...])
    active = jnp.maximum(dot(normed, up_ref[...]), 0.0).astype(jnp.bfloat16)
    down = dot(active, down_ref[...])
    if exchanged:
        kept_ref, sent_ref = outs
        columns = kept_ref.shape[1]
        low = lax.axis_index("head") == 0
        left, right = slice(0, columns), slice(columns, 2 * columns)
        kept = middle + down

        @pl.when(low)
        def _():
            kept_ref[...] = kept[:, left]
            sent_ref[...] = down[:, right].astype(jnp.bfloat16)

        @pl.when(jnp.logical_not(low))
        def _():
            kept_ref[...] = kept[:, right]
            sent_ref[...] = down[:, left].astype(jnp.bfloat16)

    else:
        middle_ref, down_out_ref = outs
        middle_ref[...] = middle
        down_out_ref[...] = down.astype(jnp.bfloat16)


def loading(*arrays):
    return pl.CostEstimate(
        flops=0, bytes_accessed=sum(2 * array.size for array in arrays), transcendentals=0
    )


def in_hbm(*arrays):
    return [pltpu.with_memory_space_constraint(array, pltpu.HBM) for array in arrays]


def xor_pairs(size, step):
    return [(i, i ^ step) for i in range(size)]


def per_device(
    hidden_in, attention_gain, mlp_gain, qkv_weight, out_weight, up_weight, down_weight,
    position_bias, bucket_edges, cache_keys, cache_values, lengths, page_request, page_index,
):
    f32, bf16 = jnp.float32, jnp.bfloat16
    shape = jax.ShapeDtypeStruct
    own_rows, model = hidden_in.shape
    width = qkv_weight.shape[2]
    page_count = page_request.shape[0]
    blocks = lax.axis_size("blk")
    all_rows = own_rows * blocks
    gain = attention_gain.reshape(1, model)
    query = pl.pallas_call(
        query_kernel,
        out_shape=shape((own_rows, width), bf16),
        in_specs=[HBM_SPEC] * 3,
        out_specs=VMEM_SPEC,
        scratch_shapes=[
            pltpu.VMEM((own_rows, model), f32),
            pltpu.VMEM((1, model), f32),
            pltpu.VMEM((model, width), bf16),
            pltpu.SemaphoreType.DMA((4,)),
        ],
        compiler_params=PARAMS,
        name="query",
    )(*in_hbm(hidden_in, gain, qkv_weight))

    inner = 1
    while inner * inner < blocks:
        inner *= 2
    far = [query] + [
        lax.ppermute(query, "blk", xor_pairs(blocks, step * inner))
        for step in range(1, blocks // inner)
    ]
    depth = page_count * PIECE
    early = page_count // 2
    keys, picks, place, first, apart = pl.pallas_call(
        functools.partial(page_kernel, own_rows, inner, blocks // inner),
        out_shape=(
            pltpu.VMEM((early,) + cache_keys.shape[1:], bf16),
            shape((depth, all_rows), bf16),
            shape((all_rows, depth), bf16),
            shape((all_rows, depth), bf16),
            shape((page_count, LANES), f32),
        ),
        in_specs=[ANY_SPEC, SMEM_SPEC, HBM_SPEC],
        out_specs=(VMEM_SPEC,) * 5,
        scratch_shapes=[pltpu.SemaphoreType.DMA((4,))],
        compiler_params=PARAMS,
        cost_estimate=loading(cache_keys),
        name="pages",
    )(query, page_request, *in_hbm(cache_keys))
    near, apart = lax.optimization_barrier((jnp.concatenate(far, axis=0), apart))
    gathered = [near] + [
        lax.ppermute(near, "blk", xor_pairs(blocks, step)) for step in range(1, inner)
    ]
    table = position_bias.T
    late_keys, bias = pl.pallas_call(
        bias_kernel,
        out_shape=(
            pltpu.VMEM((page_count - early,) + cache_keys.shape[1:], bf16),
            shape((page_count, PIECE, PAGE), f32),
        ),
        in_specs=[HBM_SPEC] * 4 + [SMEM_SPEC, HBM_SPEC, ANY_SPEC],
        out_specs=(VMEM_SPEC,) * 2,
        scratch_shapes=[
            pltpu.VMEM(table.shape, f32),
            pltpu.SMEM(bucket_edges.shape, jnp.int32),
            pltpu.SMEM(lengths.shape, jnp.int32),
            pltpu.SMEM(page_index.shape, jnp.int32),
            pltpu.SemaphoreType.DMA((4,)),
            pltpu.SemaphoreType.DMA((4,)),
        ],
        compiler_params=PARAMS,
        cost_estimate=loading(cache_values),
        name="bias",
    )(
        *in_hbm(table, bucket_edges, lengths, page_index), page_request,
        *in_hbm(cache_keys), near,
    )

    groups = len(gathered)
    sums = pl.pallas_call(
        functools.partial(attend_kernel, groups),
        out_shape=(shape((all_rows // groups, width + LANES), bf16),) * groups,
        in_specs=[VMEM_SPEC] * (groups + 8),
        out_specs=(VMEM_SPEC,) * groups,
        compiler_params=PARAMS,
        name="attend",
    )(*gathered, bias, picks, place, first, apart, keys, late_keys, cache_values)
    near_sums = [sums[0]] + [
        lax.ppermute(sums[step], "blk", xor_pairs(blocks, step)) for step in range(1, inner)
    ]

    own_score, value_new, out_near = pl.pallas_call(
        side_kernel,
        out_shape=(
            shape((own_rows, LANES), f32),
            shape((own_rows, width), bf16),
            pltpu.VMEM(out_weight.shape, bf16),
        ),
        in_specs=[VMEM_SPEC] * 4 + [HBM_SPEC] * 2 + [ANY_SPEC],
        out_specs=(VMEM_SPEC,) * 3,
        scratch_shapes=[
            pltpu.VMEM((2, model, width), bf16),
            pltpu.SemaphoreType.DMA((2,)),
            pltpu.SemaphoreType.DMA((4,)),
        ],
        compiler_params=PARAMS,
        cost_estimate=loading(out_weight, out_weight, out_weight),
        name="side",
    )(
        hidden_in, gain, query, table,
        *in_hbm(qkv_weight, out_weight), sums[0],
    )

    outer = blocks // inner
    sums = pl.pallas_call(
        functools.partial(combine_kernel, inner),
        out_shape=shape((outer * own_rows, width + LANES), bf16),
        in_specs=[VMEM_SPEC] * inner,
        out_specs=VMEM_SPEC,
        compiler_params=PARAMS,
        name="combine",
    )(*near_sums)
    columns_of_devices = [[low + inner * high for high in range(outer)] for low in range(inner)]
    parts = lax.all_to_all(
        sums, "blk", 0, 0, tiled=True, axis_index_groups=columns_of_devices
    )

    own_part, sent_part = pl.pallas_call(
        merge_kernel,
        out_shape=(shape((own_rows, model), f32), shape((own_rows, model), bf16)),
        in_specs=[VMEM_SPEC] * 4,
        out_specs=(VMEM_SPEC,) * 2,
        compiler_params=PARAMS,
        name="merge",
    )(parts, own_score, value_new, out_near)

    halves = lax.axis_size("head")
    columns = model // halves
    exchanged = halves == 2
    down_near = pl.pallas_call(
        load_kernel,
        out_shape=pltpu.VMEM(down_weight.shape, bf16),
        in_specs=[HBM_SPEC, ANY_SPEC],
        out_specs=VMEM_SPEC,
        scratch_shapes=[pltpu.SemaphoreType.DMA((8,))],
        compiler_params=PARAMS,
        cost_estimate=loading(down_weight),
        name="load",
    )(*in_hbm(down_weight), sent_part)
    if exchanged:
        other_part = lax.ppermute(sent_part, "head", xor_pairs(2, 1))
        mlp_out = (shape((own_rows, columns), f32), shape((own_rows, columns), bf16))
    else:
        own_part = jnp.zeros_like(own_part)
        other_part = lax.psum(sent_part, "head")
        mlp_out = (shape((own_rows, model), f32), shape((own_rows, model), bf16))

    kept, leaving = pl.pallas_call(
        functools.partial(mlp_kernel, exchanged),
        out_shape=mlp_out,
        in_specs=[VMEM_SPEC] * 6,
        out_specs=(VMEM_SPEC,) * 2,
        compiler_params=PARAMS,
        name="mlp",
    )(hidden_in, own_part, other_part, mlp_gain.reshape(1, model), up_weight, down_near)

    if exchanged:
        arrived = lax.ppermute(leaving, "head", xor_pairs(2, 1))
    else:
        kept = lax.dynamic_slice_in_dim(kept, lax.axis_index("head") * columns, columns, 1)
        arrived = lax.psum_scatter(leaving, "head", scatter_dimension=1, tiled=True)
    return kept + arrived.astype(f32)


def solution(mesh):
    in_specs = (
        P("blk", None),
        P(),
        P(),
        P(None, None, "head"),
        P("head", None),
        P(None, "head"),
        P("head", None),
        P(None, "head"),
        P(),
        P("blk", None, "head"),
        P("blk", None, "head"),
        P(),
        P("blk"),
        P("blk"),
    )
    out_specs = P("blk", "head")
    return jax.shard_map(
        per_device, mesh=mesh, in_specs=in_specs, out_specs=out_specs, check_vma=False
    )
```

```python
import functools

import jax
import jax.numpy as jnp
from jax import lax
from jax.experimental import pallas as pl
from jax.experimental.pallas import tpu as pltpu
from jax.sharding import PartitionSpec as P

HEAD_DIM = 64
PAGE = 128
LANES = 128

far_below = -1e30
epsilon = 1e-06

VMEM_SPEC = pl.BlockSpec(memory_space=pltpu.VMEM)
SMEM_SPEC = pl.BlockSpec(memory_space=pltpu.SMEM)
ANY_SPEC = pl.BlockSpec(memory_space=pl.ANY)
HBM_SPEC = pl.BlockSpec(memory_space=pltpu.HBM)
PARAMS = pltpu.CompilerParams(vmem_limit_bytes=16 * 1024 * 1024)

PIECE = 8
SUM_LANE = 3 * PIECE


def iota(shape, axis):
    return lax.broadcasted_iota(jnp.int32, shape, axis)


def split_index(x, size):
    if size & (size - 1):
        return lax.div(x, size), lax.rem(x, size)
    return x >> (size.bit_length() - 1), x & (size - 1)


def head_of(shape, axis):
    return split_index(iota(shape, axis), HEAD_DIM)[0]


def pieces(x, count):
    parts = []
    for _ in range(count):
        part = x.astype(jnp.bfloat16)
        parts.append(part)
        x = x - part.astype(jnp.float32)
    return parts


def rms_normed(x, gain):
    scale = lax.rsqrt(jnp.mean(x * x, axis=1, keepdims=True) + epsilon)
    return (x * scale * gain).astype(jnp.bfloat16)


def dot(a, b, dims=((1,), (0,)), precision=None):
    return lax.dot_general(
        a, b, (dims, ((), ())), preferred_element_type=jnp.float32, precision=precision
    )


def split_copies(source, target, sems, count):
    size = source.shape[0] // count
    return [
        pltpu.make_async_copy(
            source.at[pl.ds(i * size, size)], target.at[pl.ds(i * size, size)], sems.at[i]
        )
        for i in range(count)
    ]


def query_kernel(hidden_hbm, gain_hbm, weight_hbm, query_ref, hidden, gain, weight, sems):
    model = hidden.shape[1]
    small = [
        pltpu.make_async_copy(hidden_hbm, hidden, sems.at[0]),
        pltpu.make_async_copy(gain_hbm, gain, sems.at[1]),
    ]
    half = model // 4
    large = [
        pltpu.make_async_copy(
            weight_hbm.at[0, pl.ds(i * half, half)], weight.at[pl.ds(i * half, half)], sems.at[2 + i]
        )
        for i in range(4)
    ]
    for copy in small + large:
        copy.start()
    for copy in small:
        copy.wait()
    normed = rms_normed(hidden[...], gain[...])
    query = None
    for i, copy in enumerate(large):
        copy.wait()
        span = slice(i * half, (i + 1) * half)
        part = dot(normed[:, span], weight[span])
        query = part if query is None else query + part
    query_ref[...] = query.astype(jnp.bfloat16)


def page_kernel(
    own_rows, inner, outer, query_ref, request_ref, keys_hbm,
    keys_ref, pick_ref, place_ref, first_ref, apart_ref,
    sems,
):
    copies = split_copies(
        keys_hbm.at[pl.ds(0, keys_ref.shape[0])], keys_ref, sems, sems.shape[0]
    )
    for copy in copies:
        copy.start()
    me = lax.axis_index("blk")
    page_count = request_ref.shape[0]
    all_rows, depth = place_ref.shape
    row_of = iota((PIECE, all_rows), 1)
    page_of = split_index(iota((1, depth), 1), PIECE)[0]
    lane = iota((1, LANES), 1)
    requests = [request_ref[p] for p in range(page_count)]
    by_lane = jnp.full((1, LANES), -2, jnp.int32)
    for p in range(page_count):
        by_lane = jnp.where(lane == p, requests[p], by_lane)
    slots = jnp.full((1, depth), -1, jnp.int32)
    leads = jnp.full((1, depth), -1, jnp.int32)
    picks = []
    for p in range(page_count):
        owner = requests[p]
        device, own_row = split_index(jnp.maximum(owner, 0), own_rows)
        high, low = split_index(device ^ me, inner)
        slot = (low * outer + high) * own_rows + own_row
        slot = jnp.where(owner >= 0, slot, -1)
        picks.append((row_of == slot).astype(jnp.float32))
        slots = jnp.where(page_of == p, slot, slots)
        same = by_lane == owner
        apart_ref[p : p + 1] = jnp.where(same, 0.0, 2 * far_below)
        earlier = jnp.max(jnp.where(same & (lane < p), 1, 0), axis=1, keepdims=True)
        leads = jnp.where((page_of == p) & (earlier == 0), slot, leads)
    pick_ref[...] = jnp.concatenate(picks, axis=0).astype(jnp.bfloat16)
    row = iota((all_rows, depth), 0)
    place_ref[...] = (row == slots).astype(jnp.bfloat16)
    first_ref[...] = (row == leads).astype(jnp.bfloat16)
    for copy in copies:
        copy.wait()


def bias_kernel(
    table_hbm, edges_hbm, lengths_hbm, index_hbm, request_ref, keys_hbm, after_ref,
    keys_ref, bias_ref,
    table, edges_ref, lengths_ref, index_ref, small_sems, sems,
):
    sources = (table_hbm, edges_hbm, lengths_hbm, index_hbm)
    targets = (table, edges_ref, lengths_ref, index_ref)
    small = [
        pltpu.make_async_copy(source, target, small_sems.at[i])
        for i, (source, target) in enumerate(zip(sources, targets))
    ]
    late = keys_ref.shape[0]
    copies = split_copies(
        keys_hbm.at[pl.ds(keys_hbm.shape[0] - late, late)], keys_ref, sems, sems.shape[0]
    )
    for copy in small + copies:
        copy.start()
    for copy in small:
        copy.wait()
    heads, buckets = table.shape
    by_head = table[...]
    if heads < PIECE:
        by_head = jnp.concatenate([by_head[min(h, heads - 1)][None] for h in range(PIECE)], axis=0)
    columns = [jnp.broadcast_to(by_head[:, k : k + 1], (PIECE, PAGE)) for k in range(buckets)]
    token = iota((PIECE, PAGE), 1)
    for p in range(request_ref.shape[0]):
        owner = request_ref[p]
        left = lengths_ref[jnp.maximum(owner, 0)] - index_ref[p] * PAGE
        distance = jnp.where(owner >= 0, left, 0) - token
        bias = columns[0]
        for k in range(buckets - 1):
            bias = jnp.where(distance >= edges_ref[k], columns[k + 1], bias)
        bias_ref[p] = jnp.where(distance > 0, bias, far_below)
    for copy in copies:
        copy.wait()


def side_kernel(
    hidden_ref, gain_ref, query_ref, table_ref, weight_hbm, out_hbm, after_ref,
    score_ref, value_ref, out_ref,
    weight, weight_sems, sems,
):
    copies = [
        pltpu.make_async_copy(weight_hbm.at[1 + i], weight.at[i], weight_sems.at[i])
        for i in range(2)
    ]
    later = split_copies(out_hbm, out_ref, sems, sems.shape[0])
    for copy in copies + later:
        copy.start()
    normed = rms_normed(hidden_ref[...], gain_ref[...])
    heads = table_ref.shape[0]
    spread = iota((heads, LANES), 0) == iota((heads, LANES), 1)
    score = jnp.sum(jnp.where(spread, table_ref[:, 0:1], 0.0), axis=0, keepdims=True)
    copies[0].wait()
    key = dot(normed, weight[0]).astype(jnp.bfloat16)
    product = query_ref[...].astype(jnp.float32) * key.astype(jnp.float32)
    width = product.shape[1]
    gather = (head_of((width, LANES), 0) == iota((width, LANES), 1)).astype(jnp.bfloat16)
    for part in pieces(product, 3):
        score = score + dot(part, gather)
    score_ref[...] = score
    copies[1].wait()
    value_ref[...] = dot(normed, weight[1]).astype(jnp.bfloat16)
    for copy in later:
        copy.wait()


def load_kernel(source, after_ref, target, sems):
    copies = split_copies(source, target, sems, sems.shape[0])
    for copy in copies:
        copy.start()
    for copy in copies:
        copy.wait()


def packed_stats(peaks, sums):
    one, two, three = (part.astype(jnp.float32) for part in pieces(peaks + sums, 3))
    packed = one + pltpu.roll(two, PIECE, 1) + pltpu.roll(three, 2 * PIECE, 1)
    return packed.astype(jnp.bfloat16)


def unpacked_stats(packed, heads):
    stats = packed.astype(jnp.float32)
    stats = stats + pltpu.roll(stats, LANES - PIECE, 1) + pltpu.roll(stats, LANES - 2 * PIECE, 1)
    sums = pltpu.roll(stats, LANES - SUM_LANE, 1)
    used = iota(stats.shape, 1) < heads
    return jnp.where(used & (sums > 0.0), stats, far_below), jnp.where(used, sums, 0.0)


def over_columns(values, width):
    spread = (iota((LANES, width), 0) == head_of((LANES, width), 1)).astype(jnp.bfloat16)
    return sum(dot(part, spread) for part in pieces(values, 3))


def attend_kernel(groups, *refs):
    query_refs, refs, sums_refs = refs[:groups], refs[groups:-groups], refs[-groups:]
    bias_ref, pick_ref, place_ref, first_ref, apart_ref, keys_ref, late_ref, values_ref = refs
    page_count = apart_ref.shape[0]
    width = keys_ref.shape[2]
    early = keys_ref.shape[0]
    chunk = 2
    chunks = page_count // chunk
    queries = jnp.concatenate([ref[...] for ref in query_refs], axis=0)
    own_head = (head_of((PIECE, width), 1) == iota((PIECE, width), 0)).astype(jnp.float32)
    pair_heads = jnp.concatenate([own_head] * chunk, axis=0)
    chosen = dot(pick_ref[...], queries)
    lane = iota((PIECE, LANES), 1)
    row = iota((PIECE, LANES), 0)
    scores = []
    tops = jnp.zeros((PIECE, LANES), jnp.float32)
    for c in range(chunks):
        rows = chosen[c * chunk * PIECE : (c + 1) * chunk * PIECE]
        split = (rows * pair_heads).astype(jnp.bfloat16)
        at = c * chunk
        block = keys_ref[at : at + chunk] if at < early else late_ref[at - early : at - early + chunk]
        block = block.reshape(chunk * PAGE, width)
        raw = dot(split, block, ((1,), (1,)))
        for i in range(chunk):
            p = c * chunk + i
            part = raw[i * PIECE : (i + 1) * PIECE, i * PAGE : (i + 1) * PAGE]
            score = part + bias_ref[p]
            scores.append(score)
            tops = jnp.where(lane == p, jnp.max(score, axis=1, keepdims=True), tops)
    mixes, peaks, totals = [], [], []
    nothing = jnp.zeros((PIECE, PAGE), jnp.float32)
    for c in range(chunks):
        blocks = []
        for i in range(chunk):
            p = c * chunk + i
            peak = jnp.max(tops + apart_ref[p : p + 1], axis=1, keepdims=True)
            weight = jnp.exp(scores[p] - peak)
            total = jnp.sum(weight, axis=1, keepdims=True)
            peaks.append(jnp.where(lane == row, peak, 0.0))
            totals.append(jnp.where(lane == row + SUM_LANE, total, 0.0))
            blocks.append(
                jnp.concatenate([weight if k == i else nothing for k in range(chunk)], axis=1)
            )
        weights = jnp.concatenate(blocks, axis=0).astype(jnp.bfloat16)
        block = values_ref[c * chunk : (c + 1) * chunk].reshape(chunk * PAGE, width)
        mixes.append(dot(weights, block) * pair_heads)
    mix = jnp.concatenate(mixes, axis=0)
    place, first = place_ref[...], first_ref[...]
    high, low = pieces(mix, 2)
    sums = dot(place, high) + dot(place, low)
    collected = sum(dot(first, part) for part in pieces(jnp.concatenate(peaks, axis=0), 3))
    collected += sum(dot(place, part) for part in pieces(jnp.concatenate(totals, axis=0), 3))
    stats = packed_stats(collected, 0.0)
    size = sums_refs[0].shape[0]
    for i, sums_ref in enumerate(sums_refs):
        span = slice(i * size, (i + 1) * size)
        sums_ref[:, :width] = sums[span].astype(jnp.bfloat16)
        sums_ref[:, width:] = stats[span]


def combine_kernel(sources, *refs):
    part_refs, sums_refs = refs[:sources], refs[sources:]
    rows, columns = part_refs[0].shape
    width = columns - LANES
    stats = [unpacked_stats(ref[:, width:], width // HEAD_DIM) for ref in part_refs]
    peak = stats[0][0]
    for peaks, _ in stats[1:]:
        peak = jnp.maximum(peak, peaks)
    factors = [jnp.exp(peaks - peak) for peaks, _ in stats]
    total = sum(factor * sums for factor, (_, sums) in zip(factors, stats))
    shares = over_columns(jnp.concatenate(factors, axis=0), width)
    mixed = sum(
        ref[:, :width].astype(jnp.float32) * shares[i * rows : (i + 1) * rows]
        for i, ref in enumerate(part_refs)
    )
    packed = packed_stats(
        jnp.where(total > 0.0, peak, 0.0), pltpu.roll(total, SUM_LANE, 1)
    ).astype(jnp.float32)
    size = sums_refs[0].shape[0]
    for i, sums_ref in enumerate(sums_refs):
        span = slice(i * size, (i + 1) * size)
        sums_ref[:, :width] = mixed[span].astype(jnp.bfloat16)
        sums_ref[:, width:] = packed[span].astype(jnp.bfloat16)


def merge_kernel(sources, *refs):
    part_refs, (score_ref, value_ref, weight_ref, own_ref, send_ref) = refs[:sources], refs[sources:]
    own_rows, width = value_ref.shape
    heads = width // HEAD_DIM
    stats = [unpacked_stats(ref[:, width:], heads) for ref in part_refs]
    own_score = jnp.where(iota(score_ref.shape, 1) < heads, score_ref[...], 0.0)
    peak = own_score
    for peaks, _ in stats:
        peak = jnp.maximum(peak, peaks)
    own_weight = jnp.exp(own_score - peak)
    total = own_weight
    factors = []
    for peaks, sums in stats:
        factor = jnp.exp(peaks - peak)
        total = total + factor * sums
        factors.append(factor)
    factors.append(own_weight.astype(jnp.bfloat16).astype(jnp.float32))
    shares = jnp.concatenate([factor / total for factor in factors], axis=0)
    shares = over_columns(shares, width)
    mixed = value_ref[...].astype(jnp.float32) * shares[sources * own_rows :]
    for i, ref in enumerate(part_refs):
        rows = slice(i * own_rows, (i + 1) * own_rows)
        mixed = mixed + ref[:, :width].astype(jnp.float32) * shares[rows]
    projected = dot(mixed.astype(jnp.bfloat16), weight_ref[...])
    own_ref[...] = projected
    send_ref[...] = projected.astype(jnp.bfloat16)


def mlp_kernel(exchanged, hidden_ref, own_ref, other_ref, gain_ref, up_ref, down_ref, *outs):
    middle = hidden_ref[...] + (own_ref[...] + other_ref[...].astype(jnp.float32))
    normed = rms_normed(middle, gain_ref[...])
    active = jnp.maximum(dot(normed, up_ref[...]), 0.0).astype(jnp.bfloat16)
    down = dot(active, down_ref[...])
    if exchanged:
        kept_ref, sent_ref = outs
        columns = kept_ref.shape[1]
        low = lax.axis_index("head") == 0
        left, right = slice(0, columns), slice(columns, 2 * columns)
        kept = middle + down

        @pl.when(low)
        def _():
            kept_ref[...] = kept[:, left]
            sent_ref[...] = down[:, right].astype(jnp.bfloat16)

        @pl.when(jnp.logical_not(low))
        def _():
            kept_ref[...] = kept[:, right]
            sent_ref[...] = down[:, left].astype(jnp.bfloat16)

    else:
        middle_ref, down_out_ref = outs
        middle_ref[...] = middle
        down_out_ref[...] = down.astype(jnp.bfloat16)


def loading(*arrays):
    return pl.CostEstimate(
        flops=0, bytes_accessed=sum(2 * array.size for array in arrays), transcendentals=0
    )


def in_hbm(*arrays):
    return [pltpu.with_memory_space_constraint(array, pltpu.HBM) for array in arrays]


def xor_pairs(size, step):
    return [(i, i ^ step) for i in range(size)]


def per_device(
    hidden_in, attention_gain, mlp_gain, qkv_weight, out_weight, up_weight, down_weight,
    position_bias, bucket_edges, cache_keys, cache_values, lengths, page_request, page_index,
):
    f32, bf16 = jnp.float32, jnp.bfloat16
    shape = jax.ShapeDtypeStruct
    own_rows, model = hidden_in.shape
    width = qkv_weight.shape[2]
    page_count = page_request.shape[0]
    blocks = lax.axis_size("blk")
    all_rows = own_rows * blocks
    gain = attention_gain.reshape(1, model)
    query = pl.pallas_call(
        query_kernel,
        out_shape=shape((own_rows, width), bf16),
        in_specs=[HBM_SPEC] * 3,
        out_specs=VMEM_SPEC,
        scratch_shapes=[
            pltpu.VMEM((own_rows, model), f32),
            pltpu.VMEM((1, model), f32),
            pltpu.VMEM((model, width), bf16),
            pltpu.SemaphoreType.DMA((6,)),
        ],
        compiler_params=PARAMS,
        name="query",
    )(*in_hbm(hidden_in, gain, qkv_weight))

    inner = 1
    while inner * inner < blocks:
        inner *= 2
    far = [query] + [
        lax.ppermute(query, "blk", xor_pairs(blocks, step * inner))
        for step in range(1, blocks // inner)
    ]
    depth = page_count * PIECE
    early = page_count // 2
    keys, picks, place, first, apart = pl.pallas_call(
        functools.partial(page_kernel, own_rows, inner, blocks // inner),
        out_shape=(
            pltpu.VMEM((early,) + cache_keys.shape[1:], bf16),
            shape((depth, all_rows), bf16),
            shape((all_rows, depth), bf16),
            shape((all_rows, depth), bf16),
            shape((page_count, LANES), f32),
        ),
        in_specs=[ANY_SPEC, SMEM_SPEC, HBM_SPEC],
        out_specs=(VMEM_SPEC,) * 5,
        scratch_shapes=[pltpu.SemaphoreType.DMA((4,))],
        compiler_params=PARAMS,
        cost_estimate=loading(cache_keys),
        name="pages",
    )(query, page_request, *in_hbm(cache_keys))
    near, apart = lax.optimization_barrier((jnp.concatenate(far, axis=0), apart))
    gathered = [near] + [
        lax.ppermute(near, "blk", xor_pairs(blocks, step)) for step in range(1, inner)
    ]
    table = position_bias.T
    late_keys, bias = pl.pallas_call(
        bias_kernel,
        out_shape=(
            pltpu.VMEM((page_count - early,) + cache_keys.shape[1:], bf16),
            shape((page_count, PIECE, PAGE), f32),
        ),
        in_specs=[HBM_SPEC] * 4 + [SMEM_SPEC, HBM_SPEC, ANY_SPEC],
        out_specs=(VMEM_SPEC,) * 2,
        scratch_shapes=[
            pltpu.VMEM(table.shape, f32),
            pltpu.SMEM(bucket_edges.shape, jnp.int32),
            pltpu.SMEM(lengths.shape, jnp.int32),
            pltpu.SMEM(page_index.shape, jnp.int32),
            pltpu.SemaphoreType.DMA((4,)),
            pltpu.SemaphoreType.DMA((4,)),
        ],
        compiler_params=PARAMS,
        cost_estimate=loading(cache_values),
        name="bias",
    )(
        *in_hbm(table, bucket_edges, lengths, page_index), page_request,
        *in_hbm(cache_keys), near,
    )

    groups = len(gathered)
    sums = pl.pallas_call(
        functools.partial(attend_kernel, groups),
        out_shape=(shape((all_rows // groups, width + LANES), bf16),) * groups,
        in_specs=[VMEM_SPEC] * (groups + 8),
        out_specs=(VMEM_SPEC,) * groups,
        compiler_params=PARAMS,
        name="attend",
    )(*gathered, bias, picks, place, first, apart, keys, late_keys, cache_values)
    near_sums = [sums[0]] + [
        lax.ppermute(sums[step], "blk", xor_pairs(blocks, step)) for step in range(1, inner)
    ]

    own_score, value_new, out_near = pl.pallas_call(
        side_kernel,
        out_shape=(
            shape((own_rows, LANES), f32),
            shape((own_rows, width), bf16),
            pltpu.VMEM(out_weight.shape, bf16),
        ),
        in_specs=[VMEM_SPEC] * 4 + [HBM_SPEC] * 2 + [ANY_SPEC],
        out_specs=(VMEM_SPEC,) * 3,
        scratch_shapes=[
            pltpu.VMEM((2, model, width), bf16),
            pltpu.SemaphoreType.DMA((2,)),
            pltpu.SemaphoreType.DMA((4,)),
        ],
        compiler_params=PARAMS,
        cost_estimate=loading(out_weight, out_weight, out_weight),
        name="side",
    )(
        hidden_in, gain, query, table,
        *in_hbm(qkv_weight, out_weight), sums[0],
    )

    outer = blocks // inner
    sums = pl.pallas_call(
        functools.partial(combine_kernel, inner),
        out_shape=(shape((own_rows, width + LANES), bf16),) * outer,
        in_specs=[VMEM_SPEC] * inner,
        out_specs=(VMEM_SPEC,) * outer,
        compiler_params=PARAMS,
        name="combine",
    )(*near_sums)
    parts = [sums[0]] + [
        lax.ppermute(sums[step], "blk", xor_pairs(blocks, step * inner))
        for step in reversed(range(1, outer))
    ]

    own_part, sent_part = pl.pallas_call(
        functools.partial(merge_kernel, outer),
        out_shape=(shape((own_rows, model), f32), shape((own_rows, model), bf16)),
        in_specs=[VMEM_SPEC] * (outer + 3),
        out_specs=(VMEM_SPEC,) * 2,
        compiler_params=PARAMS,
        name="merge",
    )(*parts, own_score, value_new, out_near)

    halves = lax.axis_size("head")
    columns = model // halves
    exchanged = halves == 2
    down_near = pl.pallas_call(
        load_kernel,
        out_shape=pltpu.VMEM(down_weight.shape, bf16),
        in_specs=[HBM_SPEC, ANY_SPEC],
        out_specs=VMEM_SPEC,
        scratch_shapes=[pltpu.SemaphoreType.DMA((8,))],
        compiler_params=PARAMS,
        cost_estimate=loading(down_weight),
        name="load",
    )(*in_hbm(down_weight), sent_part)
    if exchanged:
        other_part = lax.ppermute(sent_part, "head", xor_pairs(2, 1))
        mlp_out = (shape((own_rows, columns), f32), shape((own_rows, columns), bf16))
    else:
        own_part = jnp.zeros_like(own_part)
        other_part = lax.psum(sent_part, "head")
        mlp_out = (shape((own_rows, model), f32), shape((own_rows, model), bf16))

    kept, leaving = pl.pallas_call(
        functools.partial(mlp_kernel, exchanged),
        out_shape=mlp_out,
        in_specs=[VMEM_SPEC] * 6,
        out_specs=(VMEM_SPEC,) * 2,
        compiler_params=PARAMS,
        name="mlp",
    )(hidden_in, own_part, other_part, mlp_gain.reshape(1, model), up_weight, down_near)

    if exchanged:
        both = lax.all_gather(leaving, "head")
        arrived = jnp.where(lax.axis_index("head") == 0, both[1], both[0])
    else:
        kept = lax.dynamic_slice_in_dim(kept, lax.axis_index("head") * columns, columns, 1)
        arrived = lax.psum_scatter(leaving, "head", scatter_dimension=1, tiled=True)
    return kept + arrived.astype(f32)


def solution(mesh):
    in_specs = (
        P("blk", None),
        P(),
        P(),
        P(None, None, "head"),
        P("head", None),
        P(None, "head"),
        P("head", None),
        P(None, "head"),
        P(),
        P("blk", None, "head"),
        P("blk", None, "head"),
        P(),
        P("blk"),
        P("blk"),
    )
    out_specs = P("blk", "head")
    return jax.shard_map(
        per_device, mesh=mesh, in_specs=in_specs, out_specs=out_specs, check_vma=False
    )
```

```python
import functools

import jax
import jax.numpy as jnp
from jax import lax
from jax.experimental import pallas as pl
from jax.experimental.pallas import tpu as pltpu
from jax.sharding import PartitionSpec as P

HEAD_DIM = 64
PAGE = 128
LANES = 128

far_below = -1e30
epsilon = 1e-06

VMEM_SPEC = pl.BlockSpec(memory_space=pltpu.VMEM)
SMEM_SPEC = pl.BlockSpec(memory_space=pltpu.SMEM)
ANY_SPEC = pl.BlockSpec(memory_space=pl.ANY)
HBM_SPEC = pl.BlockSpec(memory_space=pltpu.HBM)
PARAMS = pltpu.CompilerParams(vmem_limit_bytes=16 * 1024 * 1024)

PIECE = 8
SUM_LANE = 3 * PIECE


def iota(shape, axis):
    return lax.broadcasted_iota(jnp.int32, shape, axis)


def split_index(x, size):
    if size & (size - 1):
        return lax.div(x, size), lax.rem(x, size)
    return x >> (size.bit_length() - 1), x & (size - 1)


def head_of(shape, axis):
    return split_index(iota(shape, axis), HEAD_DIM)[0]


def pieces(x, count):
    parts = []
    for _ in range(count):
        part = x.astype(jnp.bfloat16)
        parts.append(part)
        x = x - part.astype(jnp.float32)
    return parts


def rms_normed(x, gain):
    scale = lax.rsqrt(jnp.mean(x * x, axis=1, keepdims=True) + epsilon)
    return (x * scale * gain).astype(jnp.bfloat16)


def dot(a, b, dims=((1,), (0,)), precision=None):
    return lax.dot_general(
        a, b, (dims, ((), ())), preferred_element_type=jnp.float32, precision=precision
    )


def split_copies(source, target, sems, count):
    size = source.shape[0] // count
    return [
        pltpu.make_async_copy(
            source.at[pl.ds(i * size, size)], target.at[pl.ds(i * size, size)], sems.at[i]
        )
        for i in range(count)
    ]


def query_kernel(hidden_hbm, gain_hbm, weight_hbm, query_ref, hidden, gain, weight, sems):
    model = hidden.shape[1]
    small = [
        pltpu.make_async_copy(hidden_hbm, hidden, sems.at[0]),
        pltpu.make_async_copy(gain_hbm, gain, sems.at[1]),
    ]
    half = model // 4
    large = [
        pltpu.make_async_copy(
            weight_hbm.at[0, pl.ds(i * half, half)], weight.at[pl.ds(i * half, half)], sems.at[2 + i]
        )
        for i in range(4)
    ]
    for copy in small + large:
        copy.start()
    for copy in small:
        copy.wait()
    normed = rms_normed(hidden[...], gain[...])
    query = None
    for i, copy in enumerate(large):
        copy.wait()
        span = slice(i * half, (i + 1) * half)
        part = dot(normed[:, span], weight[span])
        query = part if query is None else query + part
    query_ref[...] = query.astype(jnp.bfloat16)


def page_kernel(
    own_rows, inner, outer, query_ref, request_ref, keys_hbm,
    keys_ref, pick_ref, place_ref, first_ref, apart_ref,
    sems,
):
    copies = split_copies(
        keys_hbm.at[pl.ds(0, keys_ref.shape[0])], keys_ref, sems, sems.shape[0]
    )
    for copy in copies:
        copy.start()
    me = lax.axis_index("blk")
    page_count = request_ref.shape[0]
    all_rows, depth = place_ref.shape
    row_of = iota((PIECE, all_rows), 1)
    page_of = split_index(iota((1, depth), 1), PIECE)[0]
    lane = iota((1, LANES), 1)
    requests = [request_ref[p] for p in range(page_count)]
    by_lane = jnp.full((1, LANES), -2, jnp.int32)
    for p in range(page_count):
        by_lane = jnp.where(lane == p, requests[p], by_lane)
    slots = jnp.full((1, depth), -1, jnp.int32)
    leads = jnp.full((1, depth), -1, jnp.int32)
    picks = []
    for p in range(page_count):
        owner = requests[p]
        device, own_row = split_index(jnp.maximum(owner, 0), own_rows)
        high, low = split_index(device ^ me, inner)
        slot = (low * outer + high) * own_rows + own_row
        slot = jnp.where(owner >= 0, slot, -1)
        picks.append((row_of == slot).astype(jnp.float32))
        slots = jnp.where(page_of == p, slot, slots)
        same = by_lane == owner
        apart_ref[p : p + 1] = jnp.where(same, 0.0, 2 * far_below)
        earlier = jnp.max(jnp.where(same & (lane < p), 1, 0), axis=1, keepdims=True)
        leads = jnp.where((page_of == p) & (earlier == 0), slot, leads)
    pick_ref[...] = jnp.concatenate(picks, axis=0).astype(jnp.bfloat16)
    row = iota((all_rows, depth), 0)
    place_ref[...] = (row == slots).astype(jnp.bfloat16)
    first_ref[...] = (row == leads).astype(jnp.bfloat16)
    for copy in copies:
        copy.wait()


def bias_kernel(
    table_hbm, edges_hbm, lengths_hbm, index_hbm, request_ref, keys_hbm, after_ref,
    keys_ref, bias_ref,
    table, edges_ref, lengths_ref, index_ref, small_sems, sems,
):
    sources = (table_hbm, edges_hbm, lengths_hbm, index_hbm)
    targets = (table, edges_ref, lengths_ref, index_ref)
    small = [
        pltpu.make_async_copy(source, target, small_sems.at[i])
        for i, (source, target) in enumerate(zip(sources, targets))
    ]
    late = keys_ref.shape[0]
    copies = split_copies(
        keys_hbm.at[pl.ds(keys_hbm.shape[0] - late, late)], keys_ref, sems, sems.shape[0]
    )
    for copy in small + copies:
        copy.start()
    for copy in small:
        copy.wait()
    heads, buckets = table.shape
    by_head = table[...]
    if heads < PIECE:
        by_head = jnp.concatenate([by_head[min(h, heads - 1)][None] for h in range(PIECE)], axis=0)
    columns = [jnp.broadcast_to(by_head[:, k : k + 1], (PIECE, PAGE)) for k in range(buckets)]
    token = iota((PIECE, PAGE), 1)
    for p in range(request_ref.shape[0]):
        owner = request_ref[p]
        left = lengths_ref[jnp.maximum(owner, 0)] - index_ref[p] * PAGE
        distance = jnp.where(owner >= 0, left, 0) - token
        bias = columns[0]
        for k in range(buckets - 1):
            bias = jnp.where(distance >= edges_ref[k], columns[k + 1], bias)
        bias_ref[p] = jnp.where(distance > 0, bias, far_below)
    for copy in copies:
        copy.wait()


def side_kernel(
    hidden_ref, gain_ref, query_ref, table_ref, weight_hbm, out_hbm, after_ref,
    score_ref, value_ref, out_ref,
    weight, weight_sems, sems,
):
    copies = [
        pltpu.make_async_copy(weight_hbm.at[1 + i], weight.at[i], weight_sems.at[i])
        for i in range(2)
    ]
    later = split_copies(out_hbm, out_ref, sems, sems.shape[0])
    for copy in copies + later:
        copy.start()
    normed = rms_normed(hidden_ref[...], gain_ref[...])
    heads = table_ref.shape[0]
    spread = iota((heads, LANES), 0) == iota((heads, LANES), 1)
    score = jnp.sum(jnp.where(spread, table_ref[:, 0:1], 0.0), axis=0, keepdims=True)
    copies[0].wait()
    key = dot(normed, weight[0]).astype(jnp.bfloat16)
    product = query_ref[...].astype(jnp.float32) * key.astype(jnp.float32)
    width = product.shape[1]
    gather = (head_of((width, LANES), 0) == iota((width, LANES), 1)).astype(jnp.bfloat16)
    for part in pieces(product, 3):
        score = score + dot(part, gather)
    score_ref[...] = score
    copies[1].wait()
    value_ref[...] = dot(normed, weight[1]).astype(jnp.bfloat16)
    for copy in later:
        copy.wait()


def load_kernel(source, after_ref, target, sems):
    copies = split_copies(source, target, sems, sems.shape[0])
    for copy in copies:
        copy.start()
    for copy in copies:
        copy.wait()


def packed_stats(peaks, sums):
    one, two, three = (part.astype(jnp.float32) for part in pieces(peaks + sums, 3))
    packed = one + pltpu.roll(two, PIECE, 1) + pltpu.roll(three, 2 * PIECE, 1)
    return packed.astype(jnp.bfloat16)


def unpacked_stats(packed, heads):
    stats = packed.astype(jnp.float32)
    stats = stats + pltpu.roll(stats, LANES - PIECE, 1) + pltpu.roll(stats, LANES - 2 * PIECE, 1)
    sums = pltpu.roll(stats, LANES - SUM_LANE, 1)
    used = iota(stats.shape, 1) < heads
    return jnp.where(used & (sums > 0.0), stats, far_below), jnp.where(used, sums, 0.0)


def over_columns(values, width):
    spread = (iota((LANES, width), 0) == head_of((LANES, width), 1)).astype(jnp.bfloat16)
    return sum(dot(part, spread) for part in pieces(values, 3))


def attend_kernel(groups, *refs):
    query_refs, refs, sums_refs = refs[:groups], refs[groups:-groups], refs[-groups:]
    bias_ref, pick_ref, place_ref, first_ref, apart_ref, keys_ref, late_ref, values_ref = refs
    page_count = apart_ref.shape[0]
    width = keys_ref.shape[2]
    early = keys_ref.shape[0]
    chunk = 2
    chunks = page_count // chunk
    queries = jnp.concatenate([ref[...] for ref in query_refs], axis=0)
    own_head = (head_of((PIECE, width), 1) == iota((PIECE, width), 0)).astype(jnp.float32)
    pair_heads = jnp.concatenate([own_head] * chunk, axis=0)
    chosen = dot(pick_ref[...], queries)
    lane = iota((PIECE, LANES), 1)
    row = iota((PIECE, LANES), 0)
    scores = []
    tops = jnp.zeros((PIECE, LANES), jnp.float32)
    for c in range(chunks):
        rows = chosen[c * chunk * PIECE : (c + 1) * chunk * PIECE]
        split = (rows * pair_heads).astype(jnp.bfloat16)
        at = c * chunk
        block = keys_ref[at : at + chunk] if at < early else late_ref[at - early : at - early + chunk]
        block = block.reshape(chunk * PAGE, width)
        raw = dot(split, block, ((1,), (1,)))
        for i in range(chunk):
            p = c * chunk + i
            part = raw[i * PIECE : (i + 1) * PIECE, i * PAGE : (i + 1) * PAGE]
            score = part + bias_ref[p]
            scores.append(score)
            tops = jnp.where(lane == p, jnp.max(score, axis=1, keepdims=True), tops)
    mixes, peaks, totals = [], [], []
    nothing = jnp.zeros((PIECE, PAGE), jnp.float32)
    for c in range(chunks):
        blocks = []
        for i in range(chunk):
            p = c * chunk + i
            peak = jnp.max(tops + apart_ref[p : p + 1], axis=1, keepdims=True)
            weight = jnp.exp(scores[p] - peak)
            total = jnp.sum(weight, axis=1, keepdims=True)
            peaks.append(jnp.where(lane == row, peak, 0.0))
            totals.append(jnp.where(lane == row + SUM_LANE, total, 0.0))
            blocks.append(
                jnp.concatenate([weight if k == i else nothing for k in range(chunk)], axis=1)
            )
        weights = jnp.concatenate(blocks, axis=0).astype(jnp.bfloat16)
        block = values_ref[c * chunk : (c + 1) * chunk].reshape(chunk * PAGE, width)
        mixes.append(dot(weights, block) * pair_heads)
    mix = jnp.concatenate(mixes, axis=0)
    place, first = place_ref[...], first_ref[...]
    high, low = pieces(mix, 2)
    sums = dot(place, high) + dot(place, low)
    collected = sum(dot(first, part) for part in pieces(jnp.concatenate(peaks, axis=0), 3))
    collected += sum(dot(place, part) for part in pieces(jnp.concatenate(totals, axis=0), 3))
    stats = packed_stats(collected, 0.0)
    size = sums_refs[0].shape[0]
    for i, sums_ref in enumerate(sums_refs):
        span = slice(i * size, (i + 1) * size)
        sums_ref[:, :width] = sums[span].astype(jnp.bfloat16)
        sums_ref[:, width:] = stats[span]


def combine_kernel(sources, *refs):
    part_refs, sums_refs = refs[:sources], refs[sources:]
    rows, columns = part_refs[0].shape
    width = columns - LANES
    stats = [unpacked_stats(ref[:, width:], width // HEAD_DIM) for ref in part_refs]
    peak = stats[0][0]
    for peaks, _ in stats[1:]:
        peak = jnp.maximum(peak, peaks)
    factors = [jnp.exp(peaks - peak) for peaks, _ in stats]
    total = sum(factor * sums for factor, (_, sums) in zip(factors, stats))
    shares = over_columns(jnp.concatenate(factors, axis=0), width)
    mixed = sum(
        ref[:, :width].astype(jnp.float32) * shares[i * rows : (i + 1) * rows]
        for i, ref in enumerate(part_refs)
    )
    packed = packed_stats(
        jnp.where(total > 0.0, peak, 0.0), pltpu.roll(total, SUM_LANE, 1)
    ).astype(jnp.float32)
    size = sums_refs[0].shape[0]
    for i, sums_ref in enumerate(sums_refs):
        span = slice(i * size, (i + 1) * size)
        sums_ref[:, :width] = mixed[span].astype(jnp.bfloat16)
        sums_ref[:, width:] = packed[span].astype(jnp.bfloat16)


def merge_kernel(sources, *refs):
    part_refs, (score_ref, value_ref, weight_ref, own_ref, send_ref) = refs[:sources], refs[sources:]
    own_rows, width = value_ref.shape
    heads = width // HEAD_DIM
    stats = [unpacked_stats(ref[:, width:], heads) for ref in part_refs]
    own_score = jnp.where(iota(score_ref.shape, 1) < heads, score_ref[...], 0.0)
    peak = own_score
    for peaks, _ in stats:
        peak = jnp.maximum(peak, peaks)
    own_weight = jnp.exp(own_score - peak)
    total = own_weight
    factors = []
    for peaks, sums in stats:
        factor = jnp.exp(peaks - peak)
        total = total + factor * sums
        factors.append(factor)
    factors.append(own_weight.astype(jnp.bfloat16).astype(jnp.float32))
    shares = jnp.concatenate([factor / total for factor in factors], axis=0)
    shares = over_columns(shares, width)
    mixed = value_ref[...].astype(jnp.float32) * shares[sources * own_rows :]
    for i, ref in enumerate(part_refs):
        rows = slice(i * own_rows, (i + 1) * own_rows)
        mixed = mixed + ref[:, :width].astype(jnp.float32) * shares[rows]
    projected = dot(mixed.astype(jnp.bfloat16), weight_ref[...])
    own_ref[...] = projected
    send_ref[...] = projected.astype(jnp.bfloat16)


def mlp_kernel(exchanged, hidden_ref, own_ref, other_ref, gain_ref, up_ref, down_ref, *outs):
    middle = hidden_ref[...] + (own_ref[...] + other_ref[...].astype(jnp.float32))
    normed = rms_normed(middle, gain_ref[...])
    active = jnp.maximum(dot(normed, up_ref[...]), 0.0).astype(jnp.bfloat16)
    down = dot(active, down_ref[...])
    if exchanged:
        kept_ref, sent_ref = outs
        columns = kept_ref.shape[1]
        low = lax.axis_index("head") == 0
        left, right = slice(0, columns), slice(columns, 2 * columns)
        kept = middle + down

        @pl.when(low)
        def _():
            kept_ref[...] = kept[:, left]
            sent_ref[...] = down[:, right].astype(jnp.bfloat16)

        @pl.when(jnp.logical_not(low))
        def _():
            kept_ref[...] = kept[:, right]
            sent_ref[...] = down[:, left].astype(jnp.bfloat16)

    else:
        middle_ref, down_out_ref = outs
        middle_ref[...] = middle
        down_out_ref[...] = down.astype(jnp.bfloat16)


def loading(*arrays):
    return pl.CostEstimate(
        flops=0, bytes_accessed=sum(2 * array.size for array in arrays), transcendentals=0
    )


def in_hbm(*arrays):
    return [pltpu.with_memory_space_constraint(array, pltpu.HBM) for array in arrays]


def xor_pairs(size, step):
    return [(i, i ^ step) for i in range(size)]


def per_device(
    hidden_in, attention_gain, mlp_gain, qkv_weight, out_weight, up_weight, down_weight,
    position_bias, bucket_edges, cache_keys, cache_values, lengths, page_request, page_index,
):
    f32, bf16 = jnp.float32, jnp.bfloat16
    shape = jax.ShapeDtypeStruct
    own_rows, model = hidden_in.shape
    width = qkv_weight.shape[2]
    page_count = page_request.shape[0]
    blocks = lax.axis_size("blk")
    all_rows = own_rows * blocks
    gain = attention_gain.reshape(1, model)
    query = pl.pallas_call(
        query_kernel,
        out_shape=shape((own_rows, width), bf16),
        in_specs=[HBM_SPEC] * 3,
        out_specs=VMEM_SPEC,
        scratch_shapes=[
            pltpu.VMEM((own_rows, model), f32),
            pltpu.VMEM((1, model), f32),
            pltpu.VMEM((model, width), bf16),
            pltpu.SemaphoreType.DMA((6,)),
        ],
        compiler_params=PARAMS,
        name="query",
    )(*in_hbm(hidden_in, gain, qkv_weight))

    inner = 1
    while inner * inner < blocks:
        inner *= 2
    far = [query] + [
        lax.ppermute(query, "blk", xor_pairs(blocks, step * inner))
        for step in range(1, blocks // inner)
    ]
    depth = page_count * PIECE
    early = page_count // 2
    keys, picks, place, first, apart = pl.pallas_call(
        functools.partial(page_kernel, own_rows, inner, blocks // inner),
        out_shape=(
            pltpu.VMEM((early,) + cache_keys.shape[1:], bf16),
            shape((depth, all_rows), bf16),
            shape((all_rows, depth), bf16),
            shape((all_rows, depth), bf16),
            shape((page_count, LANES), f32),
        ),
        in_specs=[ANY_SPEC, SMEM_SPEC, HBM_SPEC],
        out_specs=(VMEM_SPEC,) * 5,
        scratch_shapes=[pltpu.SemaphoreType.DMA((4,))],
        compiler_params=PARAMS,
        cost_estimate=loading(cache_keys),
        name="pages",
    )(query, page_request, *in_hbm(cache_keys))
    near, apart = lax.optimization_barrier((jnp.concatenate(far, axis=0), apart))
    gathered = [near] + [
        lax.ppermute(near, "blk", xor_pairs(blocks, step)) for step in range(1, inner)
    ]
    table = position_bias.T
    late_keys, bias = pl.pallas_call(
        bias_kernel,
        out_shape=(
            pltpu.VMEM((page_count - early,) + cache_keys.shape[1:], bf16),
            shape((page_count, PIECE, PAGE), f32),
        ),
        in_specs=[HBM_SPEC] * 4 + [SMEM_SPEC, HBM_SPEC, ANY_SPEC],
        out_specs=(VMEM_SPEC,) * 2,
        scratch_shapes=[
            pltpu.VMEM(table.shape, f32),
            pltpu.SMEM(bucket_edges.shape, jnp.int32),
            pltpu.SMEM(lengths.shape, jnp.int32),
            pltpu.SMEM(page_index.shape, jnp.int32),
            pltpu.SemaphoreType.DMA((4,)),
            pltpu.SemaphoreType.DMA((4,)),
        ],
        compiler_params=PARAMS,
        cost_estimate=loading(cache_values),
        name="bias",
    )(
        *in_hbm(table, bucket_edges, lengths, page_index), page_request,
        *in_hbm(cache_keys), near,
    )

    groups = len(gathered)
    sums = pl.pallas_call(
        functools.partial(attend_kernel, groups),
        out_shape=(shape((all_rows // groups, width + LANES), bf16),) * groups,
        in_specs=[VMEM_SPEC] * (groups + 8),
        out_specs=(VMEM_SPEC,) * groups,
        compiler_params=PARAMS,
        name="attend",
    )(*gathered, bias, picks, place, first, apart, keys, late_keys, cache_values)
    near_sums = [sums[0]] + [
        lax.ppermute(sums[step], "blk", xor_pairs(blocks, step))
        for step in reversed(range(1, inner))
    ]

    own_score, value_new, out_near = pl.pallas_call(
        side_kernel,
        out_shape=(
            shape((own_rows, LANES), f32),
            shape((own_rows, width), bf16),
            pltpu.VMEM(out_weight.shape, bf16),
        ),
        in_specs=[VMEM_SPEC] * 4 + [HBM_SPEC] * 2 + [ANY_SPEC],
        out_specs=(VMEM_SPEC,) * 3,
        scratch_shapes=[
            pltpu.VMEM((2, model, width), bf16),
            pltpu.SemaphoreType.DMA((2,)),
            pltpu.SemaphoreType.DMA((4,)),
        ],
        compiler_params=PARAMS,
        cost_estimate=loading(out_weight, out_weight, out_weight),
        name="side",
    )(
        hidden_in, gain, query, table,
        *in_hbm(qkv_weight, out_weight), sums[0],
    )

    *near_sums, own_score = lax.optimization_barrier((*near_sums, own_score))
    outer = blocks // inner
    sums = pl.pallas_call(
        functools.partial(combine_kernel, inner),
        out_shape=(shape((own_rows, width + LANES), bf16),) * outer,
        in_specs=[VMEM_SPEC] * inner,
        out_specs=(VMEM_SPEC,) * outer,
        compiler_params=PARAMS,
        name="combine",
    )(*near_sums)
    parts = [sums[0]] + [
        lax.ppermute(sums[step], "blk", xor_pairs(blocks, step * inner))
        for step in reversed(range(1, outer))
    ]

    own_part, sent_part = pl.pallas_call(
        functools.partial(merge_kernel, outer),
        out_shape=(shape((own_rows, model), f32), shape((own_rows, model), bf16)),
        in_specs=[VMEM_SPEC] * (outer + 3),
        out_specs=(VMEM_SPEC,) * 2,
        compiler_params=PARAMS,
        name="merge",
    )(*parts, own_score, value_new, out_near)

    halves = lax.axis_size("head")
    columns = model // halves
    exchanged = halves == 2
    down_near = pl.pallas_call(
        load_kernel,
        out_shape=pltpu.VMEM(down_weight.shape, bf16),
        in_specs=[HBM_SPEC, ANY_SPEC],
        out_specs=VMEM_SPEC,
        scratch_shapes=[pltpu.SemaphoreType.DMA((8,))],
        compiler_params=PARAMS,
        cost_estimate=loading(down_weight),
        name="load",
    )(*in_hbm(down_weight), sent_part)
    if exchanged:
        other_part = lax.ppermute(sent_part, "head", xor_pairs(2, 1))
        mlp_out = (shape((own_rows, columns), f32), shape((own_rows, columns), bf16))
    else:
        own_part = jnp.zeros_like(own_part)
        other_part = lax.psum(sent_part, "head")
        mlp_out = (shape((own_rows, model), f32), shape((own_rows, model), bf16))

    kept, leaving = pl.pallas_call(
        functools.partial(mlp_kernel, exchanged),
        out_shape=mlp_out,
        in_specs=[VMEM_SPEC] * 6,
        out_specs=(VMEM_SPEC,) * 2,
        compiler_params=PARAMS,
        name="mlp",
    )(hidden_in, own_part, other_part, mlp_gain.reshape(1, model), up_weight, down_near)

    if exchanged:
        arrived = lax.ppermute(leaving, "head", xor_pairs(2, 1))
    else:
        kept = lax.dynamic_slice_in_dim(kept, lax.axis_index("head") * columns, columns, 1)
        arrived = lax.psum_scatter(leaving, "head", scatter_dimension=1, tiled=True)
    return kept + arrived.astype(f32)


def solution(mesh):
    in_specs = (
        P("blk", None),
        P(),
        P(),
        P(None, None, "head"),
        P("head", None),
        P(None, "head"),
        P("head", None),
        P(None, "head"),
        P(),
        P("blk", None, "head"),
        P("blk", None, "head"),
        P(),
        P("blk"),
        P("blk"),
    )
    out_specs = P("blk", "head")
    return jax.shard_map(
        per_device, mesh=mesh, in_specs=in_specs, out_specs=out_specs, check_vma=False
    )
```

```python
import functools

import jax
import jax.numpy as jnp
from jax import lax
from jax.experimental import pallas as pl
from jax.experimental.pallas import tpu as pltpu
from jax.sharding import PartitionSpec as P

HEAD_DIM = 64
PAGE = 128
LANES = 128

far_below = -1e30
epsilon = 1e-06

VMEM_SPEC = pl.BlockSpec(memory_space=pltpu.VMEM)
SMEM_SPEC = pl.BlockSpec(memory_space=pltpu.SMEM)
ANY_SPEC = pl.BlockSpec(memory_space=pl.ANY)
HBM_SPEC = pl.BlockSpec(memory_space=pltpu.HBM)
PARAMS = pltpu.CompilerParams(vmem_limit_bytes=16 * 1024 * 1024)

PIECE = 8
SUM_LANE = 3 * PIECE


def iota(shape, axis):
    return lax.broadcasted_iota(jnp.int32, shape, axis)


def split_index(x, size):
    if size & (size - 1):
        return lax.div(x, size), lax.rem(x, size)
    return x >> (size.bit_length() - 1), x & (size - 1)


def head_of(shape, axis):
    return split_index(iota(shape, axis), HEAD_DIM)[0]


def pieces(x, count):
    parts = []
    for _ in range(count):
        part = x.astype(jnp.bfloat16)
        parts.append(part)
        x = x - part.astype(jnp.float32)
    return parts


def rms_normed(x, gain):
    scale = lax.rsqrt(jnp.mean(x * x, axis=1, keepdims=True) + epsilon)
    return (x * scale * gain).astype(jnp.bfloat16)


def dot(a, b, dims=((1,), (0,)), precision=None):
    return lax.dot_general(
        a, b, (dims, ((), ())), preferred_element_type=jnp.float32, precision=precision
    )


def split_copies(source, target, sems, count):
    size = source.shape[0] // count
    return [
        pltpu.make_async_copy(
            source.at[pl.ds(i * size, size)], target.at[pl.ds(i * size, size)], sems.at[i]
        )
        for i in range(count)
    ]


def query_kernel(hidden_hbm, gain_hbm, weight_hbm, query_ref, hidden, gain, weight, sems):
    model = hidden.shape[1]
    small = [
        pltpu.make_async_copy(hidden_hbm, hidden, sems.at[0]),
        pltpu.make_async_copy(gain_hbm, gain, sems.at[1]),
    ]
    half = model // 4
    large = [
        pltpu.make_async_copy(
            weight_hbm.at[0, pl.ds(i * half, half)], weight.at[pl.ds(i * half, half)], sems.at[2 + i]
        )
        for i in range(4)
    ]
    for copy in small + large:
        copy.start()
    for copy in small:
        copy.wait()
    normed = rms_normed(hidden[...], gain[...])
    query = None
    for i, copy in enumerate(large):
        copy.wait()
        span = slice(i * half, (i + 1) * half)
        part = dot(normed[:, span], weight[span])
        query = part if query is None else query + part
    query_ref[...] = query.astype(jnp.bfloat16)


def page_kernel(
    own_rows, inner, outer, query_ref, request_ref, keys_hbm,
    keys_ref, pick_ref, place_ref, first_ref, apart_ref,
    sems,
):
    copies = split_copies(
        keys_hbm.at[pl.ds(0, keys_ref.shape[0])], keys_ref, sems, sems.shape[0]
    )
    for copy in copies:
        copy.start()
    me = lax.axis_index("blk")
    page_count = apart_ref.shape[0]
    all_rows, depth = place_ref.shape
    page, lane = iota((page_count, page_count), 0), iota((page_count, page_count), 1)
    by_lane = request_ref[...]
    owner = jnp.max(jnp.where(page == lane, by_lane, -1), axis=1, keepdims=True)
    same = by_lane == owner
    apart_ref[...] = jnp.full(apart_ref.shape, 2 * far_below, jnp.float32)
    apart_ref[:, :page_count] = jnp.where(same, 0.0, 2 * far_below)
    earlier = jnp.max(jnp.where(same & (lane < page), 1, 0), axis=1, keepdims=True)
    device, own_row = split_index(jnp.maximum(owner, 0), own_rows)
    high, low = split_index(device ^ me, inner)
    slot = (low * outer + high) * own_rows + own_row
    slot = jnp.where(owner >= 0, slot, -1)
    row_of = iota((page_count, all_rows), 1)
    picks = jnp.where(row_of == slot, 1.0, 0.0)
    picks = [jnp.broadcast_to(picks[p : p + 1], (PIECE, all_rows)) for p in range(page_count)]
    pick_ref[...] = jnp.concatenate(picks, axis=0).astype(jnp.bfloat16)
    mine = split_index(iota((page_count, depth), 1), PIECE)[0] == iota((page_count, depth), 0)
    row = iota((all_rows, depth), 0)
    spread = jnp.max(jnp.where(mine, slot, -1), axis=0, keepdims=True)
    place_ref[...] = (row == spread).astype(jnp.bfloat16)
    leads = jnp.where(earlier == 0, slot, -1)
    spread = jnp.max(jnp.where(mine, leads, -1), axis=0, keepdims=True)
    first_ref[...] = (row == spread).astype(jnp.bfloat16)
    for copy in copies:
        copy.wait()


def bias_kernel(
    table_hbm, edges_hbm, lengths_hbm, index_hbm, request_ref, keys_hbm, after_ref,
    keys_ref, bias_ref,
    table, edges_ref, lengths_ref, index_ref, small_sems, sems,
):
    sources = (table_hbm, edges_hbm, lengths_hbm, index_hbm)
    targets = (table, edges_ref, lengths_ref, index_ref)
    small = [
        pltpu.make_async_copy(source, target, small_sems.at[i])
        for i, (source, target) in enumerate(zip(sources, targets))
    ]
    late = keys_ref.shape[0]
    copies = split_copies(
        keys_hbm.at[pl.ds(keys_hbm.shape[0] - late, late)], keys_ref, sems, sems.shape[0]
    )
    for copy in small + copies:
        copy.start()
    for copy in small:
        copy.wait()
    heads, buckets = table.shape
    by_head = table[...]
    if heads < PIECE:
        by_head = jnp.concatenate([by_head[min(h, heads - 1)][None] for h in range(PIECE)], axis=0)
    columns = [jnp.broadcast_to(by_head[:, k : k + 1], (PIECE, PAGE)) for k in range(buckets)]
    token = iota((PIECE, PAGE), 1)
    for p in range(request_ref.shape[0]):
        owner = request_ref[p]
        left = lengths_ref[jnp.maximum(owner, 0)] - index_ref[p] * PAGE
        distance = jnp.where(owner >= 0, left, 0) - token
        bias = columns[0]
        for k in range(buckets - 1):
            bias = jnp.where(distance >= edges_ref[k], columns[k + 1], bias)
        bias_ref[p] = jnp.where(distance > 0, bias, far_below)
    for copy in copies:
        copy.wait()


def side_kernel(
    hidden_ref, gain_ref, query_ref, table_ref, weight_hbm, out_hbm, after_ref,
    score_ref, value_ref, out_ref,
    weight, weight_sems, sems,
):
    copies = [
        pltpu.make_async_copy(weight_hbm.at[1 + i], weight.at[i], weight_sems.at[i])
        for i in range(2)
    ]
    later = split_copies(out_hbm, out_ref, sems, sems.shape[0])
    for copy in copies + later:
        copy.start()
    normed = rms_normed(hidden_ref[...], gain_ref[...])
    heads = table_ref.shape[0]
    spread = iota((heads, LANES), 0) == iota((heads, LANES), 1)
    score = jnp.sum(jnp.where(spread, table_ref[:, 0:1], 0.0), axis=0, keepdims=True)
    copies[0].wait()
    key = dot(normed, weight[0]).astype(jnp.bfloat16)
    product = query_ref[...].astype(jnp.float32) * key.astype(jnp.float32)
    width = product.shape[1]
    gather = (head_of((width, LANES), 0) == iota((width, LANES), 1)).astype(jnp.bfloat16)
    for part in pieces(product, 3):
        score = score + dot(part, gather)
    score_ref[...] = score
    copies[1].wait()
    value_ref[...] = dot(normed, weight[1]).astype(jnp.bfloat16)
    for copy in later:
        copy.wait()


def load_kernel(start, source, after_ref, target, sems):
    rows = source.at[pl.ds(start, target.shape[0])]
    copies = split_copies(rows, target, sems, sems.shape[0])
    for copy in copies:
        copy.start()
    for copy in copies:
        copy.wait()


def packed_stats(peaks, sums):
    one, two, three = (part.astype(jnp.float32) for part in pieces(peaks + sums, 3))
    packed = one + pltpu.roll(two, PIECE, 1) + pltpu.roll(three, 2 * PIECE, 1)
    return packed.astype(jnp.bfloat16)


def unpacked_stats(packed, heads):
    stats = packed.astype(jnp.float32)
    stats = stats + pltpu.roll(stats, LANES - PIECE, 1) + pltpu.roll(stats, LANES - 2 * PIECE, 1)
    sums = pltpu.roll(stats, LANES - SUM_LANE, 1)
    used = iota(stats.shape, 1) < heads
    return jnp.where(used & (sums > 0.0), stats, far_below), jnp.where(used, sums, 0.0)


def over_columns(values, width):
    spread = (iota((LANES, width), 0) == head_of((LANES, width), 1)).astype(jnp.bfloat16)
    return sum(dot(part, spread) for part in pieces(values, 3))


def attend_kernel(groups, *refs):
    query_refs, refs, sums_refs = refs[:groups], refs[groups:-groups], refs[-groups:]
    bias_ref, pick_ref, place_ref, first_ref, apart_ref, keys_ref, late_ref, values_ref = refs
    page_count = apart_ref.shape[0]
    width = keys_ref.shape[2]
    early = keys_ref.shape[0]
    chunk = 2
    chunks = page_count // chunk
    queries = jnp.concatenate([ref[...] for ref in query_refs], axis=0)
    own_head = (head_of((PIECE, width), 1) == iota((PIECE, width), 0)).astype(jnp.float32)
    pair_heads = jnp.concatenate([own_head] * chunk, axis=0)
    chosen = dot(pick_ref[...], queries)
    lane = iota((PIECE, LANES), 1)
    row = iota((PIECE, LANES), 0)
    scores = []
    tops = jnp.zeros((PIECE, LANES), jnp.float32)
    for c in range(chunks):
        rows = chosen[c * chunk * PIECE : (c + 1) * chunk * PIECE]
        split = (rows * pair_heads).astype(jnp.bfloat16)
        at = c * chunk
        block = keys_ref[at : at + chunk] if at < early else late_ref[at - early : at - early + chunk]
        block = block.reshape(chunk * PAGE, width)
        raw = dot(split, block, ((1,), (1,)))
        for i in range(chunk):
            p = c * chunk + i
            part = raw[i * PIECE : (i + 1) * PIECE, i * PAGE : (i + 1) * PAGE]
            score = part + bias_ref[p]
            scores.append(score)
            tops = jnp.where(lane == p, jnp.max(score, axis=1, keepdims=True), tops)
    mixes, peaks, totals = [], [], []
    nothing = jnp.zeros((PIECE, PAGE), jnp.float32)
    for c in range(chunks):
        blocks = []
        for i in range(chunk):
            p = c * chunk + i
            peak = jnp.max(tops + apart_ref[p : p + 1], axis=1, keepdims=True)
            weight = jnp.exp(scores[p] - peak)
            total = jnp.sum(weight, axis=1, keepdims=True)
            peaks.append(jnp.where(lane == row, peak, 0.0))
            totals.append(jnp.where(lane == row + SUM_LANE, total, 0.0))
            blocks.append(
                jnp.concatenate([weight if k == i else nothing for k in range(chunk)], axis=1)
            )
        weights = jnp.concatenate(blocks, axis=0).astype(jnp.bfloat16)
        block = values_ref[c * chunk : (c + 1) * chunk].reshape(chunk * PAGE, width)
        mixes.append(dot(weights, block) * pair_heads)
    mix = jnp.concatenate(mixes, axis=0)
    place, first = place_ref[...], first_ref[...]
    high, low = pieces(mix, 2)
    sums = dot(place, high) + dot(place, low)
    collected = sum(dot(first, part) for part in pieces(jnp.concatenate(peaks, axis=0), 3))
    collected += sum(dot(place, part) for part in pieces(jnp.concatenate(totals, axis=0), 3))
    stats = packed_stats(collected, 0.0)
    size = sums_refs[0].shape[0]
    for i, sums_ref in enumerate(sums_refs):
        span = slice(i * size, (i + 1) * size)
        sums_ref[:, :width] = sums[span].astype(jnp.bfloat16)
        sums_ref[:, width:] = stats[span]


def combine_kernel(sources, *refs):
    part_refs, sums_refs = refs[:sources], refs[sources:]
    rows, columns = part_refs[0].shape
    width = columns - LANES
    stats = [unpacked_stats(ref[:, width:], width // HEAD_DIM) for ref in part_refs]
    peak = stats[0][0]
    for peaks, _ in stats[1:]:
        peak = jnp.maximum(peak, peaks)
    factors = [jnp.exp(peaks - peak) for peaks, _ in stats]
    total = sum(factor * sums for factor, (_, sums) in zip(factors, stats))
    shares = over_columns(jnp.concatenate(factors, axis=0), width)
    mixed = sum(
        ref[:, :width].astype(jnp.float32) * shares[i * rows : (i + 1) * rows]
        for i, ref in enumerate(part_refs)
    )
    packed = packed_stats(
        jnp.where(total > 0.0, peak, 0.0), pltpu.roll(total, SUM_LANE, 1)
    ).astype(jnp.float32)
    size = sums_refs[0].shape[0]
    for i, sums_ref in enumerate(sums_refs):
        span = slice(i * size, (i + 1) * size)
        sums_ref[:, :width] = mixed[span].astype(jnp.bfloat16)
        sums_ref[:, width:] = packed[span].astype(jnp.bfloat16)


def merge_kernel(sources, *refs):
    part_refs, (score_ref, value_ref, weight_ref, own_ref, send_ref) = refs[:sources], refs[sources:]
    own_rows, width = value_ref.shape
    heads = width // HEAD_DIM
    stats = [unpacked_stats(ref[:, width:], heads) for ref in part_refs]
    own_score = jnp.where(iota(score_ref.shape, 1) < heads, score_ref[...], 0.0)
    peak = own_score
    for peaks, _ in stats:
        peak = jnp.maximum(peak, peaks)
    own_weight = jnp.exp(own_score - peak)
    total = own_weight
    factors = []
    for peaks, sums in stats:
        factor = jnp.exp(peaks - peak)
        total = total + factor * sums
        factors.append(factor)
    factors.append(own_weight.astype(jnp.bfloat16).astype(jnp.float32))
    shares = jnp.concatenate([factor / total for factor in factors], axis=0)
    shares = over_columns(shares, width)
    mixed = value_ref[...].astype(jnp.float32) * shares[sources * own_rows :]
    for i, ref in enumerate(part_refs):
        rows = slice(i * own_rows, (i + 1) * own_rows)
        mixed = mixed + ref[:, :width].astype(jnp.float32) * shares[rows]
    projected = dot(mixed.astype(jnp.bfloat16), weight_ref[...])
    own_ref[...] = projected
    send_ref[...] = projected.astype(jnp.bfloat16)


def mlp_kernel(
    exchanged, hidden_ref, own_ref, other_ref, gain_ref, up_ref, down_ref, late_ref, *outs
):
    middle = hidden_ref[...] + (own_ref[...] + other_ref[...].astype(jnp.float32))
    normed = rms_normed(middle, gain_ref[...])
    active = jnp.maximum(dot(normed, up_ref[...]), 0.0).astype(jnp.bfloat16)
    half = down_ref.shape[0]
    down = dot(active[:, :half], down_ref[...]) + dot(active[:, half:], late_ref[...])
    if exchanged:
        kept_ref, sent_ref = outs
        columns = kept_ref.shape[1]
        low = lax.axis_index("head") == 0
        left, right = slice(0, columns), slice(columns, 2 * columns)
        kept = middle + down

        @pl.when(low)
        def _():
            kept_ref[...] = kept[:, left]
            sent_ref[...] = down[:, right].astype(jnp.bfloat16)

        @pl.when(jnp.logical_not(low))
        def _():
            kept_ref[...] = kept[:, right]
            sent_ref[...] = down[:, left].astype(jnp.bfloat16)

    else:
        middle_ref, down_out_ref = outs
        middle_ref[...] = middle
        down_out_ref[...] = down.astype(jnp.bfloat16)


def loading(*arrays):
    return pl.CostEstimate(
        flops=0, bytes_accessed=sum(2 * array.size for array in arrays), transcendentals=0
    )


def in_hbm(*arrays):
    return [pltpu.with_memory_space_constraint(array, pltpu.HBM) for array in arrays]


def xor_pairs(size, step):
    return [(i, i ^ step) for i in range(size)]


def per_device(
    hidden_in, attention_gain, mlp_gain, qkv_weight, out_weight, up_weight, down_weight,
    position_bias, bucket_edges, cache_keys, cache_values, lengths, page_request, page_index,
):
    f32, bf16 = jnp.float32, jnp.bfloat16
    shape = jax.ShapeDtypeStruct
    own_rows, model = hidden_in.shape
    width = qkv_weight.shape[2]
    page_count = page_request.shape[0]
    blocks = lax.axis_size("blk")
    all_rows = own_rows * blocks
    gain = attention_gain.reshape(1, model)
    query = pl.pallas_call(
        query_kernel,
        out_shape=shape((own_rows, width), bf16),
        in_specs=[HBM_SPEC] * 3,
        out_specs=VMEM_SPEC,
        scratch_shapes=[
            pltpu.VMEM((own_rows, model), f32),
            pltpu.VMEM((1, model), f32),
            pltpu.VMEM((model, width), bf16),
            pltpu.SemaphoreType.DMA((6,)),
        ],
        compiler_params=PARAMS,
        name="query",
    )(*in_hbm(hidden_in, gain, qkv_weight))

    inner = 1
    while inner * inner < blocks:
        inner *= 2
    far = [query] + [
        lax.ppermute(query, "blk", xor_pairs(blocks, step * inner))
        for step in range(1, blocks // inner)
    ]
    depth = page_count * PIECE
    early = page_count // 6 * 2
    keys, picks, place, first, apart = pl.pallas_call(
        functools.partial(page_kernel, own_rows, inner, blocks // inner),
        out_shape=(
            pltpu.VMEM((early,) + cache_keys.shape[1:], bf16),
            shape((depth, all_rows), bf16),
            shape((all_rows, depth), bf16),
            shape((all_rows, depth), bf16),
            shape((page_count, LANES), f32),
        ),
        in_specs=[ANY_SPEC, VMEM_SPEC, HBM_SPEC],
        out_specs=(VMEM_SPEC,) * 5,
        scratch_shapes=[pltpu.SemaphoreType.DMA((4,))],
        compiler_params=PARAMS,
        cost_estimate=loading(cache_keys),
        name="pages",
    )(query, page_request.reshape(1, page_count), *in_hbm(cache_keys))
    near, apart = lax.optimization_barrier((jnp.concatenate(far, axis=0), apart))
    gathered = [near] + [
        lax.ppermute(near, "blk", xor_pairs(blocks, step)) for step in range(1, inner)
    ]
    table = position_bias.T
    late_keys, bias = pl.pallas_call(
        bias_kernel,
        out_shape=(
            pltpu.VMEM((page_count - early,) + cache_keys.shape[1:], bf16),
            shape((page_count, PIECE, PAGE), f32),
        ),
        in_specs=[HBM_SPEC] * 4 + [SMEM_SPEC, HBM_SPEC, ANY_SPEC],
        out_specs=(VMEM_SPEC,) * 2,
        scratch_shapes=[
            pltpu.VMEM(table.shape, f32),
            pltpu.SMEM(bucket_edges.shape, jnp.int32),
            pltpu.SMEM(lengths.shape, jnp.int32),
            pltpu.SMEM(page_index.shape, jnp.int32),
            pltpu.SemaphoreType.DMA((4,)),
            pltpu.SemaphoreType.DMA((4,)),
        ],
        compiler_params=PARAMS,
        cost_estimate=loading(cache_values),
        name="bias",
    )(
        *in_hbm(table, bucket_edges, lengths, page_index), page_request,
        *in_hbm(cache_keys), near,
    )

    groups = len(gathered)
    sums = pl.pallas_call(
        functools.partial(attend_kernel, groups),
        out_shape=(shape((all_rows // groups, width + LANES), bf16),) * groups,
        in_specs=[VMEM_SPEC] * (groups + 8),
        out_specs=(VMEM_SPEC,) * groups,
        compiler_params=PARAMS,
        name="attend",
    )(*gathered, bias, picks, place, first, apart, keys, late_keys, cache_values)
    near_sums = [sums[0]] + [
        lax.ppermute(sums[step], "blk", xor_pairs(blocks, step))
        for step in reversed(range(1, inner))
    ]

    own_score, value_new, out_near = pl.pallas_call(
        side_kernel,
        out_shape=(
            shape((own_rows, LANES), f32),
            shape((own_rows, width), bf16),
            pltpu.VMEM(out_weight.shape, bf16),
        ),
        in_specs=[VMEM_SPEC] * 4 + [HBM_SPEC] * 2 + [ANY_SPEC],
        out_specs=(VMEM_SPEC,) * 3,
        scratch_shapes=[
            pltpu.VMEM((2, model, width), bf16),
            pltpu.SemaphoreType.DMA((2,)),
            pltpu.SemaphoreType.DMA((4,)),
        ],
        compiler_params=PARAMS,
        cost_estimate=loading(out_weight, out_weight, out_weight),
        name="side",
    )(
        hidden_in, gain, query, table,
        *in_hbm(qkv_weight, out_weight), sums[0],
    )

    *near_sums, own_score = lax.optimization_barrier((*near_sums, own_score))
    outer = blocks // inner
    sums = pl.pallas_call(
        functools.partial(combine_kernel, inner),
        out_shape=(shape((own_rows, width + LANES), bf16),) * outer,
        in_specs=[VMEM_SPEC] * inner,
        out_specs=(VMEM_SPEC,) * outer,
        compiler_params=PARAMS,
        name="combine",
    )(*near_sums)
    half = down_weight.shape[0] // 2

    def load_down(start, after):
        return pl.pallas_call(
            functools.partial(load_kernel, start),
            out_shape=pltpu.VMEM((half, model), bf16),
            in_specs=[HBM_SPEC, ANY_SPEC],
            out_specs=VMEM_SPEC,
            scratch_shapes=[pltpu.SemaphoreType.DMA((4,))],
            compiler_params=PARAMS,
            cost_estimate=loading(down_weight),
            name="load",
        )(*in_hbm(down_weight), after)

    down_early = load_down(0, sums[0])
    parts = [sums[0]] + [
        lax.ppermute(sums[step], "blk", xor_pairs(blocks, step * inner))
        for step in reversed(range(1, outer))
    ]

    *parts, down_early = lax.optimization_barrier((*parts, down_early))
    own_part, sent_part = pl.pallas_call(
        functools.partial(merge_kernel, outer),
        out_shape=(shape((own_rows, model), f32), shape((own_rows, model), bf16)),
        in_specs=[VMEM_SPEC] * (outer + 3),
        out_specs=(VMEM_SPEC,) * 2,
        compiler_params=PARAMS,
        name="merge",
    )(*parts, own_score, value_new, out_near)

    halves = lax.axis_size("head")
    columns = model // halves
    exchanged = halves == 2
    down_late = load_down(half, sent_part)
    if exchanged:
        other_part = lax.ppermute(sent_part, "head", xor_pairs(2, 1))
        mlp_out = (shape((own_rows, columns), f32), shape((own_rows, columns), bf16))
    else:
        own_part = jnp.zeros_like(own_part)
        other_part = lax.psum(sent_part, "head")
        mlp_out = (shape((own_rows, model), f32), shape((own_rows, model), bf16))

    kept, leaving = pl.pallas_call(
        functools.partial(mlp_kernel, exchanged),
        out_shape=mlp_out,
        in_specs=[VMEM_SPEC] * 7,
        out_specs=(VMEM_SPEC,) * 2,
        compiler_params=PARAMS,
        name="mlp",
    )(hidden_in, own_part, other_part, mlp_gain.reshape(1, model), up_weight, down_early, down_late)

    if exchanged:
        arrived = lax.ppermute(leaving, "head", xor_pairs(2, 1))
    else:
        kept = lax.dynamic_slice_in_dim(kept, lax.axis_index("head") * columns, columns, 1)
        arrived = lax.psum_scatter(leaving, "head", scatter_dimension=1, tiled=True)
    return kept + arrived.astype(f32)


def solution(mesh):
    in_specs = (
        P("blk", None),
        P(),
        P(),
        P(None, None, "head"),
        P("head", None),
        P(None, "head"),
        P("head", None),
        P(None, "head"),
        P(),
        P("blk", None, "head"),
        P("blk", None, "head"),
        P(),
        P("blk"),
        P("blk"),
    )
    out_specs = P("blk", "head")
    return jax.shard_map(
        per_device, mesh=mesh, in_specs=in_specs, out_specs=out_specs, check_vma=False
    )
```

```python
import functools

import jax
import jax.numpy as jnp
from jax import lax
from jax.experimental import pallas as pl
from jax.experimental.pallas import tpu as pltpu
from jax.sharding import PartitionSpec as P

HEAD_DIM = 64
PAGE = 128
LANES = 128

far_below = -1e30
epsilon = 1e-06

VMEM_SPEC = pl.BlockSpec(memory_space=pltpu.VMEM)
SMEM_SPEC = pl.BlockSpec(memory_space=pltpu.SMEM)
ANY_SPEC = pl.BlockSpec(memory_space=pl.ANY)
HBM_SPEC = pl.BlockSpec(memory_space=pltpu.HBM)
PARAMS = pltpu.CompilerParams(vmem_limit_bytes=16 * 1024 * 1024)

PIECE = 8
SUM_LANE = 3 * PIECE


def iota(shape, axis):
    return lax.broadcasted_iota(jnp.int32, shape, axis)


def split_index(x, size):
    if size & (size - 1):
        return lax.div(x, size), lax.rem(x, size)
    return x >> (size.bit_length() - 1), x & (size - 1)


def head_of(shape, axis):
    return split_index(iota(shape, axis), HEAD_DIM)[0]


def pieces(x, count):
    parts = []
    for _ in range(count):
        part = x.astype(jnp.bfloat16)
        parts.append(part)
        x = x - part.astype(jnp.float32)
    return parts


def rms_normed(x, gain):
    scale = lax.rsqrt(jnp.mean(x * x, axis=1, keepdims=True) + epsilon)
    return (x * scale * gain).astype(jnp.bfloat16)


def dot(a, b, dims=((1,), (0,)), precision=None):
    return lax.dot_general(
        a, b, (dims, ((), ())), preferred_element_type=jnp.float32, precision=precision
    )


def split_copies(source, target, sems, count):
    size = source.shape[0] // count
    return [
        pltpu.make_async_copy(
            source.at[pl.ds(i * size, size)], target.at[pl.ds(i * size, size)], sems.at[i]
        )
        for i in range(count)
    ]


def query_kernel(hidden_hbm, gain_hbm, weight_hbm, query_ref, hidden, gain, weight, sems):
    model = hidden.shape[1]
    small = [
        pltpu.make_async_copy(hidden_hbm, hidden, sems.at[0]),
        pltpu.make_async_copy(gain_hbm, gain, sems.at[1]),
    ]
    half = model // 4
    large = [
        pltpu.make_async_copy(
            weight_hbm.at[0, pl.ds(i * half, half)], weight.at[pl.ds(i * half, half)], sems.at[2 + i]
        )
        for i in range(4)
    ]
    for copy in small + large:
        copy.start()
    for copy in small:
        copy.wait()
    normed = rms_normed(hidden[...], gain[...])
    query = None
    for i, copy in enumerate(large):
        copy.wait()
        span = slice(i * half, (i + 1) * half)
        part = dot(normed[:, span], weight[span])
        query = part if query is None else query + part
    query_ref[...] = query.astype(jnp.bfloat16)


def page_kernel(
    own_rows, inner, outer, query_ref, request_ref, keys_hbm,
    keys_ref, pick_ref, place_ref, lead_ref, apart_ref, owners_ref,
    sems,
):
    copies = split_copies(
        keys_hbm.at[pl.ds(0, keys_ref.shape[0])], keys_ref, sems, sems.shape[0]
    )
    for copy in copies:
        copy.start()
    me = lax.axis_index("blk")
    page_count = apart_ref.shape[0]
    all_rows, depth = place_ref.shape
    page, lane = iota((page_count, page_count), 0), iota((page_count, page_count), 1)
    by_lane = request_ref[...]
    owner = jnp.max(jnp.where(page == lane, by_lane, -1), axis=1, keepdims=True)
    same = by_lane == owner
    apart_ref[...] = jnp.full(apart_ref.shape, 2 * far_below, jnp.float32)
    apart_ref[:, :page_count] = jnp.where(same, 0.0, 2 * far_below)
    earlier = jnp.max(jnp.where(same & (lane < page), 1, 0), axis=1, keepdims=True)
    lead_ref[...] = jnp.broadcast_to(jnp.where(earlier == 0, 1.0, 0.0), lead_ref.shape)
    owners_ref[...] = jnp.broadcast_to(owner, owners_ref.shape)
    device, own_row = split_index(jnp.maximum(owner, 0), own_rows)
    high, low = split_index(device ^ me, inner)
    slot = (low * outer + high) * own_rows + own_row
    slot = jnp.where(owner >= 0, slot, -1)
    row_of = iota((page_count, all_rows), 1)
    picks = jnp.where(row_of == slot, 1.0, 0.0)
    picks = [jnp.broadcast_to(picks[p : p + 1], (PIECE, all_rows)) for p in range(page_count)]
    pick_ref[...] = jnp.concatenate(picks, axis=0).astype(jnp.bfloat16)
    mine = split_index(iota((page_count, depth), 1), PIECE)[0] == iota((page_count, depth), 0)
    row = iota((all_rows, depth), 0)
    spread = jnp.max(jnp.where(mine, slot, -1), axis=0, keepdims=True)
    place_ref[...] = (row == spread).astype(jnp.bfloat16)
    for copy in copies:
        copy.wait()


def bias_kernel(
    table_hbm, edges_hbm, lengths_hbm, index_hbm, owners_ref, keys_hbm, after_ref,
    keys_ref, bias_ref,
    table, edges, lengths, index, small_sems, sems,
):
    sources, targets = (table_hbm, edges_hbm, lengths_hbm, index_hbm), (table, edges, lengths, index)
    small = [
        pltpu.make_async_copy(source, target, small_sems.at[i])
        for i, (source, target) in enumerate(zip(sources, targets))
    ]
    late = keys_ref.shape[0]
    copies = split_copies(
        keys_hbm.at[pl.ds(keys_hbm.shape[0] - late, late)], keys_ref, sems, sems.shape[0]
    )
    for copy in small + copies:
        copy.start()
    for copy in small:
        copy.wait()
    heads, buckets = table.shape
    page_count = index.shape[1]
    owner = owners_ref[:, 0:1]
    square = (page_count, page_count)
    number = jnp.where(iota(square, 0) == iota(square, 1), index[...], 0)
    number = jnp.sum(number, axis=1, keepdims=True)
    requests = lengths.shape[1]
    length = jnp.where(iota((page_count, requests), 1) == owner, lengths[...], 0)
    length = jnp.sum(length, axis=1, keepdims=True)
    distance = length - number * PAGE - iota((page_count, PAGE), 1)
    far = [distance >= edges[k] for k in range(buckets - 1)]
    usable = (owner >= 0) & (distance > 0)
    bias_ref[...] = jnp.full(bias_ref.shape, far_below, jnp.float32)
    for h in range(heads):
        bias = jnp.full((page_count, PAGE), table[h, 0], jnp.float32)
        for k in range(buckets - 1):
            bias = jnp.where(far[k], table[h, k + 1], bias)
        bias_ref[pl.ds(h, page_count, stride=PIECE), :] = jnp.where(usable, bias, far_below)
    for copy in copies:
        copy.wait()


def side_kernel(
    hidden_ref, gain_ref, query_ref, table_ref, weight_hbm, out_hbm, after_ref,
    score_ref, value_ref, out_ref,
    weight, weight_sems, sems,
):
    copies = [
        pltpu.make_async_copy(weight_hbm.at[1 + i], weight.at[i], weight_sems.at[i])
        for i in range(2)
    ]
    later = split_copies(out_hbm, out_ref, sems, sems.shape[0])
    for copy in copies + later:
        copy.start()
    normed = rms_normed(hidden_ref[...], gain_ref[...])
    heads = table_ref.shape[0]
    spread = iota((heads, LANES), 0) == iota((heads, LANES), 1)
    score = jnp.sum(jnp.where(spread, table_ref[:, 0:1], 0.0), axis=0, keepdims=True)
    copies[0].wait()
    key = dot(normed, weight[0]).astype(jnp.bfloat16)
    product = query_ref[...].astype(jnp.float32) * key.astype(jnp.float32)
    width = product.shape[1]
    gather = (head_of((width, LANES), 0) == iota((width, LANES), 1)).astype(jnp.bfloat16)
    for part in pieces(product, 3):
        score = score + dot(part, gather)
    score_ref[...] = score
    copies[1].wait()
    value_ref[...] = dot(normed, weight[1]).astype(jnp.bfloat16)
    for copy in later:
        copy.wait()


def load_kernel(start, source, after_ref, target, sems):
    rows = source.at[pl.ds(start, target.shape[0])]
    copies = split_copies(rows, target, sems, sems.shape[0])
    for copy in copies:
        copy.start()
    for copy in copies:
        copy.wait()


def packed_stats(peaks, sums):
    one, two, three = (part.astype(jnp.float32) for part in pieces(peaks + sums, 3))
    packed = one + pltpu.roll(two, PIECE, 1) + pltpu.roll(three, 2 * PIECE, 1)
    return packed.astype(jnp.bfloat16)


def unpacked_stats(packed, heads):
    stats = packed.astype(jnp.float32)
    stats = stats + pltpu.roll(stats, LANES - PIECE, 1) + pltpu.roll(stats, LANES - 2 * PIECE, 1)
    sums = pltpu.roll(stats, LANES - SUM_LANE, 1)
    used = iota(stats.shape, 1) < heads
    return jnp.where(used & (sums > 0.0), stats, far_below), jnp.where(used, sums, 0.0)


def over_columns(values, width):
    spread = (iota((LANES, width), 0) == head_of((LANES, width), 1)).astype(jnp.bfloat16)
    return sum(dot(part, spread) for part in pieces(values, 3))


def attend_kernel(groups, *refs):
    query_refs, refs, sums_refs = refs[:groups], refs[groups:-groups], refs[-groups:]
    bias_ref, pick_ref, place_ref, lead_ref, apart_ref, keys_ref, late_ref, values_ref = refs
    page_count = apart_ref.shape[0]
    width = keys_ref.shape[2]
    early = keys_ref.shape[0]
    chunk = 2
    chunks = page_count // chunk
    queries = jnp.concatenate([ref[...] for ref in query_refs], axis=0)
    own_head = (head_of((PIECE, width), 1) == iota((PIECE, width), 0)).astype(jnp.float32)
    pair_heads = jnp.concatenate([own_head] * chunk, axis=0)
    chosen = dot(pick_ref[...], queries)
    lane = iota((PIECE, LANES), 1)
    row = iota((PIECE, LANES), 0)
    scores = []
    tops = jnp.zeros((PIECE, LANES), jnp.float32)
    for c in range(chunks):
        rows = chosen[c * chunk * PIECE : (c + 1) * chunk * PIECE]
        split = (rows * pair_heads).astype(jnp.bfloat16)
        at = c * chunk
        block = keys_ref[at : at + chunk] if at < early else late_ref[at - early : at - early + chunk]
        block = block.reshape(chunk * PAGE, width)
        raw = dot(split, block, ((1,), (1,)))
        for i in range(chunk):
            p = c * chunk + i
            part = raw[i * PIECE : (i + 1) * PIECE, i * PAGE : (i + 1) * PAGE]
            score = part + bias_ref[p * PIECE : (p + 1) * PIECE]
            scores.append(score)
            tops = jnp.where(lane == p, jnp.max(score, axis=1, keepdims=True), tops)
    mixes, stats = [], []
    nothing = jnp.zeros((PIECE, PAGE), jnp.float32)
    for c in range(chunks):
        blocks = []
        for i in range(chunk):
            p = c * chunk + i
            peak = jnp.max(tops + apart_ref[p : p + 1], axis=1, keepdims=True)
            weight = jnp.exp(scores[p] - peak)
            total = jnp.sum(weight, axis=1, keepdims=True)
            kept = peak * lead_ref[p : p + 1]
            total = jnp.where(lane == row + SUM_LANE, total, 0.0)
            stats.append(jnp.where(lane == row, kept, total))
            blocks.append(
                jnp.concatenate([weight if k == i else nothing for k in range(chunk)], axis=1)
            )
        weights = jnp.concatenate(blocks, axis=0).astype(jnp.bfloat16)
        block = values_ref[c * chunk : (c + 1) * chunk].reshape(chunk * PAGE, width)
        mixes.append(dot(weights, block) * pair_heads)
    mix = jnp.concatenate(mixes, axis=0).astype(jnp.bfloat16)
    stats = pieces(jnp.concatenate(stats, axis=0), 3)
    sums = dot(place_ref[...], jnp.concatenate([mix] + stats, axis=1))
    stats = sum(sums[:, width + i * LANES : width + (i + 1) * LANES] for i in range(3))
    stats = packed_stats(stats, 0.0)
    size = sums_refs[0].shape[0]
    for i, sums_ref in enumerate(sums_refs):
        span = slice(i * size, (i + 1) * size)
        sums_ref[:, :width] = sums[span, :width].astype(jnp.bfloat16)
        sums_ref[:, width:] = stats[span]


def combine_kernel(sources, *refs):
    part_refs, sums_refs = refs[:sources], refs[sources:]
    rows, columns = part_refs[0].shape
    width = columns - LANES
    stats = [unpacked_stats(ref[:, width:], width // HEAD_DIM) for ref in part_refs]
    peak = stats[0][0]
    for peaks, _ in stats[1:]:
        peak = jnp.maximum(peak, peaks)
    factors = [jnp.exp(peaks - peak) for peaks, _ in stats]
    total = sum(factor * sums for factor, (_, sums) in zip(factors, stats))
    shares = over_columns(jnp.concatenate(factors, axis=0), width)
    mixed = sum(
        ref[:, :width].astype(jnp.float32) * shares[i * rows : (i + 1) * rows]
        for i, ref in enumerate(part_refs)
    )
    packed = packed_stats(
        jnp.where(total > 0.0, peak, 0.0), pltpu.roll(total, SUM_LANE, 1)
    ).astype(jnp.float32)
    size = sums_refs[0].shape[0]
    for i, sums_ref in enumerate(sums_refs):
        span = slice(i * size, (i + 1) * size)
        sums_ref[:, :width] = mixed[span].astype(jnp.bfloat16)
        sums_ref[:, width:] = packed[span].astype(jnp.bfloat16)


def merge_kernel(sources, *refs):
    part_refs, (score_ref, value_ref, weight_ref, own_ref, send_ref) = refs[:sources], refs[sources:]
    own_rows, width = value_ref.shape
    heads = width // HEAD_DIM
    stats = [unpacked_stats(ref[:, width:], heads) for ref in part_refs]
    own_score = jnp.where(iota(score_ref.shape, 1) < heads, score_ref[...], 0.0)
    peak = own_score
    for peaks, _ in stats:
        peak = jnp.maximum(peak, peaks)
    own_weight = jnp.exp(own_score - peak)
    total = own_weight
    factors = []
    for peaks, sums in stats:
        factor = jnp.exp(peaks - peak)
        total = total + factor * sums
        factors.append(factor)
    factors.append(own_weight.astype(jnp.bfloat16).astype(jnp.float32))
    shares = jnp.concatenate([factor / total for factor in factors], axis=0)
    shares = over_columns(shares, width)
    mixed = value_ref[...].astype(jnp.float32) * shares[sources * own_rows :]
    for i, ref in enumerate(part_refs):
        rows = slice(i * own_rows, (i + 1) * own_rows)
        mixed = mixed + ref[:, :width].astype(jnp.float32) * shares[rows]
    projected = dot(mixed.astype(jnp.bfloat16), weight_ref[...])
    own_ref[...] = projected
    send_ref[...] = projected.astype(jnp.bfloat16)


def mlp_kernel(
    exchanged, hidden_ref, own_ref, other_ref, gain_ref, up_ref, down_ref, late_ref, *outs
):
    middle = hidden_ref[...] + (own_ref[...] + other_ref[...].astype(jnp.float32))
    normed = rms_normed(middle, gain_ref[...])
    active = jnp.maximum(dot(normed, up_ref[...]), 0.0).astype(jnp.bfloat16)
    half = down_ref.shape[0]
    down = dot(active[:, :half], down_ref[...]) + dot(active[:, half:], late_ref[...])
    if exchanged:
        kept_ref, sent_ref = outs
        columns = kept_ref.shape[1]
        low = lax.axis_index("head") == 0
        left, right = slice(0, columns), slice(columns, 2 * columns)
        kept = middle + down

        @pl.when(low)
        def _():
            kept_ref[...] = kept[:, left]
            sent_ref[...] = down[:, right].astype(jnp.bfloat16)

        @pl.when(jnp.logical_not(low))
        def _():
            kept_ref[...] = kept[:, right]
            sent_ref[...] = down[:, left].astype(jnp.bfloat16)

    else:
        middle_ref, down_out_ref = outs
        middle_ref[...] = middle
        down_out_ref[...] = down.astype(jnp.bfloat16)


def loading(*arrays):
    return pl.CostEstimate(
        flops=0, bytes_accessed=sum(2 * array.size for array in arrays), transcendentals=0
    )


def in_hbm(*arrays):
    return [pltpu.with_memory_space_constraint(array, pltpu.HBM) for array in arrays]


def xor_pairs(size, step):
    return [(i, i ^ step) for i in range(size)]


def per_device(
    hidden_in, attention_gain, mlp_gain, qkv_weight, out_weight, up_weight, down_weight,
    position_bias, bucket_edges, cache_keys, cache_values, lengths, page_request, page_index,
):
    f32, bf16 = jnp.float32, jnp.bfloat16
    shape = jax.ShapeDtypeStruct
    own_rows, model = hidden_in.shape
    width = qkv_weight.shape[2]
    page_count = page_request.shape[0]
    blocks = lax.axis_size("blk")
    all_rows = own_rows * blocks
    gain = attention_gain.reshape(1, model)
    query = pl.pallas_call(
        query_kernel,
        out_shape=shape((own_rows, width), bf16),
        in_specs=[HBM_SPEC] * 3,
        out_specs=VMEM_SPEC,
        scratch_shapes=[
            pltpu.VMEM((own_rows, model), f32),
            pltpu.VMEM((1, model), f32),
            pltpu.VMEM((model, width), bf16),
            pltpu.SemaphoreType.DMA((6,)),
        ],
        compiler_params=PARAMS,
        name="query",
    )(*in_hbm(hidden_in, gain, qkv_weight))

    inner = 1
    while inner * inner < blocks:
        inner *= 2
    far = [query] + [
        lax.ppermute(query, "blk", xor_pairs(blocks, step * inner))
        for step in range(1, blocks // inner)
    ]
    depth = page_count * PIECE
    early = page_count // 6 * 2
    keys, picks, place, leads, apart, owners = pl.pallas_call(
        functools.partial(page_kernel, own_rows, inner, blocks // inner),
        out_shape=(
            pltpu.VMEM((early,) + cache_keys.shape[1:], bf16),
            shape((depth, all_rows), bf16),
            shape((all_rows, depth), bf16),
            shape((page_count, LANES), f32),
            shape((page_count, LANES), f32),
            shape((page_count, LANES), jnp.int32),
        ),
        in_specs=[ANY_SPEC, VMEM_SPEC, HBM_SPEC],
        out_specs=(VMEM_SPEC,) * 6,
        scratch_shapes=[pltpu.SemaphoreType.DMA((4,))],
        compiler_params=PARAMS,
        cost_estimate=loading(cache_keys),
        name="pages",
    )(query, page_request.reshape(1, page_count), *in_hbm(cache_keys))
    near, apart = lax.optimization_barrier((jnp.concatenate(far, axis=0), apart))
    gathered = [near] + [
        lax.ppermute(near, "blk", xor_pairs(blocks, step)) for step in range(1, inner)
    ]
    table = position_bias.T
    late_keys, bias = pl.pallas_call(
        bias_kernel,
        out_shape=(
            pltpu.VMEM((page_count - early,) + cache_keys.shape[1:], bf16),
            shape((depth, PAGE), f32),
        ),
        in_specs=[HBM_SPEC] * 4 + [VMEM_SPEC, HBM_SPEC, ANY_SPEC],
        out_specs=(VMEM_SPEC,) * 2,
        scratch_shapes=[
            pltpu.SMEM(table.shape, f32),
            pltpu.SMEM(bucket_edges.shape, jnp.int32),
            pltpu.VMEM((1,) + lengths.shape, jnp.int32),
            pltpu.VMEM((1,) + page_index.shape, jnp.int32),
            pltpu.SemaphoreType.DMA((4,)),
            pltpu.SemaphoreType.DMA((4,)),
        ],
        compiler_params=PARAMS,
        cost_estimate=loading(cache_values),
        name="bias",
    )(
        *in_hbm(table, bucket_edges, lengths[None], page_index[None]), owners,
        *in_hbm(cache_keys), near,
    )

    groups = len(gathered)
    sums = pl.pallas_call(
        functools.partial(attend_kernel, groups),
        out_shape=(shape((all_rows // groups, width + LANES), bf16),) * groups,
        in_specs=[VMEM_SPEC] * (groups + 8),
        out_specs=(VMEM_SPEC,) * groups,
        compiler_params=PARAMS,
        name="attend",
    )(*gathered, bias, picks, place, leads, apart, keys, late_keys, cache_values)
    near_sums = [sums[0]] + [
        lax.ppermute(sums[step], "blk", xor_pairs(blocks, step))
        for step in reversed(range(1, inner))
    ]

    own_score, value_new, out_near = pl.pallas_call(
        side_kernel,
        out_shape=(
            shape((own_rows, LANES), f32),
            shape((own_rows, width), bf16),
            pltpu.VMEM(out_weight.shape, bf16),
        ),
        in_specs=[VMEM_SPEC] * 4 + [HBM_SPEC] * 2 + [ANY_SPEC],
        out_specs=(VMEM_SPEC,) * 3,
        scratch_shapes=[
            pltpu.VMEM((2, model, width), bf16),
            pltpu.SemaphoreType.DMA((2,)),
            pltpu.SemaphoreType.DMA((4,)),
        ],
        compiler_params=PARAMS,
        cost_estimate=loading(out_weight, out_weight, out_weight),
        name="side",
    )(
        hidden_in, gain, query, table,
        *in_hbm(qkv_weight, out_weight), sums[0],
    )

    *near_sums, own_score = lax.optimization_barrier((*near_sums, own_score))
    outer = blocks // inner
    sums = pl.pallas_call(
        functools.partial(combine_kernel, inner),
        out_shape=(shape((own_rows, width + LANES), bf16),) * outer,
        in_specs=[VMEM_SPEC] * inner,
        out_specs=(VMEM_SPEC,) * outer,
        compiler_params=PARAMS,
        name="combine",
    )(*near_sums)
    half = down_weight.shape[0] // 2

    def load_down(start, after):
        return pl.pallas_call(
            functools.partial(load_kernel, start),
            out_shape=pltpu.VMEM((half, model), bf16),
            in_specs=[HBM_SPEC, ANY_SPEC],
            out_specs=VMEM_SPEC,
            scratch_shapes=[pltpu.SemaphoreType.DMA((4,))],
            compiler_params=PARAMS,
            cost_estimate=loading(down_weight),
            name="load",
        )(*in_hbm(down_weight), after)

    down_early = load_down(0, sums[0])
    parts = [sums[0]] + [
        lax.ppermute(sums[step], "blk", xor_pairs(blocks, step * inner))
        for step in reversed(range(1, outer))
    ]

    *parts, down_early = lax.optimization_barrier((*parts, down_early))
    own_part, sent_part = pl.pallas_call(
        functools.partial(merge_kernel, outer),
        out_shape=(shape((own_rows, model), f32), shape((own_rows, model), bf16)),
        in_specs=[VMEM_SPEC] * (outer + 3),
        out_specs=(VMEM_SPEC,) * 2,
        compiler_params=PARAMS,
        name="merge",
    )(*parts, own_score, value_new, out_near)

    halves = lax.axis_size("head")
    columns = model // halves
    exchanged = halves == 2
    down_late = load_down(half, sent_part)
    if exchanged:
        other_part = lax.ppermute(sent_part, "head", xor_pairs(2, 1))
        mlp_out = (shape((own_rows, columns), f32), shape((own_rows, columns), bf16))
    else:
        own_part = jnp.zeros_like(own_part)
        other_part = lax.psum(sent_part, "head")
        mlp_out = (shape((own_rows, model), f32), shape((own_rows, model), bf16))

    kept, leaving = pl.pallas_call(
        functools.partial(mlp_kernel, exchanged),
        out_shape=mlp_out,
        in_specs=[VMEM_SPEC] * 7,
        out_specs=(VMEM_SPEC,) * 2,
        compiler_params=PARAMS,
        name="mlp",
    )(hidden_in, own_part, other_part, mlp_gain.reshape(1, model), up_weight, down_early, down_late)

    if exchanged:
        arrived = lax.ppermute(leaving, "head", xor_pairs(2, 1))
    else:
        kept = lax.dynamic_slice_in_dim(kept, lax.axis_index("head") * columns, columns, 1)
        arrived = lax.psum_scatter(leaving, "head", scatter_dimension=1, tiled=True)
    return kept + arrived.astype(f32)


def solution(mesh):
    in_specs = (
        P("blk", None),
        P(),
        P(),
        P(None, None, "head"),
        P("head", None),
        P(None, "head"),
        P("head", None),
        P(None, "head"),
        P(),
        P("blk", None, "head"),
        P("blk", None, "head"),
        P(),
        P("blk"),
        P("blk"),
    )
    out_specs = P("blk", "head")
    return jax.shard_map(
        per_device, mesh=mesh, in_specs=in_specs, out_specs=out_specs, check_vma=False
    )
```

```python
import functools

import jax
import jax.numpy as jnp
from jax import lax
from jax.experimental import pallas as pl
from jax.experimental.pallas import tpu as pltpu
from jax.sharding import PartitionSpec as P

HEAD_DIM = 64
PAGE = 128
LANES = 128

far_below = -1e30
epsilon = 1e-06

VMEM_SPEC = pl.BlockSpec(memory_space=pltpu.VMEM)
SMEM_SPEC = pl.BlockSpec(memory_space=pltpu.SMEM)
ANY_SPEC = pl.BlockSpec(memory_space=pl.ANY)
HBM_SPEC = pl.BlockSpec(memory_space=pltpu.HBM)
PARAMS = pltpu.CompilerParams(vmem_limit_bytes=16 * 1024 * 1024)

PIECE = 8
SUM_LANE = 3 * PIECE


def iota(shape, axis):
    return lax.broadcasted_iota(jnp.int32, shape, axis)


def split_index(x, size):
    if size & (size - 1):
        return lax.div(x, size), lax.rem(x, size)
    return x >> (size.bit_length() - 1), x & (size - 1)


def head_of(shape, axis):
    return split_index(iota(shape, axis), HEAD_DIM)[0]


def pieces(x, count):
    parts = []
    for _ in range(count):
        part = x.astype(jnp.bfloat16)
        parts.append(part)
        x = x - part.astype(jnp.float32)
    return parts


def rms_normed(x, gain):
    scale = lax.rsqrt(jnp.mean(x * x, axis=1, keepdims=True) + epsilon)
    return (x * scale * gain).astype(jnp.bfloat16)


def dot(a, b, dims=((1,), (0,)), precision=None):
    return lax.dot_general(
        a, b, (dims, ((), ())), preferred_element_type=jnp.float32, precision=precision
    )


def split_copies(source, target, sems, count):
    size = source.shape[0] // count
    return [
        pltpu.make_async_copy(
            source.at[pl.ds(i * size, size)], target.at[pl.ds(i * size, size)], sems.at[i]
        )
        for i in range(count)
    ]


def query_kernel(hidden_hbm, gain_hbm, weight_hbm, query_ref, hidden, gain, weight, sems):
    model = hidden.shape[1]
    small = [
        pltpu.make_async_copy(hidden_hbm, hidden, sems.at[0]),
        pltpu.make_async_copy(gain_hbm, gain, sems.at[1]),
    ]
    half = model // 4
    large = [
        pltpu.make_async_copy(
            weight_hbm.at[0, pl.ds(i * half, half)], weight.at[pl.ds(i * half, half)], sems.at[2 + i]
        )
        for i in range(4)
    ]
    for copy in small + large:
        copy.start()
    for copy in small:
        copy.wait()
    normed = rms_normed(hidden[...], gain[...])
    query = None
    for i, copy in enumerate(large):
        copy.wait()
        span = slice(i * half, (i + 1) * half)
        part = dot(normed[:, span], weight[span])
        query = part if query is None else query + part
    query_ref[...] = query.astype(jnp.bfloat16)


def page_kernel(
    own_rows, inner, outer, query_ref, request_ref, keys_hbm,
    keys_ref, pick_ref, place_ref, lead_ref, apart_ref, owners_ref,
    sems,
):
    copies = split_copies(
        keys_hbm.at[pl.ds(0, keys_ref.shape[0])], keys_ref, sems, sems.shape[0]
    )
    for copy in copies:
        copy.start()
    me = lax.axis_index("blk")
    page_count = apart_ref.shape[0]
    all_rows, depth = place_ref.shape
    page, lane = iota((page_count, page_count), 0), iota((page_count, page_count), 1)
    by_lane = request_ref[...]
    owner = jnp.max(jnp.where(page == lane, by_lane, -1), axis=1, keepdims=True)
    same = by_lane == owner
    apart_ref[...] = jnp.full(apart_ref.shape, 2 * far_below, jnp.float32)
    apart_ref[:, :page_count] = jnp.where(same, 0.0, 2 * far_below)
    earlier = jnp.max(jnp.where(same & (lane < page), 1, 0), axis=1, keepdims=True)
    lead_ref[...] = jnp.broadcast_to(jnp.where(earlier == 0, 1.0, 0.0), lead_ref.shape)
    owners_ref[...] = jnp.broadcast_to(owner, owners_ref.shape)
    device, own_row = split_index(jnp.maximum(owner, 0), own_rows)
    high, low = split_index(device ^ me, inner)
    slot = (low * outer + high) * own_rows + own_row
    slot = jnp.where(owner >= 0, slot, -1)
    row_of = iota((page_count, all_rows), 1)
    picks = jnp.where(row_of == slot, 1.0, 0.0)
    picks = [jnp.broadcast_to(picks[p : p + 1], (PIECE, all_rows)) for p in range(page_count)]
    pick_ref[...] = jnp.concatenate(picks, axis=0).astype(jnp.bfloat16)
    mine = split_index(iota((page_count, depth), 1), PIECE)[0] == iota((page_count, depth), 0)
    row = iota((all_rows, depth), 0)
    spread = jnp.max(jnp.where(mine, slot, -1), axis=0, keepdims=True)
    place_ref[...] = (row == spread).astype(jnp.bfloat16)
    for copy in copies:
        copy.wait()


def bias_kernel(
    table_hbm, edges_hbm, lengths_hbm, index_hbm, owners_ref, keys_hbm, after_ref,
    keys_ref, bias_ref,
    table, edges, lengths, index, small_sems, sems,
):
    sources, targets = (table_hbm, edges_hbm, lengths_hbm, index_hbm), (table, edges, lengths, index)
    small = [
        pltpu.make_async_copy(source, target, small_sems.at[i])
        for i, (source, target) in enumerate(zip(sources, targets))
    ]
    late = keys_ref.shape[0]
    copies = split_copies(
        keys_hbm.at[pl.ds(keys_hbm.shape[0] - late, late)], keys_ref, sems, sems.shape[0]
    )
    for copy in small + copies:
        copy.start()
    for copy in small:
        copy.wait()
    heads, buckets = table.shape
    page_count = index.shape[1]
    owner = owners_ref[:, 0:1]
    square = (page_count, page_count)
    number = jnp.where(iota(square, 0) == iota(square, 1), index[...], 0)
    number = jnp.sum(number, axis=1, keepdims=True)
    requests = lengths.shape[1]
    length = jnp.where(iota((page_count, requests), 1) == owner, lengths[...], 0)
    length = jnp.sum(length, axis=1, keepdims=True)
    distance = length - number * PAGE - iota((page_count, PAGE), 1)
    far = [distance >= edges[k] for k in range(buckets - 1)]
    usable = (owner >= 0) & (distance > 0)
    bias_ref[...] = jnp.full(bias_ref.shape, far_below, jnp.float32)
    for h in range(heads):
        bias = jnp.full((page_count, PAGE), table[h, 0], jnp.float32)
        for k in range(buckets - 1):
            bias = jnp.where(far[k], table[h, k + 1], bias)
        bias_ref[pl.ds(h, page_count, stride=PIECE), :] = jnp.where(usable, bias, far_below)
    for copy in copies:
        copy.wait()


def side_kernel(
    hidden_ref, gain_ref, query_ref, table_ref, weight_hbm, out_hbm, after_ref,
    score_ref, value_ref, out_ref,
    weight, weight_sems, sems,
):
    copies = [
        pltpu.make_async_copy(weight_hbm.at[1 + i], weight.at[i], weight_sems.at[i])
        for i in range(2)
    ]
    later = split_copies(out_hbm, out_ref, sems, sems.shape[0])
    for copy in copies + later:
        copy.start()
    normed = rms_normed(hidden_ref[...], gain_ref[...])
    heads = table_ref.shape[0]
    spread = iota((heads, LANES), 0) == iota((heads, LANES), 1)
    score = jnp.sum(jnp.where(spread, table_ref[:, 0:1], 0.0), axis=0, keepdims=True)
    copies[0].wait()
    key = dot(normed, weight[0]).astype(jnp.bfloat16)
    product = query_ref[...].astype(jnp.float32) * key.astype(jnp.float32)
    width = product.shape[1]
    gather = (head_of((width, LANES), 0) == iota((width, LANES), 1)).astype(jnp.bfloat16)
    for part in pieces(product, 3):
        score = score + dot(part, gather)
    score_ref[...] = score
    copies[1].wait()
    value_ref[...] = dot(normed, weight[1]).astype(jnp.bfloat16)
    for copy in later:
        copy.wait()


def load_kernel(start, source, after_ref, target, sems):
    rows = source.at[pl.ds(start, target.shape[0])]
    copies = split_copies(rows, target, sems, sems.shape[0])
    for copy in copies:
        copy.start()
    for copy in copies:
        copy.wait()


def packed_stats(peaks, sums):
    one, two, three = (part.astype(jnp.float32) for part in pieces(peaks + sums, 3))
    packed = one + pltpu.roll(two, PIECE, 1) + pltpu.roll(three, 2 * PIECE, 1)
    return packed.astype(jnp.bfloat16)


def unpacked_stats(packed, heads):
    stats = packed.astype(jnp.float32)
    stats = stats + pltpu.roll(stats, LANES - PIECE, 1) + pltpu.roll(stats, LANES - 2 * PIECE, 1)
    sums = pltpu.roll(stats, LANES - SUM_LANE, 1)
    used = iota(stats.shape, 1) < heads
    return jnp.where(used & (sums > 0.0), stats, far_below), jnp.where(used, sums, 0.0)


def over_columns(values, width):
    spread = (iota((LANES, width), 0) == head_of((LANES, width), 1)).astype(jnp.bfloat16)
    return sum(dot(part, spread) for part in pieces(values, 3))


def attend_kernel(groups, *refs):
    query_refs, refs, sums_refs = refs[:groups], refs[groups:-groups], refs[-groups:]
    bias_ref, pick_ref, place_ref, lead_ref, apart_ref, keys_ref, late_ref, values_ref = refs
    page_count = apart_ref.shape[0]
    width = keys_ref.shape[2]
    early = keys_ref.shape[0]
    chunk = 2
    chunks = page_count // chunk
    queries = jnp.concatenate([ref[...] for ref in query_refs], axis=0)
    own_head = (head_of((PIECE, width), 1) == iota((PIECE, width), 0)).astype(jnp.float32)
    pair_heads = jnp.concatenate([own_head] * chunk, axis=0)
    chosen = dot(pick_ref[...], queries)
    lane = iota((PIECE, LANES), 1)
    row = iota((PIECE, LANES), 0)
    tops = jnp.zeros((PIECE, LANES), jnp.float32)
    page_tops, totals, mixes = [], [], []
    nothing = jnp.zeros((PIECE, PAGE), jnp.float32)
    for c in range(chunks):
        rows = chosen[c * chunk * PIECE : (c + 1) * chunk * PIECE]
        split = (rows * pair_heads).astype(jnp.bfloat16)
        at = c * chunk
        block = keys_ref[at : at + chunk] if at < early else late_ref[at - early : at - early + chunk]
        raw = dot(split, block.reshape(chunk * PAGE, width), ((1,), (1,)))
        blocks = []
        for i in range(chunk):
            p = at + i
            part = raw[i * PIECE : (i + 1) * PIECE, i * PAGE : (i + 1) * PAGE]
            score = part + bias_ref[p * PIECE : (p + 1) * PIECE]
            top = jnp.max(score, axis=1, keepdims=True)
            weight = jnp.exp(score - top)
            tops = jnp.where(lane == p, top, tops)
            page_tops.append(top)
            totals.append(jnp.sum(weight, axis=1, keepdims=True))
            blocks.append(
                jnp.concatenate([weight if k == i else nothing for k in range(chunk)], axis=1)
            )
        weights = jnp.concatenate(blocks, axis=0).astype(jnp.bfloat16)
        mixes.append(dot(weights, values_ref[at : at + chunk].reshape(chunk * PAGE, width)))
    stats = []
    for c in range(chunks):
        factors = []
        for p in range(c * chunk, (c + 1) * chunk):
            peak = jnp.max(tops + apart_ref[p : p + 1], axis=1, keepdims=True)
            factor = jnp.exp(page_tops[p] - peak)
            total = jnp.where(lane == row + SUM_LANE, totals[p] * factor, 0.0)
            stats.append(jnp.where(lane == row, peak * lead_ref[p : p + 1], total))
            factors.append(factor)
        mixes[c] = mixes[c] * (pair_heads * jnp.concatenate(factors, axis=0))
    mix = jnp.concatenate(mixes, axis=0).astype(jnp.bfloat16)
    stats = pieces(jnp.concatenate(stats, axis=0), 3)
    sums = dot(place_ref[...], jnp.concatenate([mix] + stats, axis=1))
    stats = sum(sums[:, width + i * LANES : width + (i + 1) * LANES] for i in range(3))
    stats = packed_stats(stats, 0.0).astype(jnp.float32)
    size = sums.shape[0] // groups
    for i, sums_ref in enumerate(sums_refs):
        first, middle, last = i * size, i * size + size // 2, (i + 1) * size
        for c in range(width // LANES):
            block = sums[first:last, c * LANES : (c + 1) * LANES]
            sums_ref[c * size : (c + 1) * size] = block.astype(jnp.bfloat16)
        both = stats[first:middle] + pltpu.roll(stats[middle:last], LANES // 2, 1)
        sums_ref[width // LANES * size :] = both.astype(jnp.bfloat16)


def combine_kernel(sources, *refs):
    part_refs, sums_refs = refs[:sources], refs[sources:]
    width = sums_refs[0].shape[1] - LANES
    rows = sum(ref.shape[0] for ref in sums_refs)
    heads, blocks = width // HEAD_DIM, width // LANES
    stats, mixes = [], []
    for ref in part_refs:
        both = ref[blocks * rows :].astype(jnp.float32)
        both = jnp.concatenate([both, pltpu.roll(both, LANES // 2, 1)], axis=0)
        stats.append(unpacked_stats(both, heads))
        mix = [ref[c * rows : (c + 1) * rows] for c in range(blocks)]
        mixes.append(jnp.concatenate(mix, axis=1).astype(jnp.float32))
    peak = stats[0][0]
    for peaks, _ in stats[1:]:
        peak = jnp.maximum(peak, peaks)
    factors = [jnp.exp(peaks - peak) for peaks, _ in stats]
    total = sum(factor * sums for factor, (_, sums) in zip(factors, stats))
    shares = over_columns(jnp.concatenate(factors, axis=0), width)
    mixed = sum(mix * shares[i * rows : (i + 1) * rows] for i, mix in enumerate(mixes))
    packed = packed_stats(
        jnp.where(total > 0.0, peak, 0.0), pltpu.roll(total, SUM_LANE, 1)
    ).astype(jnp.float32)
    size = sums_refs[0].shape[0]
    for i, sums_ref in enumerate(sums_refs):
        span = slice(i * size, (i + 1) * size)
        sums_ref[:, :width] = mixed[span].astype(jnp.bfloat16)
        sums_ref[:, width:] = packed[span].astype(jnp.bfloat16)


def merge_kernel(sources, *refs):
    part_refs, (score_ref, value_ref, weight_ref, own_ref, send_ref) = refs[:sources], refs[sources:]
    own_rows, width = value_ref.shape
    heads = width // HEAD_DIM
    stats = [unpacked_stats(ref[:, width:], heads) for ref in part_refs]
    own_score = jnp.where(iota(score_ref.shape, 1) < heads, score_ref[...], 0.0)
    peak = own_score
    for peaks, _ in stats:
        peak = jnp.maximum(peak, peaks)
    own_weight = jnp.exp(own_score - peak)
    total = own_weight
    factors = []
    for peaks, sums in stats:
        factor = jnp.exp(peaks - peak)
        total = total + factor * sums
        factors.append(factor)
    factors.append(own_weight.astype(jnp.bfloat16).astype(jnp.float32))
    shares = jnp.concatenate([factor / total for factor in factors], axis=0)
    shares = over_columns(shares, width)
    mixed = value_ref[...].astype(jnp.float32) * shares[sources * own_rows :]
    for i, ref in enumerate(part_refs):
        rows = slice(i * own_rows, (i + 1) * own_rows)
        mixed = mixed + ref[:, :width].astype(jnp.float32) * shares[rows]
    projected = dot(mixed.astype(jnp.bfloat16), weight_ref[...])
    own_ref[...] = projected
    send_ref[...] = projected.astype(jnp.bfloat16)


def mlp_kernel(
    exchanged, hidden_ref, own_ref, other_ref, gain_ref, up_ref, down_ref, late_ref, *outs
):
    middle = hidden_ref[...] + (own_ref[...] + other_ref[...].astype(jnp.float32))
    normed = rms_normed(middle, gain_ref[...])
    active = jnp.maximum(dot(normed, up_ref[...]), 0.0).astype(jnp.bfloat16)
    half = down_ref.shape[0]
    down = dot(active[:, :half], down_ref[...]) + dot(active[:, half:], late_ref[...])
    if exchanged:
        kept_ref, sent_ref = outs
        columns = kept_ref.shape[1]
        low = lax.axis_index("head") == 0
        left, right = slice(0, columns), slice(columns, 2 * columns)
        kept = middle + down

        @pl.when(low)
        def _():
            kept_ref[...] = kept[:, left]
            sent_ref[...] = down[:, right].astype(jnp.bfloat16)

        @pl.when(jnp.logical_not(low))
        def _():
            kept_ref[...] = kept[:, right]
            sent_ref[...] = down[:, left].astype(jnp.bfloat16)

    else:
        middle_ref, down_out_ref = outs
        middle_ref[...] = middle
        down_out_ref[...] = down.astype(jnp.bfloat16)


def loading(*arrays):
    return pl.CostEstimate(
        flops=0, bytes_accessed=sum(2 * array.size for array in arrays), transcendentals=0
    )


def in_hbm(*arrays):
    return [pltpu.with_memory_space_constraint(array, pltpu.HBM) for array in arrays]


def xor_pairs(size, step):
    return [(i, i ^ step) for i in range(size)]


def per_device(
    hidden_in, attention_gain, mlp_gain, qkv_weight, out_weight, up_weight, down_weight,
    position_bias, bucket_edges, cache_keys, cache_values, lengths, page_request, page_index,
):
    f32, bf16 = jnp.float32, jnp.bfloat16
    shape = jax.ShapeDtypeStruct
    own_rows, model = hidden_in.shape
    width = qkv_weight.shape[2]
    page_count = page_request.shape[0]
    blocks = lax.axis_size("blk")
    all_rows = own_rows * blocks
    gain = attention_gain.reshape(1, model)
    query = pl.pallas_call(
        query_kernel,
        out_shape=shape((own_rows, width), bf16),
        in_specs=[HBM_SPEC] * 3,
        out_specs=VMEM_SPEC,
        scratch_shapes=[
            pltpu.VMEM((own_rows, model), f32),
            pltpu.VMEM((1, model), f32),
            pltpu.VMEM((model, width), bf16),
            pltpu.SemaphoreType.DMA((6,)),
        ],
        compiler_params=PARAMS,
        name="query",
    )(*in_hbm(hidden_in, gain, qkv_weight))

    inner = 1
    while inner * inner < blocks:
        inner *= 2
    far = [query] + [
        lax.ppermute(query, "blk", xor_pairs(blocks, step * inner))
        for step in range(1, blocks // inner)
    ]
    depth = page_count * PIECE
    early = page_count // 6 * 2
    keys, picks, place, leads, apart, owners = pl.pallas_call(
        functools.partial(page_kernel, own_rows, inner, blocks // inner),
        out_shape=(
            pltpu.VMEM((early,) + cache_keys.shape[1:], bf16),
            shape((depth, all_rows), bf16),
            shape((all_rows, depth), bf16),
            shape((page_count, LANES), f32),
            shape((page_count, LANES), f32),
            shape((page_count, LANES), jnp.int32),
        ),
        in_specs=[ANY_SPEC, VMEM_SPEC, HBM_SPEC],
        out_specs=(VMEM_SPEC,) * 6,
        scratch_shapes=[pltpu.SemaphoreType.DMA((4,))],
        compiler_params=PARAMS,
        cost_estimate=loading(cache_keys),
        name="pages",
    )(query, page_request.reshape(1, page_count), *in_hbm(cache_keys))
    near, apart = lax.optimization_barrier((jnp.concatenate(far, axis=0), apart))
    gathered = [near] + [
        lax.ppermute(near, "blk", xor_pairs(blocks, step)) for step in range(1, inner)
    ]
    table = position_bias.T
    late_keys, bias = pl.pallas_call(
        bias_kernel,
        out_shape=(
            pltpu.VMEM((page_count - early,) + cache_keys.shape[1:], bf16),
            shape((depth, PAGE), f32),
        ),
        in_specs=[HBM_SPEC] * 4 + [VMEM_SPEC, HBM_SPEC, ANY_SPEC],
        out_specs=(VMEM_SPEC,) * 2,
        scratch_shapes=[
            pltpu.SMEM(table.shape, f32),
            pltpu.SMEM(bucket_edges.shape, jnp.int32),
            pltpu.VMEM((1,) + lengths.shape, jnp.int32),
            pltpu.VMEM((1,) + page_index.shape, jnp.int32),
            pltpu.SemaphoreType.DMA((4,)),
            pltpu.SemaphoreType.DMA((4,)),
        ],
        compiler_params=PARAMS,
        cost_estimate=loading(cache_values),
        name="bias",
    )(
        *in_hbm(table, bucket_edges, lengths[None], page_index[None]), owners,
        *in_hbm(cache_keys), near,
    )

    groups = len(gathered)
    size = all_rows // groups
    message = width // LANES * size + size // 2
    sums = pl.pallas_call(
        functools.partial(attend_kernel, groups),
        out_shape=(shape((message, LANES), bf16),) * groups,
        in_specs=[VMEM_SPEC] * (groups + 8),
        out_specs=(VMEM_SPEC,) * groups,
        compiler_params=PARAMS,
        name="attend",
    )(*gathered, bias, picks, place, leads, apart, keys, late_keys, cache_values)
    near_sums = [sums[0]] + [
        lax.ppermute(sums[step], "blk", xor_pairs(blocks, step))
        for step in reversed(range(1, inner))
    ]

    own_score, value_new, out_near = pl.pallas_call(
        side_kernel,
        out_shape=(
            shape((own_rows, LANES), f32),
            shape((own_rows, width), bf16),
            pltpu.VMEM(out_weight.shape, bf16),
        ),
        in_specs=[VMEM_SPEC] * 4 + [HBM_SPEC] * 2 + [ANY_SPEC],
        out_specs=(VMEM_SPEC,) * 3,
        scratch_shapes=[
            pltpu.VMEM((2, model, width), bf16),
            pltpu.SemaphoreType.DMA((2,)),
            pltpu.SemaphoreType.DMA((4,)),
        ],
        compiler_params=PARAMS,
        cost_estimate=loading(out_weight, out_weight, out_weight),
        name="side",
    )(
        hidden_in, gain, query, table,
        *in_hbm(qkv_weight, out_weight), sums[0],
    )

    *near_sums, own_score = lax.optimization_barrier((*near_sums, own_score))
    outer = blocks // inner
    sums = pl.pallas_call(
        functools.partial(combine_kernel, inner),
        out_shape=(shape((own_rows, width + LANES), bf16),) * outer,
        in_specs=[VMEM_SPEC] * inner,
        out_specs=(VMEM_SPEC,) * outer,
        compiler_params=PARAMS,
        name="combine",
    )(*near_sums)
    half = down_weight.shape[0] // 2

    def load_down(start, after):
        return pl.pallas_call(
            functools.partial(load_kernel, start),
            out_shape=pltpu.VMEM((half, model), bf16),
            in_specs=[HBM_SPEC, ANY_SPEC],
            out_specs=VMEM_SPEC,
            scratch_shapes=[pltpu.SemaphoreType.DMA((4,))],
            compiler_params=PARAMS,
            cost_estimate=loading(down_weight),
            name="load",
        )(*in_hbm(down_weight), after)

    down_early = load_down(0, sums[0])
    parts = [sums[0]] + [
        lax.ppermute(sums[step], "blk", xor_pairs(blocks, step * inner))
        for step in reversed(range(1, outer))
    ]

    *parts, down_early = lax.optimization_barrier((*parts, down_early))
    own_part, sent_part = pl.pallas_call(
        functools.partial(merge_kernel, outer),
        out_shape=(shape((own_rows, model), f32), shape((own_rows, model), bf16)),
        in_specs=[VMEM_SPEC] * (outer + 3),
        out_specs=(VMEM_SPEC,) * 2,
        compiler_params=PARAMS,
        name="merge",
    )(*parts, own_score, value_new, out_near)

    halves = lax.axis_size("head")
    columns = model // halves
    exchanged = halves == 2
    down_late = load_down(half, sent_part)
    if exchanged:
        other_part = lax.ppermute(sent_part, "head", xor_pairs(2, 1))
        mlp_out = (shape((own_rows, columns), f32), shape((own_rows, columns), bf16))
    else:
        own_part = jnp.zeros_like(own_part)
        other_part = lax.psum(sent_part, "head")
        mlp_out = (shape((own_rows, model), f32), shape((own_rows, model), bf16))

    kept, leaving = pl.pallas_call(
        functools.partial(mlp_kernel, exchanged),
        out_shape=mlp_out,
        in_specs=[VMEM_SPEC] * 7,
        out_specs=(VMEM_SPEC,) * 2,
        compiler_params=PARAMS,
        name="mlp",
    )(hidden_in, own_part, other_part, mlp_gain.reshape(1, model), up_weight, down_early, down_late)

    if exchanged:
        arrived = lax.ppermute(leaving, "head", xor_pairs(2, 1))
    else:
        kept = lax.dynamic_slice_in_dim(kept, lax.axis_index("head") * columns, columns, 1)
        arrived = lax.psum_scatter(leaving, "head", scatter_dimension=1, tiled=True)
    return kept + arrived.astype(f32)


def solution(mesh):
    in_specs = (
        P("blk", None),
        P(),
        P(),
        P(None, None, "head"),
        P("head", None),
        P(None, "head"),
        P("head", None),
        P(None, "head"),
        P(),
        P("blk", None, "head"),
        P("blk", None, "head"),
        P(),
        P("blk"),
        P("blk"),
    )
    out_specs = P("blk", "head")
    return jax.shard_map(
        per_device, mesh=mesh, in_specs=in_specs, out_specs=out_specs, check_vma=False
    )
```

```python
import functools

import jax
import jax.numpy as jnp
from jax import lax
from jax.experimental import pallas as pl
from jax.experimental.pallas import tpu as pltpu
from jax.sharding import PartitionSpec as P

HEAD_DIM = 64
PAGE = 128
LANES = 128

far_below = -1e30
epsilon = 1e-06

VMEM_SPEC = pl.BlockSpec(memory_space=pltpu.VMEM)
SMEM_SPEC = pl.BlockSpec(memory_space=pltpu.SMEM)
ANY_SPEC = pl.BlockSpec(memory_space=pl.ANY)
HBM_SPEC = pl.BlockSpec(memory_space=pltpu.HBM)
PARAMS = pltpu.CompilerParams(vmem_limit_bytes=16 * 1024 * 1024)

PIECE = 8
SUM_LANE = 3 * PIECE


def iota(shape, axis):
    return lax.broadcasted_iota(jnp.int32, shape, axis)


def split_index(x, size):
    if size & (size - 1):
        return lax.div(x, size), lax.rem(x, size)
    return x >> (size.bit_length() - 1), x & (size - 1)


def head_of(shape, axis):
    return split_index(iota(shape, axis), HEAD_DIM)[0]


def pieces(x, count):
    parts = []
    for _ in range(count):
        part = x.astype(jnp.bfloat16)
        parts.append(part)
        x = x - part.astype(jnp.float32)
    return parts


def rms_normed(x, gain):
    scale = lax.rsqrt(jnp.mean(x * x, axis=1, keepdims=True) + epsilon)
    return (x * scale * gain).astype(jnp.bfloat16)


def dot(a, b, dims=((1,), (0,)), precision=None):
    return lax.dot_general(
        a, b, (dims, ((), ())), preferred_element_type=jnp.float32, precision=precision
    )


def split_copies(source, target, sems, count):
    size = source.shape[0] // count
    return [
        pltpu.make_async_copy(
            source.at[pl.ds(i * size, size)], target.at[pl.ds(i * size, size)], sems.at[i]
        )
        for i in range(count)
    ]


def query_kernel(hidden_hbm, gain_hbm, weight_hbm, query_ref, hidden, gain, weight, sems):
    model = hidden.shape[1]
    small = [
        pltpu.make_async_copy(hidden_hbm, hidden, sems.at[0]),
        pltpu.make_async_copy(gain_hbm, gain, sems.at[1]),
    ]
    half = model // 4
    large = [
        pltpu.make_async_copy(
            weight_hbm.at[0, pl.ds(i * half, half)], weight.at[pl.ds(i * half, half)], sems.at[2 + i]
        )
        for i in range(4)
    ]
    for copy in small + large:
        copy.start()
    for copy in small:
        copy.wait()
    normed = rms_normed(hidden[...], gain[...])
    query = None
    for i, copy in enumerate(large):
        copy.wait()
        span = slice(i * half, (i + 1) * half)
        part = dot(normed[:, span], weight[span])
        query = part if query is None else query + part
    query_ref[...] = query.astype(jnp.bfloat16)


def page_kernel(
    own_rows, inner, outer, query_ref, request_ref, keys_hbm,
    keys_ref, pick_ref, place_ref, lead_ref, apart_ref, owners_ref,
    sems,
):
    copies = split_copies(
        keys_hbm.at[pl.ds(0, keys_ref.shape[0])], keys_ref, sems, sems.shape[0]
    )
    for copy in copies:
        copy.start()
    me = lax.axis_index("blk")
    page_count = apart_ref.shape[0]
    all_rows, depth = place_ref.shape
    page, lane = iota((page_count, page_count), 0), iota((page_count, page_count), 1)
    by_lane = request_ref[...]
    owner = jnp.max(jnp.where(page == lane, by_lane, -1), axis=1, keepdims=True)
    same = by_lane == owner
    apart_ref[...] = jnp.full(apart_ref.shape, 2 * far_below, jnp.float32)
    apart_ref[:, :page_count] = jnp.where(same, 0.0, 2 * far_below)
    earlier = jnp.max(jnp.where(same & (lane < page), 1, 0), axis=1, keepdims=True)
    lead_ref[...] = jnp.broadcast_to(jnp.where(earlier == 0, 1.0, 0.0), lead_ref.shape)
    owners_ref[...] = jnp.broadcast_to(owner, owners_ref.shape)
    device, own_row = split_index(jnp.maximum(owner, 0), own_rows)
    high, low = split_index(device ^ me, inner)
    slot = (low * outer + high) * own_rows + own_row
    slot = jnp.where(owner >= 0, slot, -1)
    row_of = iota((page_count, all_rows), 1)
    picks = jnp.where(row_of == slot, 1.0, 0.0)
    picks = [jnp.broadcast_to(picks[p : p + 1], (PIECE, all_rows)) for p in range(page_count)]
    pick_ref[...] = jnp.concatenate(picks, axis=0).astype(jnp.bfloat16)
    mine = split_index(iota((page_count, depth), 1), PIECE)[0] == iota((page_count, depth), 0)
    row = iota((all_rows, depth), 0)
    spread = jnp.max(jnp.where(mine, slot, -1), axis=0, keepdims=True)
    place_ref[...] = (row == spread).astype(jnp.bfloat16)
    for copy in copies:
        copy.wait()


def bias_kernel(
    table_hbm, edges_hbm, lengths_hbm, index_hbm, owners_ref, keys_hbm, after_ref,
    keys_ref, bias_ref,
    table, edges, lengths, index, small_sems, sems,
):
    sources, targets = (table_hbm, edges_hbm, lengths_hbm, index_hbm), (table, edges, lengths, index)
    small = [
        pltpu.make_async_copy(source, target, small_sems.at[i])
        for i, (source, target) in enumerate(zip(sources, targets))
    ]
    late = keys_ref.shape[0]
    copies = split_copies(
        keys_hbm.at[pl.ds(keys_hbm.shape[0] - late, late)], keys_ref, sems, sems.shape[0]
    )
    for copy in small + copies:
        copy.start()
    for copy in small:
        copy.wait()
    heads, buckets = table.shape
    page_count = index.shape[1]
    owner = owners_ref[:, 0:1]
    square = (page_count, page_count)
    number = jnp.where(iota(square, 0) == iota(square, 1), index[...], 0)
    number = jnp.sum(number, axis=1, keepdims=True)
    requests = lengths.shape[1]
    length = jnp.where(iota((page_count, requests), 1) == owner, lengths[...], 0)
    length = jnp.sum(length, axis=1, keepdims=True)
    distance = length - number * PAGE - iota((page_count, PAGE), 1)
    far = [distance >= edges[k] for k in range(buckets - 1)]
    usable = (owner >= 0) & (distance > 0)
    bias_ref[...] = jnp.full(bias_ref.shape, far_below, jnp.float32)
    for h in range(heads):
        bias = jnp.full((page_count, PAGE), table[h, 0], jnp.float32)
        for k in range(buckets - 1):
            bias = jnp.where(far[k], table[h, k + 1], bias)
        bias_ref[pl.ds(h, page_count, stride=PIECE), :] = jnp.where(usable, bias, far_below)
    for copy in copies:
        copy.wait()


def side_kernel(
    hidden_ref, gain_ref, query_ref, table_ref, weight_hbm, out_hbm, after_ref,
    score_ref, value_ref, out_ref,
    weight, weight_sems, sems,
):
    copies = [
        pltpu.make_async_copy(weight_hbm.at[1 + i], weight.at[i], weight_sems.at[i])
        for i in range(2)
    ]
    later = split_copies(out_hbm, out_ref, sems, sems.shape[0])
    for copy in copies + later:
        copy.start()
    normed = rms_normed(hidden_ref[...], gain_ref[...])
    heads = table_ref.shape[0]
    spread = iota((heads, LANES), 0) == iota((heads, LANES), 1)
    score = jnp.sum(jnp.where(spread, table_ref[:, 0:1], 0.0), axis=0, keepdims=True)
    copies[0].wait()
    key = dot(normed, weight[0]).astype(jnp.bfloat16)
    product = query_ref[...].astype(jnp.float32) * key.astype(jnp.float32)
    width = product.shape[1]
    gather = (head_of((width, LANES), 0) == iota((width, LANES), 1)).astype(jnp.bfloat16)
    for part in pieces(product, 3):
        score = score + dot(part, gather)
    score_ref[...] = score
    copies[1].wait()
    value_ref[...] = dot(normed, weight[1]).astype(jnp.bfloat16)
    for copy in later:
        copy.wait()


def load_kernel(start, source, after_ref, target, sems):
    rows = source.at[pl.ds(start, target.shape[0])]
    copies = split_copies(rows, target, sems, sems.shape[0])
    for copy in copies:
        copy.start()
    for copy in copies:
        copy.wait()


def packed_stats(peaks, sums):
    one, two, three = (part.astype(jnp.float32) for part in pieces(peaks + sums, 3))
    packed = one + pltpu.roll(two, PIECE, 1) + pltpu.roll(three, 2 * PIECE, 1)
    return packed.astype(jnp.bfloat16)


def unpacked_stats(packed, heads):
    stats = packed.astype(jnp.float32)
    stats = stats + pltpu.roll(stats, LANES - PIECE, 1) + pltpu.roll(stats, LANES - 2 * PIECE, 1)
    sums = pltpu.roll(stats, LANES - SUM_LANE, 1)
    used = iota(stats.shape, 1) < heads
    return jnp.where(used & (sums > 0.0), stats, far_below), jnp.where(used, sums, 0.0)


def over_columns(values, width):
    spread = (iota((LANES, width), 0) == head_of((LANES, width), 1)).astype(jnp.bfloat16)
    return sum(dot(part, spread) for part in pieces(values, 3))


def attend_kernel(groups, *refs):
    query_refs, refs, sums_refs = refs[:groups], refs[groups:-groups], refs[-groups:]
    bias_ref, pick_ref, place_ref, lead_ref, apart_ref, keys_ref, late_ref, values_ref = refs
    page_count = apart_ref.shape[0]
    width = keys_ref.shape[2]
    early = keys_ref.shape[0]
    chunk = 2
    chunks = page_count // chunk
    queries = jnp.concatenate([ref[...] for ref in query_refs], axis=0)
    own_head = (head_of((PIECE, width), 1) == iota((PIECE, width), 0)).astype(jnp.float32)
    pair_heads = jnp.concatenate([own_head] * chunk, axis=0)
    chosen = dot(pick_ref[...], queries)
    lane = iota((PIECE, LANES), 1)
    row = iota((PIECE, LANES), 0)
    nothing = jnp.zeros((PIECE, PAGE), jnp.float32)
    raws = []
    for c in range(chunks):
        rows = chosen[c * chunk * PIECE : (c + 1) * chunk * PIECE]
        split = (rows * pair_heads).astype(jnp.bfloat16)
        at = c * chunk
        block = keys_ref[at : at + chunk] if at < early else late_ref[at - early : at - early + chunk]
        raws.append(dot(split, block.reshape(chunk * PAGE, width), ((1,), (1,))))
    scores, page_tops = [], []
    for p in range(page_count):
        i = p % chunk
        part = raws[p // chunk][i * PIECE : (i + 1) * PIECE, i * PAGE : (i + 1) * PAGE]
        score = part + bias_ref[p * PIECE : (p + 1) * PIECE]
        scores.append(score)
        page_tops.append(jnp.max(score, axis=1, keepdims=True))
    page_weights = [jnp.exp(score - top) for score, top in zip(scores, page_tops)]
    mixes = []
    for c in range(chunks):
        blocks = []
        for i in range(chunk):
            weight = page_weights[c * chunk + i]
            blocks.append(
                jnp.concatenate([weight if k == i else nothing for k in range(chunk)], axis=1)
            )
        weights = jnp.concatenate(blocks, axis=0).astype(jnp.bfloat16)
        block = values_ref[c * chunk : (c + 1) * chunk]
        mixes.append(dot(weights, block.reshape(chunk * PAGE, width)))
    totals = [jnp.sum(weight, axis=1, keepdims=True) for weight in page_weights]
    tops = jnp.zeros((PIECE, LANES), jnp.float32)
    for p in range(page_count):
        tops = jnp.where(lane == p, page_tops[p], tops)
    stats = []
    for c in range(chunks):
        factors = []
        for p in range(c * chunk, (c + 1) * chunk):
            peak = jnp.max(tops + apart_ref[p : p + 1], axis=1, keepdims=True)
            factor = jnp.exp(page_tops[p] - peak)
            total = jnp.where(lane == row + SUM_LANE, totals[p] * factor, 0.0)
            stats.append(jnp.where(lane == row, peak * lead_ref[p : p + 1], total))
            factors.append(factor)
        mixes[c] = mixes[c] * (pair_heads * jnp.concatenate(factors, axis=0))
    mix = jnp.concatenate(mixes, axis=0).astype(jnp.bfloat16)
    stats = pieces(jnp.concatenate(stats, axis=0), 3)
    sums = dot(place_ref[...], jnp.concatenate([mix] + stats, axis=1))
    stats = sum(sums[:, width + i * LANES : width + (i + 1) * LANES] for i in range(3))
    stats = packed_stats(stats, 0.0).astype(jnp.float32)
    size = sums.shape[0] // groups
    for i, sums_ref in enumerate(sums_refs):
        first, middle, last = i * size, i * size + size // 2, (i + 1) * size
        for c in range(width // LANES):
            block = sums[first:last, c * LANES : (c + 1) * LANES]
            sums_ref[c * size : (c + 1) * size] = block.astype(jnp.bfloat16)
        both = stats[first:middle] + pltpu.roll(stats[middle:last], LANES // 2, 1)
        sums_ref[width // LANES * size :] = both.astype(jnp.bfloat16)


def combine_kernel(sources, *refs):
    part_refs, sums_refs = refs[:sources], refs[sources:]
    width = sums_refs[0].shape[1] - LANES
    rows = sum(ref.shape[0] for ref in sums_refs)
    heads, blocks = width // HEAD_DIM, width // LANES
    stats, mixes = [], []
    for ref in part_refs:
        both = ref[blocks * rows :].astype(jnp.float32)
        both = jnp.concatenate([both, pltpu.roll(both, LANES // 2, 1)], axis=0)
        stats.append(unpacked_stats(both, heads))
        mix = [ref[c * rows : (c + 1) * rows] for c in range(blocks)]
        mixes.append(jnp.concatenate(mix, axis=1).astype(jnp.float32))
    peak = stats[0][0]
    for peaks, _ in stats[1:]:
        peak = jnp.maximum(peak, peaks)
    factors = [jnp.exp(peaks - peak) for peaks, _ in stats]
    total = sum(factor * sums for factor, (_, sums) in zip(factors, stats))
    shares = over_columns(jnp.concatenate(factors, axis=0), width)
    mixed = sum(mix * shares[i * rows : (i + 1) * rows] for i, mix in enumerate(mixes))
    packed = packed_stats(
        jnp.where(total > 0.0, peak, 0.0), pltpu.roll(total, SUM_LANE, 1)
    ).astype(jnp.float32)
    size = sums_refs[0].shape[0]
    for i, sums_ref in enumerate(sums_refs):
        span = slice(i * size, (i + 1) * size)
        sums_ref[:, :width] = mixed[span].astype(jnp.bfloat16)
        sums_ref[:, width:] = packed[span].astype(jnp.bfloat16)


def merge_kernel(sources, *refs):
    part_refs, (score_ref, value_ref, weight_ref, own_ref, send_ref) = refs[:sources], refs[sources:]
    own_rows, width = value_ref.shape
    heads = width // HEAD_DIM
    stats = [unpacked_stats(ref[:, width:], heads) for ref in part_refs]
    own_score = jnp.where(iota(score_ref.shape, 1) < heads, score_ref[...], 0.0)
    peak = own_score
    for peaks, _ in stats:
        peak = jnp.maximum(peak, peaks)
    own_weight = jnp.exp(own_score - peak)
    total = own_weight
    factors = []
    for peaks, sums in stats:
        factor = jnp.exp(peaks - peak)
        total = total + factor * sums
        factors.append(factor)
    factors.append(own_weight.astype(jnp.bfloat16).astype(jnp.float32))
    shares = jnp.concatenate([factor / total for factor in factors], axis=0)
    shares = over_columns(shares, width)
    mixed = value_ref[...].astype(jnp.float32) * shares[sources * own_rows :]
    for i, ref in enumerate(part_refs):
        rows = slice(i * own_rows, (i + 1) * own_rows)
        mixed = mixed + ref[:, :width].astype(jnp.float32) * shares[rows]
    projected = dot(mixed.astype(jnp.bfloat16), weight_ref[...])
    own_ref[...] = projected
    send_ref[...] = projected.astype(jnp.bfloat16)


def mlp_kernel(
    exchanged, hidden_ref, own_ref, other_ref, gain_ref, up_ref, down_ref, late_ref, *outs
):
    middle = hidden_ref[...] + (own_ref[...] + other_ref[...].astype(jnp.float32))
    normed = rms_normed(middle, gain_ref[...])
    active = jnp.maximum(dot(normed, up_ref[...]), 0.0).astype(jnp.bfloat16)
    half = down_ref.shape[0]
    down = dot(active[:, :half], down_ref[...]) + dot(active[:, half:], late_ref[...])
    if exchanged:
        kept_ref, sent_ref = outs
        columns = kept_ref.shape[1]
        low = lax.axis_index("head") == 0
        left, right = slice(0, columns), slice(columns, 2 * columns)
        kept = middle + down

        @pl.when(low)
        def _():
            kept_ref[...] = kept[:, left]
            sent_ref[...] = down[:, right].astype(jnp.bfloat16)

        @pl.when(jnp.logical_not(low))
        def _():
            kept_ref[...] = kept[:, right]
            sent_ref[...] = down[:, left].astype(jnp.bfloat16)

    else:
        middle_ref, down_out_ref = outs
        middle_ref[...] = middle
        down_out_ref[...] = down.astype(jnp.bfloat16)


def loading(*arrays):
    return pl.CostEstimate(
        flops=0, bytes_accessed=sum(2 * array.size for array in arrays), transcendentals=0
    )


def in_hbm(*arrays):
    return [pltpu.with_memory_space_constraint(array, pltpu.HBM) for array in arrays]


def xor_pairs(size, step):
    return [(i, i ^ step) for i in range(size)]


def per_device(
    hidden_in, attention_gain, mlp_gain, qkv_weight, out_weight, up_weight, down_weight,
    position_bias, bucket_edges, cache_keys, cache_values, lengths, page_request, page_index,
):
    f32, bf16 = jnp.float32, jnp.bfloat16
    shape = jax.ShapeDtypeStruct
    own_rows, model = hidden_in.shape
    width = qkv_weight.shape[2]
    page_count = page_request.shape[0]
    blocks = lax.axis_size("blk")
    all_rows = own_rows * blocks
    gain = attention_gain.reshape(1, model)
    query = pl.pallas_call(
        query_kernel,
        out_shape=shape((own_rows, width), bf16),
        in_specs=[HBM_SPEC] * 3,
        out_specs=VMEM_SPEC,
        scratch_shapes=[
            pltpu.VMEM((own_rows, model), f32),
            pltpu.VMEM((1, model), f32),
            pltpu.VMEM((model, width), bf16),
            pltpu.SemaphoreType.DMA((6,)),
        ],
        compiler_params=PARAMS,
        name="query",
    )(*in_hbm(hidden_in, gain, qkv_weight))

    inner = 1
    while inner * inner < blocks:
        inner *= 2
    far = [query] + [
        lax.ppermute(query, "blk", xor_pairs(blocks, step * inner))
        for step in range(1, blocks // inner)
    ]
    depth = page_count * PIECE
    early = page_count // 6 * 2
    keys, picks, place, leads, apart, owners = pl.pallas_call(
        functools.partial(page_kernel, own_rows, inner, blocks // inner),
        out_shape=(
            pltpu.VMEM((early,) + cache_keys.shape[1:], bf16),
            shape((depth, all_rows), bf16),
            shape((all_rows, depth), bf16),
            shape((page_count, LANES), f32),
            shape((page_count, LANES), f32),
            shape((page_count, LANES), jnp.int32),
        ),
        in_specs=[ANY_SPEC, VMEM_SPEC, HBM_SPEC],
        out_specs=(VMEM_SPEC,) * 6,
        scratch_shapes=[pltpu.SemaphoreType.DMA((4,))],
        compiler_params=PARAMS,
        cost_estimate=loading(cache_keys),
        name="pages",
    )(query, page_request.reshape(1, page_count), *in_hbm(cache_keys))
    near, apart = lax.optimization_barrier((jnp.concatenate(far, axis=0), apart))
    gathered = [near] + [
        lax.ppermute(near, "blk", xor_pairs(blocks, step)) for step in range(1, inner)
    ]
    table = position_bias.T
    late_keys, bias = pl.pallas_call(
        bias_kernel,
        out_shape=(
            pltpu.VMEM((page_count - early,) + cache_keys.shape[1:], bf16),
            shape((depth, PAGE), f32),
        ),
        in_specs=[HBM_SPEC] * 4 + [VMEM_SPEC, HBM_SPEC, ANY_SPEC],
        out_specs=(VMEM_SPEC,) * 2,
        scratch_shapes=[
            pltpu.SMEM(table.shape, f32),
            pltpu.SMEM(bucket_edges.shape, jnp.int32),
            pltpu.VMEM((1,) + lengths.shape, jnp.int32),
            pltpu.VMEM((1,) + page_index.shape, jnp.int32),
            pltpu.SemaphoreType.DMA((4,)),
            pltpu.SemaphoreType.DMA((4,)),
        ],
        compiler_params=PARAMS,
        cost_estimate=loading(cache_values),
        name="bias",
    )(
        *in_hbm(table, bucket_edges, lengths[None], page_index[None]), owners,
        *in_hbm(cache_keys), near,
    )

    groups = len(gathered)
    size = all_rows // groups
    message = width // LANES * size + size // 2
    sums = pl.pallas_call(
        functools.partial(attend_kernel, groups),
        out_shape=(shape((message, LANES), bf16),) * groups,
        in_specs=[VMEM_SPEC] * (groups + 8),
        out_specs=(VMEM_SPEC,) * groups,
        compiler_params=PARAMS,
        name="attend",
    )(*gathered, bias, picks, place, leads, apart, keys, late_keys, cache_values)
    near_sums = [sums[0]] + [
        lax.ppermute(sums[step], "blk", xor_pairs(blocks, step))
        for step in reversed(range(1, inner))
    ]

    own_score, value_new, out_near = pl.pallas_call(
        side_kernel,
        out_shape=(
            shape((own_rows, LANES), f32),
            shape((own_rows, width), bf16),
            pltpu.VMEM(out_weight.shape, bf16),
        ),
        in_specs=[VMEM_SPEC] * 4 + [HBM_SPEC] * 2 + [ANY_SPEC],
        out_specs=(VMEM_SPEC,) * 3,
        scratch_shapes=[
            pltpu.VMEM((2, model, width), bf16),
            pltpu.SemaphoreType.DMA((2,)),
            pltpu.SemaphoreType.DMA((4,)),
        ],
        compiler_params=PARAMS,
        cost_estimate=loading(out_weight, out_weight, out_weight),
        name="side",
    )(
        hidden_in, gain, query, table,
        *in_hbm(qkv_weight, out_weight), sums[0],
    )

    *near_sums, own_score = lax.optimization_barrier((*near_sums, own_score))
    outer = blocks // inner
    sums = pl.pallas_call(
        functools.partial(combine_kernel, inner),
        out_shape=(shape((own_rows, width + LANES), bf16),) * outer,
        in_specs=[VMEM_SPEC] * inner,
        out_specs=(VMEM_SPEC,) * outer,
        compiler_params=PARAMS,
        name="combine",
    )(*near_sums)
    half = down_weight.shape[0] // 2

    def load_down(start, after):
        return pl.pallas_call(
            functools.partial(load_kernel, start),
            out_shape=pltpu.VMEM((half, model), bf16),
            in_specs=[HBM_SPEC, ANY_SPEC],
            out_specs=VMEM_SPEC,
            scratch_shapes=[pltpu.SemaphoreType.DMA((4,))],
            compiler_params=PARAMS,
            cost_estimate=loading(down_weight),
            name="load",
        )(*in_hbm(down_weight), after)

    down_early = load_down(0, sums[0])
    parts = [sums[0]] + [
        lax.ppermute(sums[step], "blk", xor_pairs(blocks, step * inner))
        for step in reversed(range(1, outer))
    ]

    *parts, down_early = lax.optimization_barrier((*parts, down_early))
    own_part, sent_part = pl.pallas_call(
        functools.partial(merge_kernel, outer),
        out_shape=(shape((own_rows, model), f32), shape((own_rows, model), bf16)),
        in_specs=[VMEM_SPEC] * (outer + 3),
        out_specs=(VMEM_SPEC,) * 2,
        compiler_params=PARAMS,
        name="merge",
    )(*parts, own_score, value_new, out_near)

    halves = lax.axis_size("head")
    columns = model // halves
    exchanged = halves == 2
    down_late = load_down(half, sent_part)
    if exchanged:
        other_part = lax.ppermute(sent_part, "head", xor_pairs(2, 1))
        mlp_out = (shape((own_rows, columns), f32), shape((own_rows, columns), bf16))
    else:
        own_part = jnp.zeros_like(own_part)
        other_part = lax.psum(sent_part, "head")
        mlp_out = (shape((own_rows, model), f32), shape((own_rows, model), bf16))

    kept, leaving = pl.pallas_call(
        functools.partial(mlp_kernel, exchanged),
        out_shape=mlp_out,
        in_specs=[VMEM_SPEC] * 7,
        out_specs=(VMEM_SPEC,) * 2,
        compiler_params=PARAMS,
        name="mlp",
    )(hidden_in, own_part, other_part, mlp_gain.reshape(1, model), up_weight, down_early, down_late)

    if exchanged:
        arrived = lax.ppermute(leaving, "head", xor_pairs(2, 1))
    else:
        kept = lax.dynamic_slice_in_dim(kept, lax.axis_index("head") * columns, columns, 1)
        arrived = lax.psum_scatter(leaving, "head", scatter_dimension=1, tiled=True)
    return kept + arrived.astype(f32)


def solution(mesh):
    in_specs = (
        P("blk", None),
        P(),
        P(),
        P(None, None, "head"),
        P("head", None),
        P(None, "head"),
        P("head", None),
        P(None, "head"),
        P(),
        P("blk", None, "head"),
        P("blk", None, "head"),
        P(),
        P("blk"),
        P("blk"),
    )
    out_specs = P("blk", "head")
    return jax.shard_map(
        per_device, mesh=mesh, in_specs=in_specs, out_specs=out_specs, check_vma=False
    )
```

```python
import functools

import jax
import jax.numpy as jnp
from jax import lax
from jax.experimental import pallas as pl
from jax.experimental.pallas import tpu as pltpu
from jax.sharding import PartitionSpec as P

HEAD_DIM = 64
PAGE = 128
LANES = 128

far_below = -1e30
epsilon = 1e-06

VMEM_SPEC = pl.BlockSpec(memory_space=pltpu.VMEM)
SMEM_SPEC = pl.BlockSpec(memory_space=pltpu.SMEM)
ANY_SPEC = pl.BlockSpec(memory_space=pl.ANY)
HBM_SPEC = pl.BlockSpec(memory_space=pltpu.HBM)
PARAMS = pltpu.CompilerParams(vmem_limit_bytes=16 * 1024 * 1024)

PIECE = 8
SUM_LANE = 3 * PIECE


def iota(shape, axis):
    return lax.broadcasted_iota(jnp.int32, shape, axis)


def split_index(x, size):
    if size & (size - 1):
        return lax.div(x, size), lax.rem(x, size)
    return x >> (size.bit_length() - 1), x & (size - 1)


def head_of(shape, axis):
    return split_index(iota(shape, axis), HEAD_DIM)[0]


def pieces(x, count):
    parts = []
    for _ in range(count):
        part = x.astype(jnp.bfloat16)
        parts.append(part)
        x = x - part.astype(jnp.float32)
    return parts


def rms_normed(x, gain):
    scale = lax.rsqrt(jnp.mean(x * x, axis=1, keepdims=True) + epsilon)
    return (x * scale * gain).astype(jnp.bfloat16)


def dot(a, b, dims=((1,), (0,)), precision=None):
    return lax.dot_general(
        a, b, (dims, ((), ())), preferred_element_type=jnp.float32, precision=precision
    )


def split_copies(source, target, sems, count):
    size = source.shape[0] // count
    return [
        pltpu.make_async_copy(
            source.at[pl.ds(i * size, size)], target.at[pl.ds(i * size, size)], sems.at[i]
        )
        for i in range(count)
    ]


def query_kernel(hidden_hbm, gain_hbm, weight_hbm, query_ref, hidden, gain, weight, sems):
    model = hidden.shape[1]
    small = [
        pltpu.make_async_copy(hidden_hbm, hidden, sems.at[0]),
        pltpu.make_async_copy(gain_hbm, gain, sems.at[1]),
    ]
    half = model // 4
    large = [
        pltpu.make_async_copy(
            weight_hbm.at[0, pl.ds(i * half, half)], weight.at[pl.ds(i * half, half)], sems.at[2 + i]
        )
        for i in range(4)
    ]
    for copy in small + large:
        copy.start()
    for copy in small:
        copy.wait()
    normed = rms_normed(hidden[...], gain[...])
    query = None
    for i, copy in enumerate(large):
        copy.wait()
        span = slice(i * half, (i + 1) * half)
        part = dot(normed[:, span], weight[span])
        query = part if query is None else query + part
    query_ref[...] = query.astype(jnp.bfloat16)


def page_kernel(
    own_rows, inner, outer, query_ref, request_ref, keys_hbm,
    keys_ref, pick_ref, place_ref, lead_ref, apart_ref, owners_ref,
    sems,
):
    copies = split_copies(
        keys_hbm.at[pl.ds(0, keys_ref.shape[0])], keys_ref, sems, sems.shape[0]
    )
    for copy in copies:
        copy.start()
    me = lax.axis_index("blk")
    page_count = apart_ref.shape[0]
    all_rows, depth = place_ref.shape
    page, lane = iota((page_count, page_count), 0), iota((page_count, page_count), 1)
    by_lane = request_ref[...]
    owner = jnp.max(jnp.where(page == lane, by_lane, -1), axis=1, keepdims=True)
    same = by_lane == owner
    apart_ref[...] = jnp.full(apart_ref.shape, 2 * far_below, jnp.float32)
    apart_ref[:, :page_count] = jnp.where(same, 0.0, 2 * far_below)
    earlier = jnp.max(jnp.where(same & (lane < page), 1, 0), axis=1, keepdims=True)
    lead_ref[...] = jnp.broadcast_to(jnp.where(earlier == 0, 1.0, 0.0), lead_ref.shape)
    owners_ref[...] = jnp.broadcast_to(owner, owners_ref.shape)
    device, own_row = split_index(jnp.maximum(owner, 0), own_rows)
    high, low = split_index(device ^ me, inner)
    high_at, low_at = -high & (outer - 1), -low & (inner - 1)
    slot = (low_at * outer + high_at) * own_rows + own_row
    slot = jnp.where(owner >= 0, slot, -1)
    pair, member = split_index(low, 2)[0], split_index(device, 2)[1]
    sum_slot = ((pair * outer + high) * 2 + member) * own_rows + own_row
    sum_slot = jnp.where(owner >= 0, sum_slot, -1)
    row_of = iota((page_count, all_rows), 1)
    picks = jnp.where(row_of == slot, 1.0, 0.0)
    picks = [jnp.broadcast_to(picks[p : p + 1], (PIECE, all_rows)) for p in range(page_count)]
    pick_ref[...] = jnp.concatenate(picks, axis=0).astype(jnp.bfloat16)
    mine = split_index(iota((page_count, depth), 1), PIECE)[0] == iota((page_count, depth), 0)
    row = iota((all_rows, depth), 0)
    spread = jnp.max(jnp.where(mine, sum_slot, -1), axis=0, keepdims=True)
    place_ref[...] = (row == spread).astype(jnp.bfloat16)
    for copy in copies:
        copy.wait()


def bias_kernel(
    table_hbm, edges_hbm, lengths_hbm, index_hbm, owners_ref, keys_hbm, after_ref,
    keys_ref, bias_ref,
    table, edges, lengths, index, small_sems, sems,
):
    sources, targets = (table_hbm, edges_hbm, lengths_hbm, index_hbm), (table, edges, lengths, index)
    small = [
        pltpu.make_async_copy(source, target, small_sems.at[i])
        for i, (source, target) in enumerate(zip(sources, targets))
    ]
    late = keys_ref.shape[0]
    copies = split_copies(
        keys_hbm.at[pl.ds(keys_hbm.shape[0] - late, late)], keys_ref, sems, sems.shape[0]
    )
    for copy in small + copies:
        copy.start()
    for copy in small:
        copy.wait()
    heads, buckets = table.shape
    page_count = index.shape[1]
    owner = owners_ref[:, 0:1]
    square = (page_count, page_count)
    number = jnp.where(iota(square, 0) == iota(square, 1), index[...], 0)
    number = jnp.sum(number, axis=1, keepdims=True)
    requests = lengths.shape[1]
    length = jnp.where(iota((page_count, requests), 1) == owner, lengths[...], 0)
    length = jnp.sum(length, axis=1, keepdims=True)
    distance = length - number * PAGE - iota((page_count, PAGE), 1)
    far = [distance >= edges[k] for k in range(buckets - 1)]
    usable = (owner >= 0) & (distance > 0)
    bias_ref[...] = jnp.full(bias_ref.shape, far_below, jnp.float32)
    for h in range(heads):
        bias = jnp.full((page_count, PAGE), table[h, 0], jnp.float32)
        for k in range(buckets - 1):
            bias = jnp.where(far[k], table[h, k + 1], bias)
        bias_ref[pl.ds(h, page_count, stride=PIECE), :] = jnp.where(usable, bias, far_below)
    for copy in copies:
        copy.wait()


def side_kernel(
    sibling_ref, hidden_ref, gain_ref, sibling_query_ref, query_ref, table_ref,
    weight_hbm, out_hbm, after_ref,
    score_ref, value_ref, out_ref,
    weight, weight_sems, sems,
):
    copies = [
        pltpu.make_async_copy(weight_hbm.at[1 + i], weight.at[i], weight_sems.at[i])
        for i in range(2)
    ]
    later = split_copies(out_hbm, out_ref, sems, sems.shape[0])
    for copy in copies + later:
        copy.start()
    both = jnp.concatenate([sibling_ref[...], hidden_ref[...]], axis=0)
    normed = rms_normed(both, gain_ref[...])
    query = [ref[...].astype(jnp.float32) for ref in (sibling_query_ref, query_ref)]
    query = jnp.concatenate(query, axis=0)
    heads = table_ref.shape[0]
    spread = iota((heads, LANES), 0) == iota((heads, LANES), 1)
    score = jnp.sum(jnp.where(spread, table_ref[:, 0:1], 0.0), axis=0, keepdims=True)
    copies[0].wait()
    key = dot(normed, weight[0]).astype(jnp.bfloat16)
    product = query * key.astype(jnp.float32)
    width = product.shape[1]
    gather = (head_of((width, LANES), 0) == iota((width, LANES), 1)).astype(jnp.bfloat16)
    for part in pieces(product, 3):
        score = score + dot(part, gather)
    score_ref[...] = score
    copies[1].wait()
    value_ref[...] = dot(normed, weight[1]).astype(jnp.bfloat16)
    for copy in later:
        copy.wait()


def load_kernel(start, source, after_ref, target, sems):
    rows = source.at[pl.ds(start, target.shape[0])]
    copies = split_copies(rows, target, sems, sems.shape[0])
    for copy in copies:
        copy.start()
    for copy in copies:
        copy.wait()


def packed_stats(peaks, sums):
    one, two, three = (part.astype(jnp.float32) for part in pieces(peaks + sums, 3))
    packed = one + pltpu.roll(two, PIECE, 1) + pltpu.roll(three, 2 * PIECE, 1)
    return packed.astype(jnp.bfloat16)


def unpacked_stats(packed, heads):
    stats = packed.astype(jnp.float32)
    stats = stats + pltpu.roll(stats, LANES - PIECE, 1) + pltpu.roll(stats, LANES - 2 * PIECE, 1)
    sums = pltpu.roll(stats, LANES - SUM_LANE, 1)
    used = iota(stats.shape, 1) < heads
    return jnp.where(used & (sums > 0.0), stats, far_below), jnp.where(used, sums, 0.0)


def over_columns(values, width):
    spread = (iota((LANES, width), 0) == head_of((LANES, width), 1)).astype(jnp.bfloat16)
    return sum(dot(part, spread) for part in pieces(values, 3))


def attend_kernel(groups, messages, *refs):
    query_refs, refs = refs[:groups], refs[groups:]
    *refs, sibling_query_ref = refs
    refs, sums_refs = refs[:-messages], refs[-messages:]
    sibling_query = query_refs[-1][...].astype(jnp.float32)[: sibling_query_ref.shape[0]]
    sibling_query_ref[...] = sibling_query.astype(jnp.bfloat16)
    bias_ref, pick_ref, place_ref, lead_ref, apart_ref, keys_ref, late_ref, values_ref = refs
    page_count = apart_ref.shape[0]
    width = keys_ref.shape[2]
    early = keys_ref.shape[0]
    chunk = 2
    chunks = page_count // chunk
    queries = jnp.concatenate([ref[...] for ref in query_refs], axis=0)
    own_head = (head_of((PIECE, width), 1) == iota((PIECE, width), 0)).astype(jnp.float32)
    pair_heads = jnp.concatenate([own_head] * chunk, axis=0)
    chosen = dot(pick_ref[...], queries)
    lane = iota((PIECE, LANES), 1)
    row = iota((PIECE, LANES), 0)
    nothing = jnp.zeros((PIECE, PAGE), jnp.float32)
    raws = []
    for c in range(chunks):
        rows = chosen[c * chunk * PIECE : (c + 1) * chunk * PIECE]
        split = (rows * pair_heads).astype(jnp.bfloat16)
        at = c * chunk
        block = keys_ref[at : at + chunk] if at < early else late_ref[at - early : at - early + chunk]
        raws.append(dot(split, block.reshape(chunk * PAGE, width), ((1,), (1,))))
    scores, page_tops = [], []
    for p in range(page_count):
        i = p % chunk
        part = raws[p // chunk][i * PIECE : (i + 1) * PIECE, i * PAGE : (i + 1) * PAGE]
        score = part + bias_ref[p * PIECE : (p + 1) * PIECE]
        scores.append(score)
        page_tops.append(jnp.max(score, axis=1, keepdims=True))
    page_weights = [jnp.exp(score - top) for score, top in zip(scores, page_tops)]
    mixes = []
    for c in range(chunks):
        blocks = []
        for i in range(chunk):
            weight = page_weights[c * chunk + i]
            blocks.append(
                jnp.concatenate([weight if k == i else nothing for k in range(chunk)], axis=1)
            )
        weights = jnp.concatenate(blocks, axis=0).astype(jnp.bfloat16)
        block = values_ref[c * chunk : (c + 1) * chunk]
        mixes.append(dot(weights, block.reshape(chunk * PAGE, width)))
    totals = [jnp.sum(weight, axis=1, keepdims=True) for weight in page_weights]
    tops = jnp.zeros((PIECE, LANES), jnp.float32)
    for p in range(page_count):
        tops = jnp.where(lane == p, page_tops[p], tops)
    stats = []
    for c in range(chunks):
        factors = []
        for p in range(c * chunk, (c + 1) * chunk):
            peak = jnp.max(tops + apart_ref[p : p + 1], axis=1, keepdims=True)
            factor = jnp.exp(page_tops[p] - peak)
            total = jnp.where(lane == row + SUM_LANE, totals[p] * factor, 0.0)
            stats.append(jnp.where(lane == row, peak * lead_ref[p : p + 1], total))
            factors.append(factor)
        mixes[c] = mixes[c] * (pair_heads * jnp.concatenate(factors, axis=0))
    mix = jnp.concatenate(mixes, axis=0).astype(jnp.bfloat16)
    stats = pieces(jnp.concatenate(stats, axis=0), 3)
    sums = dot(place_ref[...], jnp.concatenate([mix] + stats, axis=1))
    stats = sum(sums[:, width + i * LANES : width + (i + 1) * LANES] for i in range(3))
    stats = packed_stats(stats, 0.0).astype(jnp.float32)
    size = sums.shape[0] // messages
    for i, sums_ref in enumerate(sums_refs):
        first, middle, last = i * size, i * size + size // 2, (i + 1) * size
        for c in range(width // LANES):
            block = sums[first:last, c * LANES : (c + 1) * LANES]
            sums_ref[c * size : (c + 1) * size] = block.astype(jnp.bfloat16)
        both = stats[first:middle] + pltpu.roll(stats[middle:last], LANES // 2, 1)
        sums_ref[width // LANES * size :] = both.astype(jnp.bfloat16)


def combine_kernel(sources, *refs):
    part_refs, sums_refs = refs[:sources], refs[sources:]
    width = sums_refs[0].shape[1] - LANES
    rows = sum(ref.shape[0] for ref in sums_refs)
    heads, blocks = width // HEAD_DIM, width // LANES
    stats, mixes = [], []
    for ref in part_refs:
        both = ref[blocks * rows :].astype(jnp.float32)
        both = jnp.concatenate([both, pltpu.roll(both, LANES // 2, 1)], axis=0)
        stats.append(unpacked_stats(both, heads))
        mix = [ref[c * rows : (c + 1) * rows] for c in range(blocks)]
        mixes.append(jnp.concatenate(mix, axis=1).astype(jnp.float32))
    peak = stats[0][0]
    for peaks, _ in stats[1:]:
        peak = jnp.maximum(peak, peaks)
    factors = [jnp.exp(peaks - peak) for peaks, _ in stats]
    total = sum(factor * sums for factor, (_, sums) in zip(factors, stats))
    shares = over_columns(jnp.concatenate(factors, axis=0), width)
    mixed = sum(mix * shares[i * rows : (i + 1) * rows] for i, mix in enumerate(mixes))
    packed = packed_stats(
        jnp.where(total > 0.0, peak, 0.0), pltpu.roll(total, SUM_LANE, 1)
    ).astype(jnp.float32)
    size = sums_refs[0].shape[0]
    for i, sums_ref in enumerate(sums_refs):
        span = slice(i * size, (i + 1) * size)
        sums_ref[:, :width] = mixed[span].astype(jnp.bfloat16)
        sums_ref[:, width:] = packed[span].astype(jnp.bfloat16)


def merge_kernel(sources, *refs):
    part_refs, (score_ref, value_ref, weight_ref, own_ref, send_ref) = refs[:sources], refs[sources:]
    own_rows, width = value_ref.shape
    heads = width // HEAD_DIM
    stats = [unpacked_stats(ref[:, width:], heads) for ref in part_refs]
    own_score = jnp.where(iota(score_ref.shape, 1) < heads, score_ref[...], 0.0)
    peak = own_score
    for peaks, _ in stats:
        peak = jnp.maximum(peak, peaks)
    own_weight = jnp.exp(own_score - peak)
    total = own_weight
    factors = []
    for peaks, sums in stats:
        factor = jnp.exp(peaks - peak)
        total = total + factor * sums
        factors.append(factor)
    factors.append(own_weight.astype(jnp.bfloat16).astype(jnp.float32))
    shares = jnp.concatenate([factor / total for factor in factors], axis=0)
    shares = over_columns(shares, width)
    mixed = value_ref[...].astype(jnp.float32) * shares[sources * own_rows :]
    for i, ref in enumerate(part_refs):
        rows = slice(i * own_rows, (i + 1) * own_rows)
        mixed = mixed + ref[:, :width].astype(jnp.float32) * shares[rows]
    projected = dot(mixed.astype(jnp.bfloat16), weight_ref[...])
    own_ref[...] = projected
    send_ref[...] = projected.astype(jnp.bfloat16)


def mlp_kernel(
    exchanged, sibling_ref, hidden_ref, own_ref, other_ref, gain_ref, up_ref, down_ref, late_ref,
    *outs,
):
    both = jnp.concatenate([sibling_ref[...], hidden_ref[...]], axis=0)
    middle = both + (own_ref[...] + other_ref[...].astype(jnp.float32))
    normed = rms_normed(middle, gain_ref[...])
    active = jnp.maximum(dot(normed, up_ref[...]), 0.0).astype(jnp.bfloat16)
    half = down_ref.shape[0]
    down = dot(active[:, :half], down_ref[...]) + dot(active[:, half:], late_ref[...])
    if exchanged:
        own_rows, columns = outs[0].shape
        low = lax.axis_index("head") == 0
        left, right = slice(0, columns), slice(columns, 2 * columns)
        kept = middle + down

        def give(mine, theirs):
            for i in range(2):
                span = slice(i * own_rows, (i + 1) * own_rows)
                outs[2 * i][...] = kept[span, mine]
                outs[2 * i + 1][...] = down[span, theirs].astype(jnp.bfloat16)

        @pl.when(low)
        def _():
            give(left, right)

        @pl.when(jnp.logical_not(low))
        def _():
            give(right, left)

    else:
        middle_ref, down_out_ref = outs
        middle_ref[...] = middle
        down_out_ref[...] = down.astype(jnp.bfloat16)


def loading(*arrays):
    return pl.CostEstimate(
        flops=0, bytes_accessed=sum(2 * array.size for array in arrays), transcendentals=0
    )


def in_hbm(*arrays):
    return [pltpu.with_memory_space_constraint(array, pltpu.HBM) for array in arrays]


def xor_pairs(size, step):
    return [(i, i ^ step) for i in range(size)]


def to_odd(size, step):
    return [(i, i ^ step) for i in range(size) if (i ^ step) & 1]


def per_device(
    hidden_in, attention_gain, mlp_gain, qkv_weight, out_weight, up_weight, down_weight,
    position_bias, bucket_edges, cache_keys, cache_values, lengths, page_request, page_index,
):
    f32, bf16 = jnp.float32, jnp.bfloat16
    shape = jax.ShapeDtypeStruct
    own_rows, model = hidden_in.shape
    width = qkv_weight.shape[2]
    page_count = page_request.shape[0]
    blocks = lax.axis_size("blk")
    all_rows = own_rows * blocks
    gain = attention_gain.reshape(1, model)
    query, hidden = pl.pallas_call(
        query_kernel,
        out_shape=(shape((own_rows, width), bf16), pltpu.VMEM((own_rows, model), f32)),
        in_specs=[HBM_SPEC] * 3,
        out_specs=(VMEM_SPEC,) * 2,
        scratch_shapes=[
            pltpu.VMEM((1, model), f32),
            pltpu.VMEM((model, width), bf16),
            pltpu.SemaphoreType.DMA((6,)),
        ],
        compiler_params=PARAMS,
        name="query",
    )(*in_hbm(hidden_in, gain, qkv_weight))

    inner = 1
    while inner * inner < blocks:
        inner *= 2
    far = [query] + [
        lax.ppermute(query, "blk", xor_pairs(blocks, step * inner))
        for step in reversed(range(1, blocks // inner))
    ]
    depth = page_count * PIECE
    early = page_count // 6 * 2
    keys, picks, place, leads, apart, owners = pl.pallas_call(
        functools.partial(page_kernel, own_rows, inner, blocks // inner),
        out_shape=(
            pltpu.VMEM((early,) + cache_keys.shape[1:], bf16),
            shape((depth, all_rows), bf16),
            shape((all_rows, depth), bf16),
            shape((page_count, LANES), f32),
            shape((page_count, LANES), f32),
            shape((page_count, LANES), jnp.int32),
        ),
        in_specs=[ANY_SPEC, VMEM_SPEC, HBM_SPEC],
        out_specs=(VMEM_SPEC,) * 6,
        scratch_shapes=[pltpu.SemaphoreType.DMA((4,))],
        compiler_params=PARAMS,
        cost_estimate=loading(cache_keys),
        name="pages",
    )(query, page_request.reshape(1, page_count), *in_hbm(cache_keys))
    near, apart, own_hidden = lax.optimization_barrier(
        (jnp.concatenate(far, axis=0), apart, hidden)
    )
    gathered = [near] + [
        lax.ppermute(near, "blk", xor_pairs(blocks, step)) for step in reversed(range(1, inner))
    ]
    table = position_bias.T
    sibling = lax.ppermute(own_hidden, "blk", to_odd(blocks, 1))
    late_keys, bias = pl.pallas_call(
        bias_kernel,
        out_shape=(
            pltpu.VMEM((page_count - early,) + cache_keys.shape[1:], bf16),
            shape((depth, PAGE), f32),
        ),
        in_specs=[HBM_SPEC] * 4 + [VMEM_SPEC, HBM_SPEC, ANY_SPEC],
        out_specs=(VMEM_SPEC,) * 2,
        scratch_shapes=[
            pltpu.SMEM(table.shape, f32),
            pltpu.SMEM(bucket_edges.shape, jnp.int32),
            pltpu.VMEM((1,) + lengths.shape, jnp.int32),
            pltpu.VMEM((1,) + page_index.shape, jnp.int32),
            pltpu.SemaphoreType.DMA((4,)),
            pltpu.SemaphoreType.DMA((4,)),
        ],
        compiler_params=PARAMS,
        cost_estimate=loading(cache_values),
        name="bias",
    )(
        *in_hbm(table, bucket_edges, lengths[None], page_index[None]), owners,
        *in_hbm(cache_keys), near,
    )

    bias, sibling = lax.optimization_barrier((bias, sibling))
    groups = len(gathered)
    messages = inner // 2
    size = all_rows // messages
    message = width // LANES * size + size // 2
    *sums, sibling_query = pl.pallas_call(
        functools.partial(attend_kernel, groups, messages),
        out_shape=(shape((message, LANES), bf16),) * messages + (shape(query.shape, bf16),),
        in_specs=[VMEM_SPEC] * (groups + 8),
        out_specs=(VMEM_SPEC,) * (messages + 1),
        compiler_params=PARAMS,
        name="attend",
    )(*gathered, bias, picks, place, leads, apart, keys, late_keys, cache_values)
    near_sums = [sums[0]] + [
        lax.ppermute(sums[step // 2], "blk", to_odd(blocks, step))
        for step in reversed(range(1, inner))
    ]

    own_score, value_new, out_near = pl.pallas_call(
        side_kernel,
        out_shape=(
            shape((2 * own_rows, LANES), f32),
            shape((2 * own_rows, width), bf16),
            pltpu.VMEM(out_weight.shape, bf16),
        ),
        in_specs=[VMEM_SPEC] * 6 + [HBM_SPEC] * 2 + [ANY_SPEC],
        out_specs=(VMEM_SPEC,) * 3,
        scratch_shapes=[
            pltpu.VMEM((2, model, width), bf16),
            pltpu.SemaphoreType.DMA((2,)),
            pltpu.SemaphoreType.DMA((4,)),
        ],
        compiler_params=PARAMS,
        cost_estimate=loading(out_weight, out_weight, out_weight),
        name="side",
    )(
        sibling, hidden, gain, sibling_query, query, table,
        *in_hbm(qkv_weight, out_weight), sums[0],
    )

    *near_sums, own_score = lax.optimization_barrier((*near_sums, own_score))
    outer = blocks // inner
    sums = pl.pallas_call(
        functools.partial(combine_kernel, inner),
        out_shape=(shape((2 * own_rows, width + LANES), bf16),) * outer,
        in_specs=[VMEM_SPEC] * inner,
        out_specs=(VMEM_SPEC,) * outer,
        compiler_params=PARAMS,
        name="combine",
    )(*near_sums)
    half = down_weight.shape[0] // 2

    def load_down(start, after):
        return pl.pallas_call(
            functools.partial(load_kernel, start),
            out_shape=pltpu.VMEM((half, model), bf16),
            in_specs=[HBM_SPEC, ANY_SPEC],
            out_specs=VMEM_SPEC,
            scratch_shapes=[pltpu.SemaphoreType.DMA((4,))],
            compiler_params=PARAMS,
            cost_estimate=loading(down_weight),
            name="load",
        )(*in_hbm(down_weight), after)

    down_early = load_down(0, sums[0])
    parts = [sums[0]] + [
        lax.ppermute(sums[step], "blk", to_odd(blocks, step * inner))
        for step in reversed(range(1, outer))
    ]

    *parts, down_early = lax.optimization_barrier((*parts, down_early))
    own_part, sent_part = pl.pallas_call(
        functools.partial(merge_kernel, outer),
        out_shape=(shape((2 * own_rows, model), f32), shape((2 * own_rows, model), bf16)),
        in_specs=[VMEM_SPEC] * (outer + 3),
        out_specs=(VMEM_SPEC,) * 2,
        compiler_params=PARAMS,
        name="merge",
    )(*parts, own_score, value_new, out_near)

    halves = lax.axis_size("head")
    columns = model // halves
    exchanged = halves == 2
    down_late = load_down(half, sent_part)
    if exchanged:
        axes = ("head", "blk")
        everyone = [(h, i) for h in range(2) for i in range(blocks)]

        def flat(h, i):
            return h * blocks + i

        def from_odd(swap, step):
            return [
                (flat(h, i), flat(h ^ swap, i ^ step)) for h, i in everyone if i & 1
            ]

        other_part = lax.ppermute(sent_part, axes, from_odd(1, 0))
        mlp_out = (shape((own_rows, columns), f32), shape((own_rows, columns), bf16)) * 2
    else:
        own_part = jnp.zeros_like(own_part)
        other_part = lax.psum(sent_part, "head")
        mlp_out = (shape((2 * own_rows, model), f32), shape((2 * own_rows, model), bf16))

    outs = pl.pallas_call(
        functools.partial(mlp_kernel, exchanged),
        out_shape=mlp_out,
        in_specs=[VMEM_SPEC] * 8,
        out_specs=(VMEM_SPEC,) * len(mlp_out),
        compiler_params=PARAMS,
        name="mlp",
    )(
        sibling, hidden, own_part, other_part, mlp_gain.reshape(1, model),
        up_weight, down_early, down_late,
    )

    odd = lax.axis_index("blk") & 1 == 1
    if exchanged:
        sibling_kept, sibling_leaving, kept, leaving = outs
        far_part = lax.ppermute(sibling_leaving, axes, from_odd(1, 1))
        near_part = lax.ppermute(sibling_kept, axes, from_odd(0, 1))
        arrived = lax.ppermute(leaving, axes, from_odd(1, 0))
        kept = jnp.where(odd, kept, near_part)
        return kept + jnp.where(jnp.logical_not(odd), far_part, arrived).astype(f32)
    middle, leaving = outs
    middle = lax.dynamic_slice_in_dim(middle, lax.axis_index("head") * columns, columns, 1)
    arrived = lax.psum_scatter(leaving, "head", scatter_dimension=1, tiled=True)
    both = middle + arrived.astype(f32)
    near_part = lax.ppermute(both[:own_rows], "blk", xor_pairs(blocks, 1))
    return jnp.where(odd, both[own_rows:], near_part)


def solution(mesh):
    in_specs = (
        P("blk", None),
        P(),
        P(),
        P(None, None, "head"),
        P("head", None),
        P(None, "head"),
        P("head", None),
        P(None, "head"),
        P(),
        P("blk", None, "head"),
        P("blk", None, "head"),
        P(),
        P("blk"),
        P("blk"),
    )
    out_specs = P("blk", "head")
    return jax.shard_map(
        per_device, mesh=mesh, in_specs=in_specs, out_specs=out_specs, check_vma=False
    )
```

```python
import functools

import jax
import jax.numpy as jnp
from jax import lax
from jax.experimental import pallas as pl
from jax.experimental.pallas import tpu as pltpu
from jax.sharding import PartitionSpec as P

HEAD_DIM = 64
PAGE = 128
LANES = 128

far_below = -1e30
epsilon = 1e-06

VMEM_SPEC = pl.BlockSpec(memory_space=pltpu.VMEM)
SMEM_SPEC = pl.BlockSpec(memory_space=pltpu.SMEM)
ANY_SPEC = pl.BlockSpec(memory_space=pl.ANY)
HBM_SPEC = pl.BlockSpec(memory_space=pltpu.HBM)
PARAMS = pltpu.CompilerParams(vmem_limit_bytes=16 * 1024 * 1024)

PIECE = 8
SUM_LANE = 3 * PIECE


def iota(shape, axis):
    return lax.broadcasted_iota(jnp.int32, shape, axis)


def split_index(x, size):
    if size & (size - 1):
        return lax.div(x, size), lax.rem(x, size)
    return x >> (size.bit_length() - 1), x & (size - 1)


def head_of(shape, axis):
    return split_index(iota(shape, axis), HEAD_DIM)[0]


def pieces(x, count):
    parts = []
    for _ in range(count):
        part = x.astype(jnp.bfloat16)
        parts.append(part)
        x = x - part.astype(jnp.float32)
    return parts


def rms_normed(x, gain):
    scale = lax.rsqrt(jnp.mean(x * x, axis=1, keepdims=True) + epsilon)
    return (x * scale * gain).astype(jnp.bfloat16)


def dot(a, b, dims=((1,), (0,)), precision=None):
    return lax.dot_general(
        a, b, (dims, ((), ())), preferred_element_type=jnp.float32, precision=precision
    )


def split_copies(source, target, sems, count):
    size = source.shape[0] // count
    return [
        pltpu.make_async_copy(
            source.at[pl.ds(i * size, size)], target.at[pl.ds(i * size, size)], sems.at[i]
        )
        for i in range(count)
    ]


def query_kernel(hidden_hbm, gain_hbm, weight_hbm, query_ref, hidden, gain, weight, sems):
    model = hidden.shape[1]
    small = [
        pltpu.make_async_copy(hidden_hbm, hidden, sems.at[0]),
        pltpu.make_async_copy(gain_hbm, gain, sems.at[1]),
    ]
    half = model // 4
    large = [
        pltpu.make_async_copy(
            weight_hbm.at[0, pl.ds(i * half, half)], weight.at[pl.ds(i * half, half)], sems.at[2 + i]
        )
        for i in range(4)
    ]
    for copy in small + large:
        copy.start()
    for copy in small:
        copy.wait()
    normed = rms_normed(hidden[...], gain[...])
    query = None
    for i, copy in enumerate(large):
        copy.wait()
        span = slice(i * half, (i + 1) * half)
        part = dot(normed[:, span], weight[span])
        query = part if query is None else query + part
    query_ref[...] = query.astype(jnp.bfloat16)


def page_kernel(
    own_rows, inner, outer, query_ref, request_ref, keys_hbm,
    keys_ref, pick_ref, place_ref, lead_ref, apart_ref, owners_ref,
    sems,
):
    copies = split_copies(
        keys_hbm.at[pl.ds(0, keys_ref.shape[0])], keys_ref, sems, sems.shape[0]
    )
    for copy in copies:
        copy.start()
    me = lax.axis_index("blk")
    page_count = apart_ref.shape[0]
    all_rows, depth = place_ref.shape
    page, lane = iota((page_count, page_count), 0), iota((page_count, page_count), 1)
    by_lane = request_ref[...]
    owner = jnp.max(jnp.where(page == lane, by_lane, -1), axis=1, keepdims=True)
    same = by_lane == owner
    apart_ref[...] = jnp.full(apart_ref.shape, 2 * far_below, jnp.float32)
    apart_ref[:, :page_count] = jnp.where(same, 0.0, 2 * far_below)
    earlier = jnp.max(jnp.where(same & (lane < page), 1, 0), axis=1, keepdims=True)
    lead_ref[...] = jnp.broadcast_to(jnp.where(earlier == 0, 1.0, 0.0), lead_ref.shape)
    owners_ref[...] = jnp.broadcast_to(owner, owners_ref.shape)
    device, own_row = split_index(jnp.maximum(owner, 0), own_rows)
    high, low = split_index(device ^ me, inner)
    low = jnp.where(high == 0, low, low ^ 1)
    slot = (low * outer + high) * own_rows + own_row
    slot = jnp.where(owner >= 0, slot, -1)
    row_of = iota((page_count, all_rows), 1)
    picks = jnp.where(row_of == slot, 1.0, 0.0)
    picks = [jnp.broadcast_to(picks[p : p + 1], (PIECE, all_rows)) for p in range(page_count)]
    pick_ref[...] = jnp.concatenate(picks, axis=0).astype(jnp.bfloat16)
    mine = split_index(iota((page_count, depth), 1), PIECE)[0] == iota((page_count, depth), 0)
    row = iota((all_rows, depth), 0)
    spread = jnp.max(jnp.where(mine, slot, -1), axis=0, keepdims=True)
    place_ref[...] = (row == spread).astype(jnp.bfloat16)
    for copy in copies:
        copy.wait()


def bias_kernel(
    table_hbm, edges_hbm, lengths_hbm, index_hbm, owners_ref, keys_hbm, after_ref,
    keys_ref, bias_ref,
    table, edges, lengths, index, small_sems, sems,
):
    sources, targets = (table_hbm, edges_hbm, lengths_hbm, index_hbm), (table, edges, lengths, index)
    small = [
        pltpu.make_async_copy(source, target, small_sems.at[i])
        for i, (source, target) in enumerate(zip(sources, targets))
    ]
    late = keys_ref.shape[0]
    copies = split_copies(
        keys_hbm.at[pl.ds(keys_hbm.shape[0] - late, late)], keys_ref, sems, sems.shape[0]
    )
    for copy in small + copies:
        copy.start()
    for copy in small:
        copy.wait()
    heads, buckets = table.shape
    page_count = index.shape[1]
    owner = owners_ref[:, 0:1]
    square = (page_count, page_count)
    number = jnp.where(iota(square, 0) == iota(square, 1), index[...], 0)
    number = jnp.sum(number, axis=1, keepdims=True)
    requests = lengths.shape[1]
    length = jnp.where(iota((page_count, requests), 1) == owner, lengths[...], 0)
    length = jnp.sum(length, axis=1, keepdims=True)
    distance = length - number * PAGE - iota((page_count, PAGE), 1)
    far = [distance >= edges[k] for k in range(buckets - 1)]
    usable = (owner >= 0) & (distance > 0)
    bias_ref[...] = jnp.full(bias_ref.shape, far_below, jnp.float32)
    for h in range(heads):
        bias = jnp.full((page_count, PAGE), table[h, 0], jnp.float32)
        for k in range(buckets - 1):
            bias = jnp.where(far[k], table[h, k + 1], bias)
        bias_ref[pl.ds(h, page_count, stride=PIECE), :] = jnp.where(usable, bias, far_below)
    for copy in copies:
        copy.wait()


def side_kernel(
    hidden_ref, gain_ref, query_ref, table_ref, weight_hbm, out_hbm, after_ref,
    score_ref, value_ref, out_ref,
    weight, weight_sems, sems,
):
    copies = [
        pltpu.make_async_copy(weight_hbm.at[1 + i], weight.at[i], weight_sems.at[i])
        for i in range(2)
    ]
    later = split_copies(out_hbm, out_ref, sems, sems.shape[0])
    for copy in copies + later:
        copy.start()
    normed = rms_normed(hidden_ref[...], gain_ref[...])
    heads = table_ref.shape[0]
    spread = iota((heads, LANES), 0) == iota((heads, LANES), 1)
    score = jnp.sum(jnp.where(spread, table_ref[:, 0:1], 0.0), axis=0, keepdims=True)
    copies[0].wait()
    key = dot(normed, weight[0]).astype(jnp.bfloat16)
    product = query_ref[...].astype(jnp.float32) * key.astype(jnp.float32)
    width = product.shape[1]
    gather = (head_of((width, LANES), 0) == iota((width, LANES), 1)).astype(jnp.bfloat16)
    for part in pieces(product, 3):
        score = score + dot(part, gather)
    score_ref[...] = score
    copies[1].wait()
    value_ref[...] = dot(normed, weight[1]).astype(jnp.bfloat16)
    for copy in later:
        copy.wait()


def load_kernel(start, source, after_ref, target, sems):
    rows = source.at[pl.ds(start, target.shape[0])]
    copies = split_copies(rows, target, sems, sems.shape[0])
    for copy in copies:
        copy.start()
    for copy in copies:
        copy.wait()


def packed_stats(peaks, sums):
    one, two, three = (part.astype(jnp.float32) for part in pieces(peaks + sums, 3))
    packed = one + pltpu.roll(two, PIECE, 1) + pltpu.roll(three, 2 * PIECE, 1)
    return packed.astype(jnp.bfloat16)


def unpacked_stats(packed, heads):
    stats = packed.astype(jnp.float32)
    stats = stats + pltpu.roll(stats, LANES - PIECE, 1) + pltpu.roll(stats, LANES - 2 * PIECE, 1)
    sums = pltpu.roll(stats, LANES - SUM_LANE, 1)
    used = iota(stats.shape, 1) < heads
    return jnp.where(used & (sums > 0.0), stats, far_below), jnp.where(used, sums, 0.0)


def over_columns(values, width):
    spread = (iota((LANES, width), 0) == head_of((LANES, width), 1)).astype(jnp.bfloat16)
    return sum(dot(part, spread) for part in pieces(values, 3))


def attend_kernel(groups, *refs):
    query_refs, refs, sums_refs = refs[:groups], refs[groups:-groups], refs[-groups:]
    bias_ref, pick_ref, place_ref, lead_ref, apart_ref, keys_ref, late_ref, values_ref = refs
    page_count = apart_ref.shape[0]
    width = keys_ref.shape[2]
    early = keys_ref.shape[0]
    chunk = 2
    chunks = page_count // chunk
    queries = jnp.concatenate([ref[...] for ref in query_refs], axis=0)
    own_head = (head_of((PIECE, width), 1) == iota((PIECE, width), 0)).astype(jnp.float32)
    pair_heads = jnp.concatenate([own_head] * chunk, axis=0)
    chosen = dot(pick_ref[...], queries)
    lane = iota((PIECE, LANES), 1)
    row = iota((PIECE, LANES), 0)
    nothing = jnp.zeros((PIECE, PAGE), jnp.float32)
    raws = []
    for c in range(chunks):
        rows = chosen[c * chunk * PIECE : (c + 1) * chunk * PIECE]
        split = (rows * pair_heads).astype(jnp.bfloat16)
        at = c * chunk
        block = keys_ref[at : at + chunk] if at < early else late_ref[at - early : at - early + chunk]
        raws.append(dot(split, block.reshape(chunk * PAGE, width), ((1,), (1,))))
    scores, page_tops = [], []
    for p in range(page_count):
        i = p % chunk
        part = raws[p // chunk][i * PIECE : (i + 1) * PIECE, i * PAGE : (i + 1) * PAGE]
        score = part + bias_ref[p * PIECE : (p + 1) * PIECE]
        scores.append(score)
        page_tops.append(jnp.max(score, axis=1, keepdims=True))
    page_weights = [jnp.exp(score - top) for score, top in zip(scores, page_tops)]
    mixes = []
    for c in range(chunks):
        blocks = []
        for i in range(chunk):
            weight = page_weights[c * chunk + i]
            blocks.append(
                jnp.concatenate([weight if k == i else nothing for k in range(chunk)], axis=1)
            )
        weights = jnp.concatenate(blocks, axis=0).astype(jnp.bfloat16)
        block = values_ref[c * chunk : (c + 1) * chunk]
        mixes.append(dot(weights, block.reshape(chunk * PAGE, width)))
    totals = [jnp.sum(weight, axis=1, keepdims=True) for weight in page_weights]
    tops = jnp.zeros((PIECE, LANES), jnp.float32)
    for p in range(page_count):
        tops = jnp.where(lane == p, page_tops[p], tops)
    stats = []
    for c in range(chunks):
        factors = []
        for p in range(c * chunk, (c + 1) * chunk):
            peak = jnp.max(tops + apart_ref[p : p + 1], axis=1, keepdims=True)
            factor = jnp.exp(page_tops[p] - peak)
            total = jnp.where(lane == row + SUM_LANE, totals[p] * factor, 0.0)
            stats.append(jnp.where(lane == row, peak * lead_ref[p : p + 1], total))
            factors.append(factor)
        mixes[c] = mixes[c] * (pair_heads * jnp.concatenate(factors, axis=0))
    mix = jnp.concatenate(mixes, axis=0).astype(jnp.bfloat16)
    stats = pieces(jnp.concatenate(stats, axis=0), 3)
    sums = dot(place_ref[...], jnp.concatenate([mix] + stats, axis=1))
    stats = sum(sums[:, width + i * LANES : width + (i + 1) * LANES] for i in range(3))
    stats = packed_stats(stats, 0.0).astype(jnp.float32)
    size = sums.shape[0] // groups
    for i, sums_ref in enumerate(sums_refs):
        first, middle, last = i * size, i * size + size // 2, (i + 1) * size
        for c in range(width // LANES):
            block = sums[first:last, c * LANES : (c + 1) * LANES]
            sums_ref[c * size : (c + 1) * size] = block.astype(jnp.bfloat16)
        both = stats[first:middle] + pltpu.roll(stats[middle:last], LANES // 2, 1)
        sums_ref[width // LANES * size :] = both.astype(jnp.bfloat16)


def combine_kernel(sources, *refs):
    part_refs, sums_refs = refs[:sources], refs[sources:]
    width = sums_refs[0].shape[1] - LANES
    rows = sum(ref.shape[0] for ref in sums_refs)
    heads, blocks = width // HEAD_DIM, width // LANES
    stats, mixes = [], []
    for ref in part_refs:
        both = ref[blocks * rows :].astype(jnp.float32)
        both = jnp.concatenate([both, pltpu.roll(both, LANES // 2, 1)], axis=0)
        stats.append(unpacked_stats(both, heads))
        mix = [ref[c * rows : (c + 1) * rows] for c in range(blocks)]
        mixes.append(jnp.concatenate(mix, axis=1).astype(jnp.float32))
    peak = stats[0][0]
    for peaks, _ in stats[1:]:
        peak = jnp.maximum(peak, peaks)
    factors = [jnp.exp(peaks - peak) for peaks, _ in stats]
    total = sum(factor * sums for factor, (_, sums) in zip(factors, stats))
    shares = over_columns(jnp.concatenate(factors, axis=0), width)
    mixed = sum(mix * shares[i * rows : (i + 1) * rows] for i, mix in enumerate(mixes))
    packed = packed_stats(
        jnp.where(total > 0.0, peak, 0.0), pltpu.roll(total, SUM_LANE, 1)
    ).astype(jnp.float32)
    size = sums_refs[0].shape[0]
    for i, sums_ref in enumerate(sums_refs):
        span = slice(i * size, (i + 1) * size)
        sums_ref[:, :width] = mixed[span].astype(jnp.bfloat16)
        sums_ref[:, width:] = packed[span].astype(jnp.bfloat16)


def merge_kernel(sources, *refs):
    part_refs, (score_ref, value_ref, weight_ref, own_ref, send_ref) = refs[:sources], refs[sources:]
    own_rows, width = value_ref.shape
    heads = width // HEAD_DIM
    stats = [unpacked_stats(ref[:, width:], heads) for ref in part_refs]
    own_score = jnp.where(iota(score_ref.shape, 1) < heads, score_ref[...], 0.0)
    peak = own_score
    for peaks, _ in stats:
        peak = jnp.maximum(peak, peaks)
    own_weight = jnp.exp(own_score - peak)
    total = own_weight
    factors = []
    for peaks, sums in stats:
        factor = jnp.exp(peaks - peak)
        total = total + factor * sums
        factors.append(factor)
    factors.append(own_weight.astype(jnp.bfloat16).astype(jnp.float32))
    shares = jnp.concatenate([factor / total for factor in factors], axis=0)
    shares = over_columns(shares, width)
    mixed = value_ref[...].astype(jnp.float32) * shares[sources * own_rows :]
    for i, ref in enumerate(part_refs):
        rows = slice(i * own_rows, (i + 1) * own_rows)
        mixed = mixed + ref[:, :width].astype(jnp.float32) * shares[rows]
    projected = dot(mixed.astype(jnp.bfloat16), weight_ref[...])
    own_ref[...] = projected
    send_ref[...] = projected.astype(jnp.bfloat16)


def mlp_kernel(
    exchanged, hidden_ref, own_ref, other_ref, gain_ref, up_ref, down_ref, late_ref, *outs
):
    middle = hidden_ref[...] + (own_ref[...] + other_ref[...].astype(jnp.float32))
    normed = rms_normed(middle, gain_ref[...])
    active = jnp.maximum(dot(normed, up_ref[...]), 0.0).astype(jnp.bfloat16)
    half = down_ref.shape[0]
    down = dot(active[:, :half], down_ref[...]) + dot(active[:, half:], late_ref[...])
    if exchanged:
        kept_ref, sent_ref = outs
        columns = kept_ref.shape[1]
        low = lax.axis_index("head") == 0
        left, right = slice(0, columns), slice(columns, 2 * columns)
        kept = middle + down

        @pl.when(low)
        def _():
            kept_ref[...] = kept[:, left]
            sent_ref[...] = down[:, right].astype(jnp.bfloat16)

        @pl.when(jnp.logical_not(low))
        def _():
            kept_ref[...] = kept[:, right]
            sent_ref[...] = down[:, left].astype(jnp.bfloat16)

    else:
        middle_ref, down_out_ref = outs
        middle_ref[...] = middle
        down_out_ref[...] = down.astype(jnp.bfloat16)


def loading(*arrays):
    return pl.CostEstimate(
        flops=0, bytes_accessed=sum(2 * array.size for array in arrays), transcendentals=0
    )


def in_hbm(*arrays):
    return [pltpu.with_memory_space_constraint(array, pltpu.HBM) for array in arrays]


def xor_pairs(size, step):
    return [(i, i ^ step) for i in range(size)]


def per_device(
    hidden_in, attention_gain, mlp_gain, qkv_weight, out_weight, up_weight, down_weight,
    position_bias, bucket_edges, cache_keys, cache_values, lengths, page_request, page_index,
):
    f32, bf16 = jnp.float32, jnp.bfloat16
    shape = jax.ShapeDtypeStruct
    own_rows, model = hidden_in.shape
    width = qkv_weight.shape[2]
    page_count = page_request.shape[0]
    blocks = lax.axis_size("blk")
    all_rows = own_rows * blocks
    gain = attention_gain.reshape(1, model)
    query = pl.pallas_call(
        query_kernel,
        out_shape=shape((own_rows, width), bf16),
        in_specs=[HBM_SPEC] * 3,
        out_specs=VMEM_SPEC,
        scratch_shapes=[
            pltpu.VMEM((own_rows, model), f32),
            pltpu.VMEM((1, model), f32),
            pltpu.VMEM((model, width), bf16),
            pltpu.SemaphoreType.DMA((6,)),
        ],
        compiler_params=PARAMS,
        name="query",
    )(*in_hbm(hidden_in, gain, qkv_weight))

    inner = 1
    while inner * inner < blocks:
        inner *= 2
    far = [query] + [
        lax.ppermute(query, "blk", xor_pairs(blocks, step * inner ^ 1))
        for step in range(1, blocks // inner)
    ]
    depth = page_count * PIECE
    early = page_count // 6 * 2
    keys, picks, place, leads, apart, owners = pl.pallas_call(
        functools.partial(page_kernel, own_rows, inner, blocks // inner),
        out_shape=(
            pltpu.VMEM((early,) + cache_keys.shape[1:], bf16),
            shape((depth, all_rows), bf16),
            shape((all_rows, depth), bf16),
            shape((page_count, LANES), f32),
            shape((page_count, LANES), f32),
            shape((page_count, LANES), jnp.int32),
        ),
        in_specs=[ANY_SPEC, VMEM_SPEC, HBM_SPEC],
        out_specs=(VMEM_SPEC,) * 6,
        scratch_shapes=[pltpu.SemaphoreType.DMA((4,))],
        compiler_params=PARAMS,
        cost_estimate=loading(cache_keys),
        name="pages",
    )(query, page_request.reshape(1, page_count), *in_hbm(cache_keys))
    near, apart = lax.optimization_barrier((jnp.concatenate(far, axis=0), apart))
    gathered = [near] + [
        lax.ppermute(near, "blk", xor_pairs(blocks, step)) for step in range(1, inner)
    ]
    table = position_bias.T
    late_keys, bias = pl.pallas_call(
        bias_kernel,
        out_shape=(
            pltpu.VMEM((page_count - early,) + cache_keys.shape[1:], bf16),
            shape((depth, PAGE), f32),
        ),
        in_specs=[HBM_SPEC] * 4 + [VMEM_SPEC, HBM_SPEC, ANY_SPEC],
        out_specs=(VMEM_SPEC,) * 2,
        scratch_shapes=[
            pltpu.SMEM(table.shape, f32),
            pltpu.SMEM(bucket_edges.shape, jnp.int32),
            pltpu.VMEM((1,) + lengths.shape, jnp.int32),
            pltpu.VMEM((1,) + page_index.shape, jnp.int32),
            pltpu.SemaphoreType.DMA((4,)),
            pltpu.SemaphoreType.DMA((4,)),
        ],
        compiler_params=PARAMS,
        cost_estimate=loading(cache_values),
        name="bias",
    )(
        *in_hbm(table, bucket_edges, lengths[None], page_index[None]), owners,
        *in_hbm(cache_keys), near,
    )

    groups = len(gathered)
    size = all_rows // groups
    message = width // LANES * size + size // 2
    sums = pl.pallas_call(
        functools.partial(attend_kernel, groups),
        out_shape=(shape((message, LANES), bf16),) * groups,
        in_specs=[VMEM_SPEC] * (groups + 8),
        out_specs=(VMEM_SPEC,) * groups,
        compiler_params=PARAMS,
        name="attend",
    )(*gathered, bias, picks, place, leads, apart, keys, late_keys, cache_values)
    near_sums = [sums[0]] + [
        lax.ppermute(sums[step], "blk", xor_pairs(blocks, step))
        for step in reversed(range(1, inner))
    ]

    own_score, value_new, out_near = pl.pallas_call(
        side_kernel,
        out_shape=(
            shape((own_rows, LANES), f32),
            shape((own_rows, width), bf16),
            pltpu.VMEM(out_weight.shape, bf16),
        ),
        in_specs=[VMEM_SPEC] * 4 + [HBM_SPEC] * 2 + [ANY_SPEC],
        out_specs=(VMEM_SPEC,) * 3,
        scratch_shapes=[
            pltpu.VMEM((2, model, width), bf16),
            pltpu.SemaphoreType.DMA((2,)),
            pltpu.SemaphoreType.DMA((4,)),
        ],
        compiler_params=PARAMS,
        cost_estimate=loading(out_weight, out_weight, out_weight),
        name="side",
    )(
        hidden_in, gain, query, table,
        *in_hbm(qkv_weight, out_weight), sums[0],
    )

    *near_sums, own_score = lax.optimization_barrier((*near_sums, own_score))
    outer = blocks // inner
    sums = pl.pallas_call(
        functools.partial(combine_kernel, inner),
        out_shape=(shape((own_rows, width + LANES), bf16),) * outer,
        in_specs=[VMEM_SPEC] * inner,
        out_specs=(VMEM_SPEC,) * outer,
        compiler_params=PARAMS,
        name="combine",
    )(*near_sums)
    half = down_weight.shape[0] // 2

    def load_down(start, after):
        return pl.pallas_call(
            functools.partial(load_kernel, start),
            out_shape=pltpu.VMEM((half, model), bf16),
            in_specs=[HBM_SPEC, ANY_SPEC],
            out_specs=VMEM_SPEC,
            scratch_shapes=[pltpu.SemaphoreType.DMA((4,))],
            compiler_params=PARAMS,
            cost_estimate=loading(down_weight),
            name="load",
        )(*in_hbm(down_weight), after)

    down_early = load_down(0, sums[0])
    parts = [sums[0]] + [
        lax.ppermute(sums[step], "blk", xor_pairs(blocks, step * inner ^ 1))
        for step in reversed(range(1, outer))
    ]

    *parts, down_early = lax.optimization_barrier((*parts, down_early))
    own_part, sent_part = pl.pallas_call(
        functools.partial(merge_kernel, outer),
        out_shape=(shape((own_rows, model), f32), shape((own_rows, model), bf16)),
        in_specs=[VMEM_SPEC] * (outer + 3),
        out_specs=(VMEM_SPEC,) * 2,
        compiler_params=PARAMS,
        name="merge",
    )(*parts, own_score, value_new, out_near)

    halves = lax.axis_size("head")
    columns = model // halves
    exchanged = halves == 2
    down_late = load_down(half, sent_part)
    if exchanged:
        other_part = lax.ppermute(sent_part, "head", xor_pairs(2, 1))
        mlp_out = (shape((own_rows, columns), f32), shape((own_rows, columns), bf16))
    else:
        own_part = jnp.zeros_like(own_part)
        other_part = lax.psum(sent_part, "head")
        mlp_out = (shape((own_rows, model), f32), shape((own_rows, model), bf16))

    kept, leaving = pl.pallas_call(
        functools.partial(mlp_kernel, exchanged),
        out_shape=mlp_out,
        in_specs=[VMEM_SPEC] * 7,
        out_specs=(VMEM_SPEC,) * 2,
        compiler_params=PARAMS,
        name="mlp",
    )(hidden_in, own_part, other_part, mlp_gain.reshape(1, model), up_weight, down_early, down_late)

    if exchanged:
        arrived = lax.ppermute(leaving, "head", xor_pairs(2, 1))
    else:
        kept = lax.dynamic_slice_in_dim(kept, lax.axis_index("head") * columns, columns, 1)
        arrived = lax.psum_scatter(leaving, "head", scatter_dimension=1, tiled=True)
    return kept + arrived.astype(f32)


def solution(mesh):
    in_specs = (
        P("blk", None),
        P(),
        P(),
        P(None, None, "head"),
        P("head", None),
        P(None, "head"),
        P("head", None),
        P(None, "head"),
        P(),
        P("blk", None, "head"),
        P("blk", None, "head"),
        P(),
        P("blk"),
        P("blk"),
    )
    out_specs = P("blk", "head")
    return jax.shard_map(
        per_device, mesh=mesh, in_specs=in_specs, out_specs=out_specs, check_vma=False
    )
```

```python
import functools

import jax
import jax.numpy as jnp
from jax import lax
from jax.experimental import pallas as pl
from jax.experimental.pallas import tpu as pltpu
from jax.sharding import PartitionSpec as P

HEAD_DIM = 64
PAGE = 128
LANES = 128

far_below = -1e30
epsilon = 1e-06

VMEM_SPEC = pl.BlockSpec(memory_space=pltpu.VMEM)
SMEM_SPEC = pl.BlockSpec(memory_space=pltpu.SMEM)
ANY_SPEC = pl.BlockSpec(memory_space=pl.ANY)
HBM_SPEC = pl.BlockSpec(memory_space=pltpu.HBM)
PARAMS = pltpu.CompilerParams(vmem_limit_bytes=16 * 1024 * 1024)

PIECE = 8
SUM_LANE = 3 * PIECE


def iota(shape, axis):
    return lax.broadcasted_iota(jnp.int32, shape, axis)


def split_index(x, size):
    if size & (size - 1):
        return lax.div(x, size), lax.rem(x, size)
    return x >> (size.bit_length() - 1), x & (size - 1)


def head_of(shape, axis):
    return split_index(iota(shape, axis), HEAD_DIM)[0]


def pieces(x, count):
    parts = []
    for _ in range(count):
        part = x.astype(jnp.bfloat16)
        parts.append(part)
        x = x - part.astype(jnp.float32)
    return parts


def rms_normed(x, gain):
    scale = lax.rsqrt(jnp.mean(x * x, axis=1, keepdims=True) + epsilon)
    return (x * scale * gain).astype(jnp.bfloat16)


def dot(a, b, dims=((1,), (0,)), precision=None):
    return lax.dot_general(
        a, b, (dims, ((), ())), preferred_element_type=jnp.float32, precision=precision
    )


def split_copies(source, target, sems, count):
    size = source.shape[0] // count
    return [
        pltpu.make_async_copy(
            source.at[pl.ds(i * size, size)], target.at[pl.ds(i * size, size)], sems.at[i]
        )
        for i in range(count)
    ]


def query_kernel(hidden_hbm, gain_hbm, weight_hbm, query_ref, hidden, gain, weight, sems):
    model = hidden.shape[1]
    small = [
        pltpu.make_async_copy(hidden_hbm, hidden, sems.at[0]),
        pltpu.make_async_copy(gain_hbm, gain, sems.at[1]),
    ]
    half = model // 4
    large = [
        pltpu.make_async_copy(
            weight_hbm.at[0, pl.ds(i * half, half)], weight.at[pl.ds(i * half, half)], sems.at[2 + i]
        )
        for i in range(4)
    ]
    for copy in small + large:
        copy.start()
    for copy in small:
        copy.wait()
    normed = rms_normed(hidden[...], gain[...])
    query = None
    for i, copy in enumerate(large):
        copy.wait()
        span = slice(i * half, (i + 1) * half)
        part = dot(normed[:, span], weight[span])
        query = part if query is None else query + part
    query_ref[...] = query.astype(jnp.bfloat16)


def page_kernel(
    own_rows, inner, outer, query_ref, request_ref, keys_hbm,
    keys_ref, pick_ref, place_ref, lead_ref, apart_ref, owners_ref,
    sems,
):
    copies = split_copies(
        keys_hbm.at[pl.ds(0, keys_ref.shape[0])], keys_ref, sems, sems.shape[0]
    )
    for copy in copies:
        copy.start()
    me = lax.axis_index("blk")
    page_count = apart_ref.shape[0]
    all_rows, depth = place_ref.shape
    page, lane = iota((page_count, page_count), 0), iota((page_count, page_count), 1)
    by_lane = request_ref[...]
    owner = jnp.max(jnp.where(page == lane, by_lane, -1), axis=1, keepdims=True)
    same = by_lane == owner
    apart_ref[...] = jnp.full(apart_ref.shape, 2 * far_below, jnp.float32)
    apart_ref[:, :page_count] = jnp.where(same, 0.0, 2 * far_below)
    earlier = jnp.max(jnp.where(same & (lane < page), 1, 0), axis=1, keepdims=True)
    lead_ref[...] = jnp.broadcast_to(jnp.where(earlier == 0, 1.0, 0.0), lead_ref.shape)
    owners_ref[...] = jnp.broadcast_to(owner, owners_ref.shape)
    device, own_row = split_index(jnp.maximum(owner, 0), own_rows)
    high, low = split_index(device ^ me, inner)
    low = jnp.where(high == 0, low, low ^ 1)
    slot = ((low ^ (low >> 1)) * outer + high) * own_rows + own_row
    slot = jnp.where(owner >= 0, slot, -1)
    row_of = iota((page_count, all_rows), 1)
    picks = jnp.where(row_of == slot, 1.0, 0.0)
    picks = [jnp.broadcast_to(picks[p : p + 1], (PIECE, all_rows)) for p in range(page_count)]
    pick_ref[...] = jnp.concatenate(picks, axis=0).astype(jnp.bfloat16)
    mine = split_index(iota((page_count, depth), 1), PIECE)[0] == iota((page_count, depth), 0)
    row = iota((all_rows, depth), 0)
    spread = jnp.max(jnp.where(mine, slot, -1), axis=0, keepdims=True)
    place_ref[...] = (row == spread).astype(jnp.bfloat16)
    for copy in copies:
        copy.wait()


def bias_kernel(
    table_hbm, edges_hbm, lengths_hbm, index_hbm, owners_ref, keys_hbm, after_ref,
    keys_ref, bias_ref,
    table, edges, lengths, index, small_sems, sems,
):
    sources, targets = (table_hbm, edges_hbm, lengths_hbm, index_hbm), (table, edges, lengths, index)
    small = [
        pltpu.make_async_copy(source, target, small_sems.at[i])
        for i, (source, target) in enumerate(zip(sources, targets))
    ]
    late = keys_ref.shape[0]
    copies = split_copies(
        keys_hbm.at[pl.ds(keys_hbm.shape[0] - late, late)], keys_ref, sems, sems.shape[0]
    )
    for copy in small + copies:
        copy.start()
    for copy in small:
        copy.wait()
    heads, buckets = table.shape
    page_count = index.shape[1]
    owner = owners_ref[:, 0:1]
    square = (page_count, page_count)
    number = jnp.where(iota(square, 0) == iota(square, 1), index[...], 0)
    number = jnp.sum(number, axis=1, keepdims=True)
    requests = lengths.shape[1]
    length = jnp.where(iota((page_count, requests), 1) == owner, lengths[...], 0)
    length = jnp.sum(length, axis=1, keepdims=True)
    distance = length - number * PAGE - iota((page_count, PAGE), 1)
    far = [distance >= edges[k] for k in range(buckets - 1)]
    usable = (owner >= 0) & (distance > 0)
    bias_ref[...] = jnp.full(bias_ref.shape, far_below, jnp.float32)
    for h in range(heads):
        bias = jnp.full((page_count, PAGE), table[h, 0], jnp.float32)
        for k in range(buckets - 1):
            bias = jnp.where(far[k], table[h, k + 1], bias)
        bias_ref[pl.ds(h, page_count, stride=PIECE), :] = jnp.where(usable, bias, far_below)
    for copy in copies:
        copy.wait()


def side_kernel(
    hidden_ref, gain_ref, query_ref, table_ref, weight_hbm, out_hbm, after_ref,
    score_ref, value_ref, out_ref,
    weight, weight_sems, sems,
):
    copies = [
        pltpu.make_async_copy(weight_hbm.at[1 + i], weight.at[i], weight_sems.at[i])
        for i in range(2)
    ]
    later = split_copies(out_hbm, out_ref, sems, sems.shape[0])
    for copy in copies + later:
        copy.start()
    normed = rms_normed(hidden_ref[...], gain_ref[...])
    heads = table_ref.shape[0]
    spread = iota((heads, LANES), 0) == iota((heads, LANES), 1)
    score = jnp.sum(jnp.where(spread, table_ref[:, 0:1], 0.0), axis=0, keepdims=True)
    copies[0].wait()
    key = dot(normed, weight[0]).astype(jnp.bfloat16)
    product = query_ref[...].astype(jnp.float32) * key.astype(jnp.float32)
    width = product.shape[1]
    gather = (head_of((width, LANES), 0) == iota((width, LANES), 1)).astype(jnp.bfloat16)
    for part in pieces(product, 3):
        score = score + dot(part, gather)
    score_ref[...] = score
    copies[1].wait()
    value_ref[...] = dot(normed, weight[1]).astype(jnp.bfloat16)
    for copy in later:
        copy.wait()


def load_kernel(start, source, after_ref, target, sems):
    rows = source.at[pl.ds(start, target.shape[0])]
    copies = split_copies(rows, target, sems, sems.shape[0])
    for copy in copies:
        copy.start()
    for copy in copies:
        copy.wait()


def packed_stats(peaks, sums):
    one, two, three = (part.astype(jnp.float32) for part in pieces(peaks + sums, 3))
    packed = one + pltpu.roll(two, PIECE, 1) + pltpu.roll(three, 2 * PIECE, 1)
    return packed.astype(jnp.bfloat16)


def unpacked_stats(packed, heads):
    stats = packed.astype(jnp.float32)
    stats = stats + pltpu.roll(stats, LANES - PIECE, 1) + pltpu.roll(stats, LANES - 2 * PIECE, 1)
    sums = pltpu.roll(stats, LANES - SUM_LANE, 1)
    used = iota(stats.shape, 1) < heads
    return jnp.where(used & (sums > 0.0), stats, far_below), jnp.where(used, sums, 0.0)


def over_columns(values, width):
    spread = (iota((LANES, width), 0) == head_of((LANES, width), 1)).astype(jnp.bfloat16)
    return sum(dot(part, spread) for part in pieces(values, 3))


def attend_kernel(groups, *refs):
    query_refs, refs, sums_refs = refs[:groups], refs[groups:-groups], refs[-groups:]
    bias_ref, pick_ref, place_ref, lead_ref, apart_ref, keys_ref, late_ref, values_ref = refs
    page_count = apart_ref.shape[0]
    width = keys_ref.shape[2]
    early = keys_ref.shape[0]
    chunk = 2
    chunks = page_count // chunk
    queries = jnp.concatenate([ref[...] for ref in query_refs], axis=0)
    own_head = (head_of((PIECE, width), 1) == iota((PIECE, width), 0)).astype(jnp.float32)
    pair_heads = jnp.concatenate([own_head] * chunk, axis=0)
    chosen = dot(pick_ref[...], queries)
    lane = iota((PIECE, LANES), 1)
    row = iota((PIECE, LANES), 0)
    nothing = jnp.zeros((PIECE, PAGE), jnp.float32)
    raws = []
    for c in range(chunks):
        rows = chosen[c * chunk * PIECE : (c + 1) * chunk * PIECE]
        split = (rows * pair_heads).astype(jnp.bfloat16)
        at = c * chunk
        block = keys_ref[at : at + chunk] if at < early else late_ref[at - early : at - early + chunk]
        raws.append(dot(split, block.reshape(chunk * PAGE, width), ((1,), (1,))))
    scores, page_tops = [], []
    for p in range(page_count):
        i = p % chunk
        part = raws[p // chunk][i * PIECE : (i + 1) * PIECE, i * PAGE : (i + 1) * PAGE]
        score = part + bias_ref[p * PIECE : (p + 1) * PIECE]
        scores.append(score)
        page_tops.append(jnp.max(score, axis=1, keepdims=True))
    page_weights = [jnp.exp(score - top) for score, top in zip(scores, page_tops)]
    mixes = []
    for c in range(chunks):
        blocks = []
        for i in range(chunk):
            weight = page_weights[c * chunk + i]
            blocks.append(
                jnp.concatenate([weight if k == i else nothing for k in range(chunk)], axis=1)
            )
        weights = jnp.concatenate(blocks, axis=0).astype(jnp.bfloat16)
        block = values_ref[c * chunk : (c + 1) * chunk]
        mixes.append(dot(weights, block.reshape(chunk * PAGE, width)))
    totals = [jnp.sum(weight, axis=1, keepdims=True) for weight in page_weights]
    tops = jnp.zeros((PIECE, LANES), jnp.float32)
    for p in range(page_count):
        tops = jnp.where(lane == p, page_tops[p], tops)
    stats = []
    for c in range(chunks):
        factors = []
        for p in range(c * chunk, (c + 1) * chunk):
            peak = jnp.max(tops + apart_ref[p : p + 1], axis=1, keepdims=True)
            factor = jnp.exp(page_tops[p] - peak)
            total = jnp.where(lane == row + SUM_LANE, totals[p] * factor, 0.0)
            stats.append(jnp.where(lane == row, peak * lead_ref[p : p + 1], total))
            factors.append(factor)
        mixes[c] = mixes[c] * (pair_heads * jnp.concatenate(factors, axis=0))
    mix = jnp.concatenate(mixes, axis=0).astype(jnp.bfloat16)
    stats = pieces(jnp.concatenate(stats, axis=0), 3)
    sums = dot(place_ref[...], jnp.concatenate([mix] + stats, axis=1))
    stats = sum(sums[:, width + i * LANES : width + (i + 1) * LANES] for i in range(3))
    stats = packed_stats(stats, 0.0).astype(jnp.float32)
    size = sums.shape[0] // groups
    for i, sums_ref in enumerate(sums_refs):
        first, middle, last = i * size, i * size + size // 2, (i + 1) * size
        for c in range(width // LANES):
            block = sums[first:last, c * LANES : (c + 1) * LANES]
            sums_ref[c * size : (c + 1) * size] = block.astype(jnp.bfloat16)
        both = stats[first:middle] + pltpu.roll(stats[middle:last], LANES // 2, 1)
        sums_ref[width // LANES * size :] = both.astype(jnp.bfloat16)


def combine_kernel(sources, *refs):
    part_refs, sums_refs = refs[:sources], refs[sources:]
    width = sums_refs[0].shape[1] - LANES
    rows = sum(ref.shape[0] for ref in sums_refs)
    heads, blocks = width // HEAD_DIM, width // LANES
    stats, mixes = [], []
    for ref in part_refs:
        both = ref[blocks * rows :].astype(jnp.float32)
        both = jnp.concatenate([both, pltpu.roll(both, LANES // 2, 1)], axis=0)
        stats.append(unpacked_stats(both, heads))
        mix = [ref[c * rows : (c + 1) * rows] for c in range(blocks)]
        mixes.append(jnp.concatenate(mix, axis=1).astype(jnp.float32))
    peak = stats[0][0]
    for peaks, _ in stats[1:]:
        peak = jnp.maximum(peak, peaks)
    factors = [jnp.exp(peaks - peak) for peaks, _ in stats]
    total = sum(factor * sums for factor, (_, sums) in zip(factors, stats))
    shares = over_columns(jnp.concatenate(factors, axis=0), width)
    mixed = sum(mix * shares[i * rows : (i + 1) * rows] for i, mix in enumerate(mixes))
    packed = packed_stats(
        jnp.where(total > 0.0, peak, 0.0), pltpu.roll(total, SUM_LANE, 1)
    ).astype(jnp.float32)
    size = sums_refs[0].shape[0]
    for i, sums_ref in enumerate(sums_refs):
        span = slice(i * size, (i + 1) * size)
        sums_ref[:, :width] = mixed[span].astype(jnp.bfloat16)
        sums_ref[:, width:] = packed[span].astype(jnp.bfloat16)


def merge_kernel(sources, *refs):
    part_refs, (score_ref, value_ref, weight_ref, own_ref, send_ref) = refs[:sources], refs[sources:]
    own_rows, width = value_ref.shape
    heads = width // HEAD_DIM
    stats = [unpacked_stats(ref[:, width:], heads) for ref in part_refs]
    own_score = jnp.where(iota(score_ref.shape, 1) < heads, score_ref[...], 0.0)
    peak = own_score
    for peaks, _ in stats:
        peak = jnp.maximum(peak, peaks)
    own_weight = jnp.exp(own_score - peak)
    total = own_weight
    factors = []
    for peaks, sums in stats:
        factor = jnp.exp(peaks - peak)
        total = total + factor * sums
        factors.append(factor)
    factors.append(own_weight.astype(jnp.bfloat16).astype(jnp.float32))
    shares = jnp.concatenate([factor / total for factor in factors], axis=0)
    shares = over_columns(shares, width)
    mixed = value_ref[...].astype(jnp.float32) * shares[sources * own_rows :]
    for i, ref in enumerate(part_refs):
        rows = slice(i * own_rows, (i + 1) * own_rows)
        mixed = mixed + ref[:, :width].astype(jnp.float32) * shares[rows]
    projected = dot(mixed.astype(jnp.bfloat16), weight_ref[...])
    own_ref[...] = projected
    send_ref[...] = projected.astype(jnp.bfloat16)


def mlp_kernel(
    exchanged, hidden_ref, own_ref, other_ref, gain_ref, up_ref, down_ref, late_ref, *outs
):
    middle = hidden_ref[...] + (own_ref[...] + other_ref[...].astype(jnp.float32))
    normed = rms_normed(middle, gain_ref[...])
    active = jnp.maximum(dot(normed, up_ref[...]), 0.0).astype(jnp.bfloat16)
    half = down_ref.shape[0]
    down = dot(active[:, :half], down_ref[...]) + dot(active[:, half:], late_ref[...])
    if exchanged:
        kept_ref, sent_ref = outs
        columns = kept_ref.shape[1]
        low = lax.axis_index("head") == 0
        left, right = slice(0, columns), slice(columns, 2 * columns)
        kept = middle + down

        @pl.when(low)
        def _():
            kept_ref[...] = kept[:, left]
            sent_ref[...] = down[:, right].astype(jnp.bfloat16)

        @pl.when(jnp.logical_not(low))
        def _():
            kept_ref[...] = kept[:, right]
            sent_ref[...] = down[:, left].astype(jnp.bfloat16)

    else:
        middle_ref, down_out_ref = outs
        middle_ref[...] = middle
        down_out_ref[...] = down.astype(jnp.bfloat16)


def loading(*arrays):
    return pl.CostEstimate(
        flops=0, bytes_accessed=sum(2 * array.size for array in arrays), transcendentals=0
    )


def in_hbm(*arrays):
    return [pltpu.with_memory_space_constraint(array, pltpu.HBM) for array in arrays]


def xor_pairs(size, step):
    return [(i, i ^ step) for i in range(size)]


def per_device(
    hidden_in, attention_gain, mlp_gain, qkv_weight, out_weight, up_weight, down_weight,
    position_bias, bucket_edges, cache_keys, cache_values, lengths, page_request, page_index,
):
    f32, bf16 = jnp.float32, jnp.bfloat16
    shape = jax.ShapeDtypeStruct
    own_rows, model = hidden_in.shape
    width = qkv_weight.shape[2]
    page_count = page_request.shape[0]
    blocks = lax.axis_size("blk")
    all_rows = own_rows * blocks
    gain = attention_gain.reshape(1, model)
    query = pl.pallas_call(
        query_kernel,
        out_shape=shape((own_rows, width), bf16),
        in_specs=[HBM_SPEC] * 3,
        out_specs=VMEM_SPEC,
        scratch_shapes=[
            pltpu.VMEM((own_rows, model), f32),
            pltpu.VMEM((1, model), f32),
            pltpu.VMEM((model, width), bf16),
            pltpu.SemaphoreType.DMA((6,)),
        ],
        compiler_params=PARAMS,
        name="query",
    )(*in_hbm(hidden_in, gain, qkv_weight))

    inner = 1
    while inner * inner < blocks:
        inner *= 2
    far = [query] + [
        lax.ppermute(query, "blk", xor_pairs(blocks, step * inner ^ 1))
        for step in range(1, blocks // inner)
    ]
    depth = page_count * PIECE
    early = page_count // 6 * 2
    keys, picks, place, leads, apart, owners = pl.pallas_call(
        functools.partial(page_kernel, own_rows, inner, blocks // inner),
        out_shape=(
            pltpu.VMEM((early,) + cache_keys.shape[1:], bf16),
            shape((depth, all_rows), bf16),
            shape((all_rows, depth), bf16),
            shape((page_count, LANES), f32),
            shape((page_count, LANES), f32),
            shape((page_count, LANES), jnp.int32),
        ),
        in_specs=[ANY_SPEC, VMEM_SPEC, HBM_SPEC],
        out_specs=(VMEM_SPEC,) * 6,
        scratch_shapes=[pltpu.SemaphoreType.DMA((4,))],
        compiler_params=PARAMS,
        cost_estimate=loading(cache_keys),
        name="pages",
    )(query, page_request.reshape(1, page_count), *in_hbm(cache_keys))
    near, apart = lax.optimization_barrier((jnp.concatenate(far, axis=0), apart))
    steps = sorted(range(inner), key=lambda step: step ^ (step >> 1))
    gathered = [near] + [lax.ppermute(near, "blk", xor_pairs(blocks, step)) for step in steps[1:]]
    table = position_bias.T
    late_keys, bias = pl.pallas_call(
        bias_kernel,
        out_shape=(
            pltpu.VMEM((page_count - early,) + cache_keys.shape[1:], bf16),
            shape((depth, PAGE), f32),
        ),
        in_specs=[HBM_SPEC] * 4 + [VMEM_SPEC, HBM_SPEC, ANY_SPEC],
        out_specs=(VMEM_SPEC,) * 2,
        scratch_shapes=[
            pltpu.SMEM(table.shape, f32),
            pltpu.SMEM(bucket_edges.shape, jnp.int32),
            pltpu.VMEM((1,) + lengths.shape, jnp.int32),
            pltpu.VMEM((1,) + page_index.shape, jnp.int32),
            pltpu.SemaphoreType.DMA((4,)),
            pltpu.SemaphoreType.DMA((4,)),
        ],
        compiler_params=PARAMS,
        cost_estimate=loading(cache_values),
        name="bias",
    )(
        *in_hbm(table, bucket_edges, lengths[None], page_index[None]), owners,
        *in_hbm(cache_keys), near,
    )

    groups = len(gathered)
    size = all_rows // groups
    message = width // LANES * size + size // 2
    sums = pl.pallas_call(
        functools.partial(attend_kernel, groups),
        out_shape=(shape((message, LANES), bf16),) * groups,
        in_specs=[VMEM_SPEC] * (groups + 8),
        out_specs=(VMEM_SPEC,) * groups,
        compiler_params=PARAMS,
        name="attend",
    )(*gathered, bias, picks, place, leads, apart, keys, late_keys, cache_values)
    near_sums = [sums[0]] + [
        lax.ppermute(sums[i], "blk", xor_pairs(blocks, steps[i]))
        for i in reversed(range(1, inner))
    ]

    own_score, value_new, out_near = pl.pallas_call(
        side_kernel,
        out_shape=(
            shape((own_rows, LANES), f32),
            shape((own_rows, width), bf16),
            pltpu.VMEM(out_weight.shape, bf16),
        ),
        in_specs=[VMEM_SPEC] * 4 + [HBM_SPEC] * 2 + [ANY_SPEC],
        out_specs=(VMEM_SPEC,) * 3,
        scratch_shapes=[
            pltpu.VMEM((2, model, width), bf16),
            pltpu.SemaphoreType.DMA((2,)),
            pltpu.SemaphoreType.DMA((4,)),
        ],
        compiler_params=PARAMS,
        cost_estimate=loading(out_weight, out_weight, out_weight),
        name="side",
    )(
        hidden_in, gain, query, table,
        *in_hbm(qkv_weight, out_weight), sums[0],
    )

    *near_sums, own_score = lax.optimization_barrier((*near_sums, own_score))
    outer = blocks // inner
    sums = pl.pallas_call(
        functools.partial(combine_kernel, inner),
        out_shape=(shape((own_rows, width + LANES), bf16),) * outer,
        in_specs=[VMEM_SPEC] * inner,
        out_specs=(VMEM_SPEC,) * outer,
        compiler_params=PARAMS,
        name="combine",
    )(*near_sums)
    half = down_weight.shape[0] // 2

    def load_down(start, after):
        return pl.pallas_call(
            functools.partial(load_kernel, start),
            out_shape=pltpu.VMEM((half, model), bf16),
            in_specs=[HBM_SPEC, ANY_SPEC],
            out_specs=VMEM_SPEC,
            scratch_shapes=[pltpu.SemaphoreType.DMA((4,))],
            compiler_params=PARAMS,
            cost_estimate=loading(down_weight),
            name="load",
        )(*in_hbm(down_weight), after)

    down_early = load_down(0, sums[0])
    parts = [sums[0]] + [
        lax.ppermute(sums[step], "blk", xor_pairs(blocks, step * inner ^ 1))
        for step in reversed(range(1, outer))
    ]

    *parts, down_early = lax.optimization_barrier((*parts, down_early))
    own_part, sent_part = pl.pallas_call(
        functools.partial(merge_kernel, outer),
        out_shape=(shape((own_rows, model), f32), shape((own_rows, model), bf16)),
        in_specs=[VMEM_SPEC] * (outer + 3),
        out_specs=(VMEM_SPEC,) * 2,
        compiler_params=PARAMS,
        name="merge",
    )(*parts, own_score, value_new, out_near)

    halves = lax.axis_size("head")
    columns = model // halves
    exchanged = halves == 2
    down_late = load_down(half, sent_part)
    if exchanged:
        other_part = lax.ppermute(sent_part, "head", xor_pairs(2, 1))
        mlp_out = (shape((own_rows, columns), f32), shape((own_rows, columns), bf16))
    else:
        own_part = jnp.zeros_like(own_part)
        other_part = lax.psum(sent_part, "head")
        mlp_out = (shape((own_rows, model), f32), shape((own_rows, model), bf16))

    kept, leaving = pl.pallas_call(
        functools.partial(mlp_kernel, exchanged),
        out_shape=mlp_out,
        in_specs=[VMEM_SPEC] * 7,
        out_specs=(VMEM_SPEC,) * 2,
        compiler_params=PARAMS,
        name="mlp",
    )(hidden_in, own_part, other_part, mlp_gain.reshape(1, model), up_weight, down_early, down_late)

    if exchanged:
        arrived = lax.ppermute(leaving, "head", xor_pairs(2, 1))
    else:
        kept = lax.dynamic_slice_in_dim(kept, lax.axis_index("head") * columns, columns, 1)
        arrived = lax.psum_scatter(leaving, "head", scatter_dimension=1, tiled=True)
    return kept + arrived.astype(f32)


def solution(mesh):
    in_specs = (
        P("blk", None),
        P(),
        P(),
        P(None, None, "head"),
        P("head", None),
        P(None, "head"),
        P("head", None),
        P(None, "head"),
        P(),
        P("blk", None, "head"),
        P("blk", None, "head"),
        P(),
        P("blk"),
        P("blk"),
    )
    out_specs = P("blk", "head")
    return jax.shard_map(
        per_device, mesh=mesh, in_specs=in_specs, out_specs=out_specs, check_vma=False
    )
```

```python
import functools

import jax
import jax.numpy as jnp
from jax import lax
from jax.experimental import pallas as pl
from jax.experimental.pallas import tpu as pltpu
from jax.sharding import PartitionSpec as P

HEAD_DIM = 64
PAGE = 128
LANES = 128

far_below = -1e30
epsilon = 1e-06

VMEM_SPEC = pl.BlockSpec(memory_space=pltpu.VMEM)
SMEM_SPEC = pl.BlockSpec(memory_space=pltpu.SMEM)
ANY_SPEC = pl.BlockSpec(memory_space=pl.ANY)
HBM_SPEC = pl.BlockSpec(memory_space=pltpu.HBM)
PARAMS = pltpu.CompilerParams(vmem_limit_bytes=16 * 1024 * 1024)

PIECE = 8
SUM_LANE = 3 * PIECE


def iota(shape, axis):
    return lax.broadcasted_iota(jnp.int32, shape, axis)


def split_index(x, size):
    if size & (size - 1):
        return lax.div(x, size), lax.rem(x, size)
    return x >> (size.bit_length() - 1), x & (size - 1)


def head_of(shape, axis):
    return split_index(iota(shape, axis), HEAD_DIM)[0]


def pieces(x, count):
    parts = []
    for _ in range(count):
        part = x.astype(jnp.bfloat16)
        parts.append(part)
        x = x - part.astype(jnp.float32)
    return parts


def rms_normed(x, gain):
    scale = lax.rsqrt(jnp.mean(x * x, axis=1, keepdims=True) + epsilon)
    return (x * scale * gain).astype(jnp.bfloat16)


def dot(a, b, dims=((1,), (0,)), precision=None):
    return lax.dot_general(
        a, b, (dims, ((), ())), preferred_element_type=jnp.float32, precision=precision
    )


def split_copies(source, target, sems, count):
    size = source.shape[0] // count
    return [
        pltpu.make_async_copy(
            source.at[pl.ds(i * size, size)], target.at[pl.ds(i * size, size)], sems.at[i]
        )
        for i in range(count)
    ]


def query_kernel(hidden_hbm, gain_hbm, weight_hbm, query_ref, hidden, gain, weight, sems):
    model = hidden.shape[1]
    small = [
        pltpu.make_async_copy(hidden_hbm, hidden, sems.at[0]),
        pltpu.make_async_copy(gain_hbm, gain, sems.at[1]),
    ]
    half = model // 4
    large = [
        pltpu.make_async_copy(
            weight_hbm.at[0, pl.ds(i * half, half)], weight.at[pl.ds(i * half, half)], sems.at[2 + i]
        )
        for i in range(4)
    ]
    for copy in small + large:
        copy.start()
    for copy in small:
        copy.wait()
    normed = rms_normed(hidden[...], gain[...])
    query = None
    for i, copy in enumerate(large):
        copy.wait()
        span = slice(i * half, (i + 1) * half)
        part = dot(normed[:, span], weight[span])
        query = part if query is None else query + part
    query_ref[...] = query.astype(jnp.bfloat16)


def page_kernel(
    own_rows, inner, outer, swapped, query_ref, request_ref, keys_hbm,
    keys_ref, pick_ref, place_ref, lead_ref, apart_ref, owners_ref,
    sems,
):
    copies = split_copies(
        keys_hbm.at[pl.ds(0, keys_ref.shape[0])], keys_ref, sems, sems.shape[0]
    )
    for copy in copies:
        copy.start()
    me = lax.axis_index("blk")
    page_count = apart_ref.shape[0]
    all_rows, depth = place_ref.shape
    page, lane = iota((page_count, page_count), 0), iota((page_count, page_count), 1)
    by_lane = request_ref[...]
    owner = jnp.max(jnp.where(page == lane, by_lane, -1), axis=1, keepdims=True)
    same = by_lane == owner
    apart_ref[...] = jnp.full(apart_ref.shape, 2 * far_below, jnp.float32)
    apart_ref[:, :page_count] = jnp.where(same, 0.0, 2 * far_below)
    earlier = jnp.max(jnp.where(same & (lane < page), 1, 0), axis=1, keepdims=True)
    lead_ref[...] = jnp.broadcast_to(jnp.where(earlier == 0, 1.0, 0.0), lead_ref.shape)
    owners_ref[...] = jnp.broadcast_to(owner, owners_ref.shape)
    device, own_row = split_index(jnp.maximum(owner, 0), own_rows)

    def slot_of(device):
        high, low = split_index(device ^ me, inner)
        low = jnp.where(high == 0, low, low ^ 1)
        low = -(low ^ (low >> 1)) & (inner - 1)
        slot = (low * outer + high) * own_rows + own_row
        return jnp.where(owner >= 0, slot, -1)

    slot = slot_of(device)
    sum_slot = slot_of(device ^ lax.axis_index("head")) if swapped else slot
    row_of = iota((page_count, all_rows), 1)
    picks = jnp.where(row_of == slot, 1.0, 0.0)
    picks = [jnp.broadcast_to(picks[p : p + 1], (PIECE, all_rows)) for p in range(page_count)]
    pick_ref[...] = jnp.concatenate(picks, axis=0).astype(jnp.bfloat16)
    mine = split_index(iota((page_count, depth), 1), PIECE)[0] == iota((page_count, depth), 0)
    row = iota((all_rows, depth), 0)
    spread = jnp.max(jnp.where(mine, sum_slot, -1), axis=0, keepdims=True)
    place_ref[...] = (row == spread).astype(jnp.bfloat16)
    for copy in copies:
        copy.wait()


def bias_kernel(
    table_hbm, edges_hbm, lengths_hbm, index_hbm, owners_ref, keys_hbm, after_ref,
    keys_ref, bias_ref,
    table, edges, lengths, index, small_sems, sems,
):
    sources, targets = (table_hbm, edges_hbm, lengths_hbm, index_hbm), (table, edges, lengths, index)
    small = [
        pltpu.make_async_copy(source, target, small_sems.at[i])
        for i, (source, target) in enumerate(zip(sources, targets))
    ]
    late = keys_ref.shape[0]
    copies = split_copies(
        keys_hbm.at[pl.ds(keys_hbm.shape[0] - late, late)], keys_ref, sems, sems.shape[0]
    )
    for copy in small + copies:
        copy.start()
    for copy in small:
        copy.wait()
    heads, buckets = table.shape
    page_count = index.shape[1]
    owner = owners_ref[:, 0:1]
    square = (page_count, page_count)
    number = jnp.where(iota(square, 0) == iota(square, 1), index[...], 0)
    number = jnp.sum(number, axis=1, keepdims=True)
    requests = lengths.shape[1]
    length = jnp.where(iota((page_count, requests), 1) == owner, lengths[...], 0)
    length = jnp.sum(length, axis=1, keepdims=True)
    distance = length - number * PAGE - iota((page_count, PAGE), 1)
    far = [distance >= edges[k] for k in range(buckets - 1)]
    usable = (owner >= 0) & (distance > 0)
    bias_ref[...] = jnp.full(bias_ref.shape, far_below, jnp.float32)
    for h in range(heads):
        bias = jnp.full((page_count, PAGE), table[h, 0], jnp.float32)
        for k in range(buckets - 1):
            bias = jnp.where(far[k], table[h, k + 1], bias)
        bias_ref[pl.ds(h, page_count, stride=PIECE), :] = jnp.where(usable, bias, far_below)
    for copy in copies:
        copy.wait()


def side_kernel(
    hidden_ref, gain_ref, query_ref, table_ref, weight_hbm, out_hbm, after_ref,
    fresh_ref, out_ref,
    weight, weight_sems, sems,
):
    copies = [
        pltpu.make_async_copy(weight_hbm.at[1 + i], weight.at[i], weight_sems.at[i])
        for i in range(2)
    ]
    later = split_copies(out_hbm, out_ref, sems, sems.shape[0])
    for copy in copies + later:
        copy.start()
    normed = rms_normed(hidden_ref[...], gain_ref[...])
    heads = table_ref.shape[0]
    spread = iota((heads, LANES), 0) == iota((heads, LANES), 1)
    score = jnp.sum(jnp.where(spread, table_ref[:, 0:1], 0.0), axis=0, keepdims=True)
    copies[0].wait()
    key = dot(normed, weight[0]).astype(jnp.bfloat16)
    product = query_ref[...].astype(jnp.float32) * key.astype(jnp.float32)
    width = product.shape[1]
    gather = (head_of((width, LANES), 0) == iota((width, LANES), 1)).astype(jnp.bfloat16)
    for part in pieces(product, 3):
        score = score + dot(part, gather)
    lane = iota(score.shape, 1)
    used = width // HEAD_DIM
    peak = jnp.where(lane < used, score, 0.0)
    total = jnp.where((lane >= SUM_LANE) & (lane < SUM_LANE + used), 1.0, 0.0)
    fresh_ref[:, width:] = packed_stats(peak, total)
    copies[1].wait()
    fresh_ref[:, :width] = dot(normed, weight[1]).astype(jnp.bfloat16)
    for copy in later:
        copy.wait()


def load_kernel(start, source, after_ref, target, sems):
    rows = source.at[pl.ds(start, target.shape[0])]
    copies = split_copies(rows, target, sems, sems.shape[0])
    for copy in copies:
        copy.start()
    for copy in copies:
        copy.wait()


def packed_stats(peaks, sums):
    one, two, three = (part.astype(jnp.float32) for part in pieces(peaks + sums, 3))
    packed = one + pltpu.roll(two, PIECE, 1) + pltpu.roll(three, 2 * PIECE, 1)
    return packed.astype(jnp.bfloat16)


def unpacked_stats(packed, heads):
    stats = packed.astype(jnp.float32)
    stats = stats + pltpu.roll(stats, LANES - PIECE, 1) + pltpu.roll(stats, LANES - 2 * PIECE, 1)
    sums = pltpu.roll(stats, LANES - SUM_LANE, 1)
    used = iota(stats.shape, 1) < heads
    return jnp.where(used & (sums > 0.0), stats, far_below), jnp.where(used, sums, 0.0)


def over_columns(values, width):
    spread = (iota((LANES, width), 0) == head_of((LANES, width), 1)).astype(jnp.bfloat16)
    return sum(dot(part, spread) for part in pieces(values, 3))


def attend_kernel(groups, *refs):
    query_refs, refs, sums_refs = refs[:groups], refs[groups:-groups], refs[-groups:]
    bias_ref, pick_ref, place_ref, lead_ref, apart_ref, keys_ref, late_ref, values_ref = refs
    page_count = apart_ref.shape[0]
    width = keys_ref.shape[2]
    early = keys_ref.shape[0]
    chunk = 2
    chunks = page_count // chunk
    queries = jnp.concatenate([ref[...] for ref in query_refs], axis=0)
    own_head = (head_of((PIECE, width), 1) == iota((PIECE, width), 0)).astype(jnp.float32)
    pair_heads = jnp.concatenate([own_head] * chunk, axis=0)
    chosen = dot(pick_ref[...], queries)
    lane = iota((PIECE, LANES), 1)
    row = iota((PIECE, LANES), 0)
    nothing = jnp.zeros((PIECE, PAGE), jnp.float32)
    raws = []
    for c in range(chunks):
        rows = chosen[c * chunk * PIECE : (c + 1) * chunk * PIECE]
        split = (rows * pair_heads).astype(jnp.bfloat16)
        at = c * chunk
        block = keys_ref[at : at + chunk] if at < early else late_ref[at - early : at - early + chunk]
        raws.append(dot(split, block.reshape(chunk * PAGE, width), ((1,), (1,))))
    scores, page_tops = [], []
    for p in range(page_count):
        i = p % chunk
        part = raws[p // chunk][i * PIECE : (i + 1) * PIECE, i * PAGE : (i + 1) * PAGE]
        score = part + bias_ref[p * PIECE : (p + 1) * PIECE]
        scores.append(score)
        page_tops.append(jnp.max(score, axis=1, keepdims=True))
    page_weights = [jnp.exp(score - top) for score, top in zip(scores, page_tops)]
    mixes = []
    for c in range(chunks):
        blocks = []
        for i in range(chunk):
            weight = page_weights[c * chunk + i]
            blocks.append(
                jnp.concatenate([weight if k == i else nothing for k in range(chunk)], axis=1)
            )
        weights = jnp.concatenate(blocks, axis=0).astype(jnp.bfloat16)
        block = values_ref[c * chunk : (c + 1) * chunk]
        mixes.append(dot(weights, block.reshape(chunk * PAGE, width)))
    totals = [jnp.sum(weight, axis=1, keepdims=True) for weight in page_weights]
    tops = jnp.zeros((PIECE, LANES), jnp.float32)
    for p in range(page_count):
        tops = jnp.where(lane == p, page_tops[p], tops)
    stats = []
    for c in range(chunks):
        factors = []
        for p in range(c * chunk, (c + 1) * chunk):
            peak = jnp.max(tops + apart_ref[p : p + 1], axis=1, keepdims=True)
            factor = jnp.exp(page_tops[p] - peak)
            total = jnp.where(lane == row + SUM_LANE, totals[p] * factor, 0.0)
            stats.append(jnp.where(lane == row, peak * lead_ref[p : p + 1], total))
            factors.append(factor)
        mixes[c] = mixes[c] * (pair_heads * jnp.concatenate(factors, axis=0))
    mix = jnp.concatenate(mixes, axis=0).astype(jnp.bfloat16)
    stats = pieces(jnp.concatenate(stats, axis=0), 3)
    sums = dot(place_ref[...], jnp.concatenate([mix] + stats, axis=1))
    stats = sum(sums[:, width + i * LANES : width + (i + 1) * LANES] for i in range(3))
    stats = packed_stats(stats, 0.0).astype(jnp.float32)
    size = sums.shape[0] // groups
    for i, sums_ref in enumerate(sums_refs):
        first, middle, last = i * size, i * size + size // 2, (i + 1) * size
        for c in range(width // LANES):
            block = sums[first:last, c * LANES : (c + 1) * LANES]
            sums_ref[c * size : (c + 1) * size] = block.astype(jnp.bfloat16)
        both = stats[first:middle] + pltpu.roll(stats[middle:last], LANES // 2, 1)
        sums_ref[width // LANES * size :] = both.astype(jnp.bfloat16)


def combine_kernel(sources, *refs):
    part_refs, sums_refs = refs[:sources], refs[sources:]
    width = sums_refs[0].shape[1] - LANES
    rows = sum(ref.shape[0] for ref in sums_refs)
    heads, blocks = width // HEAD_DIM, width // LANES
    stats, mixes = [], []
    for ref in part_refs:
        both = ref[blocks * rows :].astype(jnp.float32)
        both = jnp.concatenate([both, pltpu.roll(both, LANES // 2, 1)], axis=0)
        stats.append(unpacked_stats(both, heads))
        mix = [ref[c * rows : (c + 1) * rows] for c in range(blocks)]
        mixes.append(jnp.concatenate(mix, axis=1).astype(jnp.float32))
    peak = stats[0][0]
    for peaks, _ in stats[1:]:
        peak = jnp.maximum(peak, peaks)
    factors = [jnp.exp(peaks - peak) for peaks, _ in stats]
    total = sum(factor * sums for factor, (_, sums) in zip(factors, stats))
    shares = over_columns(jnp.concatenate(factors, axis=0), width)
    mixed = sum(mix * shares[i * rows : (i + 1) * rows] for i, mix in enumerate(mixes))
    packed = packed_stats(
        jnp.where(total > 0.0, peak, 0.0), pltpu.roll(total, SUM_LANE, 1)
    ).astype(jnp.float32)
    size = sums_refs[0].shape[0]
    for i, sums_ref in enumerate(sums_refs):
        span = slice(i * size, (i + 1) * size)
        sums_ref[:, :width] = mixed[span].astype(jnp.bfloat16)
        sums_ref[:, width:] = packed[span].astype(jnp.bfloat16)


def merge_kernel(
    swapped, sources, hidden_ref, fresh_ref, moved_ref, weight_ref, *refs
):
    part_refs, (own_ref, send_ref) = refs[:sources], refs[sources:]
    width = fresh_ref.shape[1] - LANES
    heads = width // HEAD_DIM
    parts = [ref[...].astype(jnp.float32) for ref in part_refs]
    fresh = fresh_ref[...].astype(jnp.float32)
    if swapped:
        first = lax.axis_index("head") == 0
        fresh = jnp.where(first, fresh, moved_ref[...].astype(jnp.float32))
    parts.append(fresh)
    stats = [unpacked_stats(part[:, width:], heads) for part in parts]
    peak = stats[0][0]
    for peaks, _ in stats[1:]:
        peak = jnp.maximum(peak, peaks)
    factors = [jnp.exp(peaks - peak) for peaks, _ in stats]
    total = sum(factor * sums for factor, (_, sums) in zip(factors, stats))
    total = jnp.where(total > 0.0, total, 1.0)
    shares = over_columns(jnp.concatenate([f / total for f in factors], axis=0), width)
    rows = fresh_ref.shape[0]
    mixed = sum(
        part[:, :width] * shares[i * rows : (i + 1) * rows] for i, part in enumerate(parts)
    )
    projected = dot(mixed.astype(jnp.bfloat16), weight_ref[...])
    if swapped:
        projected = projected + jnp.where(first, hidden_ref[...], 0.0)
        own_ref[...] = projected
        both = [part.astype(jnp.float32) for part in pieces(projected, 2)]
        send_ref[...] = jnp.concatenate(both, axis=0).astype(jnp.bfloat16)
    else:
        own_ref[...] = hidden_ref[...]
        send_ref[...] = projected.astype(jnp.bfloat16)


def mlp_kernel(
    exchanged, own_ref, other_ref, gain_ref, up_ref, down_ref, late_ref, *outs
):
    other = other_ref[...].astype(jnp.float32)
    rows = own_ref.shape[0]
    middle = own_ref[...]
    for at in range(0, other.shape[0], rows):
        middle = middle + other[at : at + rows]
    normed = rms_normed(middle, gain_ref[...])
    active = jnp.maximum(dot(normed, up_ref[...]), 0.0).astype(jnp.bfloat16)
    half = down_ref.shape[0]
    down = dot(active[:, :half], down_ref[...]) + dot(active[:, half:], late_ref[...])
    if exchanged:
        kept_ref, sent_ref = outs
        columns = kept_ref.shape[1]
        low = lax.axis_index("head") == 0
        left, right = slice(0, columns), slice(columns, 2 * columns)
        kept = middle + down

        @pl.when(low)
        def _():
            kept_ref[...] = kept[:, left]
            sent_ref[...] = down[:, right]

        @pl.when(jnp.logical_not(low))
        def _():
            kept_ref[...] = kept[:, right]
            sent_ref[...] = down[:, left]

    else:
        middle_ref, down_out_ref = outs
        middle_ref[...] = middle
        down_out_ref[...] = down.astype(jnp.bfloat16)


def loading(*arrays):
    return pl.CostEstimate(
        flops=0, bytes_accessed=sum(2 * array.size for array in arrays), transcendentals=0
    )


def in_hbm(*arrays):
    return [pltpu.with_memory_space_constraint(array, pltpu.HBM) for array in arrays]


def xor_pairs(size, step):
    return [(i, i ^ step) for i in range(size)]


def per_device(
    hidden_in, attention_gain, mlp_gain, qkv_weight, out_weight, up_weight, down_weight,
    position_bias, bucket_edges, cache_keys, cache_values, lengths, page_request, page_index,
):
    f32, bf16 = jnp.float32, jnp.bfloat16
    shape = jax.ShapeDtypeStruct
    own_rows, model = hidden_in.shape
    width = qkv_weight.shape[2]
    page_count = page_request.shape[0]
    blocks = lax.axis_size("blk")
    all_rows = own_rows * blocks
    halves = lax.axis_size("head")
    columns = model // halves
    exchanged = halves == 2
    gain = attention_gain.reshape(1, model)
    query = pl.pallas_call(
        query_kernel,
        out_shape=shape((own_rows, width), bf16),
        in_specs=[HBM_SPEC] * 3,
        out_specs=VMEM_SPEC,
        scratch_shapes=[
            pltpu.VMEM((own_rows, model), f32),
            pltpu.VMEM((1, model), f32),
            pltpu.VMEM((model, width), bf16),
            pltpu.SemaphoreType.DMA((6,)),
        ],
        compiler_params=PARAMS,
        name="query",
    )(*in_hbm(hidden_in, gain, qkv_weight))

    inner = 1
    while inner * inner < blocks:
        inner *= 2
    far = [query] + [
        lax.ppermute(query, "blk", xor_pairs(blocks, step * inner ^ 1))
        for step in range(1, blocks // inner)
    ]
    depth = page_count * PIECE
    early = page_count // 6 * 2
    keys, picks, place, leads, apart, owners = pl.pallas_call(
        functools.partial(page_kernel, own_rows, inner, blocks // inner, exchanged),
        out_shape=(
            pltpu.VMEM((early,) + cache_keys.shape[1:], bf16),
            shape((depth, all_rows), bf16),
            shape((all_rows, depth), bf16),
            shape((page_count, LANES), f32),
            shape((page_count, LANES), f32),
            shape((page_count, LANES), jnp.int32),
        ),
        in_specs=[ANY_SPEC, VMEM_SPEC, HBM_SPEC],
        out_specs=(VMEM_SPEC,) * 6,
        scratch_shapes=[pltpu.SemaphoreType.DMA((4,))],
        compiler_params=PARAMS,
        cost_estimate=loading(cache_keys),
        name="pages",
    )(query, page_request.reshape(1, page_count), *in_hbm(cache_keys))
    near, apart = lax.optimization_barrier((jnp.concatenate(far, axis=0), apart))
    steps = sorted(range(inner), key=lambda step: -(step ^ (step >> 1)) & (inner - 1))
    gathered = [near] + [lax.ppermute(near, "blk", xor_pairs(blocks, step)) for step in steps[1:]]
    table = position_bias.T
    late_keys, bias = pl.pallas_call(
        bias_kernel,
        out_shape=(
            pltpu.VMEM((page_count - early,) + cache_keys.shape[1:], bf16),
            shape((depth, PAGE), f32),
        ),
        in_specs=[HBM_SPEC] * 4 + [VMEM_SPEC, HBM_SPEC, ANY_SPEC],
        out_specs=(VMEM_SPEC,) * 2,
        scratch_shapes=[
            pltpu.SMEM(table.shape, f32),
            pltpu.SMEM(bucket_edges.shape, jnp.int32),
            pltpu.VMEM((1,) + lengths.shape, jnp.int32),
            pltpu.VMEM((1,) + page_index.shape, jnp.int32),
            pltpu.SemaphoreType.DMA((4,)),
            pltpu.SemaphoreType.DMA((4,)),
        ],
        compiler_params=PARAMS,
        cost_estimate=loading(cache_values),
        name="bias",
    )(
        *in_hbm(table, bucket_edges, lengths[None], page_index[None]), owners,
        *in_hbm(cache_keys), near,
    )

    groups = len(gathered)
    size = all_rows // groups
    message = width // LANES * size + size // 2
    sums = pl.pallas_call(
        functools.partial(attend_kernel, groups),
        out_shape=(shape((message, LANES), bf16),) * groups,
        in_specs=[VMEM_SPEC] * (groups + 8),
        out_specs=(VMEM_SPEC,) * groups,
        compiler_params=PARAMS,
        name="attend",
    )(*gathered, bias, picks, place, leads, apart, keys, late_keys, cache_values)
    near_sums = [sums[0]] + [
        lax.ppermute(sums[i], "blk", xor_pairs(blocks, steps[i]))
        for i in range(1, inner)
    ]

    fresh, out_near = pl.pallas_call(
        side_kernel,
        out_shape=(
            shape((own_rows, width + LANES), bf16),
            pltpu.VMEM(out_weight.shape, bf16),
        ),
        in_specs=[VMEM_SPEC] * 4 + [HBM_SPEC] * 2 + [ANY_SPEC],
        out_specs=(VMEM_SPEC,) * 2,
        scratch_shapes=[
            pltpu.VMEM((2, model, width), bf16),
            pltpu.SemaphoreType.DMA((2,)),
            pltpu.SemaphoreType.DMA((4,)),
        ],
        compiler_params=PARAMS,
        cost_estimate=loading(out_weight, out_weight, out_weight),
        name="side",
    )(
        hidden_in, gain, query, table,
        *in_hbm(qkv_weight, out_weight), sums[0],
    )

    *near_sums, fresh = lax.optimization_barrier((*near_sums, fresh))
    outer = blocks // inner
    sums = pl.pallas_call(
        functools.partial(combine_kernel, inner),
        out_shape=(shape((own_rows, width + LANES), bf16),) * outer,
        in_specs=[VMEM_SPEC] * inner,
        out_specs=(VMEM_SPEC,) * outer,
        compiler_params=PARAMS,
        name="combine",
    )(*near_sums)
    half = down_weight.shape[0] // 2

    def load_down(start, after):
        return pl.pallas_call(
            functools.partial(load_kernel, start),
            out_shape=pltpu.VMEM((half, model), bf16),
            in_specs=[HBM_SPEC, ANY_SPEC],
            out_specs=VMEM_SPEC,
            scratch_shapes=[pltpu.SemaphoreType.DMA((4,))],
            compiler_params=PARAMS,
            cost_estimate=loading(down_weight),
            name="load",
        )(*in_hbm(down_weight), after)

    down_early = load_down(0, sums[0])
    parts = [sums[0]] + [
        lax.ppermute(sums[step], "blk", xor_pairs(blocks, step * inner ^ 1))
        for step in reversed(range(1, outer))
    ]

    moved = lax.ppermute(fresh, "blk", xor_pairs(blocks, 1)) if exchanged else fresh
    *parts, down_early = lax.optimization_barrier((*parts, down_early))
    own_part, sent_part = pl.pallas_call(
        functools.partial(merge_kernel, exchanged, outer),
        out_shape=(
            shape((own_rows, model), f32),
            shape(((2 if exchanged else 1) * own_rows, model), bf16),
        ),
        in_specs=[VMEM_SPEC] * (outer + 4),
        out_specs=(VMEM_SPEC,) * 2,
        compiler_params=PARAMS,
        name="merge",
    )(hidden_in, fresh, moved, out_near, *parts)

    down_late = load_down(half, sent_part)
    axes = ("head", "blk")
    across = [(i, blocks + (i ^ 1)) for i in range(blocks)]
    back = [(b, a) for a, b in across]
    if exchanged:
        other_part = lax.ppermute(sent_part, axes, across + back)
        mlp_out = (shape((own_rows, columns), f32), shape((own_rows, columns), f32))
    else:
        other_part = lax.psum(sent_part, "head")
        mlp_out = (shape((own_rows, model), f32), shape((own_rows, model), bf16))

    kept, leaving = pl.pallas_call(
        functools.partial(mlp_kernel, exchanged),
        out_shape=mlp_out,
        in_specs=[VMEM_SPEC] * 6,
        out_specs=(VMEM_SPEC,) * 2,
        compiler_params=PARAMS,
        name="mlp",
    )(own_part, other_part, mlp_gain.reshape(1, model), up_weight, down_early, down_late)

    if exchanged:
        straight = [(i, blocks + i) for i in range(blocks)]
        arrived = lax.ppermute(leaving, axes, straight + back)
        moved = lax.ppermute(kept, "blk", xor_pairs(blocks, 1))
        kept = jnp.where(lax.axis_index("head") == 0, kept, moved)
    else:
        kept = lax.dynamic_slice_in_dim(kept, lax.axis_index("head") * columns, columns, 1)
        arrived = lax.psum_scatter(leaving, "head", scatter_dimension=1, tiled=True)
    return kept + arrived.astype(f32)


def solution(mesh):
    in_specs = (
        P("blk", None),
        P(),
        P(),
        P(None, None, "head"),
        P("head", None),
        P(None, "head"),
        P("head", None),
        P(None, "head"),
        P(),
        P("blk", None, "head"),
        P("blk", None, "head"),
        P(),
        P("blk"),
        P("blk"),
    )
    out_specs = P("blk", "head")
    return jax.shard_map(
        per_device, mesh=mesh, in_specs=in_specs, out_specs=out_specs, check_vma=False
    )
```

```python
import functools

import jax
import jax.numpy as jnp
from jax import lax
from jax.experimental import pallas as pl
from jax.experimental.pallas import tpu as pltpu
from jax.sharding import PartitionSpec as P

HEAD_DIM = 64
PAGE = 128
LANES = 128

far_below = -1e30
epsilon = 1e-06

VMEM_SPEC = pl.BlockSpec(memory_space=pltpu.VMEM)
SMEM_SPEC = pl.BlockSpec(memory_space=pltpu.SMEM)
ANY_SPEC = pl.BlockSpec(memory_space=pl.ANY)
HBM_SPEC = pl.BlockSpec(memory_space=pltpu.HBM)
PARAMS = pltpu.CompilerParams(vmem_limit_bytes=16 * 1024 * 1024)

PIECE = 8
SUM_LANE = 3 * PIECE


def iota(shape, axis):
    return lax.broadcasted_iota(jnp.int32, shape, axis)


def split_index(x, size):
    if size & (size - 1):
        return lax.div(x, size), lax.rem(x, size)
    return x >> (size.bit_length() - 1), x & (size - 1)


def head_of(shape, axis):
    return split_index(iota(shape, axis), HEAD_DIM)[0]


def pieces(x, count):
    parts = []
    for _ in range(count):
        part = x.astype(jnp.bfloat16)
        parts.append(part)
        x = x - part.astype(jnp.float32)
    return parts


def rms_normed(x, gain):
    scale = lax.rsqrt(jnp.mean(x * x, axis=1, keepdims=True) + epsilon)
    return (x * scale * gain).astype(jnp.bfloat16)


def dot(a, b, dims=((1,), (0,)), precision=None):
    return lax.dot_general(
        a, b, (dims, ((), ())), preferred_element_type=jnp.float32, precision=precision
    )


def split_copies(source, target, sems, count):
    size = source.shape[0] // count
    return [
        pltpu.make_async_copy(
            source.at[pl.ds(i * size, size)], target.at[pl.ds(i * size, size)], sems.at[i]
        )
        for i in range(count)
    ]


def query_kernel(hidden_hbm, gain_hbm, weight_hbm, query_ref, hidden, gain, weight, sems):
    model = hidden.shape[1]
    small = [
        pltpu.make_async_copy(hidden_hbm, hidden, sems.at[0]),
        pltpu.make_async_copy(gain_hbm, gain, sems.at[1]),
    ]
    half = model // 4
    large = [
        pltpu.make_async_copy(
            weight_hbm.at[0, pl.ds(i * half, half)], weight.at[pl.ds(i * half, half)], sems.at[2 + i]
        )
        for i in range(4)
    ]
    for copy in small + large:
        copy.start()
    for copy in small:
        copy.wait()
    normed = rms_normed(hidden[...], gain[...])
    query = None
    for i, copy in enumerate(large):
        copy.wait()
        span = slice(i * half, (i + 1) * half)
        part = dot(normed[:, span], weight[span])
        query = part if query is None else query + part
    query_ref[...] = query.astype(jnp.bfloat16)


def page_kernel(
    own_rows, inner, outer, swapped, query_ref, request_ref, keys_hbm,
    keys_ref, pick_ref, place_ref, lead_ref, apart_ref, owners_ref,
    sems,
):
    copies = split_copies(
        keys_hbm.at[pl.ds(0, keys_ref.shape[0])], keys_ref, sems, sems.shape[0]
    )
    for copy in copies:
        copy.start()
    me = lax.axis_index("blk")
    page_count = apart_ref.shape[0]
    all_rows, depth = place_ref.shape
    page, lane = iota((page_count, page_count), 0), iota((page_count, page_count), 1)
    by_lane = request_ref[...]
    owner = jnp.max(jnp.where(page == lane, by_lane, -1), axis=1, keepdims=True)
    same = by_lane == owner
    apart_ref[...] = jnp.full(apart_ref.shape, 2 * far_below, jnp.float32)
    apart_ref[:, :page_count] = jnp.where(same, 0.0, 2 * far_below)
    earlier = jnp.max(jnp.where(same & (lane < page), 1, 0), axis=1, keepdims=True)
    lead_ref[...] = jnp.broadcast_to(jnp.where(earlier == 0, 1.0, 0.0), lead_ref.shape)
    owners_ref[...] = jnp.broadcast_to(owner, owners_ref.shape)
    device, own_row = split_index(jnp.maximum(owner, 0), own_rows)

    def slot_of(device, order):
        high, low = split_index(device ^ me, inner)
        low = jnp.where(high == 0, low, low ^ 1)
        low = -(low ^ (low >> 1)) & (inner - 1)
        slot = (low * outer + order(high)) * own_rows + own_row
        return jnp.where(owner >= 0, slot, -1)

    slot = slot_of(device, lambda high: high ^ (high >> 1))
    sum_device = device ^ lax.axis_index("head") if swapped else device
    sum_slot = slot_of(sum_device, lambda high: high)
    row_of = iota((page_count, all_rows), 1)
    picks = jnp.where(row_of == slot, 1.0, 0.0)
    picks = [jnp.broadcast_to(picks[p : p + 1], (PIECE, all_rows)) for p in range(page_count)]
    pick_ref[...] = jnp.concatenate(picks, axis=0).astype(jnp.bfloat16)
    mine = split_index(iota((page_count, depth), 1), PIECE)[0] == iota((page_count, depth), 0)
    row = iota((all_rows, depth), 0)
    spread = jnp.max(jnp.where(mine, sum_slot, -1), axis=0, keepdims=True)
    place_ref[...] = (row == spread).astype(jnp.bfloat16)
    for copy in copies:
        copy.wait()


def bias_kernel(
    table_hbm, edges_hbm, lengths_hbm, index_hbm, owners_ref, keys_hbm, after_ref,
    keys_ref, bias_ref,
    table, edges, lengths, index, small_sems, sems,
):
    sources, targets = (table_hbm, edges_hbm, lengths_hbm, index_hbm), (table, edges, lengths, index)
    small = [
        pltpu.make_async_copy(source, target, small_sems.at[i])
        for i, (source, target) in enumerate(zip(sources, targets))
    ]
    late = keys_ref.shape[0]
    copies = split_copies(
        keys_hbm.at[pl.ds(keys_hbm.shape[0] - late, late)], keys_ref, sems, sems.shape[0]
    )
    for copy in small + copies:
        copy.start()
    for copy in small:
        copy.wait()
    heads, buckets = table.shape
    page_count = index.shape[1]
    owner = owners_ref[:, 0:1]
    square = (page_count, page_count)
    number = jnp.where(iota(square, 0) == iota(square, 1), index[...], 0)
    number = jnp.sum(number, axis=1, keepdims=True)
    requests = lengths.shape[1]
    length = jnp.where(iota((page_count, requests), 1) == owner, lengths[...], 0)
    length = jnp.sum(length, axis=1, keepdims=True)
    distance = length - number * PAGE - iota((page_count, PAGE), 1)
    far = [distance >= edges[k] for k in range(buckets - 1)]
    usable = (owner >= 0) & (distance > 0)
    bias_ref[...] = jnp.full(bias_ref.shape, far_below, jnp.float32)
    for h in range(heads):
        bias = jnp.full((page_count, PAGE), table[h, 0], jnp.float32)
        for k in range(buckets - 1):
            bias = jnp.where(far[k], table[h, k + 1], bias)
        bias_ref[pl.ds(h, page_count, stride=PIECE), :] = jnp.where(usable, bias, far_below)
    for copy in copies:
        copy.wait()


def side_kernel(
    hidden_ref, gain_ref, query_ref, table_ref, weight_hbm, out_hbm, after_ref,
    fresh_ref, out_ref,
    weight, weight_sems, sems,
):
    copies = [
        pltpu.make_async_copy(weight_hbm.at[1 + i], weight.at[i], weight_sems.at[i])
        for i in range(2)
    ]
    later = split_copies(out_hbm, out_ref, sems, sems.shape[0])
    for copy in copies + later:
        copy.start()
    normed = rms_normed(hidden_ref[...], gain_ref[...])
    heads = table_ref.shape[0]
    spread = iota((heads, LANES), 0) == iota((heads, LANES), 1)
    score = jnp.sum(jnp.where(spread, table_ref[:, 0:1], 0.0), axis=0, keepdims=True)
    copies[0].wait()
    key = dot(normed, weight[0]).astype(jnp.bfloat16)
    product = query_ref[...].astype(jnp.float32) * key.astype(jnp.float32)
    width = product.shape[1]
    gather = (head_of((width, LANES), 0) == iota((width, LANES), 1)).astype(jnp.bfloat16)
    for part in pieces(product, 3):
        score = score + dot(part, gather)
    lane = iota(score.shape, 1)
    used = width // HEAD_DIM
    peak = jnp.where(lane < used, score, 0.0)
    total = jnp.where((lane >= SUM_LANE) & (lane < SUM_LANE + used), 1.0, 0.0)
    fresh_ref[:, width:] = packed_stats(peak, total)
    copies[1].wait()
    fresh_ref[:, :width] = dot(normed, weight[1]).astype(jnp.bfloat16)
    for copy in later:
        copy.wait()


def load_kernel(start, source, after_ref, target, sems):
    rows = source.at[pl.ds(start, target.shape[0])]
    copies = split_copies(rows, target, sems, sems.shape[0])
    for copy in copies:
        copy.start()
    for copy in copies:
        copy.wait()


def packed_stats(peaks, sums):
    one, two, three = (part.astype(jnp.float32) for part in pieces(peaks + sums, 3))
    packed = one + pltpu.roll(two, PIECE, 1) + pltpu.roll(three, 2 * PIECE, 1)
    return packed.astype(jnp.bfloat16)


def unpacked_stats(packed, heads):
    stats = packed.astype(jnp.float32)
    stats = stats + pltpu.roll(stats, LANES - PIECE, 1) + pltpu.roll(stats, LANES - 2 * PIECE, 1)
    sums = pltpu.roll(stats, LANES - SUM_LANE, 1)
    used = iota(stats.shape, 1) < heads
    return jnp.where(used & (sums > 0.0), stats, far_below), jnp.where(used, sums, 0.0)


def over_columns(values, width):
    spread = (iota((LANES, width), 0) == head_of((LANES, width), 1)).astype(jnp.bfloat16)
    return sum(dot(part, spread) for part in pieces(values, 3))


def attend_kernel(groups, *refs):
    query_refs, refs, sums_refs = refs[:groups], refs[groups:-groups], refs[-groups:]
    bias_ref, pick_ref, place_ref, lead_ref, apart_ref, keys_ref, late_ref, values_ref = refs
    page_count = apart_ref.shape[0]
    width = keys_ref.shape[2]
    early = keys_ref.shape[0]
    chunk = 2
    chunks = page_count // chunk
    queries = jnp.concatenate([ref[...] for ref in query_refs], axis=0)
    own_head = (head_of((PIECE, width), 1) == iota((PIECE, width), 0)).astype(jnp.float32)
    pair_heads = jnp.concatenate([own_head] * chunk, axis=0)
    chosen = dot(pick_ref[...], queries)
    lane = iota((PIECE, LANES), 1)
    row = iota((PIECE, LANES), 0)
    nothing = jnp.zeros((PIECE, PAGE), jnp.float32)
    raws = []
    for c in range(chunks):
        rows = chosen[c * chunk * PIECE : (c + 1) * chunk * PIECE]
        split = (rows * pair_heads).astype(jnp.bfloat16)
        at = c * chunk
        block = keys_ref[at : at + chunk] if at < early else late_ref[at - early : at - early + chunk]
        raws.append(dot(split, block.reshape(chunk * PAGE, width), ((1,), (1,))))
    scores, page_tops = [], []
    for p in range(page_count):
        i = p % chunk
        part = raws[p // chunk][i * PIECE : (i + 1) * PIECE, i * PAGE : (i + 1) * PAGE]
        score = part + bias_ref[p * PIECE : (p + 1) * PIECE]
        scores.append(score)
        page_tops.append(jnp.max(score, axis=1, keepdims=True))
    page_weights = [jnp.exp(score - top) for score, top in zip(scores, page_tops)]
    mixes = []
    for c in range(chunks):
        blocks = []
        for i in range(chunk):
            weight = page_weights[c * chunk + i]
            blocks.append(
                jnp.concatenate([weight if k == i else nothing for k in range(chunk)], axis=1)
            )
        weights = jnp.concatenate(blocks, axis=0).astype(jnp.bfloat16)
        block = values_ref[c * chunk : (c + 1) * chunk]
        mixes.append(dot(weights, block.reshape(chunk * PAGE, width)))
    totals = [jnp.sum(weight, axis=1, keepdims=True) for weight in page_weights]
    tops = jnp.zeros((PIECE, LANES), jnp.float32)
    for p in range(page_count):
        tops = jnp.where(lane == p, page_tops[p], tops)
    stats = []
    for c in range(chunks):
        factors = []
        for p in range(c * chunk, (c + 1) * chunk):
            peak = jnp.max(tops + apart_ref[p : p + 1], axis=1, keepdims=True)
            factor = jnp.exp(page_tops[p] - peak)
            total = jnp.where(lane == row + SUM_LANE, totals[p] * factor, 0.0)
            stats.append(jnp.where(lane == row, peak * lead_ref[p : p + 1], total))
            factors.append(factor)
        mixes[c] = mixes[c] * (pair_heads * jnp.concatenate(factors, axis=0))
    mix = jnp.concatenate(mixes, axis=0).astype(jnp.bfloat16)
    stats = pieces(jnp.concatenate(stats, axis=0), 3)
    sums = dot(place_ref[...], jnp.concatenate([mix] + stats, axis=1))
    stats = sum(sums[:, width + i * LANES : width + (i + 1) * LANES] for i in range(3))
    stats = packed_stats(stats, 0.0).astype(jnp.float32)
    size = sums.shape[0] // groups
    for i, sums_ref in enumerate(sums_refs):
        first, middle, last = i * size, i * size + size // 2, (i + 1) * size
        for c in range(width // LANES):
            block = sums[first:last, c * LANES : (c + 1) * LANES]
            sums_ref[c * size : (c + 1) * size] = block.astype(jnp.bfloat16)
        both = stats[first:middle] + pltpu.roll(stats[middle:last], LANES // 2, 1)
        sums_ref[width // LANES * size :] = both.astype(jnp.bfloat16)


def combine_kernel(sources, *refs):
    part_refs, sums_refs = refs[:sources], refs[sources:]
    width = sums_refs[0].shape[1] - LANES
    rows = sum(ref.shape[0] for ref in sums_refs)
    heads, blocks = width // HEAD_DIM, width // LANES
    stats, mixes = [], []
    for ref in part_refs:
        both = ref[blocks * rows :].astype(jnp.float32)
        both = jnp.concatenate([both, pltpu.roll(both, LANES // 2, 1)], axis=0)
        stats.append(unpacked_stats(both, heads))
        mix = [ref[c * rows : (c + 1) * rows] for c in range(blocks)]
        mixes.append(jnp.concatenate(mix, axis=1).astype(jnp.float32))
    peak = stats[0][0]
    for peaks, _ in stats[1:]:
        peak = jnp.maximum(peak, peaks)
    factors = [jnp.exp(peaks - peak) for peaks, _ in stats]
    total = sum(factor * sums for factor, (_, sums) in zip(factors, stats))
    shares = over_columns(jnp.concatenate(factors, axis=0), width)
    mixed = sum(mix * shares[i * rows : (i + 1) * rows] for i, mix in enumerate(mixes))
    packed = packed_stats(
        jnp.where(total > 0.0, peak, 0.0), pltpu.roll(total, SUM_LANE, 1)
    ).astype(jnp.float32)
    size = sums_refs[0].shape[0]
    for i, sums_ref in enumerate(sums_refs):
        span = slice(i * size, (i + 1) * size)
        sums_ref[:, :width] = mixed[span].astype(jnp.bfloat16)
        sums_ref[:, width:] = packed[span].astype(jnp.bfloat16)


def merge_kernel(
    swapped, sources, hidden_ref, fresh_ref, moved_ref, weight_ref, *refs
):
    part_refs, (own_ref, send_ref) = refs[:sources], refs[sources:]
    width = fresh_ref.shape[1] - LANES
    heads = width // HEAD_DIM
    parts = [ref[...].astype(jnp.float32) for ref in part_refs]
    fresh = fresh_ref[...].astype(jnp.float32)
    if swapped:
        first = lax.axis_index("head") == 0
        fresh = jnp.where(first, fresh, moved_ref[...].astype(jnp.float32))
    parts.append(fresh)
    stats = [unpacked_stats(part[:, width:], heads) for part in parts]
    peak = stats[0][0]
    for peaks, _ in stats[1:]:
        peak = jnp.maximum(peak, peaks)
    factors = [jnp.exp(peaks - peak) for peaks, _ in stats]
    total = sum(factor * sums for factor, (_, sums) in zip(factors, stats))
    total = jnp.where(total > 0.0, total, 1.0)
    shares = over_columns(jnp.concatenate([f / total for f in factors], axis=0), width)
    rows = fresh_ref.shape[0]
    mixed = sum(
        part[:, :width] * shares[i * rows : (i + 1) * rows] for i, part in enumerate(parts)
    )
    projected = dot(mixed.astype(jnp.bfloat16), weight_ref[...])
    if swapped:
        projected = projected + jnp.where(first, hidden_ref[...], 0.0)
        own_ref[...] = projected
        both = [part.astype(jnp.float32) for part in pieces(projected, 2)]
        send_ref[...] = jnp.concatenate(both, axis=0).astype(jnp.bfloat16)
    else:
        own_ref[...] = hidden_ref[...]
        send_ref[...] = projected.astype(jnp.bfloat16)


def mlp_kernel(
    exchanged, own_ref, other_ref, gain_ref, up_ref, down_ref, late_ref, *outs
):
    other = other_ref[...].astype(jnp.float32)
    rows = own_ref.shape[0]
    middle = own_ref[...]
    for at in range(0, other.shape[0], rows):
        middle = middle + other[at : at + rows]
    normed = rms_normed(middle, gain_ref[...])
    active = jnp.maximum(dot(normed, up_ref[...]), 0.0).astype(jnp.bfloat16)
    half = down_ref.shape[0]
    down = dot(active[:, :half], down_ref[...]) + dot(active[:, half:], late_ref[...])
    if exchanged:
        kept_ref, sent_ref = outs
        columns = kept_ref.shape[1]
        low = lax.axis_index("head") == 0
        left, right = slice(0, columns), slice(columns, 2 * columns)
        kept = middle + down

        @pl.when(low)
        def _():
            kept_ref[...] = kept[:, left]
            sent_ref[...] = down[:, right]

        @pl.when(jnp.logical_not(low))
        def _():
            kept_ref[...] = kept[:, right]
            sent_ref[...] = down[:, left]

    else:
        middle_ref, down_out_ref = outs
        middle_ref[...] = middle
        down_out_ref[...] = down.astype(jnp.bfloat16)


def loading(*arrays):
    return pl.CostEstimate(
        flops=0, bytes_accessed=sum(2 * array.size for array in arrays), transcendentals=0
    )


def in_hbm(*arrays):
    return [pltpu.with_memory_space_constraint(array, pltpu.HBM) for array in arrays]


def xor_pairs(size, step):
    return [(i, i ^ step) for i in range(size)]


def per_device(
    hidden_in, attention_gain, mlp_gain, qkv_weight, out_weight, up_weight, down_weight,
    position_bias, bucket_edges, cache_keys, cache_values, lengths, page_request, page_index,
):
    f32, bf16 = jnp.float32, jnp.bfloat16
    shape = jax.ShapeDtypeStruct
    own_rows, model = hidden_in.shape
    width = qkv_weight.shape[2]
    page_count = page_request.shape[0]
    blocks = lax.axis_size("blk")
    all_rows = own_rows * blocks
    halves = lax.axis_size("head")
    columns = model // halves
    exchanged = halves == 2
    gain = attention_gain.reshape(1, model)
    query = pl.pallas_call(
        query_kernel,
        out_shape=shape((own_rows, width), bf16),
        in_specs=[HBM_SPEC] * 3,
        out_specs=VMEM_SPEC,
        scratch_shapes=[
            pltpu.VMEM((own_rows, model), f32),
            pltpu.VMEM((1, model), f32),
            pltpu.VMEM((model, width), bf16),
            pltpu.SemaphoreType.DMA((6,)),
        ],
        compiler_params=PARAMS,
        name="query",
    )(*in_hbm(hidden_in, gain, qkv_weight))

    inner = 1
    while inner * inner < blocks:
        inner *= 2
    far = [query] + [
        lax.ppermute(query, "blk", xor_pairs(blocks, step * inner ^ 1))
        for step in sorted(range(blocks // inner), key=lambda step: step ^ (step >> 1))[1:]
    ]
    depth = page_count * PIECE
    early = page_count // 6 * 2
    keys, picks, place, leads, apart, owners = pl.pallas_call(
        functools.partial(page_kernel, own_rows, inner, blocks // inner, exchanged),
        out_shape=(
            pltpu.VMEM((early,) + cache_keys.shape[1:], bf16),
            shape((depth, all_rows), bf16),
            shape((all_rows, depth), bf16),
            shape((page_count, LANES), f32),
            shape((page_count, LANES), f32),
            shape((page_count, LANES), jnp.int32),
        ),
        in_specs=[ANY_SPEC, VMEM_SPEC, HBM_SPEC],
        out_specs=(VMEM_SPEC,) * 6,
        scratch_shapes=[pltpu.SemaphoreType.DMA((4,))],
        compiler_params=PARAMS,
        cost_estimate=loading(cache_keys),
        name="pages",
    )(query, page_request.reshape(1, page_count), *in_hbm(cache_keys))
    near, apart = lax.optimization_barrier((jnp.concatenate(far, axis=0), apart))
    steps = sorted(range(inner), key=lambda step: -(step ^ (step >> 1)) & (inner - 1))
    gathered = [near] + [lax.ppermute(near, "blk", xor_pairs(blocks, step)) for step in steps[1:]]
    table = position_bias.T
    late_keys, bias = pl.pallas_call(
        bias_kernel,
        out_shape=(
            pltpu.VMEM((page_count - early,) + cache_keys.shape[1:], bf16),
            shape((depth, PAGE), f32),
        ),
        in_specs=[HBM_SPEC] * 4 + [VMEM_SPEC, HBM_SPEC, ANY_SPEC],
        out_specs=(VMEM_SPEC,) * 2,
        scratch_shapes=[
            pltpu.SMEM(table.shape, f32),
            pltpu.SMEM(bucket_edges.shape, jnp.int32),
            pltpu.VMEM((1,) + lengths.shape, jnp.int32),
            pltpu.VMEM((1,) + page_index.shape, jnp.int32),
            pltpu.SemaphoreType.DMA((4,)),
            pltpu.SemaphoreType.DMA((4,)),
        ],
        compiler_params=PARAMS,
        cost_estimate=loading(cache_values),
        name="bias",
    )(
        *in_hbm(table, bucket_edges, lengths[None], page_index[None]), owners,
        *in_hbm(cache_keys), near,
    )

    groups = len(gathered)
    size = all_rows // groups
    message = width // LANES * size + size // 2
    sums = pl.pallas_call(
        functools.partial(attend_kernel, groups),
        out_shape=(shape((message, LANES), bf16),) * groups,
        in_specs=[VMEM_SPEC] * (groups + 8),
        out_specs=(VMEM_SPEC,) * groups,
        compiler_params=PARAMS,
        name="attend",
    )(*gathered, bias, picks, place, leads, apart, keys, late_keys, cache_values)
    near_sums = [sums[0]] + [
        lax.ppermute(sums[i], "blk", xor_pairs(blocks, steps[i]))
        for i in range(1, inner)
    ]

    fresh, out_near = pl.pallas_call(
        side_kernel,
        out_shape=(
            shape((own_rows, width + LANES), bf16),
            pltpu.VMEM(out_weight.shape, bf16),
        ),
        in_specs=[VMEM_SPEC] * 4 + [HBM_SPEC] * 2 + [ANY_SPEC],
        out_specs=(VMEM_SPEC,) * 2,
        scratch_shapes=[
            pltpu.VMEM((2, model, width), bf16),
            pltpu.SemaphoreType.DMA((2,)),
            pltpu.SemaphoreType.DMA((4,)),
        ],
        compiler_params=PARAMS,
        cost_estimate=loading(out_weight, out_weight, out_weight),
        name="side",
    )(
        hidden_in, gain, query, table,
        *in_hbm(qkv_weight, out_weight), sums[0],
    )

    *near_sums, fresh = lax.optimization_barrier((*near_sums, fresh))
    outer = blocks // inner
    sums = pl.pallas_call(
        functools.partial(combine_kernel, inner),
        out_shape=(shape((own_rows, width + LANES), bf16),) * outer,
        in_specs=[VMEM_SPEC] * inner,
        out_specs=(VMEM_SPEC,) * outer,
        compiler_params=PARAMS,
        name="combine",
    )(*near_sums)
    half = down_weight.shape[0] // 2

    def load_down(start, after):
        return pl.pallas_call(
            functools.partial(load_kernel, start),
            out_shape=pltpu.VMEM((half, model), bf16),
            in_specs=[HBM_SPEC, ANY_SPEC],
            out_specs=VMEM_SPEC,
            scratch_shapes=[pltpu.SemaphoreType.DMA((4,))],
            compiler_params=PARAMS,
            cost_estimate=loading(down_weight),
            name="load",
        )(*in_hbm(down_weight), after)

    down_early = load_down(0, sums[0])
    parts = [sums[0]] + [
        lax.ppermute(sums[step], "blk", xor_pairs(blocks, step * inner ^ 1))
        for step in reversed(range(1, outer))
    ]

    moved = lax.ppermute(fresh, "blk", xor_pairs(blocks, 1)) if exchanged else fresh
    *parts, down_early = lax.optimization_barrier((*parts, down_early))
    own_part, sent_part = pl.pallas_call(
        functools.partial(merge_kernel, exchanged, outer),
        out_shape=(
            shape((own_rows, model), f32),
            shape(((2 if exchanged else 1) * own_rows, model), bf16),
        ),
        in_specs=[VMEM_SPEC] * (outer + 4),
        out_specs=(VMEM_SPEC,) * 2,
        compiler_params=PARAMS,
        name="merge",
    )(hidden_in, fresh, moved, out_near, *parts)

    down_late = load_down(half, sent_part)
    axes = ("head", "blk")
    across = [(i, blocks + (i ^ 1)) for i in range(blocks)]
    back = [(b, a) for a, b in across]
    if exchanged:
        other_part = lax.ppermute(sent_part, axes, across + back)
        mlp_out = (shape((own_rows, columns), f32), shape((own_rows, columns), f32))
    else:
        other_part = lax.psum(sent_part, "head")
        mlp_out = (shape((own_rows, model), f32), shape((own_rows, model), bf16))

    kept, leaving = pl.pallas_call(
        functools.partial(mlp_kernel, exchanged),
        out_shape=mlp_out,
        in_specs=[VMEM_SPEC] * 6,
        out_specs=(VMEM_SPEC,) * 2,
        compiler_params=PARAMS,
        name="mlp",
    )(own_part, other_part, mlp_gain.reshape(1, model), up_weight, down_early, down_late)

    if exchanged:
        straight = [(i, blocks + i) for i in range(blocks)]
        arrived = lax.ppermute(leaving, axes, straight + back)
        moved = lax.ppermute(kept, "blk", xor_pairs(blocks, 1))
        kept = jnp.where(lax.axis_index("head") == 0, kept, moved)
    else:
        kept = lax.dynamic_slice_in_dim(kept, lax.axis_index("head") * columns, columns, 1)
        arrived = lax.psum_scatter(leaving, "head", scatter_dimension=1, tiled=True)
    return kept + arrived.astype(f32)


def solution(mesh):
    in_specs = (
        P("blk", None),
        P(),
        P(),
        P(None, None, "head"),
        P("head", None),
        P(None, "head"),
        P("head", None),
        P(None, "head"),
        P(),
        P("blk", None, "head"),
        P("blk", None, "head"),
        P(),
        P("blk"),
        P("blk"),
    )
    out_specs = P("blk", "head")
    return jax.shard_map(
        per_device, mesh=mesh, in_specs=in_specs, out_specs=out_specs, check_vma=False
    )
```

```python
import functools

import jax
import jax.numpy as jnp
from jax import lax
from jax.experimental import pallas as pl
from jax.experimental.pallas import tpu as pltpu
from jax.sharding import PartitionSpec as P

HEAD_DIM = 64
PAGE = 128
LANES = 128

far_below = -1e30
epsilon = 1e-06

VMEM_SPEC = pl.BlockSpec(memory_space=pltpu.VMEM)
SMEM_SPEC = pl.BlockSpec(memory_space=pltpu.SMEM)
ANY_SPEC = pl.BlockSpec(memory_space=pl.ANY)
HBM_SPEC = pl.BlockSpec(memory_space=pltpu.HBM)
PARAMS = pltpu.CompilerParams(vmem_limit_bytes=16 * 1024 * 1024)

PIECE = 8
SUM_LANE = 3 * PIECE


def iota(shape, axis):
    return lax.broadcasted_iota(jnp.int32, shape, axis)


def split_index(x, size):
    if size & (size - 1):
        return lax.div(x, size), lax.rem(x, size)
    return x >> (size.bit_length() - 1), x & (size - 1)


def head_of(shape, axis):
    return split_index(iota(shape, axis), HEAD_DIM)[0]


def pieces(x, count):
    parts = []
    for _ in range(count):
        part = x.astype(jnp.bfloat16)
        parts.append(part)
        x = x - part.astype(jnp.float32)
    return parts


def rms_normed(x, gain):
    scale = lax.rsqrt(jnp.mean(x * x, axis=1, keepdims=True) + epsilon)
    return (x * scale * gain).astype(jnp.bfloat16)


def dot(a, b, dims=((1,), (0,)), precision=None):
    return lax.dot_general(
        a, b, (dims, ((), ())), preferred_element_type=jnp.float32, precision=precision
    )


def split_copies(source, target, sems, count):
    size = source.shape[0] // count
    return [
        pltpu.make_async_copy(
            source.at[pl.ds(i * size, size)], target.at[pl.ds(i * size, size)], sems.at[i]
        )
        for i in range(count)
    ]


def query_kernel(hidden_hbm, gain_hbm, weight_hbm, query_ref, hidden, gain, weight, sems):
    model = hidden.shape[1]
    small = [
        pltpu.make_async_copy(hidden_hbm, hidden, sems.at[0]),
        pltpu.make_async_copy(gain_hbm, gain, sems.at[1]),
    ]
    half = model // 4
    large = [
        pltpu.make_async_copy(
            weight_hbm.at[0, pl.ds(i * half, half)], weight.at[pl.ds(i * half, half)], sems.at[2 + i]
        )
        for i in range(4)
    ]
    for copy in small + large:
        copy.start()
    for copy in small:
        copy.wait()
    normed = rms_normed(hidden[...], gain[...])
    query = None
    for i, copy in enumerate(large):
        copy.wait()
        span = slice(i * half, (i + 1) * half)
        part = dot(normed[:, span], weight[span])
        query = part if query is None else query + part
    query_ref[...] = query.astype(jnp.bfloat16)


def page_kernel(
    own_rows, inner, outer, swapped, query_ref, request_ref, keys_hbm,
    keys_ref, pick_ref, place_ref, lead_ref, apart_ref, owners_ref,
    sems,
):
    copies = split_copies(
        keys_hbm.at[pl.ds(0, keys_ref.shape[0])], keys_ref, sems, sems.shape[0]
    )
    for copy in copies:
        copy.start()
    me = lax.axis_index("blk")
    page_count = apart_ref.shape[0]
    all_rows, depth = place_ref.shape
    page, lane = iota((page_count, page_count), 0), iota((page_count, page_count), 1)
    by_lane = request_ref[...]
    owner = jnp.max(jnp.where(page == lane, by_lane, -1), axis=1, keepdims=True)
    same = by_lane == owner
    apart_ref[...] = jnp.full(apart_ref.shape, 2 * far_below, jnp.float32)
    apart_ref[:, :page_count] = jnp.where(same, 0.0, 2 * far_below)
    earlier = jnp.max(jnp.where(same & (lane < page), 1, 0), axis=1, keepdims=True)
    lead_ref[...] = jnp.broadcast_to(jnp.where(earlier == 0, 1.0, 0.0), lead_ref.shape)
    owners_ref[...] = jnp.broadcast_to(owner, owners_ref.shape)
    device, own_row = split_index(jnp.maximum(owner, 0), own_rows)

    def slot_of(device):
        high, low = split_index(device ^ me, inner)
        low = jnp.where(high == 0, low, low ^ 1)
        low = -(low ^ (low >> 1)) & (inner - 1)
        slot = (low * outer + high) * own_rows + own_row
        return jnp.where(owner >= 0, slot, -1)

    slot = slot_of(device)
    sum_slot = slot_of(device ^ lax.axis_index("head")) if swapped else slot
    row_of = iota((page_count, all_rows), 1)
    picks = jnp.where(row_of == slot, 1.0, 0.0)
    picks = [jnp.broadcast_to(picks[p : p + 1], (PIECE, all_rows)) for p in range(page_count)]
    pick_ref[...] = jnp.concatenate(picks, axis=0).astype(jnp.bfloat16)
    mine = split_index(iota((page_count, depth), 1), PIECE)[0] == iota((page_count, depth), 0)
    row = iota((all_rows, depth), 0)
    spread = jnp.max(jnp.where(mine, sum_slot, -1), axis=0, keepdims=True)
    place_ref[...] = (row == spread).astype(jnp.bfloat16)
    for copy in copies:
        copy.wait()


def bias_kernel(
    table_hbm, edges_hbm, lengths_hbm, index_hbm, owners_ref, keys_hbm, after_ref,
    keys_ref, bias_ref,
    table, edges, lengths, index, small_sems, sems,
):
    sources, targets = (table_hbm, edges_hbm, lengths_hbm, index_hbm), (table, edges, lengths, index)
    small = [
        pltpu.make_async_copy(source, target, small_sems.at[i])
        for i, (source, target) in enumerate(zip(sources, targets))
    ]
    late = keys_ref.shape[0]
    copies = split_copies(
        keys_hbm.at[pl.ds(keys_hbm.shape[0] - late, late)], keys_ref, sems, sems.shape[0]
    )
    for copy in small + copies:
        copy.start()
    for copy in small:
        copy.wait()
    heads, buckets = table.shape
    page_count = index.shape[1]
    owner = owners_ref[:, 0:1]
    square = (page_count, page_count)
    number = jnp.where(iota(square, 0) == iota(square, 1), index[...], 0)
    number = jnp.sum(number, axis=1, keepdims=True)
    requests = lengths.shape[1]
    length = jnp.where(iota((page_count, requests), 1) == owner, lengths[...], 0)
    length = jnp.sum(length, axis=1, keepdims=True)
    distance = length - number * PAGE - iota((page_count, PAGE), 1)
    far = [distance >= edges[k] for k in range(buckets - 1)]
    usable = (owner >= 0) & (distance > 0)
    bias_ref[...] = jnp.full(bias_ref.shape, far_below, jnp.float32)
    for h in range(heads):
        bias = jnp.full((page_count, PAGE), table[h, 0], jnp.float32)
        for k in range(buckets - 1):
            bias = jnp.where(far[k], table[h, k + 1], bias)
        bias_ref[pl.ds(h, page_count, stride=PIECE), :] = jnp.where(usable, bias, far_below)
    for copy in copies:
        copy.wait()


def side_kernel(
    hidden_ref, gain_ref, query_ref, table_ref, weight_hbm, out_hbm, after_ref,
    fresh_ref, out_ref, spread_ref,
    weight, weight_sems, sems,
):
    copies = [
        pltpu.make_async_copy(weight_hbm.at[1 + i], weight.at[i], weight_sems.at[i])
        for i in range(2)
    ]
    later = split_copies(out_hbm, out_ref, sems, sems.shape[0])
    for copy in copies + later:
        copy.start()
    normed = rms_normed(hidden_ref[...], gain_ref[...])
    heads = table_ref.shape[0]
    spread = iota((heads, LANES), 0) == iota((heads, LANES), 1)
    score = jnp.sum(jnp.where(spread, table_ref[:, 0:1], 0.0), axis=0, keepdims=True)
    copies[0].wait()
    key = dot(normed, weight[0]).astype(jnp.bfloat16)
    product = query_ref[...].astype(jnp.float32) * key.astype(jnp.float32)
    width = product.shape[1]
    gather = (head_of((width, LANES), 0) == iota((width, LANES), 1)).astype(jnp.bfloat16)
    for part in pieces(product, 3):
        score = score + dot(part, gather)
    lane = iota(score.shape, 1)
    used = width // HEAD_DIM
    peak = jnp.where(lane < used, score, 0.0)
    total = jnp.where((lane >= SUM_LANE) & (lane < SUM_LANE + used), 1.0, 0.0)
    fresh_ref[:, width:] = packed_stats(peak, total)
    spread = (iota((LANES, width), 0) == head_of((LANES, width), 1)).astype(jnp.bfloat16)
    spread_ref[:LANES] = spread
    spread_ref[LANES:] = spread
    copies[1].wait()
    fresh_ref[:, :width] = dot(normed, weight[1]).astype(jnp.bfloat16)
    for copy in later:
        copy.wait()


def load_kernel(start, source, after_ref, target, sems):
    rows = source.at[pl.ds(start, target.shape[0])]
    copies = split_copies(rows, target, sems, sems.shape[0])
    for copy in copies:
        copy.start()
    for copy in copies:
        copy.wait()


def packed_stats(peaks, sums):
    one, two, three = (part.astype(jnp.float32) for part in pieces(peaks + sums, 3))
    packed = one + pltpu.roll(two, PIECE, 1) + pltpu.roll(three, 2 * PIECE, 1)
    return packed.astype(jnp.bfloat16)


def unpacked_stats(packed, heads):
    stats = packed.astype(jnp.float32)
    stats = stats + pltpu.roll(stats, LANES - PIECE, 1) + pltpu.roll(stats, LANES - 2 * PIECE, 1)
    sums = pltpu.roll(stats, LANES - SUM_LANE, 1)
    used = iota(stats.shape, 1) < heads
    return jnp.where(used & (sums > 0.0), stats, far_below), jnp.where(used, sums, 0.0)


def over_columns(values, spread):
    return dot(jnp.concatenate(pieces(values, 2), axis=1), spread)


def attend_kernel(groups, *refs):
    query_refs, refs, sums_refs = refs[:groups], refs[groups:-groups], refs[-groups:]
    bias_ref, pick_ref, place_ref, lead_ref, apart_ref, keys_ref, late_ref, values_ref = refs
    page_count = apart_ref.shape[0]
    width = keys_ref.shape[2]
    early = keys_ref.shape[0]
    chunk = 2
    chunks = page_count // chunk
    queries = jnp.concatenate([ref[...] for ref in query_refs], axis=0)
    own_head = (head_of((PIECE, width), 1) == iota((PIECE, width), 0)).astype(jnp.float32)
    pair_heads = jnp.concatenate([own_head] * chunk, axis=0)
    chosen = dot(pick_ref[...], queries)
    lane = iota((PIECE, LANES), 1)
    row = iota((PIECE, LANES), 0)
    nothing = jnp.zeros((PIECE, PAGE), jnp.float32)
    raws = []
    for c in range(chunks):
        rows = chosen[c * chunk * PIECE : (c + 1) * chunk * PIECE]
        split = (rows * pair_heads).astype(jnp.bfloat16)
        at = c * chunk
        block = keys_ref[at : at + chunk] if at < early else late_ref[at - early : at - early + chunk]
        raws.append(dot(split, block.reshape(chunk * PAGE, width), ((1,), (1,))))
    scores, page_tops = [], []
    for p in range(page_count):
        i = p % chunk
        part = raws[p // chunk][i * PIECE : (i + 1) * PIECE, i * PAGE : (i + 1) * PAGE]
        score = part + bias_ref[p * PIECE : (p + 1) * PIECE]
        scores.append(score)
        page_tops.append(jnp.max(score, axis=1, keepdims=True))
    page_weights = [jnp.exp(score - top) for score, top in zip(scores, page_tops)]
    mixes = []
    for c in range(chunks):
        blocks = []
        for i in range(chunk):
            weight = page_weights[c * chunk + i]
            blocks.append(
                jnp.concatenate([weight if k == i else nothing for k in range(chunk)], axis=1)
            )
        weights = jnp.concatenate(blocks, axis=0).astype(jnp.bfloat16)
        block = values_ref[c * chunk : (c + 1) * chunk]
        mixes.append(dot(weights, block.reshape(chunk * PAGE, width)))
    totals = [jnp.sum(weight, axis=1, keepdims=True) for weight in page_weights]
    tops = jnp.zeros((PIECE, LANES), jnp.float32)
    for p in range(page_count):
        tops = jnp.where(lane == p, page_tops[p], tops)
    stats = []
    for c in range(chunks):
        factors = []
        for p in range(c * chunk, (c + 1) * chunk):
            peak = jnp.max(tops + apart_ref[p : p + 1], axis=1, keepdims=True)
            factor = jnp.exp(page_tops[p] - peak)
            total = jnp.where(lane == row + SUM_LANE, totals[p] * factor, 0.0)
            stats.append(jnp.where(lane == row, peak * lead_ref[p : p + 1], total))
            factors.append(factor)
        mixes[c] = mixes[c] * (pair_heads * jnp.concatenate(factors, axis=0))
    mix = jnp.concatenate(mixes, axis=0).astype(jnp.bfloat16)
    stats = pieces(jnp.concatenate(stats, axis=0), 3)
    sums = dot(place_ref[...], jnp.concatenate([mix] + stats, axis=1))
    stats = sum(sums[:, width + i * LANES : width + (i + 1) * LANES] for i in range(3))
    stats = packed_stats(stats, 0.0).astype(jnp.float32)
    size = sums.shape[0] // groups
    for i, sums_ref in enumerate(sums_refs):
        first, middle, last = i * size, i * size + size // 2, (i + 1) * size
        for c in range(width // LANES):
            block = sums[first:last, c * LANES : (c + 1) * LANES]
            sums_ref[c * size : (c + 1) * size] = block.astype(jnp.bfloat16)
        both = stats[first:middle] + pltpu.roll(stats[middle:last], LANES // 2, 1)
        sums_ref[width // LANES * size :] = both.astype(jnp.bfloat16)


def combine_kernel(sources, *refs):
    part_refs, spread_ref, sums_refs = refs[:sources], refs[sources], refs[sources + 1 :]
    width = spread_ref.shape[1]
    rows = sum(ref.shape[0] for ref in sums_refs)
    heads, blocks = width // HEAD_DIM, width // LANES
    stats, mixes = [], []
    for ref in part_refs:
        both = ref[blocks * rows :].astype(jnp.float32)
        both = jnp.concatenate([both, pltpu.roll(both, LANES // 2, 1)], axis=0)
        stats.append(unpacked_stats(both, heads))
        mix = [ref[c * rows : (c + 1) * rows] for c in range(blocks)]
        mixes.append(jnp.concatenate(mix, axis=1).astype(jnp.float32))
    peak = stats[0][0]
    for peaks, _ in stats[1:]:
        peak = jnp.maximum(peak, peaks)
    factors = [jnp.exp(peaks - peak) for peaks, _ in stats]
    total = sum(factor * sums for factor, (_, sums) in zip(factors, stats))
    shares = over_columns(jnp.concatenate(factors, axis=0), spread_ref[...])
    mixed = sum(mix * shares[i * rows : (i + 1) * rows] for i, mix in enumerate(mixes))
    packed = packed_stats(
        jnp.where(total > 0.0, peak, 0.0), pltpu.roll(total, SUM_LANE, 1)
    ).astype(jnp.float32)
    size = sums_refs[0].shape[0]
    for i, sums_ref in enumerate(sums_refs):
        span = slice(i * size, (i + 1) * size)
        sums_ref[:, :width] = mixed[span].astype(jnp.bfloat16)
        sums_ref[:, width:] = packed[span].astype(jnp.bfloat16)


def merge_kernel(
    swapped, sources, hidden_ref, fresh_ref, moved_ref, weight_ref, spread_ref, *refs
):
    part_refs, (own_ref, send_ref) = refs[:sources], refs[sources:]
    width = fresh_ref.shape[1] - LANES
    heads = width // HEAD_DIM
    parts = [ref[...].astype(jnp.float32) for ref in part_refs]
    fresh = fresh_ref[...].astype(jnp.float32)
    if swapped:
        first = lax.axis_index("head") == 0
        fresh = jnp.where(first, fresh, moved_ref[...].astype(jnp.float32))
    parts.append(fresh)
    stats = [unpacked_stats(part[:, width:], heads) for part in parts]
    peak = stats[0][0]
    for peaks, _ in stats[1:]:
        peak = jnp.maximum(peak, peaks)
    factors = [jnp.exp(peaks - peak) for peaks, _ in stats]
    total = sum(factor * sums for factor, (_, sums) in zip(factors, stats))
    total = jnp.where(total > 0.0, total, 1.0)
    shares = jnp.concatenate([f / total for f in factors], axis=0)
    shares = over_columns(shares, spread_ref[...])
    rows = fresh_ref.shape[0]
    mixed = sum(
        part[:, :width] * shares[i * rows : (i + 1) * rows] for i, part in enumerate(parts)
    )
    projected = dot(mixed.astype(jnp.bfloat16), weight_ref[...])
    if swapped:
        projected = projected + jnp.where(first, hidden_ref[...], 0.0)
        own_ref[...] = projected
        both = [part.astype(jnp.float32) for part in pieces(projected, 2)]
        send_ref[...] = jnp.concatenate(both, axis=0).astype(jnp.bfloat16)
    else:
        own_ref[...] = hidden_ref[...]
        send_ref[...] = projected.astype(jnp.bfloat16)


def mlp_kernel(
    exchanged, own_ref, other_ref, gain_ref, up_ref, down_ref, late_ref, *outs
):
    other = other_ref[...].astype(jnp.float32)
    rows = own_ref.shape[0]
    middle = own_ref[...]
    for at in range(0, other.shape[0], rows):
        middle = middle + other[at : at + rows]
    normed = rms_normed(middle, gain_ref[...])
    active = jnp.maximum(dot(normed, up_ref[...]), 0.0).astype(jnp.bfloat16)
    half = down_ref.shape[0]
    down = dot(active[:, :half], down_ref[...]) + dot(active[:, half:], late_ref[...])
    if exchanged:
        kept_ref, sent_ref = outs
        columns = kept_ref.shape[1]
        low = lax.axis_index("head") == 0
        left, right = slice(0, columns), slice(columns, 2 * columns)
        kept = middle + down

        @pl.when(low)
        def _():
            kept_ref[...] = kept[:, left]
            sent_ref[...] = down[:, right]

        @pl.when(jnp.logical_not(low))
        def _():
            kept_ref[...] = kept[:, right]
            sent_ref[...] = down[:, left]

    else:
        middle_ref, down_out_ref = outs
        middle_ref[...] = middle
        down_out_ref[...] = down.astype(jnp.bfloat16)


def loading(*arrays):
    return pl.CostEstimate(
        flops=0, bytes_accessed=sum(2 * array.size for array in arrays), transcendentals=0
    )


def in_hbm(*arrays):
    return [pltpu.with_memory_space_constraint(array, pltpu.HBM) for array in arrays]


def xor_pairs(size, step):
    return [(i, i ^ step) for i in range(size)]


def per_device(
    hidden_in, attention_gain, mlp_gain, qkv_weight, out_weight, up_weight, down_weight,
    position_bias, bucket_edges, cache_keys, cache_values, lengths, page_request, page_index,
):
    f32, bf16 = jnp.float32, jnp.bfloat16
    shape = jax.ShapeDtypeStruct
    own_rows, model = hidden_in.shape
    width = qkv_weight.shape[2]
    page_count = page_request.shape[0]
    blocks = lax.axis_size("blk")
    all_rows = own_rows * blocks
    halves = lax.axis_size("head")
    columns = model // halves
    exchanged = halves == 2
    gain = attention_gain.reshape(1, model)
    query = pl.pallas_call(
        query_kernel,
        out_shape=shape((own_rows, width), bf16),
        in_specs=[HBM_SPEC] * 3,
        out_specs=VMEM_SPEC,
        scratch_shapes=[
            pltpu.VMEM((own_rows, model), f32),
            pltpu.VMEM((1, model), f32),
            pltpu.VMEM((model, width), bf16),
            pltpu.SemaphoreType.DMA((6,)),
        ],
        compiler_params=PARAMS,
        name="query",
    )(*in_hbm(hidden_in, gain, qkv_weight))

    inner = 1
    while inner * inner < blocks:
        inner *= 2
    far = [query] + [
        lax.ppermute(query, "blk", xor_pairs(blocks, step * inner ^ 1))
        for step in range(1, blocks // inner)
    ]
    depth = page_count * PIECE
    early = page_count // 6 * 2
    keys, picks, place, leads, apart, owners = pl.pallas_call(
        functools.partial(page_kernel, own_rows, inner, blocks // inner, exchanged),
        out_shape=(
            pltpu.VMEM((early,) + cache_keys.shape[1:], bf16),
            shape((depth, all_rows), bf16),
            shape((all_rows, depth), bf16),
            shape((page_count, LANES), f32),
            shape((page_count, LANES), f32),
            shape((page_count, LANES), jnp.int32),
        ),
        in_specs=[ANY_SPEC, VMEM_SPEC, HBM_SPEC],
        out_specs=(VMEM_SPEC,) * 6,
        scratch_shapes=[pltpu.SemaphoreType.DMA((4,))],
        compiler_params=PARAMS,
        cost_estimate=loading(cache_keys),
        name="pages",
    )(query, page_request.reshape(1, page_count), *in_hbm(cache_keys))
    near, apart = lax.optimization_barrier((jnp.concatenate(far, axis=0), apart))
    steps = sorted(range(inner), key=lambda step: -(step ^ (step >> 1)) & (inner - 1))
    gathered = [near] + [lax.ppermute(near, "blk", xor_pairs(blocks, step)) for step in steps[1:]]
    table = position_bias.T
    late_keys, bias = pl.pallas_call(
        bias_kernel,
        out_shape=(
            pltpu.VMEM((page_count - early,) + cache_keys.shape[1:], bf16),
            shape((depth, PAGE), f32),
        ),
        in_specs=[HBM_SPEC] * 4 + [VMEM_SPEC, HBM_SPEC, ANY_SPEC],
        out_specs=(VMEM_SPEC,) * 2,
        scratch_shapes=[
            pltpu.SMEM(table.shape, f32),
            pltpu.SMEM(bucket_edges.shape, jnp.int32),
            pltpu.VMEM((1,) + lengths.shape, jnp.int32),
            pltpu.VMEM((1,) + page_index.shape, jnp.int32),
            pltpu.SemaphoreType.DMA((4,)),
            pltpu.SemaphoreType.DMA((4,)),
        ],
        compiler_params=PARAMS,
        cost_estimate=loading(cache_values),
        name="bias",
    )(
        *in_hbm(table, bucket_edges, lengths[None], page_index[None]), owners,
        *in_hbm(cache_keys), near,
    )

    groups = len(gathered)
    size = all_rows // groups
    message = width // LANES * size + size // 2
    sums = pl.pallas_call(
        functools.partial(attend_kernel, groups),
        out_shape=(shape((message, LANES), bf16),) * groups,
        in_specs=[VMEM_SPEC] * (groups + 8),
        out_specs=(VMEM_SPEC,) * groups,
        compiler_params=PARAMS,
        name="attend",
    )(*gathered, bias, picks, place, leads, apart, keys, late_keys, cache_values)
    near_sums = [sums[0]] + [
        lax.ppermute(sums[i], "blk", xor_pairs(blocks, steps[i]))
        for i in range(1, inner)
    ]

    fresh, out_near, spread = pl.pallas_call(
        side_kernel,
        out_shape=(
            shape((own_rows, width + LANES), bf16),
            pltpu.VMEM(out_weight.shape, bf16),
            shape((2 * LANES, width), bf16),
        ),
        in_specs=[VMEM_SPEC] * 4 + [HBM_SPEC] * 2 + [ANY_SPEC],
        out_specs=(VMEM_SPEC,) * 3,
        scratch_shapes=[
            pltpu.VMEM((2, model, width), bf16),
            pltpu.SemaphoreType.DMA((2,)),
            pltpu.SemaphoreType.DMA((4,)),
        ],
        compiler_params=PARAMS,
        cost_estimate=loading(out_weight, out_weight, out_weight),
        name="side",
    )(
        hidden_in, gain, query, table,
        *in_hbm(qkv_weight, out_weight), sums[0],
    )

    *near_sums, fresh = lax.optimization_barrier((*near_sums, fresh))
    outer = blocks // inner
    sums = pl.pallas_call(
        functools.partial(combine_kernel, inner),
        out_shape=(shape((own_rows, width + LANES), bf16),) * outer,
        in_specs=[VMEM_SPEC] * (inner + 1),
        out_specs=(VMEM_SPEC,) * outer,
        compiler_params=PARAMS,
        name="combine",
    )(*near_sums, spread)
    half = down_weight.shape[0] // 2

    def load_down(start, after):
        return pl.pallas_call(
            functools.partial(load_kernel, start),
            out_shape=pltpu.VMEM((half, model), bf16),
            in_specs=[HBM_SPEC, ANY_SPEC],
            out_specs=VMEM_SPEC,
            scratch_shapes=[pltpu.SemaphoreType.DMA((4,))],
            compiler_params=PARAMS,
            cost_estimate=loading(down_weight),
            name="load",
        )(*in_hbm(down_weight), after)

    down_early = load_down(0, sums[0])
    parts = [sums[0]] + [
        lax.ppermute(sums[step], "blk", xor_pairs(blocks, step * inner ^ 1))
        for step in reversed(range(1, outer))
    ]

    moved = lax.ppermute(fresh, "blk", xor_pairs(blocks, 1)) if exchanged else fresh
    *parts, down_early = lax.optimization_barrier((*parts, down_early))
    own_part, sent_part = pl.pallas_call(
        functools.partial(merge_kernel, exchanged, outer),
        out_shape=(
            shape((own_rows, model), f32),
            shape(((2 if exchanged else 1) * own_rows, model), bf16),
        ),
        in_specs=[VMEM_SPEC] * (outer + 5),
        out_specs=(VMEM_SPEC,) * 2,
        compiler_params=PARAMS,
        name="merge",
    )(hidden_in, fresh, moved, out_near, spread, *parts)

    down_late = load_down(half, sent_part)
    axes = ("head", "blk")
    across = [(i, blocks + (i ^ 1)) for i in range(blocks)]
    back = [(b, a) for a, b in across]
    if exchanged:
        other_part = lax.ppermute(sent_part, axes, across + back)
        mlp_out = (shape((own_rows, columns), f32), shape((own_rows, columns), f32))
    else:
        other_part = lax.psum(sent_part, "head")
        mlp_out = (shape((own_rows, model), f32), shape((own_rows, model), bf16))

    kept, leaving = pl.pallas_call(
        functools.partial(mlp_kernel, exchanged),
        out_shape=mlp_out,
        in_specs=[VMEM_SPEC] * 6,
        out_specs=(VMEM_SPEC,) * 2,
        compiler_params=PARAMS,
        name="mlp",
    )(own_part, other_part, mlp_gain.reshape(1, model), up_weight, down_early, down_late)

    if exchanged:
        straight = [(i, blocks + i) for i in range(blocks)]
        arrived = lax.ppermute(leaving, axes, straight + back)
        moved = lax.ppermute(kept, "blk", xor_pairs(blocks, 1))
        kept = jnp.where(lax.axis_index("head") == 0, kept, moved)
    else:
        kept = lax.dynamic_slice_in_dim(kept, lax.axis_index("head") * columns, columns, 1)
        arrived = lax.psum_scatter(leaving, "head", scatter_dimension=1, tiled=True)
    return kept + arrived.astype(f32)


def solution(mesh):
    in_specs = (
        P("blk", None),
        P(),
        P(),
        P(None, None, "head"),
        P("head", None),
        P(None, "head"),
        P("head", None),
        P(None, "head"),
        P(),
        P("blk", None, "head"),
        P("blk", None, "head"),
        P(),
        P("blk"),
        P("blk"),
    )
    out_specs = P("blk", "head")
    return jax.shard_map(
        per_device, mesh=mesh, in_specs=in_specs, out_specs=out_specs, check_vma=False
    )
```

```python
import functools

import jax
import jax.numpy as jnp
from jax import lax
from jax.experimental import pallas as pl
from jax.experimental.pallas import tpu as pltpu
from jax.sharding import PartitionSpec as P

HEAD_DIM = 64
PAGE = 128
LANES = 128

far_below = -1e30
epsilon = 1e-06

VMEM_SPEC = pl.BlockSpec(memory_space=pltpu.VMEM)
SMEM_SPEC = pl.BlockSpec(memory_space=pltpu.SMEM)
ANY_SPEC = pl.BlockSpec(memory_space=pl.ANY)
HBM_SPEC = pl.BlockSpec(memory_space=pltpu.HBM)
PARAMS = pltpu.CompilerParams(vmem_limit_bytes=16 * 1024 * 1024)

PIECE = 8
SUM_LANE = 3 * PIECE


def iota(shape, axis):
    return lax.broadcasted_iota(jnp.int32, shape, axis)


def split_index(x, size):
    if size & (size - 1):
        return lax.div(x, size), lax.rem(x, size)
    return x >> (size.bit_length() - 1), x & (size - 1)


def head_of(shape, axis):
    return split_index(iota(shape, axis), HEAD_DIM)[0]


def pieces(x, count):
    parts = []
    for _ in range(count):
        part = x.astype(jnp.bfloat16)
        parts.append(part)
        x = x - part.astype(jnp.float32)
    return parts


def rms_normed(x, gain):
    scale = lax.rsqrt(jnp.mean(x * x, axis=1, keepdims=True) + epsilon)
    return (x * scale * gain).astype(jnp.bfloat16)


def dot(a, b, dims=((1,), (0,)), precision=None):
    return lax.dot_general(
        a, b, (dims, ((), ())), preferred_element_type=jnp.float32, precision=precision
    )


def split_copies(source, target, sems, count):
    size = source.shape[0] // count
    return [
        pltpu.make_async_copy(
            source.at[pl.ds(i * size, size)], target.at[pl.ds(i * size, size)], sems.at[i]
        )
        for i in range(count)
    ]


def query_kernel(hidden_hbm, gain_hbm, weight_hbm, query_ref, hidden, gain, weight, sems):
    model = hidden.shape[1]
    small = [
        pltpu.make_async_copy(hidden_hbm, hidden, sems.at[0]),
        pltpu.make_async_copy(gain_hbm, gain, sems.at[1]),
    ]
    half = model // 4
    large = [
        pltpu.make_async_copy(
            weight_hbm.at[0, pl.ds(i * half, half)], weight.at[pl.ds(i * half, half)], sems.at[2 + i]
        )
        for i in range(4)
    ]
    for copy in small + large:
        copy.start()
    for copy in small:
        copy.wait()
    normed = rms_normed(hidden[...], gain[...])
    query = None
    for i, copy in enumerate(large):
        copy.wait()
        span = slice(i * half, (i + 1) * half)
        part = dot(normed[:, span], weight[span])
        query = part if query is None else query + part
    query_ref[...] = query.astype(jnp.bfloat16)


def page_kernel(
    own_rows, inner, outer, swapped, query_ref, request_ref, keys_hbm,
    keys_ref, pick_ref, place_ref, lead_ref, apart_ref, owners_ref,
    sems,
):
    copies = split_copies(
        keys_hbm.at[pl.ds(0, keys_ref.shape[0])], keys_ref, sems, sems.shape[0]
    )
    for copy in copies:
        copy.start()
    me = lax.axis_index("blk")
    page_count = apart_ref.shape[0]
    all_rows, depth = place_ref.shape
    page, lane = iota((page_count, page_count), 0), iota((page_count, page_count), 1)
    by_lane = request_ref[...]
    owner = jnp.max(jnp.where(page == lane, by_lane, -1), axis=1, keepdims=True)
    same = by_lane == owner
    apart_ref[...] = jnp.full(apart_ref.shape, 2 * far_below, jnp.float32)
    apart_ref[:, :page_count] = jnp.where(same, 0.0, 2 * far_below)
    earlier = jnp.max(jnp.where(same & (lane < page), 1, 0), axis=1, keepdims=True)
    lead_ref[...] = jnp.broadcast_to(jnp.where(earlier == 0, 1.0, 0.0), lead_ref.shape)
    owners_ref[...] = jnp.broadcast_to(owner, owners_ref.shape)
    device, own_row = split_index(jnp.maximum(owner, 0), own_rows)

    def slot_of(device):
        high, low = split_index(device ^ me, inner)
        low = jnp.where(high == 0, low, low ^ 1)
        low = -(low ^ (low >> 1)) & (inner - 1)
        slot = (low * outer + high) * own_rows + own_row
        return jnp.where(owner >= 0, slot, -1)

    slot = slot_of(device)
    sum_slot = slot_of(device ^ lax.axis_index("head")) if swapped else slot
    row_of = iota((page_count, all_rows), 1)
    picks = jnp.where(row_of == slot, 1.0, 0.0)
    picks = [jnp.broadcast_to(picks[p : p + 1], (PIECE, all_rows)) for p in range(page_count)]
    pick_ref[...] = jnp.concatenate(picks, axis=0).astype(jnp.bfloat16)
    mine = split_index(iota((page_count, depth), 1), PIECE)[0] == iota((page_count, depth), 0)
    row = iota((all_rows, depth), 0)
    spread = jnp.max(jnp.where(mine, sum_slot, -1), axis=0, keepdims=True)
    place_ref[...] = (row == spread).astype(jnp.bfloat16)
    for copy in copies:
        copy.wait()


def bias_kernel(
    table_hbm, edges_hbm, lengths_hbm, index_hbm, owners_ref, keys_hbm, after_ref,
    keys_ref, bias_ref,
    table, edges, lengths, index, small_sems, sems,
):
    sources, targets = (table_hbm, edges_hbm, lengths_hbm, index_hbm), (table, edges, lengths, index)
    small = [
        pltpu.make_async_copy(source, target, small_sems.at[i])
        for i, (source, target) in enumerate(zip(sources, targets))
    ]
    late = keys_ref.shape[0]
    copies = split_copies(
        keys_hbm.at[pl.ds(keys_hbm.shape[0] - late, late)], keys_ref, sems, sems.shape[0]
    )
    for copy in small + copies:
        copy.start()
    for copy in small:
        copy.wait()
    heads, buckets = table.shape
    page_count = index.shape[1]
    owner = owners_ref[:, 0:1]
    square = (page_count, page_count)
    number = jnp.where(iota(square, 0) == iota(square, 1), index[...], 0)
    number = jnp.sum(number, axis=1, keepdims=True)
    requests = lengths.shape[1]
    length = jnp.where(iota((page_count, requests), 1) == owner, lengths[...], 0)
    length = jnp.sum(length, axis=1, keepdims=True)
    distance = length - number * PAGE - iota((page_count, PAGE), 1)
    far = [distance >= edges[k] for k in range(buckets - 1)]
    usable = (owner >= 0) & (distance > 0)
    bias_ref[...] = jnp.full(bias_ref.shape, far_below, jnp.float32)
    for h in range(heads):
        bias = jnp.full((page_count, PAGE), table[h, 0], jnp.float32)
        for k in range(buckets - 1):
            bias = jnp.where(far[k], table[h, k + 1], bias)
        bias_ref[pl.ds(h, page_count, stride=PIECE), :] = jnp.where(usable, bias, far_below)
    for copy in copies:
        copy.wait()


def side_kernel(
    hidden_ref, gain_ref, query_ref, table_ref, weight_hbm, out_hbm, after_ref,
    fresh_ref, out_ref, spread_ref,
    weight, weight_sems, sems,
):
    copies = [
        pltpu.make_async_copy(weight_hbm.at[1 + i], weight.at[i], weight_sems.at[i])
        for i in range(2)
    ]
    later = split_copies(out_hbm, out_ref, sems, sems.shape[0])
    for copy in copies + later:
        copy.start()
    normed = rms_normed(hidden_ref[...], gain_ref[...])
    heads = table_ref.shape[0]
    spread = iota((heads, LANES), 0) == iota((heads, LANES), 1)
    score = jnp.sum(jnp.where(spread, table_ref[:, 0:1], 0.0), axis=0, keepdims=True)
    copies[0].wait()
    key = dot(normed, weight[0]).astype(jnp.bfloat16)
    product = query_ref[...].astype(jnp.float32) * key.astype(jnp.float32)
    width = product.shape[1]
    gather = (head_of((width, LANES), 0) == iota((width, LANES), 1)).astype(jnp.bfloat16)
    for part in pieces(product, 2):
        score = score + dot(part, gather)
    lane = iota(score.shape, 1)
    used = width // HEAD_DIM
    peak = jnp.where(lane < used, score, 0.0)
    total = jnp.where((lane >= SUM_LANE) & (lane < SUM_LANE + used), 1.0, 0.0)
    fresh_ref[:, width:] = packed_stats(peak, total)
    spread = (iota((LANES, width), 0) == head_of((LANES, width), 1)).astype(jnp.bfloat16)
    spread_ref[:LANES] = spread
    spread_ref[LANES:] = spread
    copies[1].wait()
    fresh_ref[:, :width] = dot(normed, weight[1]).astype(jnp.bfloat16)
    for copy in later:
        copy.wait()


def load_kernel(start, source, after_ref, target, sems):
    rows = source.at[pl.ds(start, target.shape[0])]
    copies = split_copies(rows, target, sems, sems.shape[0])
    for copy in copies:
        copy.start()
    for copy in copies:
        copy.wait()


def packed_stats(peaks, sums):
    one, two, three = (part.astype(jnp.float32) for part in pieces(peaks + sums, 3))
    packed = one + pltpu.roll(two, PIECE, 1) + pltpu.roll(three, 2 * PIECE, 1)
    return packed.astype(jnp.bfloat16)


def unpacked_stats(packed, heads):
    stats = packed.astype(jnp.float32)
    stats = stats + pltpu.roll(stats, LANES - PIECE, 1) + pltpu.roll(stats, LANES - 2 * PIECE, 1)
    sums = pltpu.roll(stats, LANES - SUM_LANE, 1)
    used = iota(stats.shape, 1) < heads
    return jnp.where(used & (sums > 0.0), stats, far_below), jnp.where(used, sums, 0.0)


def over_columns(values, spread):
    return dot(jnp.concatenate(pieces(values, 2), axis=1), spread)


def attend_kernel(groups, *refs):
    query_refs, refs, sums_refs = refs[:groups], refs[groups:-groups], refs[-groups:]
    bias_ref, pick_ref, place_ref, lead_ref, apart_ref, keys_ref, late_ref, values_ref = refs
    page_count = apart_ref.shape[0]
    width = keys_ref.shape[2]
    early = keys_ref.shape[0]
    chunk = 2
    chunks = page_count // chunk
    queries = jnp.concatenate([ref[...] for ref in query_refs], axis=0)
    own_head = (head_of((PIECE, width), 1) == iota((PIECE, width), 0)).astype(jnp.float32)
    pair_heads = jnp.concatenate([own_head] * chunk, axis=0)
    chosen = dot(pick_ref[...], queries)
    lane = iota((PIECE, LANES), 1)
    row = iota((PIECE, LANES), 0)
    nothing = jnp.zeros((PIECE, PAGE), jnp.float32)
    raws = []
    for c in range(chunks):
        rows = chosen[c * chunk * PIECE : (c + 1) * chunk * PIECE]
        split = rows.astype(jnp.bfloat16) * pair_heads.astype(jnp.bfloat16)
        at = c * chunk
        block = keys_ref[at : at + chunk] if at < early else late_ref[at - early : at - early + chunk]
        raws.append(dot(split, block.reshape(chunk * PAGE, width), ((1,), (1,))))
    scores, page_tops = [], []
    for p in range(page_count):
        i = p % chunk
        part = raws[p // chunk][i * PIECE : (i + 1) * PIECE, i * PAGE : (i + 1) * PAGE]
        score = part + bias_ref[p * PIECE : (p + 1) * PIECE]
        scores.append(score)
        page_tops.append(jnp.max(score, axis=1, keepdims=True))
    page_weights = [jnp.exp(score - top) for score, top in zip(scores, page_tops)]
    mixes = []
    for c in range(chunks):
        blocks = []
        for i in range(chunk):
            weight = page_weights[c * chunk + i]
            blocks.append(
                jnp.concatenate([weight if k == i else nothing for k in range(chunk)], axis=1)
            )
        weights = jnp.concatenate(blocks, axis=0).astype(jnp.bfloat16)
        block = values_ref[c * chunk : (c + 1) * chunk]
        mixes.append(dot(weights, block.reshape(chunk * PAGE, width)))
    totals = [jnp.sum(weight, axis=1, keepdims=True) for weight in page_weights]
    tops = jnp.zeros((PIECE, LANES), jnp.float32)
    for p in range(page_count):
        tops = jnp.where(lane == p, page_tops[p], tops)
    stats = []
    for c in range(chunks):
        factors = []
        for p in range(c * chunk, (c + 1) * chunk):
            peak = jnp.max(tops + apart_ref[p : p + 1], axis=1, keepdims=True)
            factor = jnp.exp(page_tops[p] - peak)
            total = jnp.where(lane == row + SUM_LANE, totals[p] * factor, 0.0)
            stats.append(jnp.where(lane == row, peak * lead_ref[p : p + 1], total))
            factors.append(factor)
        mixes[c] = mixes[c] * (pair_heads * jnp.concatenate(factors, axis=0))
    mix = jnp.concatenate(mixes, axis=0).astype(jnp.bfloat16)
    stats = pieces(jnp.concatenate(stats, axis=0), 3)
    sums = dot(place_ref[...], jnp.concatenate([mix] + stats, axis=1))
    stats = sum(sums[:, width + i * LANES : width + (i + 1) * LANES] for i in range(3))
    stats = packed_stats(stats, 0.0).astype(jnp.float32)
    size = sums.shape[0] // groups
    for i, sums_ref in enumerate(sums_refs):
        first, middle, last = i * size, i * size + size // 2, (i + 1) * size
        for c in range(width // LANES):
            block = sums[first:last, c * LANES : (c + 1) * LANES]
            sums_ref[c * size : (c + 1) * size] = block.astype(jnp.bfloat16)
        both = stats[first:middle] + pltpu.roll(stats[middle:last], LANES // 2, 1)
        sums_ref[width // LANES * size :] = both.astype(jnp.bfloat16)


def combine_kernel(sources, *refs):
    part_refs, spread_ref, sums_refs = refs[:sources], refs[sources], refs[sources + 1 :]
    width = spread_ref.shape[1]
    rows = sum(ref.shape[0] for ref in sums_refs)
    heads, blocks = width // HEAD_DIM, width // LANES
    stats, mixes = [], []
    for ref in part_refs:
        both = ref[blocks * rows :].astype(jnp.float32)
        both = jnp.concatenate([both, pltpu.roll(both, LANES // 2, 1)], axis=0)
        stats.append(unpacked_stats(both, heads))
        mix = [ref[c * rows : (c + 1) * rows] for c in range(blocks)]
        mixes.append(jnp.concatenate(mix, axis=1).astype(jnp.float32))
    peak = stats[0][0]
    for peaks, _ in stats[1:]:
        peak = jnp.maximum(peak, peaks)
    factors = [jnp.exp(peaks - peak) for peaks, _ in stats]
    total = sum(factor * sums for factor, (_, sums) in zip(factors, stats))
    shares = over_columns(jnp.concatenate(factors, axis=0), spread_ref[...])
    mixed = sum(mix * shares[i * rows : (i + 1) * rows] for i, mix in enumerate(mixes))
    packed = packed_stats(
        jnp.where(total > 0.0, peak, 0.0), pltpu.roll(total, SUM_LANE, 1)
    ).astype(jnp.float32)
    size = sums_refs[0].shape[0]
    for i, sums_ref in enumerate(sums_refs):
        span = slice(i * size, (i + 1) * size)
        sums_ref[:, :width] = mixed[span].astype(jnp.bfloat16)
        sums_ref[:, width:] = packed[span].astype(jnp.bfloat16)


def merge_kernel(
    swapped, sources, hidden_ref, fresh_ref, moved_ref, weight_ref, spread_ref, *refs
):
    part_refs, (own_ref, send_ref) = refs[:sources], refs[sources:]
    width = fresh_ref.shape[1] - LANES
    heads = width // HEAD_DIM
    parts = [ref[...].astype(jnp.float32) for ref in part_refs]
    fresh = fresh_ref[...].astype(jnp.float32)
    if swapped:
        first = lax.axis_index("head") == 0
        fresh = jnp.where(first, fresh, moved_ref[...].astype(jnp.float32))
    parts.append(fresh)
    stats = [unpacked_stats(part[:, width:], heads) for part in parts]
    peak = stats[0][0]
    for peaks, _ in stats[1:]:
        peak = jnp.maximum(peak, peaks)
    factors = [jnp.exp(peaks - peak) for peaks, _ in stats]
    total = sum(factor * sums for factor, (_, sums) in zip(factors, stats))
    total = jnp.where(total > 0.0, total, 1.0)
    shares = jnp.concatenate([f / total for f in factors], axis=0)
    shares = over_columns(shares, spread_ref[...])
    rows = fresh_ref.shape[0]
    mixed = sum(
        part[:, :width] * shares[i * rows : (i + 1) * rows] for i, part in enumerate(parts)
    )
    projected = dot(mixed.astype(jnp.bfloat16), weight_ref[...])
    if swapped:
        projected = projected + jnp.where(first, hidden_ref[...], 0.0)
        own_ref[...] = projected
        both = [part.astype(jnp.float32) for part in pieces(projected, 2)]
        send_ref[...] = jnp.concatenate(both, axis=0).astype(jnp.bfloat16)
    else:
        own_ref[...] = hidden_ref[...]
        send_ref[...] = projected.astype(jnp.bfloat16)


def mlp_kernel(
    exchanged, own_ref, other_ref, gain_ref, up_ref, down_ref, late_ref, *outs
):
    other = other_ref[...].astype(jnp.float32)
    rows = own_ref.shape[0]
    middle = own_ref[...]
    for at in range(0, other.shape[0], rows):
        middle = middle + other[at : at + rows]
    normed = rms_normed(middle, gain_ref[...])
    active = jnp.maximum(dot(normed, up_ref[...]), 0.0).astype(jnp.bfloat16)
    half = down_ref.shape[0]
    down = dot(active[:, :half], down_ref[...]) + dot(active[:, half:], late_ref[...])
    if exchanged:
        kept_ref, sent_ref = outs
        columns = kept_ref.shape[1]
        low = lax.axis_index("head") == 0
        left, right = slice(0, columns), slice(columns, 2 * columns)
        kept = middle + down

        @pl.when(low)
        def _():
            kept_ref[...] = kept[:, left]
            sent_ref[...] = down[:, right]

        @pl.when(jnp.logical_not(low))
        def _():
            kept_ref[...] = kept[:, right]
            sent_ref[...] = down[:, left]

    else:
        middle_ref, down_out_ref = outs
        middle_ref[...] = middle
        down_out_ref[...] = down.astype(jnp.bfloat16)


def loading(*arrays):
    return pl.CostEstimate(
        flops=0, bytes_accessed=sum(2 * array.size for array in arrays), transcendentals=0
    )


def in_hbm(*arrays):
    return [pltpu.with_memory_space_constraint(array, pltpu.HBM) for array in arrays]


def xor_pairs(size, step):
    return [(i, i ^ step) for i in range(size)]


def per_device(
    hidden_in, attention_gain, mlp_gain, qkv_weight, out_weight, up_weight, down_weight,
    position_bias, bucket_edges, cache_keys, cache_values, lengths, page_request, page_index,
):
    f32, bf16 = jnp.float32, jnp.bfloat16
    shape = jax.ShapeDtypeStruct
    own_rows, model = hidden_in.shape
    width = qkv_weight.shape[2]
    page_count = page_request.shape[0]
    blocks = lax.axis_size("blk")
    all_rows = own_rows * blocks
    halves = lax.axis_size("head")
    columns = model // halves
    exchanged = halves == 2
    gain = attention_gain.reshape(1, model)
    query = pl.pallas_call(
        query_kernel,
        out_shape=shape((own_rows, width), bf16),
        in_specs=[HBM_SPEC] * 3,
        out_specs=VMEM_SPEC,
        scratch_shapes=[
            pltpu.VMEM((own_rows, model), f32),
            pltpu.VMEM((1, model), f32),
            pltpu.VMEM((model, width), bf16),
            pltpu.SemaphoreType.DMA((6,)),
        ],
        compiler_params=PARAMS,
        name="query",
    )(*in_hbm(hidden_in, gain, qkv_weight))

    inner = 1
    while inner * inner < blocks:
        inner *= 2
    far = [query] + [
        lax.ppermute(query, "blk", xor_pairs(blocks, step * inner ^ 1))
        for step in range(1, blocks // inner)
    ]
    depth = page_count * PIECE
    early = page_count // 6 * 2
    keys, picks, place, leads, apart, owners = pl.pallas_call(
        functools.partial(page_kernel, own_rows, inner, blocks // inner, exchanged),
        out_shape=(
            pltpu.VMEM((early,) + cache_keys.shape[1:], bf16),
            shape((depth, all_rows), bf16),
            shape((all_rows, depth), bf16),
            shape((page_count, LANES), f32),
            shape((page_count, LANES), f32),
            shape((page_count, LANES), jnp.int32),
        ),
        in_specs=[ANY_SPEC, VMEM_SPEC, HBM_SPEC],
        out_specs=(VMEM_SPEC,) * 6,
        scratch_shapes=[pltpu.SemaphoreType.DMA((4,))],
        compiler_params=PARAMS,
        cost_estimate=loading(cache_keys),
        name="pages",
    )(query, page_request.reshape(1, page_count), *in_hbm(cache_keys))
    near, apart = lax.optimization_barrier((jnp.concatenate(far, axis=0), apart))
    steps = sorted(range(inner), key=lambda step: -(step ^ (step >> 1)) & (inner - 1))
    gathered = [near] + [lax.ppermute(near, "blk", xor_pairs(blocks, step)) for step in steps[1:]]
    table = position_bias.T
    late_keys, bias = pl.pallas_call(
        bias_kernel,
        out_shape=(
            pltpu.VMEM((page_count - early,) + cache_keys.shape[1:], bf16),
            shape((depth, PAGE), f32),
        ),
        in_specs=[HBM_SPEC] * 4 + [VMEM_SPEC, HBM_SPEC, ANY_SPEC],
        out_specs=(VMEM_SPEC,) * 2,
        scratch_shapes=[
            pltpu.SMEM(table.shape, f32),
            pltpu.SMEM(bucket_edges.shape, jnp.int32),
            pltpu.VMEM((1,) + lengths.shape, jnp.int32),
            pltpu.VMEM((1,) + page_index.shape, jnp.int32),
            pltpu.SemaphoreType.DMA((4,)),
            pltpu.SemaphoreType.DMA((4,)),
        ],
        compiler_params=PARAMS,
        cost_estimate=loading(cache_values),
        name="bias",
    )(
        *in_hbm(table, bucket_edges, lengths[None], page_index[None]), owners,
        *in_hbm(cache_keys), near,
    )

    groups = len(gathered)
    size = all_rows // groups
    message = width // LANES * size + size // 2
    sums = pl.pallas_call(
        functools.partial(attend_kernel, groups),
        out_shape=(shape((message, LANES), bf16),) * groups,
        in_specs=[VMEM_SPEC] * (groups + 8),
        out_specs=(VMEM_SPEC,) * groups,
        compiler_params=PARAMS,
        name="attend",
    )(*gathered, bias, picks, place, leads, apart, keys, late_keys, cache_values)
    near_sums = [sums[0]] + [
        lax.ppermute(sums[i], "blk", xor_pairs(blocks, steps[i]))
        for i in range(1, inner)
    ]

    fresh, out_near, spread = pl.pallas_call(
        side_kernel,
        out_shape=(
            shape((own_rows, width + LANES), bf16),
            pltpu.VMEM(out_weight.shape, bf16),
            shape((2 * LANES, width), bf16),
        ),
        in_specs=[VMEM_SPEC] * 4 + [HBM_SPEC] * 2 + [ANY_SPEC],
        out_specs=(VMEM_SPEC,) * 3,
        scratch_shapes=[
            pltpu.VMEM((2, model, width), bf16),
            pltpu.SemaphoreType.DMA((2,)),
            pltpu.SemaphoreType.DMA((4,)),
        ],
        compiler_params=PARAMS,
        cost_estimate=loading(out_weight, out_weight, out_weight),
        name="side",
    )(
        hidden_in, gain, query, table,
        *in_hbm(qkv_weight, out_weight), sums[0],
    )

    *near_sums, fresh = lax.optimization_barrier((*near_sums, fresh))
    outer = blocks // inner
    sums = pl.pallas_call(
        functools.partial(combine_kernel, inner),
        out_shape=(shape((own_rows, width + LANES), bf16),) * outer,
        in_specs=[VMEM_SPEC] * (inner + 1),
        out_specs=(VMEM_SPEC,) * outer,
        compiler_params=PARAMS,
        name="combine",
    )(*near_sums, spread)
    units = down_weight.shape[0]
    cut = units // 8 * 3

    def load_down(start, stop, after):
        return pl.pallas_call(
            functools.partial(load_kernel, start),
            out_shape=pltpu.VMEM((stop - start, model), bf16),
            in_specs=[HBM_SPEC, ANY_SPEC],
            out_specs=VMEM_SPEC,
            scratch_shapes=[pltpu.SemaphoreType.DMA((4,))],
            compiler_params=PARAMS,
            cost_estimate=loading(down_weight),
            name="load",
        )(*in_hbm(down_weight), after)

    down_early = load_down(0, cut, sums[0])
    parts = [sums[0]] + [
        lax.ppermute(sums[step], "blk", xor_pairs(blocks, step * inner ^ 1))
        for step in reversed(range(1, outer))
    ]

    moved = lax.ppermute(fresh, "blk", xor_pairs(blocks, 1)) if exchanged else fresh
    *parts, down_early = lax.optimization_barrier((*parts, down_early))
    own_part, sent_part = pl.pallas_call(
        functools.partial(merge_kernel, exchanged, outer),
        out_shape=(
            shape((own_rows, model), f32),
            shape(((2 if exchanged else 1) * own_rows, model), bf16),
        ),
        in_specs=[VMEM_SPEC] * (outer + 5),
        out_specs=(VMEM_SPEC,) * 2,
        compiler_params=PARAMS,
        name="merge",
    )(hidden_in, fresh, moved, out_near, spread, *parts)

    down_late = load_down(cut, units, sent_part)
    axes = ("head", "blk")
    across = [(i, blocks + (i ^ 1)) for i in range(blocks)]
    back = [(b, a) for a, b in across]
    if exchanged:
        other_part = lax.ppermute(sent_part, axes, across + back)
        mlp_out = (shape((own_rows, columns), f32), shape((own_rows, columns), f32))
    else:
        other_part = lax.psum(sent_part, "head")
        mlp_out = (shape((own_rows, model), f32), shape((own_rows, model), bf16))

    kept, leaving = pl.pallas_call(
        functools.partial(mlp_kernel, exchanged),
        out_shape=mlp_out,
        in_specs=[VMEM_SPEC] * 6,
        out_specs=(VMEM_SPEC,) * 2,
        compiler_params=PARAMS,
        name="mlp",
    )(own_part, other_part, mlp_gain.reshape(1, model), up_weight, down_early, down_late)

    if exchanged:
        straight = [(i, blocks + i) for i in range(blocks)]
        arrived = lax.ppermute(leaving, axes, straight + back)
        moved = lax.ppermute(kept, "blk", xor_pairs(blocks, 1))
        kept = jnp.where(lax.axis_index("head") == 0, kept, moved)
    else:
        kept = lax.dynamic_slice_in_dim(kept, lax.axis_index("head") * columns, columns, 1)
        arrived = lax.psum_scatter(leaving, "head", scatter_dimension=1, tiled=True)
    return kept + arrived.astype(f32)


def solution(mesh):
    in_specs = (
        P("blk", None),
        P(),
        P(),
        P(None, None, "head"),
        P("head", None),
        P(None, "head"),
        P("head", None),
        P(None, "head"),
        P(),
        P("blk", None, "head"),
        P("blk", None, "head"),
        P(),
        P("blk"),
        P("blk"),
    )
    out_specs = P("blk", "head")
    return jax.shard_map(
        per_device, mesh=mesh, in_specs=in_specs, out_specs=out_specs, check_vma=False
    )
```

```python
import functools

import jax
import jax.numpy as jnp
from jax import lax
from jax.experimental import pallas as pl
from jax.experimental.pallas import tpu as pltpu
from jax.sharding import PartitionSpec as P

HEAD_DIM = 64
PAGE = 128
LANES = 128

far_below = -1e30
epsilon = 1e-06

VMEM_SPEC = pl.BlockSpec(memory_space=pltpu.VMEM)
SMEM_SPEC = pl.BlockSpec(memory_space=pltpu.SMEM)
ANY_SPEC = pl.BlockSpec(memory_space=pl.ANY)
HBM_SPEC = pl.BlockSpec(memory_space=pltpu.HBM)
PARAMS = pltpu.CompilerParams(vmem_limit_bytes=16 * 1024 * 1024)

PIECE = 8
SUM_LANE = 3 * PIECE


def iota(shape, axis):
    return lax.broadcasted_iota(jnp.int32, shape, axis)


def split_index(x, size):
    if size & (size - 1):
        return lax.div(x, size), lax.rem(x, size)
    return x >> (size.bit_length() - 1), x & (size - 1)


def head_of(shape, axis):
    return split_index(iota(shape, axis), HEAD_DIM)[0]


def pieces(x, count):
    parts = []
    for _ in range(count):
        part = x.astype(jnp.bfloat16)
        parts.append(part)
        x = x - part.astype(jnp.float32)
    return parts


def rms_normed(x, gain):
    scale = lax.rsqrt(jnp.mean(x * x, axis=1, keepdims=True) + epsilon)
    return (x * scale * gain).astype(jnp.bfloat16)


def dot(a, b, dims=((1,), (0,)), precision=None):
    return lax.dot_general(
        a, b, (dims, ((), ())), preferred_element_type=jnp.float32, precision=precision
    )


def split_copies(source, target, sems, count):
    size = source.shape[0] // count
    return [
        pltpu.make_async_copy(
            source.at[pl.ds(i * size, size)], target.at[pl.ds(i * size, size)], sems.at[i]
        )
        for i in range(count)
    ]


def query_kernel(hidden_hbm, gain_hbm, weight_hbm, query_ref, hidden, gain, weight, sems):
    model = hidden.shape[1]
    small = [
        pltpu.make_async_copy(hidden_hbm, hidden, sems.at[0]),
        pltpu.make_async_copy(gain_hbm, gain, sems.at[1]),
    ]
    half = model // 4
    large = [
        pltpu.make_async_copy(
            weight_hbm.at[0, pl.ds(i * half, half)], weight.at[pl.ds(i * half, half)], sems.at[2 + i]
        )
        for i in range(4)
    ]
    for copy in small + large:
        copy.start()
    for copy in small:
        copy.wait()
    normed = rms_normed(hidden[...], gain[...])
    query = None
    for i, copy in enumerate(large):
        copy.wait()
        span = slice(i * half, (i + 1) * half)
        part = dot(normed[:, span], weight[span])
        query = part if query is None else query + part
    query_ref[...] = query.astype(jnp.bfloat16)


def page_kernel(
    own_rows, inner, outer, swapped, query_ref, request_ref, keys_hbm,
    keys_ref, pick_ref, place_ref, lead_ref, apart_ref, owners_ref,
    sems,
):
    copies = split_copies(
        keys_hbm.at[pl.ds(0, keys_ref.shape[0])], keys_ref, sems, sems.shape[0]
    )
    for copy in copies:
        copy.start()
    me = lax.axis_index("blk")
    page_count = apart_ref.shape[0]
    all_rows, depth = place_ref.shape
    page, lane = iota((page_count, page_count), 0), iota((page_count, page_count), 1)
    by_lane = request_ref[...]
    owner = jnp.max(jnp.where(page == lane, by_lane, -1), axis=1, keepdims=True)
    same = by_lane == owner
    apart_ref[...] = jnp.full(apart_ref.shape, 2 * far_below, jnp.float32)
    apart_ref[:, :page_count] = jnp.where(same, 0.0, 2 * far_below)
    earlier = jnp.max(jnp.where(same & (lane < page), 1, 0), axis=1, keepdims=True)
    lead_ref[...] = jnp.broadcast_to(jnp.where(earlier == 0, 1.0, 0.0), lead_ref.shape)
    owners_ref[...] = jnp.broadcast_to(owner, owners_ref.shape)
    device, own_row = split_index(jnp.maximum(owner, 0), own_rows)

    def slot_of(device):
        high, low = split_index(device ^ me, inner)
        low = jnp.where(high == 0, low, low ^ 1)
        low = -(low ^ (low >> 1)) & (inner - 1)
        slot = (low * outer + high) * own_rows + own_row
        return jnp.where(owner >= 0, slot, -1)

    slot = slot_of(device)
    sum_slot = slot_of(device ^ lax.axis_index("head")) if swapped else slot
    row_of = iota((page_count, all_rows), 1)
    picks = jnp.where(row_of == slot, 1.0, 0.0)
    picks = [jnp.broadcast_to(picks[p : p + 1], (PIECE, all_rows)) for p in range(page_count)]
    pick_ref[...] = jnp.concatenate(picks, axis=0).astype(jnp.bfloat16)
    mine = split_index(iota((page_count, depth), 1), PIECE)[0] == iota((page_count, depth), 0)
    row = iota((all_rows, depth), 0)
    spread = jnp.max(jnp.where(mine, sum_slot, -1), axis=0, keepdims=True)
    place_ref[...] = (row == spread).astype(jnp.bfloat16)
    for copy in copies:
        copy.wait()


def bias_kernel(
    table_hbm, edges_hbm, lengths_hbm, index_hbm, owners_ref, keys_hbm, after_ref,
    keys_ref, bias_ref,
    table, edges, lengths, index, small_sems, sems,
):
    sources, targets = (table_hbm, edges_hbm, lengths_hbm, index_hbm), (table, edges, lengths, index)
    small = [
        pltpu.make_async_copy(source, target, small_sems.at[i])
        for i, (source, target) in enumerate(zip(sources, targets))
    ]
    late = keys_ref.shape[0]
    copies = split_copies(
        keys_hbm.at[pl.ds(keys_hbm.shape[0] - late, late)], keys_ref, sems, sems.shape[0]
    )
    for copy in small + copies:
        copy.start()
    for copy in small:
        copy.wait()
    heads, buckets = table.shape
    page_count = index.shape[1]
    owner = owners_ref[:, 0:1]
    square = (page_count, page_count)
    number = jnp.where(iota(square, 0) == iota(square, 1), index[...], 0)
    number = jnp.sum(number, axis=1, keepdims=True)
    requests = lengths.shape[1]
    length = jnp.where(iota((page_count, requests), 1) == owner, lengths[...], 0)
    length = jnp.sum(length, axis=1, keepdims=True)
    distance = length - number * PAGE - iota((page_count, PAGE), 1)
    far = [distance >= edges[k] for k in range(buckets - 1)]
    usable = (owner >= 0) & (distance > 0)
    bias_ref[...] = jnp.full(bias_ref.shape, far_below, jnp.float32)
    for h in range(heads):
        bias = jnp.full((page_count, PAGE), table[h, 0], jnp.float32)
        for k in range(buckets - 1):
            bias = jnp.where(far[k], table[h, k + 1], bias)
        bias_ref[pl.ds(h, page_count, stride=PIECE), :] = jnp.where(usable, bias, far_below)
    for copy in copies:
        copy.wait()


def side_kernel(
    hidden_ref, gain_ref, query_ref, table_ref, weight_hbm, out_hbm, after_ref,
    fresh_ref, out_ref, spread_ref,
    weight, weight_sems, sems,
):
    copies = [
        pltpu.make_async_copy(weight_hbm.at[1 + i], weight.at[i], weight_sems.at[i])
        for i in range(2)
    ]
    later = split_copies(out_hbm, out_ref, sems, sems.shape[0])
    for copy in copies + later:
        copy.start()
    normed = rms_normed(hidden_ref[...], gain_ref[...])
    heads = table_ref.shape[0]
    spread = iota((heads, LANES), 0) == iota((heads, LANES), 1)
    score = jnp.sum(jnp.where(spread, table_ref[:, 0:1], 0.0), axis=0, keepdims=True)
    copies[0].wait()
    key = dot(normed, weight[0]).astype(jnp.bfloat16)
    product = query_ref[...].astype(jnp.float32) * key.astype(jnp.float32)
    width = product.shape[1]
    gather = (head_of((width, LANES), 0) == iota((width, LANES), 1)).astype(jnp.bfloat16)
    for part in pieces(product, 2):
        score = score + dot(part, gather)
    lane = iota(score.shape, 1)
    used = width // HEAD_DIM
    peak = jnp.where(lane < used, score, 0.0)
    total = jnp.where((lane >= SUM_LANE) & (lane < SUM_LANE + used), 1.0, 0.0)
    fresh_ref[:, width:] = packed_stats(peak, total)
    spread = (iota((LANES, width), 0) == head_of((LANES, width), 1)).astype(jnp.bfloat16)
    spread_ref[:LANES] = spread
    spread_ref[LANES:] = spread
    copies[1].wait()
    fresh_ref[:, :width] = dot(normed, weight[1]).astype(jnp.bfloat16)
    for copy in later:
        copy.wait()


def load_kernel(start, source, after_ref, target, sems):
    rows = source.at[pl.ds(start, target.shape[0])]
    copies = split_copies(rows, target, sems, sems.shape[0])
    for copy in copies:
        copy.start()
    for copy in copies:
        copy.wait()


def packed_stats(peaks, sums):
    one, two, three = (part.astype(jnp.float32) for part in pieces(peaks + sums, 3))
    packed = one + pltpu.roll(two, PIECE, 1) + pltpu.roll(three, 2 * PIECE, 1)
    return packed.astype(jnp.bfloat16)


def unpacked_stats(packed, heads):
    stats = packed.astype(jnp.float32)
    stats = stats + pltpu.roll(stats, LANES - PIECE, 1) + pltpu.roll(stats, LANES - 2 * PIECE, 1)
    sums = pltpu.roll(stats, LANES - SUM_LANE, 1)
    used = iota(stats.shape, 1) < heads
    return jnp.where(used & (sums > 0.0), stats, far_below), jnp.where(used, sums, 0.0)


def over_columns(values, spread):
    return dot(jnp.concatenate(pieces(values, 2), axis=1), spread)


def attend_kernel(groups, *refs):
    query_refs, refs, sums_refs = refs[:groups], refs[groups:-groups], refs[-groups:]
    bias_ref, pick_ref, place_ref, lead_ref, apart_ref, keys_ref, late_ref, values_ref = refs
    page_count = apart_ref.shape[0]
    width = keys_ref.shape[2]
    early = keys_ref.shape[0]
    chunk = 2
    chunks = page_count // chunk
    queries = jnp.concatenate([ref[...] for ref in query_refs], axis=0)
    own_head = (head_of((PIECE, width), 1) == iota((PIECE, width), 0)).astype(jnp.float32)
    pair_heads = jnp.concatenate([own_head] * chunk, axis=0)
    chosen = dot(pick_ref[...], queries)
    lane = iota((PIECE, LANES), 1)
    row = iota((PIECE, LANES), 0)
    nothing = jnp.zeros((PIECE, PAGE), jnp.float32)
    raws = []
    for c in range(chunks):
        rows = chosen[c * chunk * PIECE : (c + 1) * chunk * PIECE]
        split = rows.astype(jnp.bfloat16) * pair_heads.astype(jnp.bfloat16)
        at = c * chunk
        block = keys_ref[at : at + chunk] if at < early else late_ref[at - early : at - early + chunk]
        raws.append(dot(split, block.reshape(chunk * PAGE, width), ((1,), (1,))))
    scores, page_tops = [], []
    for p in range(page_count):
        i = p % chunk
        part = raws[p // chunk][i * PIECE : (i + 1) * PIECE, i * PAGE : (i + 1) * PAGE]
        score = part + bias_ref[p * PIECE : (p + 1) * PIECE]
        scores.append(score)
        page_tops.append(jnp.max(score, axis=1, keepdims=True))
    page_weights = [jnp.exp(score - top) for score, top in zip(scores, page_tops)]
    mixes = []
    for c in range(chunks):
        blocks = []
        for i in range(chunk):
            weight = page_weights[c * chunk + i]
            blocks.append(
                jnp.concatenate([weight if k == i else nothing for k in range(chunk)], axis=1)
            )
        weights = jnp.concatenate(blocks, axis=0).astype(jnp.bfloat16)
        block = values_ref[c * chunk : (c + 1) * chunk]
        mixes.append(dot(weights, block.reshape(chunk * PAGE, width)))
    ones = jnp.ones((2 * PAGE, LANES), jnp.bfloat16)
    totals = pieces(jnp.concatenate(page_weights, axis=0), 2)
    totals = dot(jnp.concatenate(totals, axis=1), ones)
    tops = jnp.zeros((PIECE, LANES), jnp.float32)
    for p in range(page_count):
        tops = jnp.where(lane == p, page_tops[p], tops)
    stats = []
    for c in range(chunks):
        factors = []
        for p in range(c * chunk, (c + 1) * chunk):
            peak = jnp.max(tops + apart_ref[p : p + 1], axis=1, keepdims=True)
            factor = jnp.exp(page_tops[p] - peak)
            total = totals[p * PIECE : (p + 1) * PIECE] * factor
            total = jnp.where(lane == row + SUM_LANE, total, 0.0)
            stats.append(jnp.where(lane == row, peak * lead_ref[p : p + 1], total))
            factors.append(factor)
        mixes[c] = mixes[c] * (pair_heads * jnp.concatenate(factors, axis=0))
    mix = jnp.concatenate(mixes, axis=0).astype(jnp.bfloat16)
    stats = pieces(jnp.concatenate(stats, axis=0), 3)
    sums = dot(place_ref[...], jnp.concatenate([mix] + stats, axis=1))
    stats = sum(sums[:, width + i * LANES : width + (i + 1) * LANES] for i in range(3))
    stats = packed_stats(stats, 0.0).astype(jnp.float32)
    size = sums.shape[0] // groups
    for i, sums_ref in enumerate(sums_refs):
        first, middle, last = i * size, i * size + size // 2, (i + 1) * size
        for c in range(width // LANES):
            block = sums[first:last, c * LANES : (c + 1) * LANES]
            sums_ref[c * size : (c + 1) * size] = block.astype(jnp.bfloat16)
        both = stats[first:middle] + pltpu.roll(stats[middle:last], LANES // 2, 1)
        sums_ref[width // LANES * size :] = both.astype(jnp.bfloat16)


def combine_kernel(sources, *refs):
    part_refs, spread_ref, sums_refs = refs[:sources], refs[sources], refs[sources + 1 :]
    width = spread_ref.shape[1]
    rows = sum(ref.shape[0] for ref in sums_refs)
    heads, blocks = width // HEAD_DIM, width // LANES
    stats, mixes = [], []
    for ref in part_refs:
        both = ref[blocks * rows :].astype(jnp.float32)
        both = jnp.concatenate([both, pltpu.roll(both, LANES // 2, 1)], axis=0)
        stats.append(unpacked_stats(both, heads))
        mix = [ref[c * rows : (c + 1) * rows] for c in range(blocks)]
        mixes.append(jnp.concatenate(mix, axis=1).astype(jnp.float32))
    peak = stats[0][0]
    for peaks, _ in stats[1:]:
        peak = jnp.maximum(peak, peaks)
    factors = [jnp.exp(peaks - peak) for peaks, _ in stats]
    total = sum(factor * sums for factor, (_, sums) in zip(factors, stats))
    shares = over_columns(jnp.concatenate(factors, axis=0), spread_ref[...])
    mixed = sum(mix * shares[i * rows : (i + 1) * rows] for i, mix in enumerate(mixes))
    packed = packed_stats(
        jnp.where(total > 0.0, peak, 0.0), pltpu.roll(total, SUM_LANE, 1)
    ).astype(jnp.float32)
    size = sums_refs[0].shape[0]
    for i, sums_ref in enumerate(sums_refs):
        span = slice(i * size, (i + 1) * size)
        sums_ref[:, :width] = mixed[span].astype(jnp.bfloat16)
        sums_ref[:, width:] = packed[span].astype(jnp.bfloat16)


def merge_kernel(
    swapped, sources, hidden_ref, fresh_ref, moved_ref, weight_ref, spread_ref, *refs
):
    part_refs, (own_ref, send_ref) = refs[:sources], refs[sources:]
    width = fresh_ref.shape[1] - LANES
    heads = width // HEAD_DIM
    parts = [ref[...].astype(jnp.float32) for ref in part_refs]
    fresh = fresh_ref[...].astype(jnp.float32)
    if swapped:
        first = lax.axis_index("head") == 0
        fresh = jnp.where(first, fresh, moved_ref[...].astype(jnp.float32))
    parts.append(fresh)
    stats = [unpacked_stats(part[:, width:], heads) for part in parts]
    peak = stats[0][0]
    for peaks, _ in stats[1:]:
        peak = jnp.maximum(peak, peaks)
    factors = [jnp.exp(peaks - peak) for peaks, _ in stats]
    total = sum(factor * sums for factor, (_, sums) in zip(factors, stats))
    total = jnp.where(total > 0.0, total, 1.0)
    shares = jnp.concatenate([f / total for f in factors], axis=0)
    shares = over_columns(shares, spread_ref[...])
    rows = fresh_ref.shape[0]
    mixed = sum(
        part[:, :width] * shares[i * rows : (i + 1) * rows] for i, part in enumerate(parts)
    )
    projected = dot(mixed.astype(jnp.bfloat16), weight_ref[...])
    if swapped:
        projected = projected + jnp.where(first, hidden_ref[...], 0.0)
        own_ref[...] = projected
        both = [part.astype(jnp.float32) for part in pieces(projected, 2)]
        send_ref[...] = jnp.concatenate(both, axis=0).astype(jnp.bfloat16)
    else:
        own_ref[...] = hidden_ref[...]
        send_ref[...] = projected.astype(jnp.bfloat16)


def mlp_kernel(
    exchanged, own_ref, other_ref, gain_ref, up_ref, down_ref, late_ref, *outs
):
    other = other_ref[...].astype(jnp.float32)
    rows = own_ref.shape[0]
    middle = own_ref[...]
    for at in range(0, other.shape[0], rows):
        middle = middle + other[at : at + rows]
    normed = rms_normed(middle, gain_ref[...])
    active = jnp.maximum(dot(normed, up_ref[...]), 0.0).astype(jnp.bfloat16)
    half = down_ref.shape[0]
    down = dot(active[:, :half], down_ref[...]) + dot(active[:, half:], late_ref[...])
    if exchanged:
        kept_ref, sent_ref = outs
        columns = kept_ref.shape[1]
        low = lax.axis_index("head") == 0
        left, right = slice(0, columns), slice(columns, 2 * columns)
        kept = middle + down

        @pl.when(low)
        def _():
            kept_ref[...] = kept[:, left]
            sent_ref[...] = down[:, right]

        @pl.when(jnp.logical_not(low))
        def _():
            kept_ref[...] = kept[:, right]
            sent_ref[...] = down[:, left]

    else:
        middle_ref, down_out_ref = outs
        middle_ref[...] = middle
        down_out_ref[...] = down.astype(jnp.bfloat16)


def loading(*arrays):
    return pl.CostEstimate(
        flops=0, bytes_accessed=sum(2 * array.size for array in arrays), transcendentals=0
    )


def in_hbm(*arrays):
    return [pltpu.with_memory_space_constraint(array, pltpu.HBM) for array in arrays]


def xor_pairs(size, step):
    return [(i, i ^ step) for i in range(size)]


def per_device(
    hidden_in, attention_gain, mlp_gain, qkv_weight, out_weight, up_weight, down_weight,
    position_bias, bucket_edges, cache_keys, cache_values, lengths, page_request, page_index,
):
    f32, bf16 = jnp.float32, jnp.bfloat16
    shape = jax.ShapeDtypeStruct
    own_rows, model = hidden_in.shape
    width = qkv_weight.shape[2]
    page_count = page_request.shape[0]
    blocks = lax.axis_size("blk")
    all_rows = own_rows * blocks
    halves = lax.axis_size("head")
    columns = model // halves
    exchanged = halves == 2
    gain = attention_gain.reshape(1, model)
    query = pl.pallas_call(
        query_kernel,
        out_shape=shape((own_rows, width), bf16),
        in_specs=[HBM_SPEC] * 3,
        out_specs=VMEM_SPEC,
        scratch_shapes=[
            pltpu.VMEM((own_rows, model), f32),
            pltpu.VMEM((1, model), f32),
            pltpu.VMEM((model, width), bf16),
            pltpu.SemaphoreType.DMA((6,)),
        ],
        compiler_params=PARAMS,
        name="query",
    )(*in_hbm(hidden_in, gain, qkv_weight))

    inner = 1
    while inner * inner < blocks:
        inner *= 2
    far = [query] + [
        lax.ppermute(query, "blk", xor_pairs(blocks, step * inner ^ 1))
        for step in range(1, blocks // inner)
    ]
    depth = page_count * PIECE
    early = page_count // 6 * 2
    keys, picks, place, leads, apart, owners = pl.pallas_call(
        functools.partial(page_kernel, own_rows, inner, blocks // inner, exchanged),
        out_shape=(
            pltpu.VMEM((early,) + cache_keys.shape[1:], bf16),
            shape((depth, all_rows), bf16),
            shape((all_rows, depth), bf16),
            shape((page_count, LANES), f32),
            shape((page_count, LANES), f32),
            shape((page_count, LANES), jnp.int32),
        ),
        in_specs=[ANY_SPEC, VMEM_SPEC, HBM_SPEC],
        out_specs=(VMEM_SPEC,) * 6,
        scratch_shapes=[pltpu.SemaphoreType.DMA((4,))],
        compiler_params=PARAMS,
        cost_estimate=loading(cache_keys),
        name="pages",
    )(query, page_request.reshape(1, page_count), *in_hbm(cache_keys))
    near, apart = lax.optimization_barrier((jnp.concatenate(far, axis=0), apart))
    steps = sorted(range(inner), key=lambda step: -(step ^ (step >> 1)) & (inner - 1))
    gathered = [near] + [lax.ppermute(near, "blk", xor_pairs(blocks, step)) for step in steps[1:]]
    table = position_bias.T
    late_keys, bias = pl.pallas_call(
        bias_kernel,
        out_shape=(
            pltpu.VMEM((page_count - early,) + cache_keys.shape[1:], bf16),
            shape((depth, PAGE), f32),
        ),
        in_specs=[HBM_SPEC] * 4 + [VMEM_SPEC, HBM_SPEC, ANY_SPEC],
        out_specs=(VMEM_SPEC,) * 2,
        scratch_shapes=[
            pltpu.SMEM(table.shape, f32),
            pltpu.SMEM(bucket_edges.shape, jnp.int32),
            pltpu.VMEM((1,) + lengths.shape, jnp.int32),
            pltpu.VMEM((1,) + page_index.shape, jnp.int32),
            pltpu.SemaphoreType.DMA((4,)),
            pltpu.SemaphoreType.DMA((4,)),
        ],
        compiler_params=PARAMS,
        cost_estimate=loading(cache_values),
        name="bias",
    )(
        *in_hbm(table, bucket_edges, lengths[None], page_index[None]), owners,
        *in_hbm(cache_keys), near,
    )

    groups = len(gathered)
    size = all_rows // groups
    message = width // LANES * size + size // 2
    sums = pl.pallas_call(
        functools.partial(attend_kernel, groups),
        out_shape=(shape((message, LANES), bf16),) * groups,
        in_specs=[VMEM_SPEC] * (groups + 8),
        out_specs=(VMEM_SPEC,) * groups,
        compiler_params=PARAMS,
        name="attend",
    )(*gathered, bias, picks, place, leads, apart, keys, late_keys, cache_values)
    near_sums = [sums[0]] + [
        lax.ppermute(sums[i], "blk", xor_pairs(blocks, steps[i]))
        for i in range(1, inner)
    ]

    fresh, out_near, spread = pl.pallas_call(
        side_kernel,
        out_shape=(
            shape((own_rows, width + LANES), bf16),
            pltpu.VMEM(out_weight.shape, bf16),
            shape((2 * LANES, width), bf16),
        ),
        in_specs=[VMEM_SPEC] * 4 + [HBM_SPEC] * 2 + [ANY_SPEC],
        out_specs=(VMEM_SPEC,) * 3,
        scratch_shapes=[
            pltpu.VMEM((2, model, width), bf16),
            pltpu.SemaphoreType.DMA((2,)),
            pltpu.SemaphoreType.DMA((4,)),
        ],
        compiler_params=PARAMS,
        cost_estimate=loading(out_weight, out_weight, out_weight),
        name="side",
    )(
        hidden_in, gain, query, table,
        *in_hbm(qkv_weight, out_weight), sums[0],
    )

    *near_sums, fresh = lax.optimization_barrier((*near_sums, fresh))
    outer = blocks // inner
    sums = pl.pallas_call(
        functools.partial(combine_kernel, inner),
        out_shape=(shape((own_rows, width + LANES), bf16),) * outer,
        in_specs=[VMEM_SPEC] * (inner + 1),
        out_specs=(VMEM_SPEC,) * outer,
        compiler_params=PARAMS,
        name="combine",
    )(*near_sums, spread)
    units = down_weight.shape[0]
    cut = units // 8 * 3

    def load_down(start, stop, after):
        return pl.pallas_call(
            functools.partial(load_kernel, start),
            out_shape=pltpu.VMEM((stop - start, model), bf16),
            in_specs=[HBM_SPEC, ANY_SPEC],
            out_specs=VMEM_SPEC,
            scratch_shapes=[pltpu.SemaphoreType.DMA((4,))],
            compiler_params=PARAMS,
            cost_estimate=loading(down_weight),
            name="load",
        )(*in_hbm(down_weight), after)

    down_early = load_down(0, cut, sums[0])
    parts = [sums[0]] + [
        lax.ppermute(sums[step], "blk", xor_pairs(blocks, step * inner ^ 1))
        for step in reversed(range(1, outer))
    ]

    moved = lax.ppermute(fresh, "blk", xor_pairs(blocks, 1)) if exchanged else fresh
    *parts, down_early = lax.optimization_barrier((*parts, down_early))
    own_part, sent_part = pl.pallas_call(
        functools.partial(merge_kernel, exchanged, outer),
        out_shape=(
            shape((own_rows, model), f32),
            shape(((2 if exchanged else 1) * own_rows, model), bf16),
        ),
        in_specs=[VMEM_SPEC] * (outer + 5),
        out_specs=(VMEM_SPEC,) * 2,
        compiler_params=PARAMS,
        name="merge",
    )(hidden_in, fresh, moved, out_near, spread, *parts)

    down_late = load_down(cut, units, sent_part)
    axes = ("head", "blk")
    across = [(i, blocks + (i ^ 1)) for i in range(blocks)]
    back = [(b, a) for a, b in across]
    if exchanged:
        other_part = lax.ppermute(sent_part, axes, across + back)
        mlp_out = (shape((own_rows, columns), f32), shape((own_rows, columns), f32))
    else:
        other_part = lax.psum(sent_part, "head")
        mlp_out = (shape((own_rows, model), f32), shape((own_rows, model), bf16))

    kept, leaving = pl.pallas_call(
        functools.partial(mlp_kernel, exchanged),
        out_shape=mlp_out,
        in_specs=[VMEM_SPEC] * 6,
        out_specs=(VMEM_SPEC,) * 2,
        compiler_params=PARAMS,
        name="mlp",
    )(own_part, other_part, mlp_gain.reshape(1, model), up_weight, down_early, down_late)

    if exchanged:
        straight = [(i, blocks + i) for i in range(blocks)]
        arrived = lax.ppermute(leaving, axes, straight + back)
        moved = lax.ppermute(kept, "blk", xor_pairs(blocks, 1))
        kept = jnp.where(lax.axis_index("head") == 0, kept, moved)
    else:
        kept = lax.dynamic_slice_in_dim(kept, lax.axis_index("head") * columns, columns, 1)
        arrived = lax.psum_scatter(leaving, "head", scatter_dimension=1, tiled=True)
    return kept + arrived.astype(f32)


def solution(mesh):
    in_specs = (
        P("blk", None),
        P(),
        P(),
        P(None, None, "head"),
        P("head", None),
        P(None, "head"),
        P("head", None),
        P(None, "head"),
        P(),
        P("blk", None, "head"),
        P("blk", None, "head"),
        P(),
        P("blk"),
        P("blk"),
    )
    out_specs = P("blk", "head")
    return jax.shard_map(
        per_device, mesh=mesh, in_specs=in_specs, out_specs=out_specs, check_vma=False
    )
```

```python
import functools

import jax
import jax.numpy as jnp
from jax import lax
from jax.experimental import pallas as pl
from jax.experimental.pallas import tpu as pltpu
from jax.sharding import PartitionSpec as P

HEAD_DIM = 64
PAGE = 128
LANES = 128

far_below = -1e30
epsilon = 1e-06

VMEM_SPEC = pl.BlockSpec(memory_space=pltpu.VMEM)
SMEM_SPEC = pl.BlockSpec(memory_space=pltpu.SMEM)
ANY_SPEC = pl.BlockSpec(memory_space=pl.ANY)
HBM_SPEC = pl.BlockSpec(memory_space=pltpu.HBM)
PARAMS = pltpu.CompilerParams(vmem_limit_bytes=16 * 1024 * 1024)

PIECE = 8
SUM_LANE = 3 * PIECE


def iota(shape, axis):
    return lax.broadcasted_iota(jnp.int32, shape, axis)


def split_index(x, size):
    if size & (size - 1):
        return lax.div(x, size), lax.rem(x, size)
    return x >> (size.bit_length() - 1), x & (size - 1)


def head_of(shape, axis):
    return split_index(iota(shape, axis), HEAD_DIM)[0]


def pieces(x, count):
    parts = []
    for _ in range(count):
        part = x.astype(jnp.bfloat16)
        parts.append(part)
        x = x - part.astype(jnp.float32)
    return parts


def rms_normed(x, gain):
    scale = lax.rsqrt(jnp.mean(x * x, axis=1, keepdims=True) + epsilon)
    return (x * scale * gain).astype(jnp.bfloat16)


def dot(a, b, dims=((1,), (0,)), precision=None):
    return lax.dot_general(
        a, b, (dims, ((), ())), preferred_element_type=jnp.float32, precision=precision
    )


def split_copies(source, target, sems, count):
    size = source.shape[0] // count
    return [
        pltpu.make_async_copy(
            source.at[pl.ds(i * size, size)], target.at[pl.ds(i * size, size)], sems.at[i]
        )
        for i in range(count)
    ]


def query_kernel(hidden_hbm, gain_hbm, weight_hbm, query_ref, hidden, gain, weight, sems):
    model = hidden.shape[1]
    small = [
        pltpu.make_async_copy(hidden_hbm, hidden, sems.at[0]),
        pltpu.make_async_copy(gain_hbm, gain, sems.at[1]),
    ]
    half = model // 4
    large = [
        pltpu.make_async_copy(
            weight_hbm.at[0, pl.ds(i * half, half)], weight.at[pl.ds(i * half, half)], sems.at[2 + i]
        )
        for i in range(4)
    ]
    for copy in small + large:
        copy.start()
    for copy in small:
        copy.wait()
    normed = rms_normed(hidden[...], gain[...])
    query = None
    for i, copy in enumerate(large):
        copy.wait()
        span = slice(i * half, (i + 1) * half)
        part = dot(normed[:, span], weight[span])
        query = part if query is None else query + part
    query_ref[...] = query.astype(jnp.bfloat16)


def page_kernel(
    own_rows, inner, outer, swapped, query_ref, request_ref, keys_hbm,
    keys_ref, pick_ref, place_ref, lead_ref, apart_ref, owners_ref,
    sems,
):
    copies = split_copies(
        keys_hbm.at[pl.ds(0, keys_ref.shape[0])], keys_ref, sems, sems.shape[0]
    )
    for copy in copies:
        copy.start()
    me = lax.axis_index("blk")
    page_count = apart_ref.shape[0]
    all_rows, depth = place_ref.shape
    page, lane = iota((page_count, page_count), 0), iota((page_count, page_count), 1)
    by_lane = request_ref[...]
    owner = jnp.max(jnp.where(page == lane, by_lane, -1), axis=1, keepdims=True)
    same = by_lane == owner
    apart_ref[...] = jnp.full(apart_ref.shape, 2 * far_below, jnp.float32)
    apart_ref[:, :page_count] = jnp.where(same, 0.0, 2 * far_below)
    earlier = jnp.max(jnp.where(same & (lane < page), 1, 0), axis=1, keepdims=True)
    lead_ref[...] = jnp.broadcast_to(jnp.where(earlier == 0, 1.0, 0.0), lead_ref.shape)
    owners_ref[...] = jnp.broadcast_to(owner, owners_ref.shape)
    device, own_row = split_index(jnp.maximum(owner, 0), own_rows)

    def slot_of(device):
        high, low = split_index(device ^ me, inner)
        low = jnp.where(high == 0, low, low ^ 1)
        low = -(low ^ (low >> 1)) & (inner - 1)
        slot = (low * outer + high) * own_rows + own_row
        return jnp.where(owner >= 0, slot, -1)

    slot = slot_of(device)
    sum_slot = slot_of(device ^ lax.axis_index("head")) if swapped else slot
    row_of = iota((page_count, all_rows), 1)
    picks = jnp.where(row_of == slot, 1.0, 0.0)
    picks = [jnp.broadcast_to(picks[p : p + 1], (PIECE, all_rows)) for p in range(page_count)]
    pick_ref[...] = jnp.concatenate(picks, axis=0).astype(jnp.bfloat16)
    mine = split_index(iota((page_count, depth), 1), PIECE)[0] == iota((page_count, depth), 0)
    row = iota((all_rows, depth), 0)
    spread = jnp.max(jnp.where(mine, sum_slot, -1), axis=0, keepdims=True)
    place_ref[...] = (row == spread).astype(jnp.bfloat16)
    for copy in copies:
        copy.wait()


def bias_kernel(
    table_hbm, edges_hbm, lengths_hbm, index_hbm, owners_ref, keys_hbm, after_ref,
    keys_ref, bias_ref,
    table, edges, lengths, index, small_sems, sems,
):
    sources, targets = (table_hbm, edges_hbm, lengths_hbm, index_hbm), (table, edges, lengths, index)
    small = [
        pltpu.make_async_copy(source, target, small_sems.at[i])
        for i, (source, target) in enumerate(zip(sources, targets))
    ]
    late = keys_ref.shape[0]
    copies = split_copies(
        keys_hbm.at[pl.ds(keys_hbm.shape[0] - late, late)], keys_ref, sems, sems.shape[0]
    )
    for copy in small + copies:
        copy.start()
    for copy in small:
        copy.wait()
    heads, buckets = table.shape
    page_count = index.shape[1]
    owner = owners_ref[:, 0:1]
    square = (page_count, page_count)
    number = jnp.where(iota(square, 0) == iota(square, 1), index[...], 0)
    number = jnp.sum(number, axis=1, keepdims=True)
    requests = lengths.shape[1]
    length = jnp.where(iota((page_count, requests), 1) == owner, lengths[...], 0)
    length = jnp.sum(length, axis=1, keepdims=True)
    distance = length - number * PAGE - iota((page_count, PAGE), 1)
    far = [distance >= edges[k] for k in range(buckets - 1)]
    usable = (owner >= 0) & (distance > 0)
    bias_ref[...] = jnp.full(bias_ref.shape, far_below, jnp.float32)
    for h in range(heads):
        bias = jnp.full((page_count, PAGE), table[h, 0], jnp.float32)
        for k in range(buckets - 1):
            bias = jnp.where(far[k], table[h, k + 1], bias)
        bias_ref[pl.ds(h, page_count, stride=PIECE), :] = jnp.where(usable, bias, far_below)
    for copy in copies:
        copy.wait()


def side_kernel(
    hidden_ref, gain_ref, query_ref, table_ref, weight_hbm, out_hbm, after_ref,
    fresh_ref, out_ref, spread_ref,
    weight, weight_sems, sems,
):
    copies = [
        pltpu.make_async_copy(weight_hbm.at[1 + i], weight.at[i], weight_sems.at[i])
        for i in range(2)
    ]
    later = split_copies(out_hbm, out_ref, sems, sems.shape[0])
    for copy in copies + later:
        copy.start()
    normed = rms_normed(hidden_ref[...], gain_ref[...])
    heads = table_ref.shape[0]
    spread = iota((heads, LANES), 0) == iota((heads, LANES), 1)
    score = jnp.sum(jnp.where(spread, table_ref[:, 0:1], 0.0), axis=0, keepdims=True)
    copies[0].wait()
    key = dot(normed, weight[0]).astype(jnp.bfloat16)
    product = query_ref[...].astype(jnp.float32) * key.astype(jnp.float32)
    width = product.shape[1]
    gather = (head_of((width, LANES), 0) == iota((width, LANES), 1)).astype(jnp.bfloat16)
    for part in pieces(product, 2):
        score = score + dot(part, gather)
    lane = iota(score.shape, 1)
    used = width // HEAD_DIM
    peak = jnp.where(lane < used, score, 0.0)
    total = jnp.where((lane >= SUM_LANE) & (lane < SUM_LANE + used), 1.0, 0.0)
    fresh_ref[:, width:] = packed_stats(peak, total)
    spread = (iota((LANES, width), 0) == head_of((LANES, width), 1)).astype(jnp.bfloat16)
    spread_ref[:LANES] = spread
    spread_ref[LANES:] = spread
    copies[1].wait()
    fresh_ref[:, :width] = dot(normed, weight[1]).astype(jnp.bfloat16)
    for copy in later:
        copy.wait()


def load_kernel(start, source, after_ref, target, sems):
    rows = source.at[pl.ds(start, target.shape[0])]
    copies = split_copies(rows, target, sems, sems.shape[0])
    for copy in copies:
        copy.start()
    for copy in copies:
        copy.wait()


def packed_stats(peaks, sums):
    one, two, three = (part.astype(jnp.float32) for part in pieces(peaks + sums, 3))
    packed = one + pltpu.roll(two, PIECE, 1) + pltpu.roll(three, 2 * PIECE, 1)
    return packed.astype(jnp.bfloat16)


def unpacked_stats(packed, heads):
    stats = packed.astype(jnp.float32)
    stats = stats + pltpu.roll(stats, LANES - PIECE, 1) + pltpu.roll(stats, LANES - 2 * PIECE, 1)
    sums = pltpu.roll(stats, LANES - SUM_LANE, 1)
    used = iota(stats.shape, 1) < heads
    return jnp.where(used & (sums > 0.0), stats, far_below), jnp.where(used, sums, 0.0)


def over_columns(values, spread):
    return dot(jnp.concatenate(pieces(values, 2), axis=1), spread)


def attend_kernel(groups, *refs):
    query_refs, refs, sums_refs = refs[:groups], refs[groups:-groups], refs[-groups:]
    bias_ref, pick_ref, place_ref, lead_ref, apart_ref, keys_ref, late_ref, values_ref = refs
    page_count = apart_ref.shape[0]
    width = keys_ref.shape[2]
    early = keys_ref.shape[0]
    chunk = 2
    chunks = page_count // chunk
    queries = jnp.concatenate([ref[...] for ref in query_refs], axis=0)
    own_head = (head_of((PIECE, width), 1) == iota((PIECE, width), 0)).astype(jnp.float32)
    pair_heads = jnp.concatenate([own_head] * chunk, axis=0)
    chosen = dot(pick_ref[...], queries)
    lane = iota((PIECE, LANES), 1)
    row = iota((PIECE, LANES), 0)
    nothing = jnp.zeros((PIECE, PAGE), jnp.float32)
    raws = []
    for c in range(chunks):
        rows = chosen[c * chunk * PIECE : (c + 1) * chunk * PIECE]
        split = rows.astype(jnp.bfloat16) * pair_heads.astype(jnp.bfloat16)
        at = c * chunk
        block = keys_ref[at : at + chunk] if at < early else late_ref[at - early : at - early + chunk]
        raws.append(dot(split, block.reshape(chunk * PAGE, width), ((1,), (1,))))
    scores, page_tops = [], []
    for p in range(page_count):
        i = p % chunk
        part = raws[p // chunk][i * PIECE : (i + 1) * PIECE, i * PAGE : (i + 1) * PAGE]
        score = part + bias_ref[p * PIECE : (p + 1) * PIECE]
        scores.append(score)
        page_tops.append(jnp.max(score, axis=1, keepdims=True))
    page_weights = [jnp.exp(score - top) for score, top in zip(scores, page_tops)]
    mixes = []
    for c in range(chunks):
        blocks = []
        for i in range(chunk):
            weight = page_weights[c * chunk + i]
            blocks.append(
                jnp.concatenate([weight if k == i else nothing for k in range(chunk)], axis=1)
            )
        weights = jnp.concatenate(blocks, axis=0).astype(jnp.bfloat16)
        block = values_ref[c * chunk : (c + 1) * chunk]
        mixes.append(dot(weights, block.reshape(chunk * PAGE, width)))
    totals = [jnp.sum(weight, axis=1, keepdims=True) for weight in page_weights]
    tops = jnp.zeros((PIECE, LANES), jnp.float32)
    for p in range(page_count):
        tops = jnp.where(lane == p, page_tops[p], tops)
    stats = []
    for c in range(chunks):
        factors = []
        for p in range(c * chunk, (c + 1) * chunk):
            peak = jnp.max(tops + apart_ref[p : p + 1], axis=1, keepdims=True)
            factor = jnp.exp(page_tops[p] - peak)
            total = jnp.where(lane == row + SUM_LANE, totals[p] * factor, 0.0)
            stats.append(jnp.where(lane == row, peak * lead_ref[p : p + 1], total))
            factors.append(factor)
        mixes[c] = mixes[c] * (pair_heads * jnp.concatenate(factors, axis=0))
    mix = jnp.concatenate(mixes, axis=0).astype(jnp.bfloat16)
    stats = pieces(jnp.concatenate(stats, axis=0), 3)
    sums = dot(place_ref[...], jnp.concatenate([mix] + stats, axis=1))
    stats = sum(sums[:, width + i * LANES : width + (i + 1) * LANES] for i in range(3))
    stats = packed_stats(stats, 0.0).astype(jnp.float32)
    size = sums.shape[0] // groups
    for i, sums_ref in enumerate(sums_refs):
        first, middle, last = i * size, i * size + size // 2, (i + 1) * size
        for c in range(width // LANES):
            block = sums[first:last, c * LANES : (c + 1) * LANES]
            sums_ref[c * size : (c + 1) * size] = block.astype(jnp.bfloat16)
        both = stats[first:middle] + pltpu.roll(stats[middle:last], LANES // 2, 1)
        sums_ref[width // LANES * size :] = both.astype(jnp.bfloat16)


def combine_kernel(sources, *refs):
    part_refs, spread_ref, sums_refs = refs[:sources], refs[sources], refs[sources + 1 :]
    width = spread_ref.shape[1]
    rows = sum(ref.shape[0] for ref in sums_refs)
    heads, blocks = width // HEAD_DIM, width // LANES
    stats, mixes = [], []
    for ref in part_refs:
        both = ref[blocks * rows :].astype(jnp.float32)
        both = jnp.concatenate([both, pltpu.roll(both, LANES // 2, 1)], axis=0)
        stats.append(unpacked_stats(both, heads))
        mix = [ref[c * rows : (c + 1) * rows] for c in range(blocks)]
        mixes.append(jnp.concatenate(mix, axis=1).astype(jnp.float32))
    peak = stats[0][0]
    for peaks, _ in stats[1:]:
        peak = jnp.maximum(peak, peaks)
    factors = [jnp.exp(peaks - peak) for peaks, _ in stats]
    total = sum(factor * sums for factor, (_, sums) in zip(factors, stats))
    shares = over_columns(jnp.concatenate(factors, axis=0), spread_ref[...])
    mixed = sum(mix * shares[i * rows : (i + 1) * rows] for i, mix in enumerate(mixes))
    packed = packed_stats(
        jnp.where(total > 0.0, peak, 0.0), pltpu.roll(total, SUM_LANE, 1)
    ).astype(jnp.float32)
    size = sums_refs[0].shape[0]
    for i, sums_ref in enumerate(sums_refs):
        span = slice(i * size, (i + 1) * size)
        sums_ref[:, :width] = mixed[span].astype(jnp.bfloat16)
        sums_ref[:, width:] = packed[span].astype(jnp.bfloat16)


def merge_kernel(
    swapped, sources, hidden_ref, fresh_ref, moved_ref, weight_ref, spread_ref, *refs
):
    part_refs, (own_ref, send_ref) = refs[:sources], refs[sources:]
    width = fresh_ref.shape[1] - LANES
    heads = width // HEAD_DIM
    parts = [ref[...].astype(jnp.float32) for ref in part_refs]
    fresh = fresh_ref[...].astype(jnp.float32)
    if swapped:
        first = lax.axis_index("head") == 0
        fresh = jnp.where(first, fresh, moved_ref[...].astype(jnp.float32))
    parts.append(fresh)
    stats = [unpacked_stats(part[:, width:], heads) for part in parts]
    peak = stats[0][0]
    for peaks, _ in stats[1:]:
        peak = jnp.maximum(peak, peaks)
    factors = [jnp.exp(peaks - peak) for peaks, _ in stats]
    total = sum(factor * sums for factor, (_, sums) in zip(factors, stats))
    total = jnp.where(total > 0.0, total, 1.0)
    shares = jnp.concatenate([f / total for f in factors], axis=0)
    shares = over_columns(shares, spread_ref[...])
    rows = fresh_ref.shape[0]
    mixed = sum(
        part[:, :width] * shares[i * rows : (i + 1) * rows] for i, part in enumerate(parts)
    )
    projected = dot(mixed.astype(jnp.bfloat16), weight_ref[...])
    if swapped:
        projected = projected + jnp.where(first, hidden_ref[...], 0.0)
        own_ref[...] = projected
        both = [part.astype(jnp.float32) for part in pieces(projected, 2)]
        send_ref[...] = jnp.concatenate(both, axis=0).astype(jnp.bfloat16)
    else:
        own_ref[...] = hidden_ref[...]
        send_ref[...] = projected.astype(jnp.bfloat16)


def mlp_kernel(
    exchanged, own_ref, other_ref, gain_ref, up_ref, down_ref, late_ref, *outs
):
    other = other_ref[...].astype(jnp.float32)
    rows = own_ref.shape[0]
    middle = own_ref[...]
    for at in range(0, other.shape[0], rows):
        middle = middle + other[at : at + rows]
    normed = rms_normed(middle, gain_ref[...])
    active = jnp.maximum(dot(normed, up_ref[...]), 0.0).astype(jnp.bfloat16)
    half = down_ref.shape[0]
    down = dot(active[:, :half], down_ref[...]) + dot(active[:, half:], late_ref[...])
    if exchanged:
        kept_ref, sent_ref = outs
        columns = kept_ref.shape[1]
        low = lax.axis_index("head") == 0
        left, right = slice(0, columns), slice(columns, 2 * columns)
        kept = middle + down

        @pl.when(low)
        def _():
            kept_ref[...] = kept[:, left]
            sent_ref[...] = down[:, right]

        @pl.when(jnp.logical_not(low))
        def _():
            kept_ref[...] = kept[:, right]
            sent_ref[...] = down[:, left]

    else:
        middle_ref, down_out_ref = outs
        middle_ref[...] = middle
        down_out_ref[...] = down.astype(jnp.bfloat16)


def loading(*arrays):
    return pl.CostEstimate(
        flops=0, bytes_accessed=sum(2 * array.size for array in arrays), transcendentals=0
    )


def in_hbm(*arrays):
    return [pltpu.with_memory_space_constraint(array, pltpu.HBM) for array in arrays]


def xor_pairs(size, step):
    return [(i, i ^ step) for i in range(size)]


def per_device(
    hidden_in, attention_gain, mlp_gain, qkv_weight, out_weight, up_weight, down_weight,
    position_bias, bucket_edges, cache_keys, cache_values, lengths, page_request, page_index,
):
    f32, bf16 = jnp.float32, jnp.bfloat16
    shape = jax.ShapeDtypeStruct
    own_rows, model = hidden_in.shape
    width = qkv_weight.shape[2]
    page_count = page_request.shape[0]
    blocks = lax.axis_size("blk")
    all_rows = own_rows * blocks
    halves = lax.axis_size("head")
    columns = model // halves
    exchanged = halves == 2
    gain = attention_gain.reshape(1, model)
    query = pl.pallas_call(
        query_kernel,
        out_shape=shape((own_rows, width), bf16),
        in_specs=[HBM_SPEC] * 3,
        out_specs=VMEM_SPEC,
        scratch_shapes=[
            pltpu.VMEM((own_rows, model), f32),
            pltpu.VMEM((1, model), f32),
            pltpu.VMEM((model, width), bf16),
            pltpu.SemaphoreType.DMA((6,)),
        ],
        compiler_params=PARAMS,
        name="query",
    )(*in_hbm(hidden_in, gain, qkv_weight))

    inner = 1
    while inner * inner < blocks:
        inner *= 2
    far = [query] + [
        lax.ppermute(query, "blk", xor_pairs(blocks, step * inner ^ 1))
        for step in range(1, blocks // inner)
    ]
    depth = page_count * PIECE
    early = page_count // 12 * 2
    keys, picks, place, leads, apart, owners = pl.pallas_call(
        functools.partial(page_kernel, own_rows, inner, blocks // inner, exchanged),
        out_shape=(
            pltpu.VMEM((early,) + cache_keys.shape[1:], bf16),
            shape((depth, all_rows), bf16),
            shape((all_rows, depth), bf16),
            shape((page_count, LANES), f32),
            shape((page_count, LANES), f32),
            shape((page_count, LANES), jnp.int32),
        ),
        in_specs=[ANY_SPEC, VMEM_SPEC, HBM_SPEC],
        out_specs=(VMEM_SPEC,) * 6,
        scratch_shapes=[pltpu.SemaphoreType.DMA((4,))],
        compiler_params=PARAMS,
        cost_estimate=loading(cache_keys),
        name="pages",
    )(query, page_request.reshape(1, page_count), *in_hbm(cache_keys))
    near, apart = lax.optimization_barrier((jnp.concatenate(far, axis=0), apart))
    steps = sorted(range(inner), key=lambda step: -(step ^ (step >> 1)) & (inner - 1))
    gathered = [near] + [lax.ppermute(near, "blk", xor_pairs(blocks, step)) for step in steps[1:]]
    table = position_bias.T
    late_keys, bias = pl.pallas_call(
        bias_kernel,
        out_shape=(
            pltpu.VMEM((page_count - early,) + cache_keys.shape[1:], bf16),
            shape((depth, PAGE), f32),
        ),
        in_specs=[HBM_SPEC] * 4 + [VMEM_SPEC, HBM_SPEC, ANY_SPEC],
        out_specs=(VMEM_SPEC,) * 2,
        scratch_shapes=[
            pltpu.SMEM(table.shape, f32),
            pltpu.SMEM(bucket_edges.shape, jnp.int32),
            pltpu.VMEM((1,) + lengths.shape, jnp.int32),
            pltpu.VMEM((1,) + page_index.shape, jnp.int32),
            pltpu.SemaphoreType.DMA((4,)),
            pltpu.SemaphoreType.DMA((4,)),
        ],
        compiler_params=PARAMS,
        cost_estimate=loading(cache_values),
        name="bias",
    )(
        *in_hbm(table, bucket_edges, lengths[None], page_index[None]), owners,
        *in_hbm(cache_keys), near,
    )

    groups = len(gathered)
    size = all_rows // groups
    message = width // LANES * size + size // 2
    sums = pl.pallas_call(
        functools.partial(attend_kernel, groups),
        out_shape=(shape((message, LANES), bf16),) * groups,
        in_specs=[VMEM_SPEC] * (groups + 8),
        out_specs=(VMEM_SPEC,) * groups,
        compiler_params=PARAMS,
        name="attend",
    )(*gathered, bias, picks, place, leads, apart, keys, late_keys, cache_values)
    near_sums = [sums[0]] + [
        lax.ppermute(sums[i], "blk", xor_pairs(blocks, steps[i]))
        for i in range(1, inner)
    ]

    fresh, out_near, spread = pl.pallas_call(
        side_kernel,
        out_shape=(
            shape((own_rows, width + LANES), bf16),
            pltpu.VMEM(out_weight.shape, bf16),
            shape((2 * LANES, width), bf16),
        ),
        in_specs=[VMEM_SPEC] * 4 + [HBM_SPEC] * 2 + [ANY_SPEC],
        out_specs=(VMEM_SPEC,) * 3,
        scratch_shapes=[
            pltpu.VMEM((2, model, width), bf16),
            pltpu.SemaphoreType.DMA((2,)),
            pltpu.SemaphoreType.DMA((4,)),
        ],
        compiler_params=PARAMS,
        cost_estimate=loading(out_weight, out_weight, out_weight),
        name="side",
    )(
        hidden_in, gain, query, table,
        *in_hbm(qkv_weight, out_weight), sums[0],
    )

    *near_sums, fresh = lax.optimization_barrier((*near_sums, fresh))
    outer = blocks // inner
    sums = pl.pallas_call(
        functools.partial(combine_kernel, inner),
        out_shape=(shape((own_rows, width + LANES), bf16),) * outer,
        in_specs=[VMEM_SPEC] * (inner + 1),
        out_specs=(VMEM_SPEC,) * outer,
        compiler_params=PARAMS,
        name="combine",
    )(*near_sums, spread)
    units = down_weight.shape[0]
    cut = units // 8 * 3

    def load_down(start, stop, after):
        return pl.pallas_call(
            functools.partial(load_kernel, start),
            out_shape=pltpu.VMEM((stop - start, model), bf16),
            in_specs=[HBM_SPEC, ANY_SPEC],
            out_specs=VMEM_SPEC,
            scratch_shapes=[pltpu.SemaphoreType.DMA((4,))],
            compiler_params=PARAMS,
            cost_estimate=loading(down_weight),
            name="load",
        )(*in_hbm(down_weight), after)

    down_early = load_down(0, cut, sums[0])
    parts = [sums[0]] + [
        lax.ppermute(sums[step], "blk", xor_pairs(blocks, step * inner ^ 1))
        for step in reversed(range(1, outer))
    ]

    moved = lax.ppermute(fresh, "blk", xor_pairs(blocks, 1)) if exchanged else fresh
    *parts, down_early = lax.optimization_barrier((*parts, down_early))
    own_part, sent_part = pl.pallas_call(
        functools.partial(merge_kernel, exchanged, outer),
        out_shape=(
            shape((own_rows, model), f32),
            shape(((2 if exchanged else 1) * own_rows, model), bf16),
        ),
        in_specs=[VMEM_SPEC] * (outer + 5),
        out_specs=(VMEM_SPEC,) * 2,
        compiler_params=PARAMS,
        name="merge",
    )(hidden_in, fresh, moved, out_near, spread, *parts)

    down_late = load_down(cut, units, sent_part)
    axes = ("head", "blk")
    across = [(i, blocks + (i ^ 1)) for i in range(blocks)]
    back = [(b, a) for a, b in across]
    if exchanged:
        other_part = lax.ppermute(sent_part, axes, across + back)
        mlp_out = (shape((own_rows, columns), f32), shape((own_rows, columns), f32))
    else:
        other_part = lax.psum(sent_part, "head")
        mlp_out = (shape((own_rows, model), f32), shape((own_rows, model), bf16))

    kept, leaving = pl.pallas_call(
        functools.partial(mlp_kernel, exchanged),
        out_shape=mlp_out,
        in_specs=[VMEM_SPEC] * 6,
        out_specs=(VMEM_SPEC,) * 2,
        compiler_params=PARAMS,
        name="mlp",
    )(own_part, other_part, mlp_gain.reshape(1, model), up_weight, down_early, down_late)

    if exchanged:
        straight = [(i, blocks + i) for i in range(blocks)]
        arrived = lax.ppermute(leaving, axes, straight + back)
        moved = lax.ppermute(kept, "blk", xor_pairs(blocks, 1))
        kept = jnp.where(lax.axis_index("head") == 0, kept, moved)
    else:
        kept = lax.dynamic_slice_in_dim(kept, lax.axis_index("head") * columns, columns, 1)
        arrived = lax.psum_scatter(leaving, "head", scatter_dimension=1, tiled=True)
    return kept + arrived.astype(f32)


def solution(mesh):
    in_specs = (
        P("blk", None),
        P(),
        P(),
        P(None, None, "head"),
        P("head", None),
        P(None, "head"),
        P("head", None),
        P(None, "head"),
        P(),
        P("blk", None, "head"),
        P("blk", None, "head"),
        P(),
        P("blk"),
        P("blk"),
    )
    out_specs = P("blk", "head")
    return jax.shard_map(
        per_device, mesh=mesh, in_specs=in_specs, out_specs=out_specs, check_vma=False
    )
```

```python
import functools

import jax
import jax.numpy as jnp
from jax import lax
from jax.experimental import pallas as pl
from jax.experimental.pallas import tpu as pltpu
from jax.sharding import PartitionSpec as P

HEAD_DIM = 64
PAGE = 128
LANES = 128

far_below = -1e30
epsilon = 1e-06

VMEM_SPEC = pl.BlockSpec(memory_space=pltpu.VMEM)
SMEM_SPEC = pl.BlockSpec(memory_space=pltpu.SMEM)
ANY_SPEC = pl.BlockSpec(memory_space=pl.ANY)
HBM_SPEC = pl.BlockSpec(memory_space=pltpu.HBM)
PARAMS = pltpu.CompilerParams(vmem_limit_bytes=16 * 1024 * 1024)

PIECE = 8
SUM_LANE = 3 * PIECE


def iota(shape, axis):
    return lax.broadcasted_iota(jnp.int32, shape, axis)


def split_index(x, size):
    if size & (size - 1):
        return lax.div(x, size), lax.rem(x, size)
    return x >> (size.bit_length() - 1), x & (size - 1)


def head_of(shape, axis):
    return split_index(iota(shape, axis), HEAD_DIM)[0]


def pieces(x, count):
    parts = []
    for _ in range(count):
        part = x.astype(jnp.bfloat16)
        parts.append(part)
        x = x - part.astype(jnp.float32)
    return parts


def rms_normed(x, gain):
    scale = lax.rsqrt(jnp.mean(x * x, axis=1, keepdims=True) + epsilon)
    return (x * scale * gain).astype(jnp.bfloat16)


def dot(a, b, dims=((1,), (0,)), precision=None):
    return lax.dot_general(
        a, b, (dims, ((), ())), preferred_element_type=jnp.float32, precision=precision
    )


def split_copies(source, target, sems, count):
    size = source.shape[0] // count
    return [
        pltpu.make_async_copy(
            source.at[pl.ds(i * size, size)], target.at[pl.ds(i * size, size)], sems.at[i]
        )
        for i in range(count)
    ]


def query_kernel(hidden_hbm, gain_hbm, weight_hbm, query_ref, hidden, gain, weight, sems):
    model = hidden.shape[1]
    small = [
        pltpu.make_async_copy(hidden_hbm, hidden, sems.at[0]),
        pltpu.make_async_copy(gain_hbm, gain, sems.at[1]),
    ]
    half = model // 4
    large = [
        pltpu.make_async_copy(
            weight_hbm.at[0, pl.ds(i * half, half)], weight.at[pl.ds(i * half, half)], sems.at[2 + i]
        )
        for i in range(4)
    ]
    for copy in small + large:
        copy.start()
    for copy in small:
        copy.wait()
    normed = rms_normed(hidden[...], gain[...])
    query = None
    for i, copy in enumerate(large):
        copy.wait()
        span = slice(i * half, (i + 1) * half)
        part = dot(normed[:, span], weight[span])
        query = part if query is None else query + part
    query_ref[...] = query.astype(jnp.bfloat16)


def page_kernel(
    own_rows, inner, outer, swapped, query_ref, request_ref, keys_hbm,
    keys_ref, pick_ref, place_ref, lead_ref, apart_ref, owners_ref,
    sems,
):
    copies = split_copies(
        keys_hbm.at[pl.ds(0, keys_ref.shape[0])], keys_ref, sems, sems.shape[0]
    )
    for copy in copies:
        copy.start()
    me = lax.axis_index("blk")
    page_count = apart_ref.shape[0]
    all_rows, depth = place_ref.shape
    page, lane = iota((page_count, page_count), 0), iota((page_count, page_count), 1)
    by_lane = request_ref[...]
    owner = jnp.max(jnp.where(page == lane, by_lane, -1), axis=1, keepdims=True)
    same = by_lane == owner
    apart_ref[...] = jnp.full(apart_ref.shape, 2 * far_below, jnp.float32)
    apart_ref[:, :page_count] = jnp.where(same, 0.0, 2 * far_below)
    earlier = jnp.max(jnp.where(same & (lane < page), 1, 0), axis=1, keepdims=True)
    lead_ref[...] = jnp.broadcast_to(jnp.where(earlier == 0, 1.0, 0.0), lead_ref.shape)
    owners_ref[...] = jnp.broadcast_to(owner, owners_ref.shape)
    device, own_row = split_index(jnp.maximum(owner, 0), own_rows)

    def slot_of(device):
        high, low = split_index(device ^ me, inner)
        low = jnp.where(high == 0, low, low ^ 1)
        low = -(low ^ (low >> 1)) & (inner - 1)
        slot = (low * outer + high) * own_rows + own_row
        return jnp.where(owner >= 0, slot, -1)

    slot = slot_of(device)
    sum_slot = slot_of(device ^ lax.axis_index("head")) if swapped else slot
    row_of = iota((page_count, all_rows), 1)
    picks = jnp.where(row_of == slot, 1.0, 0.0)
    picks = [jnp.broadcast_to(picks[p : p + 1], (PIECE, all_rows)) for p in range(page_count)]
    pick_ref[...] = jnp.concatenate(picks, axis=0).astype(jnp.bfloat16)
    mine = split_index(iota((page_count, depth), 1), PIECE)[0] == iota((page_count, depth), 0)
    row = iota((all_rows, depth), 0)
    spread = jnp.max(jnp.where(mine, sum_slot, -1), axis=0, keepdims=True)
    place_ref[...] = (row == spread).astype(jnp.bfloat16)
    for copy in copies:
        copy.wait()


def bias_kernel(
    table_hbm, edges_hbm, lengths_hbm, index_hbm, owners_ref, keys_hbm, after_ref,
    keys_ref, bias_ref,
    table, edges, lengths, index, small_sems, sems,
):
    sources, targets = (table_hbm, edges_hbm, lengths_hbm, index_hbm), (table, edges, lengths, index)
    small = [
        pltpu.make_async_copy(source, target, small_sems.at[i])
        for i, (source, target) in enumerate(zip(sources, targets))
    ]
    late = keys_ref.shape[0]
    copies = split_copies(
        keys_hbm.at[pl.ds(keys_hbm.shape[0] - late, late)], keys_ref, sems, sems.shape[0]
    )
    for copy in small + copies:
        copy.start()
    for copy in small:
        copy.wait()
    heads, buckets = table.shape
    page_count = index.shape[1]
    owner = owners_ref[:, 0:1]
    square = (page_count, page_count)
    number = jnp.where(iota(square, 0) == iota(square, 1), index[...], 0)
    number = jnp.sum(number, axis=1, keepdims=True)
    requests = lengths.shape[1]
    length = jnp.where(iota((page_count, requests), 1) == owner, lengths[...], 0)
    length = jnp.sum(length, axis=1, keepdims=True)
    distance = length - number * PAGE - iota((page_count, PAGE), 1)
    far = [distance >= edges[k] for k in range(buckets - 1)]
    usable = (owner >= 0) & (distance > 0)
    bias_ref[...] = jnp.full(bias_ref.shape, far_below, jnp.float32)
    for h in range(heads):
        bias = jnp.full((page_count, PAGE), table[h, 0], jnp.float32)
        for k in range(buckets - 1):
            bias = jnp.where(far[k], table[h, k + 1], bias)
        bias_ref[pl.ds(h, page_count, stride=PIECE), :] = jnp.where(usable, bias, far_below)
    for copy in copies:
        copy.wait()


def side_kernel(
    hidden_ref, gain_ref, query_ref, table_ref, weight_hbm, out_hbm, after_ref,
    fresh_ref, out_ref, spread_ref,
    weight, weight_sems, sems,
):
    copies = [
        pltpu.make_async_copy(weight_hbm.at[1 + i], weight.at[i], weight_sems.at[i])
        for i in range(2)
    ]
    later = split_copies(out_hbm, out_ref, sems, sems.shape[0])
    for copy in copies + later:
        copy.start()
    normed = rms_normed(hidden_ref[...], gain_ref[...])
    heads = table_ref.shape[0]
    spread = iota((heads, LANES), 0) == iota((heads, LANES), 1)
    score = jnp.sum(jnp.where(spread, table_ref[:, 0:1], 0.0), axis=0, keepdims=True)
    copies[0].wait()
    key = dot(normed, weight[0]).astype(jnp.bfloat16)
    product = query_ref[...].astype(jnp.float32) * key.astype(jnp.float32)
    width = product.shape[1]
    gather = (head_of((width, LANES), 0) == iota((width, LANES), 1)).astype(jnp.bfloat16)
    for part in pieces(product, 2):
        score = score + dot(part, gather)
    lane = iota(score.shape, 1)
    used = width // HEAD_DIM
    peak = jnp.where(lane < used, score, 0.0)
    total = jnp.where((lane >= SUM_LANE) & (lane < SUM_LANE + used), 1.0, 0.0)
    fresh_ref[:, width:] = packed_stats(peak, total)
    spread = (iota((LANES, width), 0) == head_of((LANES, width), 1)).astype(jnp.bfloat16)
    spread_ref[:LANES] = spread
    spread_ref[LANES:] = spread
    copies[1].wait()
    fresh_ref[:, :width] = dot(normed, weight[1]).astype(jnp.bfloat16)
    for copy in later:
        copy.wait()


def load_kernel(start, source, after_ref, target, sems):
    rows = source.at[pl.ds(start, target.shape[0])]
    copies = split_copies(rows, target, sems, sems.shape[0])
    for copy in copies:
        copy.start()
    for copy in copies:
        copy.wait()


def packed_stats(peaks, sums):
    one, two, three = (part.astype(jnp.float32) for part in pieces(peaks + sums, 3))
    packed = one + pltpu.roll(two, PIECE, 1) + pltpu.roll(three, 2 * PIECE, 1)
    return packed.astype(jnp.bfloat16)


def unpacked_stats(packed, heads):
    stats = packed.astype(jnp.float32)
    stats = stats + pltpu.roll(stats, LANES - PIECE, 1) + pltpu.roll(stats, LANES - 2 * PIECE, 1)
    sums = pltpu.roll(stats, LANES - SUM_LANE, 1)
    used = iota(stats.shape, 1) < heads
    return jnp.where(used & (sums > 0.0), stats, far_below), jnp.where(used, sums, 0.0)


def over_columns(values, spread):
    return dot(jnp.concatenate(pieces(values, 2), axis=1), spread)


def attend_kernel(groups, *refs):
    query_refs, refs, sums_refs = refs[:groups], refs[groups:-groups], refs[-groups:]
    bias_ref, pick_ref, place_ref, lead_ref, apart_ref, keys_ref, late_ref, values_ref = refs
    page_count = apart_ref.shape[0]
    width = keys_ref.shape[2]
    early = keys_ref.shape[0]
    chunk = 2
    chunks = page_count // chunk
    queries = jnp.concatenate([ref[...] for ref in query_refs], axis=0)
    own_head = (head_of((PIECE, width), 1) == iota((PIECE, width), 0)).astype(jnp.float32)
    pair_heads = jnp.concatenate([own_head] * chunk, axis=0)
    chosen = dot(pick_ref[...], queries)
    lane = iota((PIECE, LANES), 1)
    row = iota((PIECE, LANES), 0)
    nothing = jnp.zeros((PIECE, PAGE), jnp.float32)
    raws = []
    for c in range(chunks):
        rows = chosen[c * chunk * PIECE : (c + 1) * chunk * PIECE]
        split = rows.astype(jnp.bfloat16) * pair_heads.astype(jnp.bfloat16)
        at = c * chunk
        block = keys_ref[at : at + chunk] if at < early else late_ref[at - early : at - early + chunk]
        raws.append(dot(split, block.reshape(chunk * PAGE, width), ((1,), (1,))))
    scores, page_tops = [], []
    for p in range(page_count):
        i = p % chunk
        part = raws[p // chunk][i * PIECE : (i + 1) * PIECE, i * PAGE : (i + 1) * PAGE]
        score = part + bias_ref[p * PIECE : (p + 1) * PIECE]
        scores.append(score)
        page_tops.append(jnp.max(score, axis=1, keepdims=True))
    page_weights = [jnp.exp(score - top) for score, top in zip(scores, page_tops)]
    mixes = []
    for c in range(chunks):
        blocks = []
        for i in range(chunk):
            weight = page_weights[c * chunk + i]
            blocks.append(
                jnp.concatenate([weight if k == i else nothing for k in range(chunk)], axis=1)
            )
        weights = jnp.concatenate(blocks, axis=0).astype(jnp.bfloat16)
        block = values_ref[c * chunk : (c + 1) * chunk]
        mixes.append(dot(weights, block.reshape(chunk * PAGE, width)))
    totals = [jnp.sum(weight, axis=1, keepdims=True) for weight in page_weights]
    tops = jnp.zeros((PIECE, LANES), jnp.float32)
    for p in range(page_count):
        tops = jnp.where(lane == p, page_tops[p], tops)
    stats = []
    for c in range(chunks):
        factors = []
        for p in range(c * chunk, (c + 1) * chunk):
            peak = jnp.max(tops + apart_ref[p : p + 1], axis=1, keepdims=True)
            factor = jnp.exp(page_tops[p] - peak)
            total = jnp.where(lane == row + SUM_LANE, totals[p] * factor, 0.0)
            stats.append(jnp.where(lane == row, peak * lead_ref[p : p + 1], total))
            factors.append(factor)
        mixes[c] = mixes[c] * (pair_heads * jnp.concatenate(factors, axis=0))
    mix = jnp.concatenate(mixes, axis=0).astype(jnp.bfloat16)
    stats = pieces(jnp.concatenate(stats, axis=0), 3)
    sums = dot(place_ref[...], jnp.concatenate([mix] + stats, axis=1))
    stats = sum(sums[:, width + i * LANES : width + (i + 1) * LANES] for i in range(3))
    stats = packed_stats(stats, 0.0).astype(jnp.float32)
    size = sums.shape[0] // groups
    for i, sums_ref in enumerate(sums_refs):
        first, middle, last = i * size, i * size + size // 2, (i + 1) * size
        for c in range(width // LANES):
            block = sums[first:last, c * LANES : (c + 1) * LANES]
            sums_ref[c * size : (c + 1) * size] = block.astype(jnp.bfloat16)
        both = stats[first:middle] + pltpu.roll(stats[middle:last], LANES // 2, 1)
        sums_ref[width // LANES * size :] = both.astype(jnp.bfloat16)


def combine_kernel(sources, *refs):
    part_refs, spread_ref, sums_refs = refs[:sources], refs[sources], refs[sources + 1 :]
    width = spread_ref.shape[1]
    rows = sum(ref.shape[0] for ref in sums_refs)
    heads, blocks = width // HEAD_DIM, width // LANES
    stats, mixes = [], []
    for ref in part_refs:
        both = ref[blocks * rows :].astype(jnp.float32)
        both = jnp.concatenate([both, pltpu.roll(both, LANES // 2, 1)], axis=0)
        stats.append(unpacked_stats(both, heads))
        mix = [ref[c * rows : (c + 1) * rows] for c in range(blocks)]
        mixes.append(jnp.concatenate(mix, axis=1).astype(jnp.float32))
    peak = stats[0][0]
    for peaks, _ in stats[1:]:
        peak = jnp.maximum(peak, peaks)
    factors = [jnp.exp(peaks - peak) for peaks, _ in stats]
    total = sum(factor * sums for factor, (_, sums) in zip(factors, stats))
    shares = over_columns(jnp.concatenate(factors, axis=0), spread_ref[...])
    mixed = sum(mix * shares[i * rows : (i + 1) * rows] for i, mix in enumerate(mixes))
    packed = packed_stats(
        jnp.where(total > 0.0, peak, 0.0), pltpu.roll(total, SUM_LANE, 1)
    ).astype(jnp.float32)
    size = sums_refs[0].shape[0]
    for i, sums_ref in enumerate(sums_refs):
        span = slice(i * size, (i + 1) * size)
        sums_ref[:, :width] = mixed[span].astype(jnp.bfloat16)
        sums_ref[:, width:] = packed[span].astype(jnp.bfloat16)


def merge_kernel(
    swapped, sources, hidden_ref, fresh_ref, moved_ref, weight_ref, spread_ref, *refs
):
    part_refs, (own_ref, send_ref) = refs[:sources], refs[sources:]
    width = fresh_ref.shape[1] - LANES
    heads = width // HEAD_DIM
    parts = [ref[...].astype(jnp.float32) for ref in part_refs]
    fresh = fresh_ref[...].astype(jnp.float32)
    if swapped:
        first = lax.axis_index("head") == 0
        fresh = jnp.where(first, fresh, moved_ref[...].astype(jnp.float32))
    parts.append(fresh)
    stats = [unpacked_stats(part[:, width:], heads) for part in parts]
    peak = stats[0][0]
    for peaks, _ in stats[1:]:
        peak = jnp.maximum(peak, peaks)
    factors = [jnp.exp(peaks - peak) for peaks, _ in stats]
    total = sum(factor * sums for factor, (_, sums) in zip(factors, stats))
    total = jnp.where(total > 0.0, total, 1.0)
    shares = jnp.concatenate([f / total for f in factors], axis=0)
    shares = over_columns(shares, spread_ref[...])
    rows = fresh_ref.shape[0]
    mixed = sum(
        part[:, :width] * shares[i * rows : (i + 1) * rows] for i, part in enumerate(parts)
    )
    projected = dot(mixed.astype(jnp.bfloat16), weight_ref[...])
    if swapped:
        projected = projected + jnp.where(first, hidden_ref[...], 0.0)
        own_ref[...] = projected
    else:
        own_ref[...] = hidden_ref[...]
    send_ref[...] = projected.astype(jnp.bfloat16)


def mlp_kernel(
    exchanged, own_ref, other_ref, gain_ref, up_ref, down_ref, late_ref, *outs
):
    own = own_ref[...]
    middle = own + other_ref[...].astype(jnp.float32)
    normed = rms_normed(middle, gain_ref[...])
    active = jnp.maximum(dot(normed, up_ref[...]), 0.0).astype(jnp.bfloat16)
    half = down_ref.shape[0]
    down = dot(active[:, :half], down_ref[...]) + dot(active[:, half:], late_ref[...])
    if exchanged:
        kept_ref, sent_ref = outs
        columns = kept_ref.shape[1]
        low = lax.axis_index("head") == 0
        left, right = slice(0, columns), slice(columns, 2 * columns)
        kept = middle + down
        down = down + (own - own.astype(jnp.bfloat16).astype(jnp.float32))

        @pl.when(low)
        def _():
            kept_ref[...] = kept[:, left]
            sent_ref[...] = down[:, right]

        @pl.when(jnp.logical_not(low))
        def _():
            kept_ref[...] = kept[:, right]
            sent_ref[...] = down[:, left]

    else:
        middle_ref, down_out_ref = outs
        middle_ref[...] = middle
        down_out_ref[...] = down.astype(jnp.bfloat16)


def loading(*arrays):
    return pl.CostEstimate(
        flops=0, bytes_accessed=sum(2 * array.size for array in arrays), transcendentals=0
    )


def in_hbm(*arrays):
    return [pltpu.with_memory_space_constraint(array, pltpu.HBM) for array in arrays]


def xor_pairs(size, step):
    return [(i, i ^ step) for i in range(size)]


def per_device(
    hidden_in, attention_gain, mlp_gain, qkv_weight, out_weight, up_weight, down_weight,
    position_bias, bucket_edges, cache_keys, cache_values, lengths, page_request, page_index,
):
    f32, bf16 = jnp.float32, jnp.bfloat16
    shape = jax.ShapeDtypeStruct
    own_rows, model = hidden_in.shape
    width = qkv_weight.shape[2]
    page_count = page_request.shape[0]
    blocks = lax.axis_size("blk")
    all_rows = own_rows * blocks
    halves = lax.axis_size("head")
    columns = model // halves
    exchanged = halves == 2
    gain = attention_gain.reshape(1, model)
    query = pl.pallas_call(
        query_kernel,
        out_shape=shape((own_rows, width), bf16),
        in_specs=[HBM_SPEC] * 3,
        out_specs=VMEM_SPEC,
        scratch_shapes=[
            pltpu.VMEM((own_rows, model), f32),
            pltpu.VMEM((1, model), f32),
            pltpu.VMEM((model, width), bf16),
            pltpu.SemaphoreType.DMA((6,)),
        ],
        compiler_params=PARAMS,
        name="query",
    )(*in_hbm(hidden_in, gain, qkv_weight))

    inner = 1
    while inner * inner < blocks:
        inner *= 2
    far = [query] + [
        lax.ppermute(query, "blk", xor_pairs(blocks, step * inner ^ 1))
        for step in range(1, blocks // inner)
    ]
    depth = page_count * PIECE
    early = page_count // 6 * 2
    keys, picks, place, leads, apart, owners = pl.pallas_call(
        functools.partial(page_kernel, own_rows, inner, blocks // inner, exchanged),
        out_shape=(
            pltpu.VMEM((early,) + cache_keys.shape[1:], bf16),
            shape((depth, all_rows), bf16),
            shape((all_rows, depth), bf16),
            shape((page_count, LANES), f32),
            shape((page_count, LANES), f32),
            shape((page_count, LANES), jnp.int32),
        ),
        in_specs=[ANY_SPEC, VMEM_SPEC, HBM_SPEC],
        out_specs=(VMEM_SPEC,) * 6,
        scratch_shapes=[pltpu.SemaphoreType.DMA((4,))],
        compiler_params=PARAMS,
        cost_estimate=loading(cache_keys),
        name="pages",
    )(query, page_request.reshape(1, page_count), *in_hbm(cache_keys))
    near, apart = lax.optimization_barrier((jnp.concatenate(far, axis=0), apart))
    steps = sorted(range(inner), key=lambda step: -(step ^ (step >> 1)) & (inner - 1))
    gathered = [near] + [lax.ppermute(near, "blk", xor_pairs(blocks, step)) for step in steps[1:]]
    table = position_bias.T
    late_keys, bias = pl.pallas_call(
        bias_kernel,
        out_shape=(
            pltpu.VMEM((page_count - early,) + cache_keys.shape[1:], bf16),
            shape((depth, PAGE), f32),
        ),
        in_specs=[HBM_SPEC] * 4 + [VMEM_SPEC, HBM_SPEC, ANY_SPEC],
        out_specs=(VMEM_SPEC,) * 2,
        scratch_shapes=[
            pltpu.SMEM(table.shape, f32),
            pltpu.SMEM(bucket_edges.shape, jnp.int32),
            pltpu.VMEM((1,) + lengths.shape, jnp.int32),
            pltpu.VMEM((1,) + page_index.shape, jnp.int32),
            pltpu.SemaphoreType.DMA((4,)),
            pltpu.SemaphoreType.DMA((4,)),
        ],
        compiler_params=PARAMS,
        cost_estimate=loading(cache_values),
        name="bias",
    )(
        *in_hbm(table, bucket_edges, lengths[None], page_index[None]), owners,
        *in_hbm(cache_keys), near,
    )

    groups = len(gathered)
    size = all_rows // groups
    message = width // LANES * size + size // 2
    sums = pl.pallas_call(
        functools.partial(attend_kernel, groups),
        out_shape=(shape((message, LANES), bf16),) * groups,
        in_specs=[VMEM_SPEC] * (groups + 8),
        out_specs=(VMEM_SPEC,) * groups,
        compiler_params=PARAMS,
        name="attend",
    )(*gathered, bias, picks, place, leads, apart, keys, late_keys, cache_values)
    near_sums = [sums[0]] + [
        lax.ppermute(sums[i], "blk", xor_pairs(blocks, steps[i]))
        for i in range(1, inner)
    ]

    fresh, out_near, spread = pl.pallas_call(
        side_kernel,
        out_shape=(
            shape((own_rows, width + LANES), bf16),
            pltpu.VMEM(out_weight.shape, bf16),
            shape((2 * LANES, width), bf16),
        ),
        in_specs=[VMEM_SPEC] * 4 + [HBM_SPEC] * 2 + [ANY_SPEC],
        out_specs=(VMEM_SPEC,) * 3,
        scratch_shapes=[
            pltpu.VMEM((2, model, width), bf16),
            pltpu.SemaphoreType.DMA((2,)),
            pltpu.SemaphoreType.DMA((4,)),
        ],
        compiler_params=PARAMS,
        cost_estimate=loading(out_weight, out_weight, out_weight),
        name="side",
    )(
        hidden_in, gain, query, table,
        *in_hbm(qkv_weight, out_weight), sums[0],
    )

    *near_sums, fresh = lax.optimization_barrier((*near_sums, fresh))
    outer = blocks // inner
    sums = pl.pallas_call(
        functools.partial(combine_kernel, inner),
        out_shape=(shape((own_rows, width + LANES), bf16),) * outer,
        in_specs=[VMEM_SPEC] * (inner + 1),
        out_specs=(VMEM_SPEC,) * outer,
        compiler_params=PARAMS,
        name="combine",
    )(*near_sums, spread)
    units = down_weight.shape[0]
    cut = units // 8 * 3

    def load_down(start, stop, after):
        return pl.pallas_call(
            functools.partial(load_kernel, start),
            out_shape=pltpu.VMEM((stop - start, model), bf16),
            in_specs=[HBM_SPEC, ANY_SPEC],
            out_specs=VMEM_SPEC,
            scratch_shapes=[pltpu.SemaphoreType.DMA((4,))],
            compiler_params=PARAMS,
            cost_estimate=loading(down_weight),
            name="load",
        )(*in_hbm(down_weight), after)

    down_early = load_down(0, cut, sums[0])
    parts = [sums[0]] + [
        lax.ppermute(sums[step], "blk", xor_pairs(blocks, step * inner ^ 1))
        for step in reversed(range(1, outer))
    ]

    moved = lax.ppermute(fresh, "blk", xor_pairs(blocks, 1)) if exchanged else fresh
    *parts, down_early = lax.optimization_barrier((*parts, down_early))
    own_part, sent_part = pl.pallas_call(
        functools.partial(merge_kernel, exchanged, outer),
        out_shape=(
            shape((own_rows, model), f32),
            shape((own_rows, model), bf16),
        ),
        in_specs=[VMEM_SPEC] * (outer + 5),
        out_specs=(VMEM_SPEC,) * 2,
        compiler_params=PARAMS,
        name="merge",
    )(hidden_in, fresh, moved, out_near, spread, *parts)

    down_late = load_down(cut, units, sent_part)
    axes = ("head", "blk")
    across = [(i, blocks + (i ^ 1)) for i in range(blocks)]
    back = [(b, a) for a, b in across]
    if exchanged:
        other_part = lax.ppermute(sent_part, axes, across + back)
        mlp_out = (shape((own_rows, columns), f32), shape((own_rows, columns), f32))
    else:
        other_part = lax.psum(sent_part, "head")
        mlp_out = (shape((own_rows, model), f32), shape((own_rows, model), bf16))

    kept, leaving = pl.pallas_call(
        functools.partial(mlp_kernel, exchanged),
        out_shape=mlp_out,
        in_specs=[VMEM_SPEC] * 6,
        out_specs=(VMEM_SPEC,) * 2,
        compiler_params=PARAMS,
        name="mlp",
    )(own_part, other_part, mlp_gain.reshape(1, model), up_weight, down_early, down_late)

    if exchanged:
        straight = [(i, blocks + i) for i in range(blocks)]
        arrived = lax.ppermute(leaving, axes, straight + back)
        moved = lax.ppermute(kept, "blk", xor_pairs(blocks, 1))
        kept = jnp.where(lax.axis_index("head") == 0, kept, moved)
    else:
        kept = lax.dynamic_slice_in_dim(kept, lax.axis_index("head") * columns, columns, 1)
        arrived = lax.psum_scatter(leaving, "head", scatter_dimension=1, tiled=True)
    return kept + arrived.astype(f32)


def solution(mesh):
    in_specs = (
        P("blk", None),
        P(),
        P(),
        P(None, None, "head"),
        P("head", None),
        P(None, "head"),
        P("head", None),
        P(None, "head"),
        P(),
        P("blk", None, "head"),
        P("blk", None, "head"),
        P(),
        P("blk"),
        P("blk"),
    )
    out_specs = P("blk", "head")
    return jax.shard_map(
        per_device, mesh=mesh, in_specs=in_specs, out_specs=out_specs, check_vma=False
    )
```

```python
import functools

import jax
import jax.numpy as jnp
from jax import lax
from jax.experimental import pallas as pl
from jax.experimental.pallas import tpu as pltpu
from jax.sharding import PartitionSpec as P

HEAD_DIM = 64
PAGE = 128
LANES = 128

far_below = -1e30
epsilon = 1e-06

VMEM_SPEC = pl.BlockSpec(memory_space=pltpu.VMEM)
SMEM_SPEC = pl.BlockSpec(memory_space=pltpu.SMEM)
ANY_SPEC = pl.BlockSpec(memory_space=pl.ANY)
HBM_SPEC = pl.BlockSpec(memory_space=pltpu.HBM)
PARAMS = pltpu.CompilerParams(vmem_limit_bytes=16 * 1024 * 1024)

PIECE = 8
SUM_LANE = 3 * PIECE


def iota(shape, axis):
    return lax.broadcasted_iota(jnp.int32, shape, axis)


def split_index(x, size):
    if size & (size - 1):
        return lax.div(x, size), lax.rem(x, size)
    return x >> (size.bit_length() - 1), x & (size - 1)


def head_of(shape, axis):
    return split_index(iota(shape, axis), HEAD_DIM)[0]


def pieces(x, count):
    parts = []
    for _ in range(count):
        part = x.astype(jnp.bfloat16)
        parts.append(part)
        x = x - part.astype(jnp.float32)
    return parts


def rms_normed(x, gain):
    scale = lax.rsqrt(jnp.mean(x * x, axis=1, keepdims=True) + epsilon)
    return (x * scale * gain).astype(jnp.bfloat16)


def dot(a, b, dims=((1,), (0,)), precision=None):
    return lax.dot_general(
        a, b, (dims, ((), ())), preferred_element_type=jnp.float32, precision=precision
    )


def split_copies(source, target, sems, count):
    size = source.shape[0] // count
    return [
        pltpu.make_async_copy(
            source.at[pl.ds(i * size, size)], target.at[pl.ds(i * size, size)], sems.at[i]
        )
        for i in range(count)
    ]


def query_kernel(hidden_hbm, gain_hbm, weight_hbm, query_ref, hidden, gain, weight, sems):
    model = hidden.shape[1]
    small = [
        pltpu.make_async_copy(hidden_hbm, hidden, sems.at[0]),
        pltpu.make_async_copy(gain_hbm, gain, sems.at[1]),
    ]
    half = model // 4
    large = [
        pltpu.make_async_copy(
            weight_hbm.at[0, pl.ds(i * half, half)], weight.at[pl.ds(i * half, half)], sems.at[2 + i]
        )
        for i in range(4)
    ]
    for copy in small + large:
        copy.start()
    for copy in small:
        copy.wait()
    normed = rms_normed(hidden[...], gain[...])
    query = None
    for i, copy in enumerate(large):
        copy.wait()
        span = slice(i * half, (i + 1) * half)
        part = dot(normed[:, span], weight[span])
        query = part if query is None else query + part
    query_ref[...] = query.astype(jnp.bfloat16)


def page_kernel(
    own_rows, inner, outer, swapped, query_ref, request_ref, keys_hbm,
    keys_ref, pick_ref, place_ref, lead_ref, apart_ref, owners_ref,
    sems,
):
    copies = split_copies(
        keys_hbm.at[pl.ds(0, keys_ref.shape[0])], keys_ref, sems, sems.shape[0]
    )
    for copy in copies:
        copy.start()
    me = lax.axis_index("blk")
    page_count = apart_ref.shape[0]
    all_rows, depth = place_ref.shape
    page, lane = iota((page_count, page_count), 0), iota((page_count, page_count), 1)
    by_lane = request_ref[...]
    owner = jnp.max(jnp.where(page == lane, by_lane, -1), axis=1, keepdims=True)
    same = by_lane == owner
    apart_ref[...] = jnp.full(apart_ref.shape, 2 * far_below, jnp.float32)
    apart_ref[:, :page_count] = jnp.where(same, 0.0, 2 * far_below)
    earlier = jnp.max(jnp.where(same & (lane < page), 1, 0), axis=1, keepdims=True)
    lead_ref[...] = jnp.broadcast_to(jnp.where(earlier == 0, 1.0, 0.0), lead_ref.shape)
    owners_ref[...] = jnp.broadcast_to(owner, owners_ref.shape)
    device, own_row = split_index(jnp.maximum(owner, 0), own_rows)

    def slot_of(device, backwards):
        high, low = split_index(device ^ me, inner)
        low = jnp.where(high == 0, low, low ^ 1)
        low = -(low ^ (low >> 1)) & (inner - 1)
        high = -high & (outer - 1) if backwards else high
        slot = (low * outer + high) * own_rows + own_row
        return jnp.where(owner >= 0, slot, -1)

    slot = slot_of(device, True)
    sum_slot = slot_of(device ^ lax.axis_index("head") if swapped else device, False)
    row_of = iota((page_count, all_rows), 1)
    picks = jnp.where(row_of == slot, 1.0, 0.0)
    picks = [jnp.broadcast_to(picks[p : p + 1], (PIECE, all_rows)) for p in range(page_count)]
    pick_ref[...] = jnp.concatenate(picks, axis=0).astype(jnp.bfloat16)
    mine = split_index(iota((page_count, depth), 1), PIECE)[0] == iota((page_count, depth), 0)
    row = iota((all_rows, depth), 0)
    spread = jnp.max(jnp.where(mine, sum_slot, -1), axis=0, keepdims=True)
    place_ref[...] = (row == spread).astype(jnp.bfloat16)
    for copy in copies:
        copy.wait()


def bias_kernel(
    table_hbm, edges_hbm, lengths_hbm, index_hbm, owners_ref, keys_hbm, after_ref,
    keys_ref, bias_ref,
    table, edges, lengths, index, small_sems, sems,
):
    sources, targets = (table_hbm, edges_hbm, lengths_hbm, index_hbm), (table, edges, lengths, index)
    small = [
        pltpu.make_async_copy(source, target, small_sems.at[i])
        for i, (source, target) in enumerate(zip(sources, targets))
    ]
    late = keys_ref.shape[0]
    copies = split_copies(
        keys_hbm.at[pl.ds(keys_hbm.shape[0] - late, late)], keys_ref, sems, sems.shape[0]
    )
    for copy in small + copies:
        copy.start()
    for copy in small:
        copy.wait()
    heads, buckets = table.shape
    page_count = index.shape[1]
    owner = owners_ref[:, 0:1]
    square = (page_count, page_count)
    number = jnp.where(iota(square, 0) == iota(square, 1), index[...], 0)
    number = jnp.sum(number, axis=1, keepdims=True)
    requests = lengths.shape[1]
    length = jnp.where(iota((page_count, requests), 1) == owner, lengths[...], 0)
    length = jnp.sum(length, axis=1, keepdims=True)
    distance = length - number * PAGE - iota((page_count, PAGE), 1)
    far = [distance >= edges[k] for k in range(buckets - 1)]
    usable = (owner >= 0) & (distance > 0)
    bias_ref[...] = jnp.full(bias_ref.shape, far_below, jnp.float32)
    for h in range(heads):
        bias = jnp.full((page_count, PAGE), table[h, 0], jnp.float32)
        for k in range(buckets - 1):
            bias = jnp.where(far[k], table[h, k + 1], bias)
        bias_ref[pl.ds(h, page_count, stride=PIECE), :] = jnp.where(usable, bias, far_below)
    for copy in copies:
        copy.wait()


def side_kernel(
    hidden_ref, gain_ref, query_ref, table_ref, weight_hbm, out_hbm, after_ref,
    fresh_ref, out_ref, spread_ref,
    weight, weight_sems, sems,
):
    copies = [
        pltpu.make_async_copy(weight_hbm.at[1 + i], weight.at[i], weight_sems.at[i])
        for i in range(2)
    ]
    later = split_copies(out_hbm, out_ref, sems, sems.shape[0])
    for copy in copies + later:
        copy.start()
    normed = rms_normed(hidden_ref[...], gain_ref[...])
    heads = table_ref.shape[0]
    spread = iota((heads, LANES), 0) == iota((heads, LANES), 1)
    score = jnp.sum(jnp.where(spread, table_ref[:, 0:1], 0.0), axis=0, keepdims=True)
    copies[0].wait()
    key = dot(normed, weight[0]).astype(jnp.bfloat16)
    product = query_ref[...].astype(jnp.float32) * key.astype(jnp.float32)
    width = product.shape[1]
    gather = (head_of((width, LANES), 0) == iota((width, LANES), 1)).astype(jnp.bfloat16)
    for part in pieces(product, 2):
        score = score + dot(part, gather)
    lane = iota(score.shape, 1)
    used = width // HEAD_DIM
    peak = jnp.where(lane < used, score, 0.0)
    total = jnp.where((lane >= SUM_LANE) & (lane < SUM_LANE + used), 1.0, 0.0)
    fresh_ref[:, width:] = packed_stats(peak, total)
    spread = (iota((LANES, width), 0) == head_of((LANES, width), 1)).astype(jnp.bfloat16)
    spread_ref[:LANES] = spread
    spread_ref[LANES:] = spread
    copies[1].wait()
    fresh_ref[:, :width] = dot(normed, weight[1]).astype(jnp.bfloat16)
    for copy in later:
        copy.wait()


def load_kernel(start, source, after_ref, target, sems):
    rows = source.at[pl.ds(start, target.shape[0])]
    copies = split_copies(rows, target, sems, sems.shape[0])
    for copy in copies:
        copy.start()
    for copy in copies:
        copy.wait()


def packed_stats(peaks, sums):
    one, two, three = (part.astype(jnp.float32) for part in pieces(peaks + sums, 3))
    packed = one + pltpu.roll(two, PIECE, 1) + pltpu.roll(three, 2 * PIECE, 1)
    return packed.astype(jnp.bfloat16)


def unpacked_stats(packed, heads):
    stats = packed.astype(jnp.float32)
    stats = stats + pltpu.roll(stats, LANES - PIECE, 1) + pltpu.roll(stats, LANES - 2 * PIECE, 1)
    sums = pltpu.roll(stats, LANES - SUM_LANE, 1)
    used = iota(stats.shape, 1) < heads
    return jnp.where(used & (sums > 0.0), stats, far_below), jnp.where(used, sums, 0.0)


def over_columns(values, spread):
    return dot(jnp.concatenate(pieces(values, 2), axis=1), spread)


def attend_kernel(groups, *refs):
    query_refs, refs, sums_refs = refs[:groups], refs[groups:-groups], refs[-groups:]
    bias_ref, pick_ref, place_ref, lead_ref, apart_ref, keys_ref, late_ref, values_ref = refs
    page_count = apart_ref.shape[0]
    width = keys_ref.shape[2]
    early = keys_ref.shape[0]
    chunk = 2
    chunks = page_count // chunk
    queries = jnp.concatenate([ref[...] for ref in query_refs], axis=0)
    own_head = (head_of((PIECE, width), 1) == iota((PIECE, width), 0)).astype(jnp.float32)
    pair_heads = jnp.concatenate([own_head] * chunk, axis=0)
    chosen = dot(pick_ref[...], queries)
    lane = iota((PIECE, LANES), 1)
    row = iota((PIECE, LANES), 0)
    nothing = jnp.zeros((PIECE, PAGE), jnp.float32)
    raws = []
    for c in range(chunks):
        rows = chosen[c * chunk * PIECE : (c + 1) * chunk * PIECE]
        split = rows.astype(jnp.bfloat16) * pair_heads.astype(jnp.bfloat16)
        at = c * chunk
        block = keys_ref[at : at + chunk] if at < early else late_ref[at - early : at - early + chunk]
        raws.append(dot(split, block.reshape(chunk * PAGE, width), ((1,), (1,))))
    scores, page_tops = [], []
    for p in range(page_count):
        i = p % chunk
        part = raws[p // chunk][i * PIECE : (i + 1) * PIECE, i * PAGE : (i + 1) * PAGE]
        score = part + bias_ref[p * PIECE : (p + 1) * PIECE]
        scores.append(score)
        page_tops.append(jnp.max(score, axis=1, keepdims=True))
    page_weights = [jnp.exp(score - top) for score, top in zip(scores, page_tops)]
    mixes = []
    for c in range(chunks):
        blocks = []
        for i in range(chunk):
            weight = page_weights[c * chunk + i]
            blocks.append(
                jnp.concatenate([weight if k == i else nothing for k in range(chunk)], axis=1)
            )
        weights = jnp.concatenate(blocks, axis=0).astype(jnp.bfloat16)
        block = values_ref[c * chunk : (c + 1) * chunk]
        mixes.append(dot(weights, block.reshape(chunk * PAGE, width)))
    totals = [jnp.sum(weight, axis=1, keepdims=True) for weight in page_weights]
    tops = jnp.zeros((PIECE, LANES), jnp.float32)
    for p in range(page_count):
        tops = jnp.where(lane == p, page_tops[p], tops)
    stats = []
    for c in range(chunks):
        factors = []
        for p in range(c * chunk, (c + 1) * chunk):
            peak = jnp.max(tops + apart_ref[p : p + 1], axis=1, keepdims=True)
            factor = jnp.exp(page_tops[p] - peak)
            total = jnp.where(lane == row + SUM_LANE, totals[p] * factor, 0.0)
            stats.append(jnp.where(lane == row, peak * lead_ref[p : p + 1], total))
            factors.append(factor)
        mixes[c] = mixes[c] * (pair_heads * jnp.concatenate(factors, axis=0))
    mix = jnp.concatenate(mixes, axis=0).astype(jnp.bfloat16)
    stats = pieces(jnp.concatenate(stats, axis=0), 3)
    sums = dot(place_ref[...], jnp.concatenate([mix] + stats, axis=1))
    stats = sum(sums[:, width + i * LANES : width + (i + 1) * LANES] for i in range(3))
    stats = packed_stats(stats, 0.0).astype(jnp.float32)
    size = sums.shape[0] // groups
    for i, sums_ref in enumerate(sums_refs):
        first, middle, last = i * size, i * size + size // 2, (i + 1) * size
        for c in range(width // LANES):
            block = sums[first:last, c * LANES : (c + 1) * LANES]
            sums_ref[c * size : (c + 1) * size] = block.astype(jnp.bfloat16)
        both = stats[first:middle] + pltpu.roll(stats[middle:last], LANES // 2, 1)
        sums_ref[width // LANES * size :] = both.astype(jnp.bfloat16)


def combine_kernel(sources, *refs):
    part_refs, spread_ref, sums_refs = refs[:sources], refs[sources], refs[sources + 1 :]
    width = spread_ref.shape[1]
    rows = sum(ref.shape[0] for ref in sums_refs)
    heads, blocks = width // HEAD_DIM, width // LANES
    stats, mixes = [], []
    for ref in part_refs:
        both = ref[blocks * rows :].astype(jnp.float32)
        both = jnp.concatenate([both, pltpu.roll(both, LANES // 2, 1)], axis=0)
        stats.append(unpacked_stats(both, heads))
        mix = [ref[c * rows : (c + 1) * rows] for c in range(blocks)]
        mixes.append(jnp.concatenate(mix, axis=1).astype(jnp.float32))
    peak = stats[0][0]
    for peaks, _ in stats[1:]:
        peak = jnp.maximum(peak, peaks)
    factors = [jnp.exp(peaks - peak) for peaks, _ in stats]
    total = sum(factor * sums for factor, (_, sums) in zip(factors, stats))
    shares = over_columns(jnp.concatenate(factors, axis=0), spread_ref[...])
    mixed = sum(mix * shares[i * rows : (i + 1) * rows] for i, mix in enumerate(mixes))
    packed = packed_stats(
        jnp.where(total > 0.0, peak, 0.0), pltpu.roll(total, SUM_LANE, 1)
    ).astype(jnp.float32)
    size = sums_refs[0].shape[0]
    for i, sums_ref in enumerate(sums_refs):
        span = slice(i * size, (i + 1) * size)
        sums_ref[:, :width] = mixed[span].astype(jnp.bfloat16)
        sums_ref[:, width:] = packed[span].astype(jnp.bfloat16)


def merge_kernel(
    swapped, sources, hidden_ref, fresh_ref, moved_ref, weight_ref, spread_ref, *refs
):
    part_refs, (own_ref, send_ref) = refs[:sources], refs[sources:]
    width = fresh_ref.shape[1] - LANES
    heads = width // HEAD_DIM
    parts = [ref[...].astype(jnp.float32) for ref in part_refs]
    fresh = fresh_ref[...].astype(jnp.float32)
    if swapped:
        first = lax.axis_index("head") == 0
        fresh = jnp.where(first, fresh, moved_ref[...].astype(jnp.float32))
    parts.append(fresh)
    stats = [unpacked_stats(part[:, width:], heads) for part in parts]
    peak = stats[0][0]
    for peaks, _ in stats[1:]:
        peak = jnp.maximum(peak, peaks)
    factors = [jnp.exp(peaks - peak) for peaks, _ in stats]
    total = sum(factor * sums for factor, (_, sums) in zip(factors, stats))
    total = jnp.where(total > 0.0, total, 1.0)
    shares = jnp.concatenate([f / total for f in factors], axis=0)
    shares = over_columns(shares, spread_ref[...])
    rows = fresh_ref.shape[0]
    mixed = sum(
        part[:, :width] * shares[i * rows : (i + 1) * rows] for i, part in enumerate(parts)
    )
    projected = dot(mixed.astype(jnp.bfloat16), weight_ref[...])
    if swapped:
        projected = projected + jnp.where(first, hidden_ref[...], 0.0)
        own_ref[...] = projected
    else:
        own_ref[...] = hidden_ref[...]
    send_ref[...] = projected.astype(jnp.bfloat16)


def mlp_kernel(
    exchanged, own_ref, other_ref, gain_ref, up_ref, down_ref, late_ref, *outs
):
    own = own_ref[...]
    middle = own + other_ref[...].astype(jnp.float32)
    normed = rms_normed(middle, gain_ref[...])
    active = jnp.maximum(dot(normed, up_ref[...]), 0.0).astype(jnp.bfloat16)
    half = down_ref.shape[0]
    down = dot(active[:, :half], down_ref[...]) + dot(active[:, half:], late_ref[...])
    if exchanged:
        kept_ref, sent_ref = outs
        columns = kept_ref.shape[1]
        low = lax.axis_index("head") == 0
        left, right = slice(0, columns), slice(columns, 2 * columns)
        kept = middle + down
        down = down + (own - own.astype(jnp.bfloat16).astype(jnp.float32))

        @pl.when(low)
        def _():
            kept_ref[...] = kept[:, left]
            sent_ref[...] = down[:, right]

        @pl.when(jnp.logical_not(low))
        def _():
            kept_ref[...] = kept[:, right]
            sent_ref[...] = down[:, left]

    else:
        middle_ref, down_out_ref = outs
        middle_ref[...] = middle
        down_out_ref[...] = down.astype(jnp.bfloat16)


def loading(*arrays):
    return pl.CostEstimate(
        flops=0, bytes_accessed=sum(2 * array.size for array in arrays), transcendentals=0
    )


def in_hbm(*arrays):
    return [pltpu.with_memory_space_constraint(array, pltpu.HBM) for array in arrays]


def xor_pairs(size, step):
    return [(i, i ^ step) for i in range(size)]


def per_device(
    hidden_in, attention_gain, mlp_gain, qkv_weight, out_weight, up_weight, down_weight,
    position_bias, bucket_edges, cache_keys, cache_values, lengths, page_request, page_index,
):
    f32, bf16 = jnp.float32, jnp.bfloat16
    shape = jax.ShapeDtypeStruct
    own_rows, model = hidden_in.shape
    width = qkv_weight.shape[2]
    page_count = page_request.shape[0]
    blocks = lax.axis_size("blk")
    all_rows = own_rows * blocks
    halves = lax.axis_size("head")
    columns = model // halves
    exchanged = halves == 2
    gain = attention_gain.reshape(1, model)
    query = pl.pallas_call(
        query_kernel,
        out_shape=shape((own_rows, width), bf16),
        in_specs=[HBM_SPEC] * 3,
        out_specs=VMEM_SPEC,
        scratch_shapes=[
            pltpu.VMEM((own_rows, model), f32),
            pltpu.VMEM((1, model), f32),
            pltpu.VMEM((model, width), bf16),
            pltpu.SemaphoreType.DMA((6,)),
        ],
        compiler_params=PARAMS,
        name="query",
    )(*in_hbm(hidden_in, gain, qkv_weight))

    inner = 1
    while inner * inner < blocks:
        inner *= 2
    far = [query] + [
        lax.ppermute(query, "blk", xor_pairs(blocks, step * inner ^ 1))
        for step in reversed(range(1, blocks // inner))
    ]
    depth = page_count * PIECE
    early = page_count // 6 * 2
    keys, picks, place, leads, apart, owners = pl.pallas_call(
        functools.partial(page_kernel, own_rows, inner, blocks // inner, exchanged),
        out_shape=(
            pltpu.VMEM((early,) + cache_keys.shape[1:], bf16),
            shape((depth, all_rows), bf16),
            shape((all_rows, depth), bf16),
            shape((page_count, LANES), f32),
            shape((page_count, LANES), f32),
            shape((page_count, LANES), jnp.int32),
        ),
        in_specs=[ANY_SPEC, VMEM_SPEC, HBM_SPEC],
        out_specs=(VMEM_SPEC,) * 6,
        scratch_shapes=[pltpu.SemaphoreType.DMA((4,))],
        compiler_params=PARAMS,
        cost_estimate=loading(cache_keys),
        name="pages",
    )(query, page_request.reshape(1, page_count), *in_hbm(cache_keys))
    near, apart = lax.optimization_barrier((jnp.concatenate(far, axis=0), apart))
    steps = sorted(range(inner), key=lambda step: -(step ^ (step >> 1)) & (inner - 1))
    gathered = [near] + [lax.ppermute(near, "blk", xor_pairs(blocks, step)) for step in steps[1:]]
    table = position_bias.T
    late_keys, bias = pl.pallas_call(
        bias_kernel,
        out_shape=(
            pltpu.VMEM((page_count - early,) + cache_keys.shape[1:], bf16),
            shape((depth, PAGE), f32),
        ),
        in_specs=[HBM_SPEC] * 4 + [VMEM_SPEC, HBM_SPEC, ANY_SPEC],
        out_specs=(VMEM_SPEC,) * 2,
        scratch_shapes=[
            pltpu.SMEM(table.shape, f32),
            pltpu.SMEM(bucket_edges.shape, jnp.int32),
            pltpu.VMEM((1,) + lengths.shape, jnp.int32),
            pltpu.VMEM((1,) + page_index.shape, jnp.int32),
            pltpu.SemaphoreType.DMA((4,)),
            pltpu.SemaphoreType.DMA((4,)),
        ],
        compiler_params=PARAMS,
        cost_estimate=loading(cache_values),
        name="bias",
    )(
        *in_hbm(table, bucket_edges, lengths[None], page_index[None]), owners,
        *in_hbm(cache_keys), near,
    )

    groups = len(gathered)
    size = all_rows // groups
    message = width // LANES * size + size // 2
    sums = pl.pallas_call(
        functools.partial(attend_kernel, groups),
        out_shape=(shape((message, LANES), bf16),) * groups,
        in_specs=[VMEM_SPEC] * (groups + 8),
        out_specs=(VMEM_SPEC,) * groups,
        compiler_params=PARAMS,
        name="attend",
    )(*gathered, bias, picks, place, leads, apart, keys, late_keys, cache_values)
    near_sums = [sums[0]] + [
        lax.ppermute(sums[i], "blk", xor_pairs(blocks, steps[i]))
        for i in range(1, inner)
    ]

    fresh, out_near, spread = pl.pallas_call(
        side_kernel,
        out_shape=(
            shape((own_rows, width + LANES), bf16),
            pltpu.VMEM(out_weight.shape, bf16),
            shape((2 * LANES, width), bf16),
        ),
        in_specs=[VMEM_SPEC] * 4 + [HBM_SPEC] * 2 + [ANY_SPEC],
        out_specs=(VMEM_SPEC,) * 3,
        scratch_shapes=[
            pltpu.VMEM((2, model, width), bf16),
            pltpu.SemaphoreType.DMA((2,)),
            pltpu.SemaphoreType.DMA((4,)),
        ],
        compiler_params=PARAMS,
        cost_estimate=loading(out_weight, out_weight, out_weight),
        name="side",
    )(
        hidden_in, gain, query, table,
        *in_hbm(qkv_weight, out_weight), sums[0],
    )

    *near_sums, fresh = lax.optimization_barrier((*near_sums, fresh))
    outer = blocks // inner
    sums = pl.pallas_call(
        functools.partial(combine_kernel, inner),
        out_shape=(shape((own_rows, width + LANES), bf16),) * outer,
        in_specs=[VMEM_SPEC] * (inner + 1),
        out_specs=(VMEM_SPEC,) * outer,
        compiler_params=PARAMS,
        name="combine",
    )(*near_sums, spread)
    units = down_weight.shape[0]
    cut = units // 8 * 3

    def load_down(start, stop, after):
        return pl.pallas_call(
            functools.partial(load_kernel, start),
            out_shape=pltpu.VMEM((stop - start, model), bf16),
            in_specs=[HBM_SPEC, ANY_SPEC],
            out_specs=VMEM_SPEC,
            scratch_shapes=[pltpu.SemaphoreType.DMA((4,))],
            compiler_params=PARAMS,
            cost_estimate=loading(down_weight),
            name="load",
        )(*in_hbm(down_weight), after)

    down_early = load_down(0, cut, sums[0])
    parts = [sums[0]] + [
        lax.ppermute(sums[step], "blk", xor_pairs(blocks, step * inner ^ 1))
        for step in reversed(range(1, outer))
    ]

    moved = lax.ppermute(fresh, "blk", xor_pairs(blocks, 1)) if exchanged else fresh
    *parts, down_early = lax.optimization_barrier((*parts, down_early))
    own_part, sent_part = pl.pallas_call(
        functools.partial(merge_kernel, exchanged, outer),
        out_shape=(
            shape((own_rows, model), f32),
            shape((own_rows, model), bf16),
        ),
        in_specs=[VMEM_SPEC] * (outer + 5),
        out_specs=(VMEM_SPEC,) * 2,
        compiler_params=PARAMS,
        name="merge",
    )(hidden_in, fresh, moved, out_near, spread, *parts)

    down_late = load_down(cut, units, sent_part)
    axes = ("head", "blk")
    across = [(i, blocks + (i ^ 1)) for i in range(blocks)]
    back = [(b, a) for a, b in across]
    if exchanged:
        other_part = lax.ppermute(sent_part, axes, across + back)
        mlp_out = (shape((own_rows, columns), f32), shape((own_rows, columns), f32))
    else:
        other_part = lax.psum(sent_part, "head")
        mlp_out = (shape((own_rows, model), f32), shape((own_rows, model), bf16))

    kept, leaving = pl.pallas_call(
        functools.partial(mlp_kernel, exchanged),
        out_shape=mlp_out,
        in_specs=[VMEM_SPEC] * 6,
        out_specs=(VMEM_SPEC,) * 2,
        compiler_params=PARAMS,
        name="mlp",
    )(own_part, other_part, mlp_gain.reshape(1, model), up_weight, down_early, down_late)

    if exchanged:
        straight = [(i, blocks + i) for i in range(blocks)]
        arrived = lax.ppermute(leaving, axes, straight + back)
        moved = lax.ppermute(kept, "blk", xor_pairs(blocks, 1))
        return arrived.astype(f32) + jnp.where(lax.axis_index("head") == 0, kept, moved)
    else:
        kept = lax.dynamic_slice_in_dim(kept, lax.axis_index("head") * columns, columns, 1)
        arrived = lax.psum_scatter(leaving, "head", scatter_dimension=1, tiled=True)
    return kept + arrived.astype(f32)


def solution(mesh):
    in_specs = (
        P("blk", None),
        P(),
        P(),
        P(None, None, "head"),
        P("head", None),
        P(None, "head"),
        P("head", None),
        P(None, "head"),
        P(),
        P("blk", None, "head"),
        P("blk", None, "head"),
        P(),
        P("blk"),
        P("blk"),
    )
    out_specs = P("blk", "head")
    return jax.shard_map(
        per_device, mesh=mesh, in_specs=in_specs, out_specs=out_specs, check_vma=False
    )
```
